32 devices in a mesh: fsdp: 2 (over core), expert: 16 (over z, y, x).
Axes of the slice: x: 2, y: 2, z: 4, core: 2. Of those that a mesh axis runs over, the one named last changes fastest.
Arguments:
- tokens: bfloat16 [16, 384, 2048], P('expert', 'fsdp'), may hold values from -6 to 6
- segments: int32 [16, 384], P('expert'), may hold values from 0 to 1, as said below
- routes: int32 [16, 384, 6], P('expert', 'fsdp'), may hold values from 0 to 15, as said below
- slot_index: int32 [16, 384, 6], P('expert', 'fsdp'), may hold values from -1 to 71, as said below
- cotangent: bfloat16 [16, 384, 2048], P('expert', 'fsdp'), may hold values from -6 to 6
- attention_norm: bfloat16 [2048], P(('fsdp', 'expert')), may hold values from 0.5 to 1.5
- query_weight: bfloat16 [2048, 3072], P(('fsdp', 'expert')), may hold values from -0.1875 to 0.1875
- latent_down: bfloat16 [2048, 576], P(('fsdp', 'expert')), may hold values from -0.125 to 0.125
- latent_norm: bfloat16 [512], P(('fsdp', 'expert')), may hold values from 0.5 to 1.5
- latent_up: bfloat16 [512, 4096], P(('fsdp', 'expert')), may hold values from -0.25 to 0.25
- output_weight: bfloat16 [2048, 2048], P(('fsdp', 'expert')), may hold values from -0.5 to 0.5
- feed_norm: bfloat16 [2048], P(('fsdp', 'expert')), may hold values from 0.5 to 1.5
- router_weight: bfloat16 [2048, 16], P(('fsdp', 'expert')), may hold values from -0.0625 to 0.0625
- shared_gate: bfloat16 [2048, 2816], P(('fsdp', 'expert')), may hold values from -0.125 to 0.125
- shared_up: bfloat16 [2048, 2816], P(('fsdp', 'expert')), may hold values from -0.125 to 0.125
- shared_down: bfloat16 [2816, 2048], P(('fsdp', 'expert')), may hold values from -0.15625 to 0.15625
- expert_gate: bfloat16 [16, 2048, 1408], P('expert', 'fsdp'), may hold values from -0.125 to 0.125
- expert_up: bfloat16 [16, 2048, 1408], P('expert', 'fsdp'), may hold values from -0.125 to 0.125
- expert_down: bfloat16 [16, 1408, 2048], P('expert', None, 'fsdp'), may hold values from -6 to 6
Outputs:
- output: bfloat16 [16, 384, 2048], P('expert', 'fsdp')
- token_grad: float32 [16, 384, 2048], P('expert', 'fsdp')
- grad_attention_norm: float32 [2048], P(('fsdp', 'expert'))
- grad_query_weight: float32 [2048, 3072], P(('fsdp', 'expert'))
- grad_latent_down: float32 [2048, 576], P(('fsdp', 'expert'))
- grad_latent_norm: float32 [512], P(('fsdp', 'expert'))
- grad_latent_up: float32 [512, 4096], P(('fsdp', 'expert'))
- grad_output_weight: float32 [2048, 2048], P(('fsdp', 'expert'))
- grad_feed_norm: float32 [2048], P(('fsdp', 'expert'))
- grad_router_weight: float32 [2048, 16], P(('fsdp', 'expert'))
- grad_shared_gate: float32 [2048, 2816], P(('fsdp', 'expert'))
- grad_shared_up: float32 [2048, 2816], P(('fsdp', 'expert'))
- grad_shared_down: float32 [2816, 2048], P(('fsdp', 'expert'))
- grad_expert_gate: float32 [16, 2048, 1408], P('expert', 'fsdp')
- grad_expert_up: float32 [16, 2048, 1408], P('expert', 'fsdp')
- grad_expert_down: float32 [16, 1408, 2048], P('expert', None, 'fsdp')
The draws below stay inside these ranges and needn't reach their ends.
Inputs may be any that keep to these rules, and one draw needn't show every extreme that they name: `segments`: each sequence holds two documents: document 0 from its first token up to a place after token 192, and document 1, cut at the sequence's end, after it. The numbers never change between token k * 192 - 1 and token k * 192. `routes`: each token names 6 different experts. `slot_index`: for the rows of one device (192 tokens in a row, pairs taken token by token, then in route order), a pair's slot is the number of earlier pairs naming the same expert if that is below 72, else -1. In every draw some expert has all 72 slots filled on every device.
All inputs are finite; a program needn't handle non-finite values.
Results may differ from the reference program's by a relative error of at most 0.023.
Values may be sent and summed in bfloat16 or wider, within the bound.
A program may use at most 384 MiB of HBM per device.

```python
import math
import jax
import jax.numpy as jnp
from jax import lax

D = 2048
HEADS = 16
NOPE = 128
ROPE = 64
VALUE = 128
LATENT = 512
FFE = 1408
FFS = 2816
TOPK = 6
TOK_DEV = 192
EXPERTS = 16
SEQ = 384
SEQS = 16
TOKENS = 6144
CAP = 72


def route_table(key):
    hot_key, noise_key, order_key, star_key = jax.random.split(key, 4)
    blocks = TOKENS // TOK_DEV
    expert_ids = jnp.arange(EXPERTS, dtype=jnp.int32)
    favour = jax.random.randint(hot_key, (EXPERTS,), 0, 2) * 65536
    noise = jax.random.randint(noise_key, (TOKENS, EXPERTS), 0, 1048576)
    star = jax.random.randint(star_key, (), 0, EXPERTS)
    orders = jax.vmap(lambda sub_key: jax.random.permutation(sub_key, TOK_DEV))(jax.random.split(order_key, blocks))
    forced = (orders < 2 * CAP).reshape(TOKENS, 1)
    boost = jnp.where(forced & (expert_ids[None, :] == star), 4194304, 0)
    score = (noise + favour[None, :] + boost) * EXPERTS + expert_ids[None, :]
    chosen = lax.top_k(score, TOPK)[1].astype(jnp.int32)
    pair_hits = (chosen.reshape(blocks, TOK_DEV * TOPK, 1) == expert_ids[None, None, :]).astype(jnp.int32)
    ranks = jnp.sum((jnp.cumsum(pair_hits, axis=1) - 1) * pair_hits, axis=-1)
    placed = jnp.where(ranks < CAP, ranks, -1).astype(jnp.int32)
    return (chosen.reshape(SEQS, SEQ, TOPK), placed.reshape(SEQS, SEQ, TOPK))


def draw_routes(key, part):
    table = route_table(key)
    return table[0]


def draw_slot_index(key, part):
    table = route_table(key)
    return table[1]


def draw_segments(key, part):
    key = jax.random.fold_in(key, 7)
    places = jnp.arange(SEQ, dtype=jnp.int32)
    starts = jax.random.randint(key, (SEQS,), TOK_DEV + TOK_DEV // 4, SEQ - TOK_DEV // 4)
    return (places[None, :] >= starts[:, None]).astype(jnp.int32)


def levels(rng, extent, pieces, least, largest):
    def one(axis_at, blocks):
        heights = jax.random.uniform(jax.random.fold_in(jax.random.fold_in(rng, 6), axis_at), (blocks,), jnp.float32, least / len(pieces), largest / len(pieces))
        return jnp.repeat(jnp.exp(heights), extent[axis_at] // blocks).reshape((-1,) + (1,) * (len(extent) - axis_at - 1))

    level = one(*pieces[0])
    for cut in pieces[1:]:
        level = level * one(*cut)
    return level


def gaussian(rng, shape, spread, most, pieces=(), held_as=jnp.bfloat16):
    factor_of = levels(rng, shape, pieces, -0.22, 0.18) if pieces else 1.0
    result = jax.random.normal(rng, shape, jnp.float32) * spread * factor_of
    return jnp.minimum(jnp.maximum(result, -most), most).astype(held_as)


def setup_inputs(seed: int = 0) -> dict:
    splits = jax.random.split(jax.random.key(seed), 20)
    return {
        "tokens": gaussian(splits[0], (SEQS, SEQ, D), 1.0, 6.0, ((0, 16), (1, 2))),
        "segments": draw_segments(jax.random.fold_in(splits[19], 71), 0),
        "routes": draw_routes(jax.random.fold_in(splits[19], 71), 0),
        "slot_index": draw_slot_index(jax.random.fold_in(splits[19], 71), 0),
        "cotangent": gaussian(splits[4], (SEQS, SEQ, D), 1.0, 6.0, ((0, 16), (1, 2))),
        "attention_norm": jnp.clip(1.0 + 0.1 * jax.random.normal(splits[5], (D,), jnp.float32), 0.5, 1.5).astype(jnp.bfloat16),
        "query_weight": gaussian(splits[6], (D, HEADS * (NOPE + ROPE)), (D // 2) ** -0.5, 0.1875, ((0, 32),)),
        "latent_down": gaussian(splits[7], (D, LATENT + ROPE), D ** -0.5, 0.125, ((0, 32),)),
        "latent_norm": jnp.clip(1.0 + 0.1 * jax.random.normal(splits[8], (LATENT,), jnp.float32), 0.5, 1.5).astype(jnp.bfloat16),
        "latent_up": gaussian(splits[9], (LATENT, HEADS * (NOPE + VALUE)), LATENT ** -0.5, 0.25, ((0, 32),)),
        "output_weight": gaussian(splits[10], (HEADS * VALUE, D), (HEADS * VALUE // 16) ** -0.5, 0.5, ((0, 32),)),
        "feed_norm": jnp.clip(1.0 + 0.1 * jax.random.normal(splits[11], (D,), jnp.float32), 0.5, 1.5).astype(jnp.bfloat16),
        "router_weight": gaussian(splits[12], (D, EXPERTS), (4 * D) ** -0.5, 0.0625, ((0, 32),)),
        "shared_gate": gaussian(splits[13], (D, FFS), D ** -0.5, 0.125, ((0, 32),)),
        "shared_up": gaussian(splits[14], (D, FFS), D ** -0.5, 0.125, ((0, 32),)),
        "shared_down": gaussian(splits[15], (FFS, D), (FFS // 2) ** -0.5, 0.15625, ((0, 32),)),
        "expert_gate": gaussian(splits[16], (EXPERTS, D, FFE), D ** -0.5, 0.125, ((0, 16), (1, 2))),
        "expert_up": gaussian(splits[17], (EXPERTS, D, FFE), D ** -0.5, 0.125, ((0, 16), (1, 2))),
        "expert_down": gaussian(splits[18], (EXPERTS, FFE, D), 1.0, 6.0, ((0, 16), (2, 2))),
    }


EPSILON = 1e-06

@jax.custom_vjp
def low(v):
    return lax.optimization_barrier(v.astype(jnp.bfloat16)).astype(jnp.float32)

@jax.custom_vjp
def low_back(v):
    return v

def low_keep(v):
    return (low(v), None)

def low_pass(kept, grad):
    return (grad,)

def back_keep(v):
    return (v, None)

def back_low(kept, grad):
    return (low(grad),)
low.defvjp(low_keep, low_pass)
low_back.defvjp(back_keep, back_low)

def norm_rows(values, gain):
    return values * lax.rsqrt(lax.optimization_barrier(jnp.mean(values * values, axis=-1, keepdims=True)) + EPSILON) * gain

def rotary_table(row_total, offset, rope_width):
    frequency_steps = jnp.arange(rope_width // 2, dtype=jnp.float32)
    inverse = jnp.exp(frequency_steps * (-2.0 * math.log(10000.0) / rope_width))
    places = (offset + jnp.arange(row_total)).astype(jnp.float32)
    angles = places[:, None] * inverse[None, :]
    return (jnp.cos(angles), jnp.sin(angles))

def rotate_forward(values, cosine, sine_table):
    middle = values.shape[-1] // 2
    front_half = values[..., :middle]
    back_half = values[..., middle:]
    return jnp.concatenate([front_half * cosine - back_half * sine_table, back_half * cosine + front_half * sine_table], axis=-1)

def forward(tokens, attention_norm, query_weight, latent_down, latent_norm, latent_up, output_weight, feed_norm, router_weight, shared_gate, shared_up, shared_down, expert_gate, expert_up, expert_down, segments, routes, slot_index):
    highest = lax.Precision.HIGHEST
    cosine, sine_table = rotary_table(SEQ, 0, ROPE)
    position = jnp.arange(SEQ)
    causal = position[None, :] <= position[:, None]
    score_scale = (NOPE + ROPE) ** (-0.5)

    def attend(packed):
        inputs, segment_row = packed
        normed = low(norm_rows(inputs, attention_norm))
        query_raw = low_back(jnp.dot(normed, query_weight, precision=highest)).reshape(SEQ, HEADS, NOPE + ROPE)
        queries = low(jnp.concatenate([query_raw[..., :NOPE], rotate_forward(query_raw[..., NOPE:], cosine[:, None, :], sine_table[:, None, :])], axis=-1))
        compressed = low_back(jnp.dot(normed, latent_down, precision=highest))
        latent = low(norm_rows(compressed[:, :LATENT], latent_norm))
        key_rope = low(rotate_forward(compressed[:, LATENT:], cosine, sine_table))
        expanded = low(low_back(jnp.dot(latent, latent_up, precision=highest))).reshape(SEQ, HEADS, NOPE + VALUE)
        scores = jnp.einsum('qhd,khd->hqk', queries[..., :NOPE], expanded[..., :NOPE], precision=highest)
        scores = scores + jnp.einsum('qhd,kd->hqk', queries[..., NOPE:], key_rope, precision=highest)
        visible = causal & (segment_row[:, None] == segment_row[None, :])
        scores = low_back(jnp.where(visible[None], scores * score_scale, -1e+30))
        weights = low(jax.nn.softmax(scores, axis=-1))
        mixed_heads = low(low_back(jnp.einsum('hqk,khd->qhd', weights, expanded[..., NOPE:], precision=highest)))
        return low_back(jnp.dot(mixed_heads.reshape(SEQ, HEADS * VALUE), output_weight, precision=highest))
    attended = lax.map(jax.checkpoint(attend), (tokens, segments))
    flat_rows = (tokens + attended).reshape(TOKENS, D)
    normed = low(norm_rows(flat_rows, feed_norm))
    logits = low_back(jnp.dot(normed, router_weight, precision=highest))
    probabilities = jax.nn.softmax(logits, axis=-1)
    route_flat = routes.reshape(TOKENS, TOPK)
    slot_flat = slot_index.reshape(TOKENS, TOPK)
    gate_values = jnp.take_along_axis(probabilities, route_flat, axis=-1)
    kept_pairs = (slot_flat >= 0).astype(jnp.float32)
    buffer_rows = TOKENS // TOK_DEV * CAP
    source = (jnp.arange(TOKENS) // TOK_DEV)[:, None]
    target_row = jnp.where(slot_flat >= 0, source * CAP + slot_flat, buffer_rows).reshape(-1)
    pair_rows = low_back(jnp.repeat(normed, TOPK, axis=0))
    dispatched = jnp.zeros((EXPERTS, buffer_rows, D), jnp.float32).at[route_flat.reshape(-1), target_row].set(pair_rows, mode='drop')
    gate_part = low_back(jnp.einsum('pjh,phy->pjy', dispatched, expert_gate, precision=highest))
    up_portion = low_back(jnp.einsum('pjh,phy->pjy', dispatched, expert_up, precision=highest))
    hidden = low(jax.nn.silu(gate_part) * up_portion)
    returned = low(low_back(jnp.einsum('erf,efd->erd', hidden, expert_down, precision=highest)))
    gathered = returned[route_flat.reshape(-1), jnp.minimum(target_row, buffer_rows - 1)].reshape(TOKENS, TOPK, D)
    routed = lax.optimization_barrier(jnp.sum((gate_values * kept_pairs)[..., None] * gathered, axis=1))
    shared_gate_part = low_back(jnp.dot(normed, shared_gate, precision=highest))
    shared_up_part = low_back(jnp.dot(normed, shared_up, precision=highest))
    shared_hidden = low(jax.nn.silu(shared_gate_part) * shared_up_part)
    shared_out = low_back(jnp.dot(shared_hidden, shared_down, precision=highest))
    return (flat_rows + routed + shared_out).reshape(SEQS, SEQ, D)

def reference(tokens, segments, routes, slot_index, cotangent, attention_norm, query_weight, latent_down, latent_norm, latent_up, output_weight, feed_norm, router_weight, shared_gate, shared_up, shared_down, expert_gate, expert_up, expert_down):
    floats = [tokens, attention_norm, query_weight, latent_down, latent_norm, latent_up, output_weight, feed_norm, router_weight, shared_gate, shared_up, shared_down, expert_gate, expert_up, expert_down]
    floats = [array_value.astype(jnp.float32) for array_value in floats]

    def closed(*arrays):
        return forward(*arrays, segments, routes, slot_index)
    output, pullback = jax.vjp(closed, *floats)
    gradients = pullback(cotangent.astype(jnp.float32))
    return (output.astype(jnp.bfloat16), gradients[0], gradients[1], gradients[2], gradients[3], gradients[4], gradients[5], gradients[6], gradients[7], gradients[8], gradients[9], gradients[10], gradients[11], gradients[12], gradients[13], gradients[14])
```

```python
import math

import jax
import jax.numpy as jnp
from jax import lax
from jax.sharding import PartitionSpec as P

D = 2048
HEADS = 16
NOPE = 128
ROPE = 64
VALUE = 128
LATENT = 512
TOPK = 6


EPSILON = 1e-06
FLOOR_SCORE = -1e30


def passed_along(value, axis, steps):
    count = lax.axis_size(axis)
    first, last = (max(0, -steps), min(count, count - steps))
    return lax.ppermute(value, axis, [(source, source + steps) for source in range(first, last)])


def norm_rows(values, gain):
    return values * lax.rsqrt(jnp.mean(values * values, axis=-1, keepdims=True) + EPSILON) * gain


def norm_back(values, gain, incoming):
    primal_out, pullback = jax.vjp(norm_rows, values, gain)
    return pullback(incoming)


def swiglu_back(gate_part, up_portion, incoming):
    primal_out, pullback = jax.vjp(
        lambda former, latter: jax.nn.silu(former) * latter, gate_part, up_portion
    )
    return pullback(incoming)


def rotary_table(row_total, offset, rope_width):
    frequency_steps = jnp.arange(rope_width // 2, dtype=jnp.float32)
    inverse = jnp.exp(frequency_steps * (-2.0 * math.log(10000.0) / rope_width))
    places = (offset + jnp.arange(row_total)).astype(jnp.float32)
    angles = places[:, None] * inverse[None, :]
    return (jnp.cos(angles), jnp.sin(angles))


def rotate_forward(values, cosine, sine_table):
    middle = values.shape[-1] // 2
    front_half = values[..., :middle]
    back_half = values[..., middle:]
    return jnp.concatenate(
        [
            front_half * cosine - back_half * sine_table,
            back_half * cosine + front_half * sine_table,
        ],
        axis=-1,
    )


def rotate_backward(values, cosine, sine_table):
    middle = values.shape[-1] // 2
    front_half = values[..., :middle]
    back_half = values[..., middle:]
    return jnp.concatenate(
        [
            front_half * cosine + back_half * sine_table,
            back_half * cosine - front_half * sine_table,
        ],
        axis=-1,
    )


def matmul(former, latter):
    return jnp.dot(former, latter, preferred_element_type=jnp.float32)


def left_matmul(former, latter):
    return lax.dot_general(
        former, latter, (((0,), (0,)), ((), ())), preferred_element_type=jnp.float32
    )


def right_matmul(former, latter):
    return lax.dot_general(
        former, latter, (((1,), (1,)), ((), ())), preferred_element_type=jnp.float32
    )


def attention_scores(queries, expanded, keys_rope, visible, score_scale):
    scores = jnp.einsum(
        "qhd,khd->hqk",
        queries[..., :NOPE],
        expanded[..., :NOPE],
        preferred_element_type=jnp.float32,
    )
    scores = scores + jnp.einsum(
        "qhd,kd->hqk", queries[..., NOPE:], keys_rope, preferred_element_type=jnp.float32
    )
    return jnp.where(visible[None], scores * score_scale, FLOOR_SCORE)


PLANE = 4


def groups(count):
    lines = count // PLANE
    plane = [[row * PLANE + spot for spot in range(PLANE)] for row in range(lines)]
    line = [[row * PLANE + spot for row in range(lines)] for spot in range(PLANE)]
    return plane, line


def gather_all(value):
    part = lax.all_gather(value, "expert", axis=0, tiled=True)
    return lax.all_gather(part, "fsdp", axis=0, tiled=True)


def scatter_all(value):
    part = lax.psum_scatter(value, "fsdp", scatter_dimension=0, tiled=True)
    return lax.psum_scatter(part, "expert", scatter_dimension=0, tiled=True)


def body(
    tokens,
    segments,
    routes,
    slot_index,
    cotangent,
    attention_norm,
    query_weight,
    latent_down,
    latent_norm,
    latent_up,
    output_weight,
    feed_norm,
    router_weight,
    shared_gate,
    shared_up,
    shared_down,
    expert_gate,
    expert_up,
    expert_down,
):
    row_count = tokens.shape[1]
    expert_total = lax.axis_size("expert")
    depth = expert_total // PLANE
    plane, line = groups(expert_total)
    place = lax.axis_index("expert")
    level = place // PLANE
    device_half = lax.axis_index("fsdp")
    capacity = row_count * TOPK // expert_total
    line_rows = depth * row_count
    inputs = tokens[0].astype(jnp.float32)

    gain_width = attention_norm.shape[0]
    latent_width = latent_norm.shape[0]
    small = jnp.concatenate(
        [attention_norm, latent_norm, feed_norm, router_weight.reshape(-1)]
    )
    small_full = gather_all(small[None])
    cuts = [
        0,
        gain_width,
        gain_width + latent_width,
        2 * gain_width + latent_width,
        small.shape[0],
    ]
    gain_one, gain_latent, gain_feed, router_full = (
        small_full[:, cuts[0] : cuts[1]].reshape(-1),
        small_full[:, cuts[1] : cuts[2]].reshape(-1),
        small_full[:, cuts[2] : cuts[3]].reshape(-1),
        small_full[:, cuts[3] : cuts[4]].reshape(-1, expert_total),
    )
    down_full = gather_all(latent_down)
    query_full = gather_all(query_weight)
    up_full = gather_all(latent_up)
    output_full = gather_all(output_weight)

    route_rows = routes[0]
    slot_rows = slot_index[0]
    target = jnp.where(
        slot_rows >= 0, route_rows * capacity + slot_rows, expert_total * capacity
    )
    target_line = lax.all_gather(target, "expert", axis_index_groups=line, axis=0)
    grad_line = lax.all_gather(
        cotangent[0], "expert", axis_index_groups=line, axis=0, tiled=True
    )
    shared_width = shared_gate.shape[1] // (2 * depth)

    def columns_to_levels(weight):
        rows = weight.shape[0]
        pieces = weight.reshape(rows, 2, depth, shared_width).transpose(2, 0, 1, 3)
        moved = lax.all_to_all(
            pieces.reshape(depth, rows, 2 * shared_width),
            "expert",
            split_axis=0,
            concat_axis=0,
            axis_index_groups=line,
            tiled=True,
        )
        across = lax.all_gather(moved, "expert", axis_index_groups=plane, axis=0)
        whole = lax.all_gather(across, "fsdp", axis=0)
        return whole.transpose(0, 2, 1, 3, 4).reshape(-1, 2 * shared_width)

    sgate_full = columns_to_levels(shared_gate)
    sup_full = columns_to_levels(shared_up)
    sdown_full = lax.all_gather(
        lax.all_gather(shared_down, "expert", axis_index_groups=plane, axis=0, tiled=True),
        "fsdp",
        axis=0,
        tiled=True,
    )
    expert_gate_full = lax.all_gather(expert_gate[0], "fsdp", axis=0, tiled=True)
    expert_up_full = lax.all_gather(expert_up[0], "fsdp", axis=0, tiled=True)
    expert_down_full = lax.all_gather(expert_down[0], "fsdp", axis=1, tiled=True)

    slot_names = level * PLANE * capacity + jnp.arange(PLANE * capacity)
    hits = target_line[:, None, :, :] == slot_names[None, :, None, None]
    choose_rows = jnp.any(hits, axis=-1).astype(jnp.bfloat16)

    def to_experts(rows_line):
        placed = jnp.einsum(
            "zst,ztd->zsd",
            choose_rows,
            rows_line.reshape(depth, row_count, D),
            preferred_element_type=jnp.float32,
        ).astype(jnp.bfloat16)
        placed = placed.reshape(depth, PLANE, capacity, D).transpose(1, 0, 2, 3)
        return lax.all_to_all(
            placed, "expert", split_axis=0, concat_axis=0, axis_index_groups=plane, tiled=True
        ).reshape(expert_total * capacity, D)

    def from_experts(rows):
        return lax.all_to_all(
            rows.reshape(PLANE, depth, capacity, -1),
            "expert",
            split_axis=0,
            concat_axis=0,
            axis_index_groups=plane,
            tiled=True,
        )

    grad_rows = to_experts(grad_line)

    cosine, sine_table = rotary_table(row_count, device_half * row_count, ROPE)
    score_scale = (NOPE + ROPE) ** (-0.5)
    gain_first = gain_one.astype(jnp.float32)
    normed_low = norm_rows(inputs, gain_first).astype(jnp.bfloat16)
    query_raw = matmul(normed_low, query_full).reshape(row_count, HEADS, NOPE + ROPE)
    queries = jnp.concatenate(
        [
            query_raw[..., :NOPE],
            rotate_forward(query_raw[..., NOPE:], cosine[:, None, :], sine_table[:, None, :]),
        ],
        axis=-1,
    ).astype(jnp.bfloat16)
    compressed = matmul(normed_low, down_full)
    latent_gain = gain_latent.astype(jnp.float32)
    latent = norm_rows(compressed[:, :LATENT], latent_gain).astype(jnp.bfloat16)
    key_rope = rotate_forward(compressed[:, LATENT:], cosine, sine_table).astype(jnp.bfloat16)
    prior_latent, prior_rope = passed_along((latent, key_rope), "fsdp", 1)
    key_latent = jnp.concatenate([prior_latent, latent], axis=0)
    keys_rope = jnp.concatenate([prior_rope, key_rope], axis=0)
    expanded = (
        matmul(key_latent, up_full).astype(jnp.bfloat16).reshape(2 * row_count, HEADS, NOPE + VALUE)
    )
    query_place = device_half * row_count + jnp.arange(row_count)
    key_place = (device_half - 1) * row_count + jnp.arange(2 * row_count)
    padded_segments = jnp.concatenate([jnp.full((row_count,), -1, jnp.int32), segments[0]])
    key_segment = lax.dynamic_slice_in_dim(padded_segments, device_half * row_count, 2 * row_count)
    query_segment = lax.dynamic_slice_in_dim(segments[0], device_half * row_count, row_count)
    visible = (key_place[None, :] <= query_place[:, None]) & (
        key_segment[None, :] == query_segment[:, None]
    )
    scores = attention_scores(queries, expanded, keys_rope, visible, score_scale)
    top_score = jnp.max(scores, axis=-1, keepdims=True)
    log_total = top_score + jnp.log(jnp.sum(jnp.exp(scores - top_score), axis=-1, keepdims=True))
    weight_low = jnp.exp(scores - log_total).astype(jnp.bfloat16)
    mixed_heads = (
        jnp.einsum(
            "hqk,khd->qhd", weight_low, expanded[..., NOPE:], preferred_element_type=jnp.float32
        )
        .reshape(row_count, HEADS * VALUE)
        .astype(jnp.bfloat16)
    )
    residual = inputs + matmul(mixed_heads, output_full)
    feed_gain = gain_feed.astype(jnp.float32)
    mixed_low = norm_rows(residual, feed_gain).astype(jnp.bfloat16)
    mixed_line = lax.all_gather(mixed_low, "expert", axis_index_groups=line, axis=0, tiled=True)
    mixed_rows = to_experts(mixed_line)
    probabilities_line = jax.nn.softmax(matmul(mixed_line, router_full), axis=-1).reshape(
        depth, row_count, expert_total
    )
    level_probs = lax.dynamic_slice_in_dim(probabilities_line, level * PLANE, PLANE, axis=2)
    hit_weights = choose_rows.astype(jnp.float32).reshape(depth, PLANE, capacity, row_count)
    weighted = hit_weights * level_probs.transpose(0, 2, 1)[:, :, None, :]
    slot_gate = jnp.sum(weighted, axis=-1).transpose(1, 0, 2).reshape(PLANE, depth, capacity, 1)
    gate_column = from_experts(slot_gate).reshape(expert_total * capacity, 1)

    gate_part = matmul(mixed_rows, expert_gate_full)
    up_portion = matmul(mixed_rows, expert_up_full)
    hidden_wide = jax.nn.silu(gate_part) * up_portion
    hidden = hidden_wide.astype(jnp.bfloat16)
    expert_out = matmul(hidden, expert_down_full).astype(jnp.bfloat16)
    returned = from_experts(expert_out)
    slot_grad = jnp.sum(
        expert_out.astype(jnp.float32) * grad_rows.astype(jnp.float32), axis=-1, keepdims=True
    )
    slot_grad_back = from_experts(slot_grad)
    hidden_grad = right_matmul(grad_rows, expert_down_full) * gate_column
    gate_part_grad, up_part_grad = swiglu_back(gate_part, up_portion, hidden_grad)
    gate_low = gate_part_grad.astype(jnp.bfloat16)
    up_low = up_part_grad.astype(jnp.bfloat16)
    input_grad = (
        right_matmul(gate_low, expert_gate_full) + right_matmul(up_low, expert_up_full)
    ).astype(jnp.bfloat16)
    back_rows = from_experts(input_grad)
    hidden_scaled = (hidden.astype(jnp.float32) * gate_column).astype(jnp.bfloat16)
    egate_grad = left_matmul(mixed_rows, gate_low).astype(jnp.bfloat16)
    eup_grad = left_matmul(mixed_rows, up_low).astype(jnp.bfloat16)
    edown_grad = left_matmul(hidden_scaled, grad_rows).astype(jnp.bfloat16)
    expert_gate_piece, expert_up_piece, expert_down_piece = (
        lax.psum_scatter(egate_grad, "fsdp", scatter_dimension=0, tiled=True),
        lax.psum_scatter(eup_grad, "fsdp", scatter_dimension=0, tiled=True),
        lax.psum_scatter(edown_grad, "fsdp", scatter_dimension=1, tiled=True),
    )

    shared_gate_part = matmul(mixed_line, sgate_full)
    shared_up_part = matmul(mixed_line, sup_full)
    shared_hidden = (jax.nn.silu(shared_gate_part) * shared_up_part).astype(jnp.bfloat16)
    shared_out = matmul(shared_hidden, sdown_full)
    shared_hidden_grad = right_matmul(grad_line, sdown_full)
    shared_gate_grad, shared_up_grad = swiglu_back(
        shared_gate_part, shared_up_part, shared_hidden_grad
    )
    shared_gate_low = shared_gate_grad.astype(jnp.bfloat16)
    shared_up_low = shared_up_grad.astype(jnp.bfloat16)
    shared_back = right_matmul(shared_gate_low, sgate_full) + right_matmul(
        shared_up_low, sup_full
    )
    sdown_grad = left_matmul(shared_hidden, grad_line).astype(jnp.bfloat16)
    sgate_grad = left_matmul(mixed_line, shared_gate_low).astype(jnp.bfloat16)
    sup_grad = left_matmul(mixed_line, shared_up_low).astype(jnp.bfloat16)

    def scatter_plane(value):
        part = lax.psum_scatter(value, "fsdp", scatter_dimension=0, tiled=True)
        return lax.psum_scatter(
            part, "expert", scatter_dimension=0, axis_index_groups=plane, tiled=True
        )

    def levels_to_columns(weight):
        rows = D // (2 * expert_total)
        pieces = weight.reshape(2, depth, PLANE, rows, 2 * shared_width).transpose(0, 2, 1, 3, 4)
        summed = scatter_plane(pieces.reshape(2 * PLANE, depth, rows, 2 * shared_width))[0]
        moved = lax.all_to_all(
            summed, "expert", split_axis=0, concat_axis=0, axis_index_groups=line, tiled=True
        )
        return (
            moved.reshape(depth, rows, 2, shared_width)
            .transpose(1, 2, 0, 3)
            .reshape(rows, -1)
            .astype(jnp.float32)
        )

    sgate_piece = levels_to_columns(sgate_grad)
    sup_piece = levels_to_columns(sup_grad)
    sdown_piece = scatter_plane(sdown_grad).astype(jnp.float32)

    choose_weighted = (
        weighted.reshape(depth, PLANE * capacity, row_count).astype(jnp.bfloat16)
    )

    def combine(matrix, rows, add):
        gathered = rows.transpose(1, 0, 2, 3).reshape(depth, PLANE * capacity, D)
        mixed = jnp.einsum("zst,zsd->ztd", matrix, gathered, preferred_element_type=jnp.float32)
        total = (mixed.reshape(line_rows, D) + add).astype(jnp.bfloat16)
        return lax.psum_scatter(
            total, "expert", scatter_dimension=0, axis_index_groups=line, tiled=True
        ).astype(jnp.float32)

    routed_and_shared = combine(choose_weighted, returned, shared_out)
    back_and_shared = combine(choose_rows, back_rows, shared_back)
    output = (residual + routed_and_shared).astype(jnp.bfloat16)
    out_grad = cotangent[0].astype(jnp.float32)

    slot_grads = slot_grad_back.transpose(1, 0, 2, 3).reshape(depth, PLANE, capacity, 1)
    prob_part = jnp.sum(hit_weights * slot_grads, axis=2)
    prob_wide = lax.dynamic_update_slice_in_dim(
        jnp.zeros((depth, expert_total, row_count), jnp.float32), prob_part, level * PLANE, axis=1
    )
    prob_grad = lax.psum_scatter(
        prob_wide, "expert", scatter_dimension=0, axis_index_groups=line, tiled=True
    )[0].T
    probabilities = lax.dynamic_index_in_dim(probabilities_line, level, axis=0, keepdims=False)
    logit_low = (
        probabilities * (prob_grad - jnp.sum(probabilities * prob_grad, axis=-1, keepdims=True))
    ).astype(jnp.bfloat16)
    router_grad = left_matmul(mixed_low, logit_low)
    mixed_grad = right_matmul(logit_low, router_full) + back_and_shared
    residual_add, feed_gain_grad = norm_back(residual, feed_gain, mixed_grad)
    residual_grad = out_grad + residual_add
    attended_low = residual_grad.astype(jnp.bfloat16)
    output_grad = left_matmul(mixed_heads, attended_low)
    heads_low = (
        right_matmul(attended_low, output_full)
        .astype(jnp.bfloat16)
        .reshape(row_count, HEADS, VALUE)
    )
    scores_again = attention_scores(queries, expanded, keys_rope, visible, score_scale)
    probs_again = jnp.exp(scores_again - log_total)
    weights_again = probs_again.astype(jnp.bfloat16)
    weight_grad = jnp.einsum(
        "qhd,khd->hqk", heads_low, expanded[..., NOPE:], preferred_element_type=jnp.float32
    )
    value_grad = jnp.einsum(
        "hqk,qhd->khd", weights_again, heads_low, preferred_element_type=jnp.float32
    )
    delta_rows = jnp.sum(probs_again * weight_grad, axis=-1, keepdims=True)
    score_low = (probs_again * (weight_grad - delta_rows)).astype(jnp.bfloat16)
    query_nope_grad = (
        jnp.einsum(
            "hqk,khd->qhd", score_low, expanded[..., :NOPE], preferred_element_type=jnp.float32
        )
        * score_scale
    )
    query_rope_grad = (
        jnp.einsum("hqk,kd->qhd", score_low, keys_rope, preferred_element_type=jnp.float32)
        * score_scale
    )
    key_nope_grad = (
        jnp.einsum(
            "hqk,qhd->khd", score_low, queries[..., :NOPE], preferred_element_type=jnp.float32
        )
        * score_scale
    )
    key_rope_grad = (
        jnp.einsum(
            "hqk,qhd->kd", score_low, queries[..., NOPE:], preferred_element_type=jnp.float32
        )
        * score_scale
    )
    expanded_grad = jnp.concatenate([key_nope_grad, value_grad], axis=-1).reshape(
        2 * row_count, HEADS * (NOPE + VALUE)
    )
    returned_expanded, returned_rope = (
        passed_along(expanded_grad[:row_count].astype(jnp.bfloat16), "fsdp", -1).astype(
            jnp.float32
        ),
        passed_along(key_rope_grad[:row_count].astype(jnp.bfloat16), "fsdp", -1).astype(
            jnp.float32
        ),
    )
    expanded_low = (expanded_grad[row_count:] + returned_expanded).astype(jnp.bfloat16)
    own_rope = key_rope_grad[row_count:] + returned_rope
    latent_grad = right_matmul(expanded_low, up_full)
    up_weight_grad = left_matmul(latent, expanded_low)
    compressed_latent_grad, latent_gain_grad = norm_back(
        compressed[:, :LATENT], latent_gain, latent_grad
    )
    compressed_low = jnp.concatenate(
        [compressed_latent_grad, rotate_backward(own_rope, cosine, sine_table)], axis=-1
    ).astype(jnp.bfloat16)
    query_low = (
        jnp.concatenate(
            [
                query_nope_grad,
                rotate_backward(query_rope_grad, cosine[:, None, :], sine_table[:, None, :]),
            ],
            axis=-1,
        )
        .reshape(row_count, HEADS * (NOPE + ROPE))
        .astype(jnp.bfloat16)
    )
    normed_grad = right_matmul(query_low, query_full) + right_matmul(compressed_low, down_full)
    query_weight_grad = left_matmul(normed_low, query_low)
    down_weight_grad = left_matmul(normed_low, compressed_low)
    input_add, first_gain_grad = norm_back(inputs, gain_first, normed_grad)
    token_grad = residual_grad + input_add
    small_grad = jnp.concatenate(
        [
            first_gain_grad.reshape(-1, gain_width),
            latent_gain_grad.reshape(-1, latent_width),
            feed_gain_grad.reshape(-1, gain_width),
            router_grad.reshape(2 * expert_total, -1),
        ],
        axis=1,
    )
    small_piece = scatter_all(small_grad)[0]

    def shard(value):
        return scatter_all(value.astype(jnp.bfloat16)).astype(jnp.float32)

    return (
        output[None],
        token_grad[None],
        small_piece[cuts[0] : cuts[1]],
        shard(query_weight_grad),
        shard(down_weight_grad),
        small_piece[cuts[1] : cuts[2]],
        shard(up_weight_grad),
        shard(output_grad),
        small_piece[cuts[2] : cuts[3]],
        small_piece[cuts[3] : cuts[4]].reshape(gain_width, expert_total),
        sgate_piece,
        sup_piece,
        sdown_piece,
        expert_gate_piece.astype(jnp.float32)[None],
        expert_up_piece.astype(jnp.float32)[None],
        expert_down_piece.astype(jnp.float32)[None],
    )


def solution(mesh):
    return jax.shard_map(
        body,
        mesh=mesh,
        in_specs=(
            P("expert", "fsdp", None),
            P("expert", None),
            P("expert", "fsdp", None),
            P("expert", "fsdp", None),
            P("expert", "fsdp", None),
            P(("fsdp", "expert")),
            P(("fsdp", "expert"), None),
            P(("fsdp", "expert"), None),
            P(("fsdp", "expert")),
            P(("fsdp", "expert"), None),
            P(("fsdp", "expert"), None),
            P(("fsdp", "expert")),
            P(("fsdp", "expert"), None),
            P(("fsdp", "expert"), None),
            P(("fsdp", "expert"), None),
            P(("fsdp", "expert"), None),
            P("expert", "fsdp", None),
            P("expert", "fsdp", None),
            P("expert", None, "fsdp"),
        ),
        out_specs=(
            P("expert", "fsdp", None),
            P("expert", "fsdp", None),
            P(("fsdp", "expert")),
            P(("fsdp", "expert"), None),
            P(("fsdp", "expert"), None),
            P(("fsdp", "expert")),
            P(("fsdp", "expert"), None),
            P(("fsdp", "expert"), None),
            P(("fsdp", "expert")),
            P(("fsdp", "expert"), None),
            P(("fsdp", "expert"), None),
            P(("fsdp", "expert"), None),
            P(("fsdp", "expert"), None),
            P("expert", "fsdp", None),
            P("expert", "fsdp", None),
            P("expert", None, "fsdp"),
        ),
        check_vma=False,
    )
```

```python
import functools
import math

import jax
import jax.numpy as jnp
from jax import lax
from jax.experimental import pallas as pl
from jax.experimental.pallas import tpu as pltpu
from jax.sharding import PartitionSpec as P

D = 2048
HEADS = 16
NOPE = 128
ROPE = 64
VALUE = 128
LATENT = 512
TOPK = 6


EPSILON = 1e-06
FLOOR_SCORE = -1e30


def passed_along(value, axis, steps):
    count = lax.axis_size(axis)
    first, last = (max(0, -steps), min(count, count - steps))
    return lax.ppermute(value, axis, [(source, source + steps) for source in range(first, last)])


def norm_rows(values, gain):
    return values * lax.rsqrt(jnp.mean(values * values, axis=-1, keepdims=True) + EPSILON) * gain


def norm_back(values, gain, incoming):
    primal_out, pullback = jax.vjp(norm_rows, values, gain)
    return pullback(incoming)


def swiglu_back(gate_part, up_portion, incoming):
    primal_out, pullback = jax.vjp(
        lambda former, latter: jax.nn.silu(former) * latter, gate_part, up_portion
    )
    return pullback(incoming)


def rotary_table(row_total, offset, rope_width):
    frequency_steps = jnp.arange(rope_width // 2, dtype=jnp.float32)
    inverse = jnp.exp(frequency_steps * (-2.0 * math.log(10000.0) / rope_width))
    places = (offset + jnp.arange(row_total)).astype(jnp.float32)
    angles = places[:, None] * inverse[None, :]
    return (jnp.cos(angles), jnp.sin(angles))


def rotate_forward(values, cosine, sine_table):
    middle = values.shape[-1] // 2
    front_half = values[..., :middle]
    back_half = values[..., middle:]
    return jnp.concatenate(
        [
            front_half * cosine - back_half * sine_table,
            back_half * cosine + front_half * sine_table,
        ],
        axis=-1,
    )


def rotate_backward(values, cosine, sine_table):
    middle = values.shape[-1] // 2
    front_half = values[..., :middle]
    back_half = values[..., middle:]
    return jnp.concatenate(
        [
            front_half * cosine + back_half * sine_table,
            back_half * cosine - front_half * sine_table,
        ],
        axis=-1,
    )


def matmul(former, latter):
    return jnp.dot(former, latter, preferred_element_type=jnp.float32)


def left_matmul(former, latter):
    return lax.dot_general(
        former, latter, (((0,), (0,)), ((), ())), preferred_element_type=jnp.float32
    )


def right_matmul(former, latter):
    return lax.dot_general(
        former, latter, (((1,), (1,)), ((), ())), preferred_element_type=jnp.float32
    )


def attention_scores(queries, expanded, keys_rope, visible, score_scale):
    scores = jnp.einsum(
        "qhd,khd->hqk",
        queries[..., :NOPE],
        expanded[..., :NOPE],
        preferred_element_type=jnp.float32,
    )
    scores = scores + jnp.einsum(
        "qhd,kd->hqk", queries[..., NOPE:], keys_rope, preferred_element_type=jnp.float32
    )
    return jnp.where(visible[None], scores * score_scale, FLOOR_SCORE)


PLANE = 4
MESH = pl.DeviceIdType.MESH
MEBIBYTE = 1024 * 1024


def groups(count):
    lines = count // PLANE
    plane = [[row * PLANE + spot for spot in range(PLANE)] for row in range(lines)]
    line = [[row * PLANE + spot for row in range(lines)] for spot in range(PLANE)]
    return plane, line


def remote(source, target, send, receive, where):
    return pltpu.make_async_remote_copy(
        src_ref=source,
        dst_ref=target,
        send_sem=send,
        recv_sem=receive,
        device_id=where,
        device_id_type=MESH,
    )


def plane_mates(place):
    spot = place % PLANE
    return (place + 1 - 2 * (spot % 2), place + 2 - 4 * (spot // 2))


def greet_neighbours(half, place, depth):
    barrier = pltpu.get_barrier_semaphore()
    level = place // PLANE

    def greet(where):
        pl.semaphore_signal(barrier, inc=1, device_id=where, device_id_type=MESH)

    for mate in plane_mates(place):
        greet((half, mate))
    greet((1 - half, place))

    @pl.when(level > 0)
    def _():
        greet((half, place - PLANE))

    @pl.when(level < depth - 1)
    def _():
        greet((half, place + PLANE))

    pl.semaphore_wait(
        barrier, 3 + jnp.where(level > 0, 1, 0) + jnp.where(level < depth - 1, 1, 0)
    )


def gather_kernel(depth, cut, in_ref, out_ref, own_sem, zs, zr, ps, pr, qs, qr, cs, cr):
    half = lax.axis_index("fsdp")
    place = lax.axis_index("expert")
    level = place // PLANE
    spot = place % PLANE
    total = depth * PLANE
    mates = plane_mates(place)
    rows, width = in_ref.shape
    columns = (pl.ds(0, cut), pl.ds(cut, width - cut))
    greet_neighbours(half, place, depth)

    def at(which, block, count=1):
        start = pl.multiple_of((half * total + block) * rows, rows)
        return out_ref.at[pl.ds(start, count * rows), columns[which]]

    def along(which, way, source, own=False):
        target = at(which, source * PLANE + spot)
        start = in_ref.at[:, columns[which]] if own else target
        return remote(
            start,
            target,
            zs.at[which, way, source],
            zr.at[which, source],
            (half, place + (2 * way - 1) * PLANE),
        )

    def plane_one(which, source, own=False):
        target = at(which, source * PLANE + spot)
        start = in_ref.at[:, columns[which]] if own else target
        return remote(
            start, target, ps.at[which, source], pr.at[which, source], (half, mates[which])
        )

    def plane_two(which, source, turn):
        base = source * PLANE
        if which == 0:
            block = at(0, base + spot - spot % 2, 2)
        else:
            block = at(1, base + (spot + 2 * turn) % PLANE)
        slot = which + turn
        return remote(
            block, block, qs.at[slot, source], qr.at[slot, source], (half, mates[1 - which])
        )

    def core(which, source):
        block = at(which, source * PLANE, PLANE)
        return remote(
            block, block, cs.at[which, source], cr.at[which, source], (1 - half, place)
        )

    seconds = ((0, 0), (1, 0), (1, 1))

    def own_copy(which):
        return pltpu.make_async_copy(
            in_ref.at[:, columns[which]], at(which, place), own_sem.at[which]
        )

    for which in range(2):

        @pl.when(level > 0)
        def _():
            along(which, 0, level, True).start()

        @pl.when(level < depth - 1)
        def _():
            along(which, 1, level, True).start()

        plane_one(which, level, True).start()
        own_copy(which).start()
    for which in range(2):
        own_copy(which).wait()

    def visit(step, act):
        if step == 0:
            act(level, None)
            return

        @pl.when(level - step >= 0)
        def _():
            act(level - step, 1)

        @pl.when(level + step < depth)
        def _():
            act(level + step, 0)

    def arrive(source, way):
        for which in range(2):
            along(which, way, source).wait_recv()

            @pl.when((level < depth - 1) if way == 1 else (level > 0))
            def _():
                along(which, way, source).start()

            plane_one(which, source).start()

    def spread(source, way):
        for which in range(2):
            plane_one(which, source).wait_recv()
            for kind, turn in seconds:
                if kind == which:
                    plane_two(kind, source, turn).start()

    def share(source, way):
        for which in range(2):
            for kind, turn in seconds:
                if kind == which:
                    plane_two(kind, source, turn).wait_recv()
            core(which, source).start()

    for step in range(depth + 2):
        if 1 <= step <= depth:
            visit(step - 1, spread)
        if 1 <= step < depth:
            visit(step, arrive)
        if step >= 2:
            visit(step - 2, share)

    def finish(source, carry):
        for which in range(2):
            core(which, source).wait_recv()
            core(which, source).wait_send()
            plane_one(which, source).wait_send()

            @pl.when((source <= level) & (level < depth - 1))
            def _():
                along(which, 1, source).wait_send()

            @pl.when((source >= level) & (level > 0))
            def _():
                along(which, 0, source).wait_send()

        for kind, turn in seconds:
            plane_two(kind, source, turn).wait_send()
        return carry

    lax.fori_loop(0, depth, finish, 0)


def gather_rows(value, cut):
    rows, width = value.shape
    total = lax.axis_size("expert")
    depth = total // PLANE
    semaphores = pltpu.SemaphoreType.DMA
    return pl.pallas_call(
        functools.partial(gather_kernel, depth, cut),
        out_shape=jax.ShapeDtypeStruct((2 * total * rows, width), value.dtype),
        in_specs=[pl.BlockSpec(memory_space=pl.ANY)],
        out_specs=pl.BlockSpec(memory_space=pl.ANY),
        scratch_shapes=[
            semaphores((2,)),
            semaphores((2, 2, depth)),
            semaphores((2, depth)),
            semaphores((2, depth)),
            semaphores((2, depth)),
            semaphores((3, depth)),
            semaphores((3, depth)),
            semaphores((2, depth)),
            semaphores((2, depth)),
        ],
        compiler_params=pltpu.CompilerParams(collective_id=1, has_side_effects=True),
    )(value)


def reduce_kernel(depth, count, cut, *refs):
    parts = refs[:count]
    out_ref = refs[count]
    acc, inc, one_a, one_b, two_a, two_b, zin = refs[count + 1 : count + 8]
    own_sem, cs, cr, ps, pr, qs, qr, zs, zr = refs[count + 8 :]
    half = lax.axis_index("fsdp")
    place = lax.axis_index("expert")
    level = place // PLANE
    spot = place % PLANE
    total = depth * PLANE
    mates = plane_mates(place)
    rows = out_ref.shape[0]
    group = PLANE * rows
    width = out_ref.shape[1]
    greet_neighbours(half, place, depth)

    starts = [sum(part.shape[1] for part in parts[:k]) for k in range(count)]

    def rows_of(k, owner, t):
        start = pl.multiple_of((owner * total + t * PLANE) * rows, group)
        return parts[k].at[pl.ds(start, group), :]

    def kept(k, t):
        return pltpu.make_async_copy(
            rows_of(k, half, t),
            acc.at[t, :, pl.ds(starts[k], parts[k].shape[1])],
            own_sem.at[k, t],
        )

    def given(k, t):
        return remote(
            rows_of(k, 1 - half, t),
            inc.at[t, :, pl.ds(starts[k], parts[k].shape[1])],
            cs.at[k, t],
            cr.at[k, t],
            (1 - half, place),
        )

    def block(t, q, n, lo, hi):
        return acc.at[t, pl.ds(pl.multiple_of(q * rows, rows), n * rows), pl.ds(lo, hi - lo)]

    pair = spot - spot % 2

    def first(t, turn):
        low = spot % 2
        if turn == 0:
            source = block(t, 2 - pair, 2, 0, cut)
            target, where = one_a.at[t], mates[1]
        else:
            source = block(t, 2 * turn - 1 - low, 1, cut, width)
            target, where = one_b.at[t, turn - 1], mates[0]
        return remote(source, target, ps.at[turn, t], pr.at[turn, t], (half, where))

    def second(t, turn):
        if turn == 0:
            source = block(t, pair + 1 - spot % 2, 1, 0, cut)
            target, where = two_a.at[t], mates[0]
        else:
            source = block(t, (spot + 2) % PLANE, 1, cut, width)
            target, where = two_b.at[t], mates[1]
        return remote(source, target, qs.at[turn, t], qr.at[turn, t], (half, where))

    def line(t, way):
        step = 2 * way - 1
        return remote(
            block(t, spot, 1, 0, width),
            zin.at[way, t],
            zs.at[way, t],
            zr.at[way, t],
            (half, place + step * PLANE),
        )

    def add_rows(t, start, n, lo, hi, piece):
        def one(i, carry):
            r = pl.multiple_of(i * 16, 16)
            at = (t, pl.ds(pl.multiple_of(start + r, 16), 16), pl.ds(lo, hi - lo))
            new = piece(pl.ds(r, 16)).astype(jnp.float32)
            acc[at] = (acc[at].astype(jnp.float32) + new).astype(acc.dtype)
            return carry

        lax.fori_loop(0, n // 16, one, 0)

    def stage_a(t):
        for k in range(count):
            kept(k, t).wait()
            given(k, t).wait_recv()
        add_rows(t, 0, group, 0, width, lambda r: inc[t, r, :])
        for turn in range(3):
            first(t, turn).start()

    def stage_b(t):
        first(t, 0).wait_recv()
        add_rows(t, pair * rows, 2 * rows, 0, cut, lambda r: one_a[t, r, :])
        second(t, 0).start()
        for turn in range(2):
            first(t, 1 + turn).wait_recv()
            add_rows(
                t,
                (spot % 2 + 2 * turn) * rows,
                rows,
                cut,
                width,
                lambda r: one_b[t, turn, r, :],
            )
        second(t, 1).start()

    def stage_c(t):
        second(t, 0).wait_recv()
        add_rows(t, spot * rows, rows, 0, cut, lambda r: two_a[t, r, :])
        second(t, 1).wait_recv()
        add_rows(t, spot * rows, rows, cut, width, lambda r: two_b[t, r, :])

        def take(way):
            line(t, way).wait_recv()
            add_rows(t, spot * rows, rows, 0, width, lambda r: zin[way, t, r, :])

        @pl.when((t >= level) & (level > 0))
        def _():
            take(1)

        @pl.when((t <= level) & (level < depth - 1))
        def _():
            take(0)

        @pl.when(t > level)
        def _():
            line(t, 1).start()

        @pl.when(t < level)
        def _():
            line(t, 0).start()

    def visit(index, act):
        if index >= depth or index < 0:
            return
        step = depth - 1 - index
        if step == 0:
            act(level)
            return

        @pl.when(level + step < depth)
        def _():
            act(level + step)

        @pl.when(level - step >= 0)
        def _():
            act(level - step)

    def begin(t):
        for k in range(count):
            given(k, t).start()
            kept(k, t).start()

    for index in range(depth):
        visit(index, begin)
    for index in range(depth + 2):
        visit(index, stage_a)
        visit(index - 1, stage_b)
        visit(index - 2, stage_c)

    def emit(i, carry):
        r = pl.multiple_of(i * 16, 16)
        at = pl.ds(pl.multiple_of(spot * rows + r, 16), 16)
        out_ref[pl.ds(r, 16), :] = acc[level, at, :].astype(out_ref.dtype)
        return carry
    lax.fori_loop(0, rows // 16, emit, 0)

    def finish(t, carry):
        for k in range(count):
            given(k, t).wait_send()
        for turn in range(3):
            first(t, turn).wait_send()
        for turn in range(2):
            second(t, turn).wait_send()

        @pl.when(t > level)
        def _():
            line(t, 1).wait_send()

        @pl.when(t < level)
        def _():
            line(t, 0).wait_send()
        return carry

    lax.fori_loop(0, depth, finish, 0)


def reduce_rows(parts, cut):
    total = lax.axis_size("expert")
    depth = total // PLANE
    rows = parts[0].shape[0] // (2 * total)
    width = sum(part.shape[1] for part in parts)
    group = PLANE * rows
    n = len(parts)
    semaphores = pltpu.SemaphoreType.DMA
    low = parts[0].dtype
    return pl.pallas_call(
        functools.partial(reduce_kernel, depth, n, cut),
        out_shape=jax.ShapeDtypeStruct((rows, width), jnp.float32),
        in_specs=[pl.BlockSpec(memory_space=pl.ANY)] * n,
        out_specs=pl.BlockSpec(memory_space=pltpu.VMEM),
        scratch_shapes=[
            pltpu.VMEM((depth, group, width), low),
            pltpu.VMEM((depth, group, width), low),
            pltpu.VMEM((depth, 2 * rows, cut), low),
            pltpu.VMEM((depth, 2, rows, width - cut), low),
            pltpu.VMEM((depth, rows, cut), low),
            pltpu.VMEM((depth, rows, width - cut), low),
            pltpu.VMEM((2, depth, rows, width), low),
            semaphores((n, depth)),
            semaphores((n, depth)),
            semaphores((n, depth)),
            semaphores((3, depth)),
            semaphores((3, depth)),
            semaphores((2, depth)),
            semaphores((2, depth)),
            semaphores((2, depth)),
            semaphores((2, depth)),
        ],
        compiler_params=pltpu.CompilerParams(
            collective_id=2, has_side_effects=True, vmem_limit_bytes=48 * MEBIBYTE
        ),
    )(*parts)


def body(
    tokens,
    segments,
    routes,
    slot_index,
    cotangent,
    attention_norm,
    query_weight,
    latent_down,
    latent_norm,
    latent_up,
    output_weight,
    feed_norm,
    router_weight,
    shared_gate,
    shared_up,
    shared_down,
    expert_gate,
    expert_up,
    expert_down,
):
    row_count = tokens.shape[1]
    expert_total = lax.axis_size("expert")
    depth = expert_total // PLANE
    plane, line = groups(expert_total)
    place = lax.axis_index("expert")
    level = place // PLANE
    device_half = lax.axis_index("fsdp")
    capacity = row_count * TOPK // expert_total
    line_rows = depth * row_count
    inputs = tokens[0].astype(jnp.float32)

    part_rows = query_weight.shape[0]
    gain_width = attention_norm.shape[0]
    latent_width = latent_norm.shape[0]
    small = jnp.concatenate([attention_norm, latent_norm, feed_norm, router_weight.reshape(-1)])
    cuts = [
        0,
        gain_width,
        gain_width + latent_width,
        2 * gain_width + latent_width,
        small.shape[0],
    ]
    small = jnp.pad(small, (0, 128 * part_rows - small.shape[0])).reshape(part_rows, 128)
    query_width = query_weight.shape[1]
    down_width = latent_down.shape[1]
    entry_width = query_width + down_width + (-down_width) % 128
    up_width = HEADS * (NOPE + VALUE)
    packed = jnp.concatenate(
        [
            query_weight,
            jnp.pad(latent_down, ((0, 0), (0, (-down_width) % 128))),
            latent_up.reshape(part_rows, -1),
            small,
        ],
        axis=1,
    )
    cut = packed.shape[1] // 256 * 128
    packed_full = gather_rows(packed, cut)
    output_full = lax.all_gather(output_weight, ("fsdp", "expert"), axis=0, tiled=True)
    entry_full = packed_full[:, :entry_width]
    up_full = packed_full[:, entry_width:-128].reshape(-1, up_width)
    small_full = packed_full[:, -128:].reshape(2 * expert_total, -1)
    gain_one, gain_latent, gain_feed, router_full = (
        small_full[:, cuts[0] : cuts[1]].reshape(-1),
        small_full[:, cuts[1] : cuts[2]].reshape(-1),
        small_full[:, cuts[2] : cuts[3]].reshape(-1),
        small_full[:, cuts[3] : cuts[4]].reshape(-1, expert_total),
    )

    route_rows = routes[0]
    slot_rows = slot_index[0]
    target = jnp.where(
        slot_rows >= 0, route_rows * capacity + slot_rows, expert_total * capacity
    )
    target_line = lax.all_gather(target, "expert", axis_index_groups=line, axis=0)
    grad_line = lax.all_gather(
        cotangent[0], "expert", axis_index_groups=line, axis=0, tiled=True
    )
    shared_width = shared_gate.shape[1] // (2 * depth)

    def columns_to_levels(weight):
        rows = weight.shape[0]
        pieces = weight.reshape(rows, 2, depth, shared_width).transpose(2, 0, 1, 3)
        moved = lax.all_to_all(
            pieces.reshape(depth, rows, 2 * shared_width),
            "expert",
            split_axis=0,
            concat_axis=0,
            axis_index_groups=line,
            tiled=True,
        )
        across = lax.all_gather(moved, "expert", axis_index_groups=plane, axis=0)
        whole = lax.all_gather(across, "fsdp", axis=0)
        return whole.transpose(0, 2, 1, 3, 4).reshape(-1, 2 * shared_width)

    sgate_full = columns_to_levels(shared_gate)
    sup_full = columns_to_levels(shared_up)
    sdown_full = lax.all_gather(
        lax.all_gather(shared_down, "expert", axis_index_groups=plane, axis=0, tiled=True),
        "fsdp",
        axis=0,
        tiled=True,
    )
    expert_gate_full = lax.all_gather(expert_gate[0], "fsdp", axis=0, tiled=True)
    expert_up_full = lax.all_gather(expert_up[0], "fsdp", axis=0, tiled=True)
    expert_down_full = lax.all_gather(expert_down[0], "fsdp", axis=1, tiled=True)

    slot_names = level * PLANE * capacity + jnp.arange(PLANE * capacity)
    hits = target_line[:, None, :, :] == slot_names[None, :, None, None]
    choose_rows = jnp.any(hits, axis=-1).astype(jnp.bfloat16)

    def to_experts(rows_line):
        placed = jnp.einsum(
            "zst,ztd->zsd",
            choose_rows,
            rows_line.reshape(depth, row_count, D),
            preferred_element_type=jnp.float32,
        ).astype(jnp.bfloat16)
        placed = placed.reshape(depth, PLANE, capacity, D).transpose(1, 0, 2, 3)
        return lax.all_to_all(
            placed, "expert", split_axis=0, concat_axis=0, axis_index_groups=plane, tiled=True
        ).reshape(expert_total * capacity, D)

    def from_experts(rows):
        return lax.all_to_all(
            rows.reshape(PLANE, depth, capacity, -1),
            "expert",
            split_axis=0,
            concat_axis=0,
            axis_index_groups=plane,
            tiled=True,
        )

    grad_rows = to_experts(grad_line)

    cosine, sine_table = rotary_table(row_count, device_half * row_count, ROPE)
    score_scale = (NOPE + ROPE) ** (-0.5)
    gain_first = gain_one.astype(jnp.float32)
    normed_low = norm_rows(inputs, gain_first).astype(jnp.bfloat16)
    entry = matmul(normed_low, entry_full)
    query_raw = entry[:, :query_width].reshape(row_count, HEADS, NOPE + ROPE)
    queries = jnp.concatenate(
        [
            query_raw[..., :NOPE],
            rotate_forward(query_raw[..., NOPE:], cosine[:, None, :], sine_table[:, None, :]),
        ],
        axis=-1,
    ).astype(jnp.bfloat16)
    compressed = entry[:, query_width : query_width + down_width]
    latent_gain = gain_latent.astype(jnp.float32)
    latent = norm_rows(compressed[:, :LATENT], latent_gain).astype(jnp.bfloat16)
    key_rope = rotate_forward(compressed[:, LATENT:], cosine, sine_table).astype(jnp.bfloat16)
    prior_latent, prior_rope = passed_along((latent, key_rope), "fsdp", 1)
    key_latent = jnp.concatenate([prior_latent, latent], axis=0)
    keys_rope = jnp.concatenate([prior_rope, key_rope], axis=0)
    expanded = (
        matmul(key_latent, up_full).astype(jnp.bfloat16).reshape(2 * row_count, HEADS, NOPE + VALUE)
    )
    query_place = device_half * row_count + jnp.arange(row_count)
    key_place = (device_half - 1) * row_count + jnp.arange(2 * row_count)
    padded_segments = jnp.concatenate([jnp.full((row_count,), -1, jnp.int32), segments[0]])
    key_segment = lax.dynamic_slice_in_dim(padded_segments, device_half * row_count, 2 * row_count)
    query_segment = lax.dynamic_slice_in_dim(segments[0], device_half * row_count, row_count)
    visible = (key_place[None, :] <= query_place[:, None]) & (
        key_segment[None, :] == query_segment[:, None]
    )
    scores = attention_scores(queries, expanded, keys_rope, visible, score_scale)
    top_score = jnp.max(scores, axis=-1, keepdims=True)
    log_total = top_score + jnp.log(jnp.sum(jnp.exp(scores - top_score), axis=-1, keepdims=True))
    weight_low = jnp.exp(scores - log_total).astype(jnp.bfloat16)
    mixed_heads = (
        jnp.einsum(
            "hqk,khd->qhd", weight_low, expanded[..., NOPE:], preferred_element_type=jnp.float32
        )
        .reshape(row_count, HEADS * VALUE)
        .astype(jnp.bfloat16)
    )
    residual = inputs + matmul(mixed_heads, output_full)
    feed_gain = gain_feed.astype(jnp.float32)
    mixed_low = norm_rows(residual, feed_gain).astype(jnp.bfloat16)
    mixed_line = lax.all_gather(mixed_low, "expert", axis_index_groups=line, axis=0, tiled=True)
    mixed_rows = to_experts(mixed_line)
    probabilities_line = jax.nn.softmax(matmul(mixed_line, router_full), axis=-1).reshape(
        depth, row_count, expert_total
    )
    level_probs = lax.dynamic_slice_in_dim(probabilities_line, level * PLANE, PLANE, axis=2)
    hit_weights = choose_rows.astype(jnp.float32).reshape(depth, PLANE, capacity, row_count)
    weighted = hit_weights * level_probs.transpose(0, 2, 1)[:, :, None, :]
    slot_gate = jnp.sum(weighted, axis=-1).transpose(1, 0, 2).reshape(PLANE, depth, capacity, 1)
    gate_column = from_experts(slot_gate).reshape(expert_total * capacity, 1)

    gate_part = matmul(mixed_rows, expert_gate_full)
    up_portion = matmul(mixed_rows, expert_up_full)
    hidden_wide = jax.nn.silu(gate_part) * up_portion
    hidden = hidden_wide.astype(jnp.bfloat16)
    expert_out = matmul(hidden, expert_down_full).astype(jnp.bfloat16)
    returned = from_experts(expert_out)
    slot_grad = jnp.sum(
        expert_out.astype(jnp.float32) * grad_rows.astype(jnp.float32), axis=-1, keepdims=True
    )
    slot_grad_back = from_experts(slot_grad)
    hidden_grad = right_matmul(grad_rows, expert_down_full) * gate_column
    gate_part_grad, up_part_grad = swiglu_back(gate_part, up_portion, hidden_grad)
    gate_low = gate_part_grad.astype(jnp.bfloat16)
    up_low = up_part_grad.astype(jnp.bfloat16)
    input_grad = (
        right_matmul(gate_low, expert_gate_full) + right_matmul(up_low, expert_up_full)
    ).astype(jnp.bfloat16)
    back_rows = from_experts(input_grad)
    hidden_scaled = (hidden.astype(jnp.float32) * gate_column).astype(jnp.bfloat16)
    egate_grad = left_matmul(mixed_rows, gate_low).astype(jnp.bfloat16)
    eup_grad = left_matmul(mixed_rows, up_low).astype(jnp.bfloat16)
    edown_grad = left_matmul(hidden_scaled, grad_rows).astype(jnp.bfloat16)
    expert_gate_piece, expert_up_piece, expert_down_piece = (
        lax.psum_scatter(egate_grad, "fsdp", scatter_dimension=0, tiled=True),
        lax.psum_scatter(eup_grad, "fsdp", scatter_dimension=0, tiled=True),
        lax.psum_scatter(edown_grad, "fsdp", scatter_dimension=1, tiled=True),
    )

    shared_gate_part = matmul(mixed_line, sgate_full)
    shared_up_part = matmul(mixed_line, sup_full)
    shared_hidden = (jax.nn.silu(shared_gate_part) * shared_up_part).astype(jnp.bfloat16)
    shared_out = matmul(shared_hidden, sdown_full)
    shared_hidden_grad = right_matmul(grad_line, sdown_full)
    shared_gate_grad, shared_up_grad = swiglu_back(
        shared_gate_part, shared_up_part, shared_hidden_grad
    )
    shared_gate_low = shared_gate_grad.astype(jnp.bfloat16)
    shared_up_low = shared_up_grad.astype(jnp.bfloat16)
    shared_back = right_matmul(shared_gate_low, sgate_full) + right_matmul(
        shared_up_low, sup_full
    )
    sdown_grad = left_matmul(shared_hidden, grad_line).astype(jnp.bfloat16)
    sgate_grad = left_matmul(mixed_line, shared_gate_low).astype(jnp.bfloat16)
    sup_grad = left_matmul(mixed_line, shared_up_low).astype(jnp.bfloat16)

    def scatter_plane(value):
        part = lax.psum_scatter(value, "fsdp", scatter_dimension=0, tiled=True)
        return lax.psum_scatter(
            part, "expert", scatter_dimension=0, axis_index_groups=plane, tiled=True
        )

    def levels_to_columns(weight):
        rows = D // (2 * expert_total)
        pieces = weight.reshape(2, depth, PLANE, rows, 2 * shared_width).transpose(0, 2, 1, 3, 4)
        summed = scatter_plane(pieces.reshape(2 * PLANE, depth, rows, 2 * shared_width))[0]
        moved = lax.all_to_all(
            summed, "expert", split_axis=0, concat_axis=0, axis_index_groups=line, tiled=True
        )
        return (
            moved.reshape(depth, rows, 2, shared_width)
            .transpose(1, 2, 0, 3)
            .reshape(rows, -1)
            .astype(jnp.float32)
        )

    sgate_piece = levels_to_columns(sgate_grad)
    sup_piece = levels_to_columns(sup_grad)
    sdown_piece = scatter_plane(sdown_grad).astype(jnp.float32)

    choose_weighted = (
        weighted.reshape(depth, PLANE * capacity, row_count).astype(jnp.bfloat16)
    )

    def combine(matrix, rows, add):
        gathered = rows.transpose(1, 0, 2, 3).reshape(depth, PLANE * capacity, D)
        mixed = jnp.einsum("zst,zsd->ztd", matrix, gathered, preferred_element_type=jnp.float32)
        total = (mixed.reshape(line_rows, D) + add).astype(jnp.bfloat16)
        return lax.psum_scatter(
            total, "expert", scatter_dimension=0, axis_index_groups=line, tiled=True
        ).astype(jnp.float32)

    routed_and_shared = combine(choose_weighted, returned, shared_out)
    back_and_shared = combine(choose_rows, back_rows, shared_back)
    output = (residual + routed_and_shared).astype(jnp.bfloat16)
    out_grad = cotangent[0].astype(jnp.float32)

    slot_grads = slot_grad_back.transpose(1, 0, 2, 3).reshape(depth, PLANE, capacity, 1)
    prob_part = jnp.sum(hit_weights * slot_grads, axis=2)
    prob_wide = lax.dynamic_update_slice_in_dim(
        jnp.zeros((depth, expert_total, row_count), jnp.float32), prob_part, level * PLANE, axis=1
    )
    prob_grad = lax.psum_scatter(
        prob_wide, "expert", scatter_dimension=0, axis_index_groups=line, tiled=True
    )[0].T
    probabilities = lax.dynamic_index_in_dim(probabilities_line, level, axis=0, keepdims=False)
    logit_low = (
        probabilities * (prob_grad - jnp.sum(probabilities * prob_grad, axis=-1, keepdims=True))
    ).astype(jnp.bfloat16)
    router_grad = left_matmul(mixed_low, logit_low)
    mixed_grad = right_matmul(logit_low, router_full) + back_and_shared
    residual_add, feed_gain_grad = norm_back(residual, feed_gain, mixed_grad)
    residual_grad = out_grad + residual_add
    attended_low = residual_grad.astype(jnp.bfloat16)
    output_grad = left_matmul(mixed_heads, attended_low)
    heads_low = (
        right_matmul(attended_low, output_full)
        .astype(jnp.bfloat16)
        .reshape(row_count, HEADS, VALUE)
    )
    scores_again = attention_scores(queries, expanded, keys_rope, visible, score_scale)
    probs_again = jnp.exp(scores_again - log_total)
    weights_again = probs_again.astype(jnp.bfloat16)
    weight_grad = jnp.einsum(
        "qhd,khd->hqk", heads_low, expanded[..., NOPE:], preferred_element_type=jnp.float32
    )
    value_grad = jnp.einsum(
        "hqk,qhd->khd", weights_again, heads_low, preferred_element_type=jnp.float32
    )
    delta_rows = jnp.sum(probs_again * weight_grad, axis=-1, keepdims=True)
    score_low = (probs_again * (weight_grad - delta_rows)).astype(jnp.bfloat16)
    query_nope_grad = (
        jnp.einsum(
            "hqk,khd->qhd", score_low, expanded[..., :NOPE], preferred_element_type=jnp.float32
        )
        * score_scale
    )
    query_rope_grad = (
        jnp.einsum("hqk,kd->qhd", score_low, keys_rope, preferred_element_type=jnp.float32)
        * score_scale
    )
    key_nope_grad = (
        jnp.einsum(
            "hqk,qhd->khd", score_low, queries[..., :NOPE], preferred_element_type=jnp.float32
        )
        * score_scale
    )
    key_rope_grad = (
        jnp.einsum(
            "hqk,qhd->kd", score_low, queries[..., NOPE:], preferred_element_type=jnp.float32
        )
        * score_scale
    )
    expanded_grad = jnp.concatenate([key_nope_grad, value_grad], axis=-1).reshape(
        2 * row_count, HEADS * (NOPE + VALUE)
    )
    returned_expanded, returned_rope = (
        passed_along(expanded_grad[:row_count].astype(jnp.bfloat16), "fsdp", -1).astype(
            jnp.float32
        ),
        passed_along(key_rope_grad[:row_count].astype(jnp.bfloat16), "fsdp", -1).astype(
            jnp.float32
        ),
    )
    expanded_low = (expanded_grad[row_count:] + returned_expanded).astype(jnp.bfloat16)
    own_rope = key_rope_grad[row_count:] + returned_rope
    latent_grad = right_matmul(expanded_low, up_full)
    up_weight_grad = left_matmul(latent, expanded_low)
    compressed_latent_grad, latent_gain_grad = norm_back(
        compressed[:, :LATENT], latent_gain, latent_grad
    )
    compressed_low = jnp.concatenate(
        [compressed_latent_grad, rotate_backward(own_rope, cosine, sine_table)], axis=-1
    ).astype(jnp.bfloat16)
    query_low = (
        jnp.concatenate(
            [
                query_nope_grad,
                rotate_backward(query_rope_grad, cosine[:, None, :], sine_table[:, None, :]),
            ],
            axis=-1,
        )
        .reshape(row_count, HEADS * (NOPE + ROPE))
        .astype(jnp.bfloat16)
    )
    entry_low = jnp.concatenate(
        [query_low, jnp.pad(compressed_low, ((0, 0), (0, (-down_width) % 128)))], axis=1
    )
    normed_grad = right_matmul(entry_low, entry_full)
    entry_grad = left_matmul(normed_low, entry_low).astype(jnp.bfloat16)
    input_add, first_gain_grad = norm_back(inputs, gain_first, normed_grad)
    token_grad = residual_grad + input_add
    small_grad = jnp.concatenate(
        [
            first_gain_grad.reshape(-1, gain_width),
            latent_gain_grad.reshape(-1, latent_width),
            feed_gain_grad.reshape(-1, gain_width),
            router_grad.reshape(2 * expert_total, -1),
        ],
        axis=1,
    )
    small_grad = jnp.pad(small_grad, ((0, 0), (0, 128 * part_rows - small_grad.shape[1])))
    packed_piece = reduce_rows(
        [
            entry_grad,
            up_weight_grad.astype(jnp.bfloat16).reshape(gain_width * 2 * expert_total, -1),
            small_grad.astype(jnp.bfloat16).reshape(-1, 128),
        ],
        cut,
    )
    small_piece = packed_piece[:, -128:].reshape(-1)
    output_piece = lax.psum_scatter(
        output_grad.astype(jnp.bfloat16), ("fsdp", "expert"), scatter_dimension=0, tiled=True
    ).astype(jnp.float32)

    return (
        output[None],
        token_grad[None],
        small_piece[cuts[0] : cuts[1]],
        packed_piece[:, :query_width],
        packed_piece[:, query_width : query_width + down_width],
        small_piece[cuts[1] : cuts[2]],
        packed_piece[:, entry_width:-128].reshape(latent_up.shape),
        output_piece,
        small_piece[cuts[2] : cuts[3]],
        small_piece[cuts[3] : cuts[4]].reshape(gain_width, expert_total),
        sgate_piece,
        sup_piece,
        sdown_piece,
        expert_gate_piece.astype(jnp.float32)[None],
        expert_up_piece.astype(jnp.float32)[None],
        expert_down_piece.astype(jnp.float32)[None],
    )


def solution(mesh):
    return jax.shard_map(
        body,
        mesh=mesh,
        in_specs=(
            P("expert", "fsdp", None),
            P("expert", None),
            P("expert", "fsdp", None),
            P("expert", "fsdp", None),
            P("expert", "fsdp", None),
            P(("fsdp", "expert")),
            P(("fsdp", "expert"), None),
            P(("fsdp", "expert"), None),
            P(("fsdp", "expert")),
            P(("fsdp", "expert"), None),
            P(("fsdp", "expert"), None),
            P(("fsdp", "expert")),
            P(("fsdp", "expert"), None),
            P(("fsdp", "expert"), None),
            P(("fsdp", "expert"), None),
            P(("fsdp", "expert"), None),
            P("expert", "fsdp", None),
            P("expert", "fsdp", None),
            P("expert", None, "fsdp"),
        ),
        out_specs=(
            P("expert", "fsdp", None),
            P("expert", "fsdp", None),
            P(("fsdp", "expert")),
            P(("fsdp", "expert"), None),
            P(("fsdp", "expert"), None),
            P(("fsdp", "expert")),
            P(("fsdp", "expert"), None),
            P(("fsdp", "expert"), None),
            P(("fsdp", "expert")),
            P(("fsdp", "expert"), None),
            P(("fsdp", "expert"), None),
            P(("fsdp", "expert"), None),
            P(("fsdp", "expert"), None),
            P("expert", "fsdp", None),
            P("expert", "fsdp", None),
            P("expert", None, "fsdp"),
        ),
        check_vma=False,
    )
```

```python
import functools
import math

import jax
import jax.numpy as jnp
from jax import lax
from jax.experimental import pallas as pl
from jax.experimental.pallas import tpu as pltpu
from jax.sharding import PartitionSpec as P

D = 2048
HEADS = 16
NOPE = 128
ROPE = 64
VALUE = 128
LATENT = 512
TOPK = 6


EPSILON = 1e-06
FLOOR_SCORE = -1e30


def passed_along(value, axis, steps):
    count = lax.axis_size(axis)
    first, last = (max(0, -steps), min(count, count - steps))
    return lax.ppermute(value, axis, [(source, source + steps) for source in range(first, last)])


def norm_rows(values, gain):
    return values * lax.rsqrt(jnp.mean(values * values, axis=-1, keepdims=True) + EPSILON) * gain


def norm_back(values, gain, incoming):
    primal_out, pullback = jax.vjp(norm_rows, values, gain)
    return pullback(incoming)


def swiglu_back(gate_part, up_portion, incoming):
    primal_out, pullback = jax.vjp(
        lambda former, latter: jax.nn.silu(former) * latter, gate_part, up_portion
    )
    return pullback(incoming)


def rotary_table(row_total, offset, rope_width):
    frequency_steps = jnp.arange(rope_width // 2, dtype=jnp.float32)
    inverse = jnp.exp(frequency_steps * (-2.0 * math.log(10000.0) / rope_width))
    places = (offset + jnp.arange(row_total)).astype(jnp.float32)
    angles = places[:, None] * inverse[None, :]
    return (jnp.cos(angles), jnp.sin(angles))


def rotate_forward(values, cosine, sine_table):
    middle = values.shape[-1] // 2
    front_half = values[..., :middle]
    back_half = values[..., middle:]
    return jnp.concatenate(
        [
            front_half * cosine - back_half * sine_table,
            back_half * cosine + front_half * sine_table,
        ],
        axis=-1,
    )


def rotate_backward(values, cosine, sine_table):
    middle = values.shape[-1] // 2
    front_half = values[..., :middle]
    back_half = values[..., middle:]
    return jnp.concatenate(
        [
            front_half * cosine + back_half * sine_table,
            back_half * cosine - front_half * sine_table,
        ],
        axis=-1,
    )


def matmul(former, latter):
    return jnp.dot(former, latter, preferred_element_type=jnp.float32)


def left_matmul(former, latter):
    return lax.dot_general(
        former, latter, (((0,), (0,)), ((), ())), preferred_element_type=jnp.float32
    )


def right_matmul(former, latter):
    return lax.dot_general(
        former, latter, (((1,), (1,)), ((), ())), preferred_element_type=jnp.float32
    )


def attention_scores(queries, expanded, keys_rope, visible, score_scale):
    scores = jnp.einsum(
        "qhd,khd->hqk",
        queries[..., :NOPE],
        expanded[..., :NOPE],
        preferred_element_type=jnp.float32,
    )
    scores = scores + jnp.einsum(
        "qhd,kd->hqk", queries[..., NOPE:], keys_rope, preferred_element_type=jnp.float32
    )
    return jnp.where(visible[None], scores * score_scale, FLOOR_SCORE)


PLANE = 4
MESH = pl.DeviceIdType.MESH
MEBIBYTE = 1024 * 1024
LONG = pl.CostEstimate(flops=100 * 10**9, bytes_accessed=0, transcendentals=0)


def groups(count):
    lines = count // PLANE
    plane = [[row * PLANE + spot for spot in range(PLANE)] for row in range(lines)]
    line = [[row * PLANE + spot for row in range(lines)] for spot in range(PLANE)]
    return plane, line


def remote(source, target, send, receive, where):
    return pltpu.make_async_remote_copy(
        src_ref=source,
        dst_ref=target,
        send_sem=send,
        recv_sem=receive,
        device_id=where,
        device_id_type=MESH,
    )


def plane_mates(place):
    spot = place % PLANE
    return (place + 1 - 2 * (spot % 2), place + 2 - 4 * (spot // 2))


def greet(partners):
    barrier = pltpu.get_barrier_semaphore()
    for where in partners:
        pl.semaphore_signal(barrier, inc=1, device_id=where, device_id_type=MESH)
    pl.semaphore_wait(barrier, len(partners))


def line_others(half, place, depth):
    total = depth * PLANE
    return [(half, (place + offset * PLANE) % total) for offset in range(1, depth)]


def plane_others(half, place):
    spot = place % PLANE
    return [(half, place - spot + (spot + offset) % PLANE) for offset in range(1, PLANE)]


def greet_neighbours(half, place, depth):
    mates = [(half, mate) for mate in plane_mates(place)]
    greet(line_others(half, place, depth) + mates + [(1 - half, place)])


def exchange_along(depth, half, place, in_ref, land, own_sem, send, receive):
    level = place // PLANE
    total = depth * PLANE

    def own():
        return pltpu.make_async_copy(in_ref.at[level], land(level), own_sem)

    def to(offset):
        where = (place + offset * PLANE) % total
        return remote(
            in_ref.at[where // PLANE],
            land(level),
            send.at[offset],
            receive.at[offset],
            (half, where),
        )

    def start():
        own().start()
        for offset in range(1, depth):
            to(offset).start()

    def finish():
        own().wait()
        for offset in range(1, depth):
            to(offset).wait()

    return start, finish


def gather_kernel(depth, cut, *refs):
    in_ref, *line_ins, move_in, down_in = refs[:5]
    out_ref, *line_outs, shared_out, down_out = refs[5:10]
    own_sem, zs, zr, ps, pr, qs, qr, cs, cr, ls, lr, ms, mr, *shared_sems = refs[10:]
    os, ore, ts, tr, us, ur = shared_sems
    half = lax.axis_index("fsdp")
    place = lax.axis_index("expert")
    level = place // PLANE
    spot = place % PLANE
    total = depth * PLANE
    mates = plane_mates(place)
    rows, width = in_ref.shape
    columns = (pl.ds(0, cut), pl.ds(cut, width - cut))
    greet_neighbours(half, place, depth)

    def at(which, block, count=1):
        start = pl.multiple_of((half * total + block) * rows, rows)
        return out_ref.at[pl.ds(start, count * rows), columns[which]]

    def along(which, way, source, own=False):
        target = at(which, source * PLANE + spot)
        start = in_ref.at[:, columns[which]] if own else target
        return remote(
            start,
            target,
            zs.at[which, way, source],
            zr.at[which, source],
            (half, place + (2 * way - 1) * PLANE),
        )

    def plane_one(which, source, own=False):
        target = at(which, source * PLANE + spot)
        start = in_ref.at[:, columns[which]] if own else target
        return remote(
            start, target, ps.at[which, source], pr.at[which, source], (half, mates[which])
        )

    def plane_two(which, source, turn):
        base = source * PLANE
        if which == 0:
            block = at(0, base + spot - spot % 2, 2)
        else:
            block = at(1, base + (spot + 2 * turn) % PLANE)
        slot = which + turn
        return remote(
            block, block, qs.at[slot, source], qr.at[slot, source], (half, mates[1 - which])
        )

    def core(which, source):
        block = at(which, source * PLANE, PLANE)
        return remote(
            block, block, cs.at[which, source], cr.at[which, source], (1 - half, place)
        )

    def trail(which, way, source, own=False):
        target = line_outs[which].at[source]
        return remote(
            line_ins[which] if own else target,
            target,
            ls.at[which, way, source],
            lr.at[which, source],
            (half, place + (2 * way - 1) * PLANE),
        )

    def trail_own(which):
        return pltpu.make_async_copy(
            line_ins[which], line_outs[which].at[level], own_sem.at[2 + which]
        )

    move_start, move_finish = exchange_along(
        depth,
        half,
        place,
        move_in,
        lambda source: shared_out.at[half, source, spot],
        own_sem.at[4],
        ms,
        mr,
    )
    items = range(depth + 2)
    down_own = pltpu.make_async_copy(down_in, down_out.at[half, spot], own_sem.at[5])

    def shared_at(item, first, count):
        if item < depth:
            return shared_out.at[half, item, pl.ds(first, count)]
        span = down_in.shape[1] // 2
        return down_out.at[
            half, pl.ds(first, count), :, pl.ds((item - depth) * span, span)
        ]

    def shared_route(item):
        return (0 if item < depth // 2 else 1) if item < depth else item - depth

    def shared_one(item):
        block = shared_at(item, spot, 1)
        mate = mates[shared_route(item)]
        return remote(block, block, os.at[item], ore.at[item], (half, mate))

    def shared_two(item):
        if shared_route(item) == 0:
            blocks = [shared_at(item, spot - spot % 2, 2)]
        else:
            blocks = [shared_at(item, (spot + 2 * turn) % PLANE, 1) for turn in range(2)]
        mate = mates[1 - shared_route(item)]
        return [
            remote(block, block, ts.at[turn, item], tr.at[turn, item], (half, mate))
            for turn, block in enumerate(blocks)
        ]

    def shared_core(item):
        block = shared_at(item, 0, PLANE)
        return remote(block, block, us.at[item], ur.at[item], (1 - half, place))

    seconds = ((0, 0), (1, 0), (1, 1))

    def own_copy(which):
        return pltpu.make_async_copy(
            in_ref.at[:, columns[which]], at(which, place), own_sem.at[which]
        )

    for which in range(2):

        @pl.when(level > 0)
        def _():
            along(which, 0, level, True).start()

        @pl.when(level < depth - 1)
        def _():
            along(which, 1, level, True).start()

        plane_one(which, level, True).start()
        own_copy(which).start()
    move_start()
    down_own.start()
    for which in range(2):
        trail_own(which).start()
    for which in range(2):
        own_copy(which).wait()

    def trail_first():
        for which in range(2):

            @pl.when(level > 0)
            def _():
                trail(which, 0, level, True).start()

            @pl.when(level < depth - 1)
            def _():
                trail(which, 1, level, True).start()

    def trail_on(source, way):
        for which in range(2):
            trail(which, way, source).wait_recv()

            @pl.when((level < depth - 1) if way == 1 else (level > 0))
            def _():
                trail(which, way, source).start()

    def visit(step, act):
        if step == 0:
            act(level, None)
            return

        @pl.when(level - step >= 0)
        def _():
            act(level - step, 1)

        @pl.when(level + step < depth)
        def _():
            act(level + step, 0)

    def arrive(source, way):
        for which in range(2):
            along(which, way, source).wait_recv()

            @pl.when((level < depth - 1) if way == 1 else (level > 0))
            def _():
                along(which, way, source).start()

            plane_one(which, source).start()

    def spread(source, way):
        for which in range(2):
            plane_one(which, source).wait_recv()
            for kind, turn in seconds:
                if kind == which:
                    plane_two(kind, source, turn).start()

    def share(source, way):
        for which in range(2):
            for kind, turn in seconds:
                if kind == which:
                    plane_two(kind, source, turn).wait_recv()
            core(which, source).start()

    for step in range(depth + 2):
        if 1 <= step <= depth:
            visit(step - 1, spread)
        if 1 <= step < depth:
            visit(step, arrive)
        if step == 1:
            trail_first()
            move_finish()
            down_own.wait()
            for item in items:
                shared_one(item).start()
        if step == 2:
            for item in items:
                shared_one(item).wait_recv()
                for copy in shared_two(item):
                    copy.start()
        if step == depth:
            for item in items:
                for copy in shared_two(item):
                    copy.wait_recv()
                shared_core(item).start()
        if step >= 2:
            visit(step - 2, share)
            if step <= depth:
                visit(step - 1, trail_on)
    for item in items:
        shared_one(item).wait_send()
        for copy in shared_two(item):
            copy.wait_send()
        shared_core(item).wait()
    for which in range(2):
        trail_own(which).wait()

    def finish(source, carry):
        for which in range(2):

            @pl.when((source <= level) & (level < depth - 1))
            def _():
                trail(which, 1, source).wait_send()

            @pl.when((source >= level) & (level > 0))
            def _():
                trail(which, 0, source).wait_send()

            core(which, source).wait_recv()
            core(which, source).wait_send()
            plane_one(which, source).wait_send()

            @pl.when((source <= level) & (level < depth - 1))
            def _():
                along(which, 1, source).wait_send()

            @pl.when((source >= level) & (level > 0))
            def _():
                along(which, 0, source).wait_send()

        for kind, turn in seconds:
            plane_two(kind, source, turn).wait_send()
        return carry

    lax.fori_loop(0, depth, finish, 0)


def gather_rows(value, first, second, moved, down, cut):
    rows, width = value.shape
    total = lax.axis_size("expert")
    depth = total // PLANE
    semaphores = pltpu.SemaphoreType.DMA
    return pl.pallas_call(
        functools.partial(gather_kernel, depth, cut),
        out_shape=[
            jax.ShapeDtypeStruct((2 * total * rows, width), value.dtype),
            jax.ShapeDtypeStruct((depth,) + first.shape, first.dtype),
            jax.ShapeDtypeStruct((depth,) + second.shape, second.dtype),
            jax.ShapeDtypeStruct((2, depth, PLANE) + moved.shape[1:], moved.dtype),
            jax.ShapeDtypeStruct((2, PLANE) + down.shape, down.dtype),
        ],
        in_specs=[pl.BlockSpec(memory_space=pl.ANY)] * 5,
        out_specs=[pl.BlockSpec(memory_space=pl.ANY)] * 5,
        scratch_shapes=[
            semaphores((6,)),
            semaphores((2, 2, depth)),
            semaphores((2, depth)),
            semaphores((2, depth)),
            semaphores((2, depth)),
            semaphores((3, depth)),
            semaphores((3, depth)),
            semaphores((2, depth)),
            semaphores((2, depth)),
            semaphores((2, 2, depth)),
            semaphores((2, depth)),
            semaphores((depth,)),
            semaphores((depth,)),
            semaphores((depth + 2,)),
            semaphores((depth + 2,)),
            semaphores((2, depth + 2)),
            semaphores((2, depth + 2)),
            semaphores((depth + 2,)),
            semaphores((depth + 2,)),
        ],
        compiler_params=pltpu.CompilerParams(collective_id=1, has_side_effects=True),
        cost_estimate=LONG,
    )(value, first, second, moved, down)


def dot_nt(former, latter):
    return lax.dot_general(
        former, latter, (((1,), (1,)), ((), ())), preferred_element_type=jnp.float32
    )


def dot_tn(former, latter):
    return lax.dot_general(
        former, latter, (((0,), (0,)), ((), ())), preferred_element_type=jnp.float32
    )


def dispatch_kernel(depth, *refs):
    x_ref, choose_ref, grad_in, shared_in, down_in = refs[:5]
    rows_out, forth_out, back_out, wide_out, tall_out = refs[5:10]
    lines, placed, grads, weights, downs, low_ref, hidden_ref, forth_ref, back_ref = refs[10:19]
    wide_ref, tall_ref, load_sem, out_sem, zs, zr, es, er, own_sem, done_sem = refs[19:]
    half = lax.axis_index("fsdp")
    place = lax.axis_index("expert")
    level = place // PLANE
    spot = place % PLANE
    padded, width = downs.shape
    true = down_in.shape[0]
    chunk = 256 if padded % 256 == 0 else 128
    greet(line_others(half, place, depth) + plane_others(half, place))

    def along(way, source):
        block = lines.at[source]
        where = (half, place + (2 * way - 1) * PLANE)
        return remote(block, block, zs.at[way, source], zr.at[source], where)

    loads = [
        pltpu.make_async_copy(shared_in, weights, load_sem.at[0]),
        pltpu.make_async_copy(down_in, downs.at[pl.ds(0, true), :], load_sem.at[1]),
        pltpu.make_async_copy(grad_in, grads, load_sem.at[2]),
    ]
    lines[level] = x_ref[...]

    def pass_on(way, source):
        @pl.when((level < depth - 1) if way == 1 else (level > 0))
        def _():
            along(way, source).start()

    for way in range(2):
        pass_on(way, level)
    for load in loads:
        load.start()
    if padded > true:
        downs[pl.ds(true, padded - true), :] = jnp.zeros((padded - true, width), downs.dtype)

    def own_rows(source):
        return pltpu.make_async_copy(
            placed.at[source, spot], rows_out.at[spot, source], own_sem.at[source]
        )

    def to_mate(offset, source):
        mate = (spot + offset) % PLANE
        return remote(
            placed.at[source, mate],
            rows_out.at[spot, source],
            es.at[offset, source],
            er.at[offset, source],
            (half, place - spot + mate),
        )

    def from_mate(offset, source):
        mate = (spot + PLANE - offset) % PLANE
        block = rows_out.at[mate, source]
        return remote(
            block,
            block,
            es.at[offset, source],
            er.at[offset, source],
            (half, place - spot + mate),
        )

    def give(source):
        def columns(n, carry):
            at = pl.ds(pl.multiple_of(n * 512, 512), 512)
            for mate in range(PLANE):
                placed[source, mate, :, at] = jnp.dot(
                    choose_ref[source, mate],
                    lines[source, :, at],
                    preferred_element_type=jnp.float32,
                ).astype(placed.dtype)
            return carry

        lax.fori_loop(0, width // 512, columns, 0)
        for offset in range(1, PLANE):
            to_mate(offset, source).start()
        own_rows(source).start()

    def shared(source):
        def inner(n, carry):
            at = pl.ds(pl.multiple_of(n * chunk, chunk), chunk)
            after = pl.ds(pl.multiple_of(padded + n * chunk, 128), chunk)
            x = lines[source]
            gate = jnp.dot(x, weights[:, at], preferred_element_type=jnp.float32)
            up = jnp.dot(x, weights[:, after], preferred_element_type=jnp.float32)
            dh = dot_nt(grads[source], downs[at, :])
            sig = 1.0 / (1.0 + jnp.exp(-gate))
            act = gate * sig
            hidden_ref[source, :, at] = (act * up).astype(hidden_ref.dtype)
            low_ref[source, :, at] = (dh * up * (sig + act * (1.0 - sig))).astype(low_ref.dtype)
            low_ref[source, :, after] = (dh * act).astype(low_ref.dtype)
            return carry

        lax.fori_loop(0, padded // chunk, inner, 0)

        def outer(n, carry):
            at = pl.ds(pl.multiple_of(n * 512, 512), 512)
            forth_ref[:, at] = jnp.dot(
                hidden_ref[source], downs[:, at], preferred_element_type=jnp.float32
            ).astype(forth_ref.dtype)
            back_ref[:, at] = dot_nt(low_ref[source], weights[at, :]).astype(back_ref.dtype)
            return carry

        lax.fori_loop(0, width // 512, outer, 0)
        outs = [
            pltpu.make_async_copy(forth_ref, forth_out.at[source], out_sem.at[0]),
            pltpu.make_async_copy(back_ref, back_out.at[source], out_sem.at[1]),
        ]
        for out in outs:
            out.start()
        for out in outs:
            out.wait()

    give(level)
    for load in loads:
        load.wait()
    shared(level)

    def step(s, carry):
        @pl.when(level - s >= 0)
        def _():
            along(1, level - s).wait_recv()
            pass_on(1, level - s)

        @pl.when(level + s < depth)
        def _():
            along(0, level + s).wait_recv()
            pass_on(0, level + s)

        def one(way, act):
            source = level + (1 - 2 * way) * s

            @pl.when((source >= 0) & (source < depth))
            def _():
                act(source)

        def both(way, carry):
            one(way, give)
            return carry

        def both_shared(way, carry):
            one(way, shared)
            return carry

        lax.fori_loop(0, 2, both, 0)
        lax.fori_loop(0, 2, both_shared, 0)
        return carry

    lax.fori_loop(1, depth, step, 0)

    tokens = x_ref.shape[0]

    def all_lines(ref, at):
        return ref[:, :, at].reshape(depth * tokens, -1)

    def write(kind, k):
        slot = k % 2
        staged, target = ((wide_ref, wide_out), (tall_ref, tall_out))[kind]
        size = staged.shape[1]
        at = pl.ds(pl.multiple_of(k * size, size), size)
        return pltpu.make_async_copy(
            staged.at[slot], target.at[at, :], done_sem.at[kind, slot]
        )

    def tile(kind, k, ref, others):
        staged = (wide_ref, tall_ref)[kind]
        size = staged.shape[1]

        @pl.when(k >= 2)
        def _():
            write(kind, k - 2).wait()

        at = pl.ds(pl.multiple_of(k * size, size), size)
        staged[k % 2] = dot_tn(
            all_lines(ref, at), others[...].reshape(depth * tokens, -1)
        ).astype(staged.dtype)
        write(kind, k).start()

    def wide_tile(k, carry):
        tile(0, k, lines, low_ref)
        return carry

    def tall_tile(k, carry):
        tile(1, k, hidden_ref, grads)
        return carry

    wide_count = width // wide_ref.shape[1]
    tall_count = padded // tall_ref.shape[1]
    lax.fori_loop(0, wide_count, wide_tile, 0)
    lax.fori_loop(0, tall_count, tall_tile, 0)
    for kind, total in ((0, wide_count), (1, tall_count)):
        for k in range(max(0, total - 2), total):
            write(kind, k).wait()

    def finish(source, carry):
        own_rows(source).wait()
        for offset in range(1, PLANE):
            from_mate(offset, source).wait_recv()
            to_mate(offset, source).wait_send()

        @pl.when((source <= level) & (level < depth - 1))
        def _():
            along(1, source).wait_send()

        @pl.when((source >= level) & (level > 0))
        def _():
            along(0, source).wait_send()

        return carry

    lax.fori_loop(0, depth, finish, 0)


def dispatch(x, choose, grad_line, shared_full, down_full):
    depth = choose.shape[0]
    tokens, width = x.shape
    capacity = choose.shape[2]
    padded = shared_full.shape[1] // 2
    semaphores = pltpu.SemaphoreType.DMA
    low = x.dtype
    anywhere = pl.BlockSpec(memory_space=pl.ANY)
    local = pl.BlockSpec(memory_space=pltpu.VMEM)
    return pl.pallas_call(
        functools.partial(dispatch_kernel, depth),
        out_shape=[
            jax.ShapeDtypeStruct((PLANE, depth, capacity, width), low),
            jax.ShapeDtypeStruct((depth, tokens, width), low),
            jax.ShapeDtypeStruct((depth, tokens, width), low),
            jax.ShapeDtypeStruct((width, 2 * padded), low),
            jax.ShapeDtypeStruct((padded, width), low),
        ],
        in_specs=[local, local, anywhere, anywhere, anywhere],
        out_specs=[anywhere] * 5,
        scratch_shapes=[
            pltpu.VMEM((depth, tokens, width), low),
            pltpu.VMEM((depth, PLANE, capacity, width), low),
            pltpu.VMEM((depth, tokens, width), low),
            pltpu.VMEM((width, 2 * padded), low),
            pltpu.VMEM((padded, width), low),
            pltpu.VMEM((depth, tokens, 2 * padded), low),
            pltpu.VMEM((depth, tokens, padded), low),
            pltpu.VMEM((tokens, width), low),
            pltpu.VMEM((tokens, width), low),
            pltpu.VMEM((2, 256, 2 * padded), low),
            pltpu.VMEM((2, 128, width), low),
            semaphores((3,)),
            semaphores((2,)),
            semaphores((2, depth)),
            semaphores((depth,)),
            semaphores((PLANE, depth)),
            semaphores((PLANE, depth)),
            semaphores((depth,)),
            semaphores((2, 2)),
        ],
        compiler_params=pltpu.CompilerParams(
            collective_id=3, has_side_effects=True, vmem_limit_bytes=56 * MEBIBYTE
        ),
        cost_estimate=LONG,
    )(x, choose, grad_line, shared_full, down_full)


def return_kernel(depth, *refs):
    rows_in, scalars_in, choose_ref, shared_in = refs[:4]
    operands_in = refs[4:9]
    back_ref, prob_ref, gate_out, up_out, down_out = refs[9:14]
    came, scalars, shared, onward, incoming, prob_send, prob_land = refs[14:21]
    held = refs[21:26]
    give_wide, give_tall, take_wide, take_tall, done_wide, done_tall = refs[26:32]
    own_sem, es, er, ss, sr, load_sem, shared_sem, cs, cr, ps, pr = refs[32:43]
    ws, wr, ts, tr, wide_sem, tall_sem = refs[43:]
    x_held, gate_held, up_held, hidden_held, grad_held = held
    half = lax.axis_index("fsdp")
    place = lax.axis_index("expert")
    level = place // PLANE
    spot = place % PLANE
    other = (1 - half, place)
    tokens, width = back_ref.shape
    capacity = choose_ref.shape[2]
    wide_count, wide_rows = take_wide.shape[1:3]
    tall_count, tall_rows, tall_width = take_tall.shape
    greet(line_others(half, place, depth) + plane_others(half, place) + [other])

    def rows_to(offset, source):
        mate = (spot + offset) % PLANE
        where = (half, place - spot + mate)
        return (
            remote(
                rows_in.at[mate, source],
                came.at[spot, source],
                es.at[offset, source],
                er.at[offset, source],
                where,
            ),
            remote(
                scalars_in.at[mate, source],
                scalars.at[spot, source],
                ss.at[offset, source],
                sr.at[offset, source],
                where,
            ),
        )

    def rows_from(offset, source):
        mate = (spot + PLANE - offset) % PLANE
        where = (half, place - spot + mate)
        block, small = came.at[mate, source], scalars.at[mate, source]
        return (
            remote(block, block, es.at[offset, source], er.at[offset, source], where),
            remote(small, small, ss.at[offset, source], sr.at[offset, source], where),
        )

    def own_rows(source):
        return (
            pltpu.make_async_copy(
                rows_in.at[spot, source], came.at[spot, source], own_sem.at[0, source]
            ),
            pltpu.make_async_copy(
                scalars_in.at[spot, source], scalars.at[spot, source], own_sem.at[1, source]
            ),
        )

    def shared_load(slot, source):
        return pltpu.make_async_copy(shared_in.at[source], shared.at[slot], shared_sem.at[slot])

    def each_way(s, act):
        def one(way, carry):
            source = level + (2 * way - 1) * s

            @pl.when((source >= 0) & (source < depth) & ((s > 0) | (way == 0)))
            def _():
                act(way, source)

            return carry

        lax.fori_loop(0, 2, one, 0)

    def begin(way, source):
        for offset in range(1, PLANE):
            for copy in rows_to(offset, source):
                copy.start()
        for copy in own_rows(source):
            copy.start()

    def begin_step(i, carry):
        each_way(depth - 1 - i, begin)
        return carry

    lax.fori_loop(0, depth, begin_step, 0)
    loads = [
        pltpu.make_async_copy(source, target, load_sem.at[k])
        for k, (source, target) in enumerate(zip(operands_in, held))
    ]
    for load in loads:
        load.start()
    for load in loads:
        load.wait()

    def wide_tiles(owner, k):
        at = pl.ds(pl.multiple_of((owner * wide_count + k) * wide_rows, wide_rows), wide_rows)
        x = x_held[:, at]
        return dot_tn(x, gate_held[...]), dot_tn(x, up_held[...])

    def tall_tile(owner, k):
        at = pl.ds(pl.multiple_of(k * tall_rows, tall_rows), tall_rows)
        over = pl.ds(pl.multiple_of(owner * tall_width, tall_width), tall_width)
        return dot_tn(hidden_held[:, at], grad_held[:, over])

    def wide_send(which, k):
        slot = k % 2
        return remote(
            give_wide.at[slot, which],
            take_wide.at[which, k],
            ws.at[slot, which],
            wr.at[which, k],
            other,
        )

    def tall_send(k):
        slot = k % 2
        return remote(give_tall.at[slot], take_tall.at[k], ts.at[slot], tr.at[k], other)

    def wide_write(which, k):
        target = (gate_out, up_out)[which]
        at = pl.ds(pl.multiple_of(k * wide_rows, wide_rows), wide_rows)
        return pltpu.make_async_copy(done_wide.at[which], target.at[at, :], wide_sem.at[which])

    def tall_write(k):
        slot = k % 2
        at = pl.ds(pl.multiple_of(k * tall_rows, tall_rows), tall_rows)
        return pltpu.make_async_copy(done_tall.at[slot], down_out.at[at, :], tall_sem.at[slot])

    def give_wide_tile(k):
        @pl.when(k >= 2)
        def _():
            for which in range(2):
                wide_send(which, k - 2).wait_send()

        for which, tile in enumerate(wide_tiles(1 - half, k)):
            give_wide[k % 2, which] = tile.astype(give_wide.dtype)
            wide_send(which, k).start()

    def give_tall_tile(k):
        @pl.when(k >= 2)
        def _():
            tall_send(k - 2).wait_send()

        give_tall[k % 2] = tall_tile(1 - half, k).astype(give_tall.dtype)
        tall_send(k).start()

    def keep_wide_tile(k):
        @pl.when(k >= 1)
        def _():
            for which in range(2):
                wide_write(which, k - 1).wait()

        for which, tile in enumerate(wide_tiles(half, k)):
            wide_send(which, k).wait_recv()
            tile = tile + take_wide[which, k].astype(jnp.float32)
            done_wide[which] = tile.astype(done_wide.dtype)
            wide_write(which, k).start()

    def keep_tall_tile(k):
        @pl.when(k >= 2)
        def _():
            tall_write(k - 2).wait()

        tile = tall_tile(half, k)
        tall_send(k).wait_recv()
        tile = tile + take_tall[k].astype(jnp.float32)
        done_tall[k % 2] = tile.astype(done_tall.dtype)
        tall_write(k).start()

    units = 2 * (wide_count + tall_count)
    each = -(-units // depth)
    bounds = (0, wide_count, wide_count + tall_count, units - tall_count, units)
    acts = (give_wide_tile, give_tall_tile, keep_wide_tile, keep_tall_tile)

    def fill(unit, carry):
        for act, low, high in zip(acts, bounds[:-1], bounds[1:]):

            @pl.when((unit >= low) & (unit < high))
            def _():
                act(unit - low)

        return carry

    def chain_out(source):
        up = jnp.where(source > level, 1, 0)
        step = 2 * up - 1
        slot = jnp.where(source == level - 1, depth, source)
        return remote(
            onward.at[up],
            incoming.at[slot],
            cs.at[source],
            cr.at[slot],
            (half, place + step * PLANE),
        )

    def chain_in(slot):
        block = incoming.at[slot]
        return remote(block, block, cs.at[0], cr.at[slot], (half, place))

    def prob_to(source):
        return remote(
            prob_send.at[source],
            prob_land.at[level],
            ps.at[source],
            pr.at[level],
            (half, source * PLANE + spot),
        )

    def prob_from(source):
        block = prob_land.at[source]
        return remote(block, block, ps.at[source], pr.at[source], (half, source * PLANE + spot))

    def add_incoming(slot):
        chain_in(slot).wait_recv()
        back_ref[...] += incoming[slot].astype(jnp.float32)

    def settle(way, source):
        for copy in own_rows(source):
            copy.wait()
        for offset in range(1, PLANE):
            for copy in rows_from(offset, source):
                copy.wait_recv()
        shared_load(way, source).wait()

        def columns(n, carry):
            at = pl.ds(pl.multiple_of(n * 512, 512), 512)
            total = shared[way, :, at].astype(jnp.float32)
            for mate in range(PLANE):
                total = total + dot_tn(choose_ref[source, mate], came[mate, source, :, at])
            back_ref[:, at] = total
            return carry

        lax.fori_loop(0, width // 512, columns, 0)
        lines = lax.broadcasted_iota(jnp.int32, (8, tokens), 0)
        probs = jnp.zeros((8, tokens), jnp.float32)
        for mate in range(PLANE):
            part = jnp.dot(
                scalars[mate, source, :, :capacity],
                choose_ref[source, mate].astype(jnp.float32),
                preferred_element_type=jnp.float32,
                precision=lax.Precision.HIGHEST,
            )
            probs = jnp.where(lines == mate, part, probs)

        @pl.when((source >= level) & (level > 0))
        def _():
            add_incoming(source)

        @pl.when((source < level) & (level < depth - 1))
        def _():
            add_incoming(source)

        @pl.when((source == level) & (level < depth - 1))
        def _():
            add_incoming(depth)

        @pl.when(source == level)
        def _():
            prob_land[level] = probs

        @pl.when(source != level)
        def _():
            prob_send[source] = probs
            prob_to(source).start()
            former = source + 2 * way - 1

            @pl.when((former >= 0) & (former < depth))
            def _():
                chain_out(former).wait_send()

            onward[way] = back_ref[...].astype(onward.dtype)
            chain_out(source).start()

    def step(i, carry):
        s = depth - 1 - i
        each_way(s, lambda way, source: shared_load(way, source).start())
        lax.fori_loop(i * each, jnp.minimum((i + 1) * each, units), fill, 0)
        each_way(s, settle)
        return carry

    lax.fori_loop(0, depth, step, 0)
    for which in range(2):
        wide_write(which, wide_count - 1).wait()
        for k in (wide_count - 2, wide_count - 1):
            wide_send(which, k).wait_send()
    for k in (tall_count - 2, tall_count - 1):
        tall_write(k).wait()
        tall_send(k).wait_send()

    def finish(source, carry):
        for offset in range(1, PLANE):
            for copy in rows_to(offset, source):
                copy.wait_send()

        @pl.when((source == level - 1) | (source == level + 1))
        def _():
            chain_out(source).wait_send()

        @pl.when(source != level)
        def _():
            prob_to(source).wait_send()
            prob_from(source).wait_recv()

        prob_ref[source] = prob_land[source]
        return carry

    lax.fori_loop(0, depth, finish, 0)


def give_back(rows, scalars, choose, shared_back, operands):
    depth, _, capacity, tokens = choose.shape
    width = rows.shape[-1]
    slots, inner = operands[1].shape
    wide_rows, tall_rows = 256 if depth <= PLANE else 128, 128
    wide_count = width // 2 // wide_rows
    tall_count = inner // tall_rows
    semaphores = pltpu.SemaphoreType.DMA
    low = rows.dtype
    wide = jnp.float32
    anywhere = pl.BlockSpec(memory_space=pl.ANY)
    local = pl.BlockSpec(memory_space=pltpu.VMEM)
    return pl.pallas_call(
        functools.partial(return_kernel, depth),
        out_shape=[
            jax.ShapeDtypeStruct((tokens, width), wide),
            jax.ShapeDtypeStruct((depth, 8, tokens), wide),
            jax.ShapeDtypeStruct((width // 2, inner), low),
            jax.ShapeDtypeStruct((width // 2, inner), low),
            jax.ShapeDtypeStruct((inner, width // 2), low),
        ],
        in_specs=[anywhere, anywhere, local, anywhere] + [anywhere] * 5,
        out_specs=[local, local, anywhere, anywhere, anywhere],
        scratch_shapes=[
            pltpu.VMEM((PLANE, depth, capacity, width), low),
            pltpu.VMEM((PLANE, depth, 8, 128), wide),
            pltpu.VMEM((2, tokens, width), low),
            pltpu.VMEM((2, tokens, width), low),
            pltpu.VMEM((depth + 1, tokens, width), low),
            pltpu.VMEM((depth, 8, tokens), wide),
            pltpu.VMEM((depth, 8, tokens), wide),
        ]
        + [pltpu.VMEM(operand.shape, low) for operand in operands]
        + [
            pltpu.VMEM((2, 2, wide_rows, inner), low),
            pltpu.VMEM((2, tall_rows, width // 2), low),
            pltpu.VMEM((2, wide_count, wide_rows, inner), low),
            pltpu.VMEM((tall_count, tall_rows, width // 2), low),
            pltpu.VMEM((2, wide_rows, inner), low),
            pltpu.VMEM((2, tall_rows, width // 2), low),
            semaphores((2, depth)),
            semaphores((PLANE, depth)),
            semaphores((PLANE, depth)),
            semaphores((PLANE, depth)),
            semaphores((PLANE, depth)),
            semaphores((5,)),
            semaphores((2,)),
            semaphores((depth,)),
            semaphores((depth + 1,)),
            semaphores((depth,)),
            semaphores((depth,)),
            semaphores((2, 2)),
            semaphores((2, wide_count)),
            semaphores((2,)),
            semaphores((tall_count,)),
            semaphores((2,)),
            semaphores((2,)),
        ],
        compiler_params=pltpu.CompilerParams(
            collective_id=4, has_side_effects=True, vmem_limit_bytes=62 * MEBIBYTE
        ),
        cost_estimate=LONG,
    )(rows, scalars, choose, shared_back, *operands)


def reduce_kernel(depth, count, cut, *refs):
    parts = refs[:count]
    move_in, out_ref, move_out = refs[count : count + 3]
    acc, inc, one_a, one_b, two_a, two_b, zin = refs[count + 3 : count + 10]
    own_sem, cs, cr, ps, pr, qs, qr, zs, zr, move_sem, ms, mr = refs[count + 10 :]
    half = lax.axis_index("fsdp")
    place = lax.axis_index("expert")
    level = place // PLANE
    spot = place % PLANE
    total = depth * PLANE
    mates = plane_mates(place)
    rows = out_ref.shape[0]
    group = PLANE * rows
    width = out_ref.shape[1]
    greet_neighbours(half, place, depth)

    starts = [sum(part.shape[1] for part in parts[:k]) for k in range(count)]

    def rows_of(k, owner, t):
        start = pl.multiple_of((owner * total + t * PLANE) * rows, group)
        return parts[k].at[pl.ds(start, group), :]

    def kept(k, t):
        return pltpu.make_async_copy(
            rows_of(k, half, t),
            acc.at[t, :, pl.ds(starts[k], parts[k].shape[1])],
            own_sem.at[k, t],
        )

    def given(k, t):
        return remote(
            rows_of(k, 1 - half, t),
            inc.at[t, :, pl.ds(starts[k], parts[k].shape[1])],
            cs.at[k, t],
            cr.at[k, t],
            (1 - half, place),
        )

    def block(t, q, n, lo, hi):
        return acc.at[t, pl.ds(pl.multiple_of(q * rows, rows), n * rows), pl.ds(lo, hi - lo)]

    pair = spot - spot % 2

    def first(t, turn):
        low = spot % 2
        if turn == 0:
            source = block(t, 2 - pair, 2, 0, cut)
            target, where = one_a.at[t], mates[1]
        else:
            source = block(t, 2 * turn - 1 - low, 1, cut, width)
            target, where = one_b.at[t, turn - 1], mates[0]
        return remote(source, target, ps.at[turn, t], pr.at[turn, t], (half, where))

    def second(t, turn):
        if turn == 0:
            source = block(t, pair + 1 - spot % 2, 1, 0, cut)
            target, where = two_a.at[t], mates[0]
        else:
            source = block(t, (spot + 2) % PLANE, 1, cut, width)
            target, where = two_b.at[t], mates[1]
        return remote(source, target, qs.at[turn, t], qr.at[turn, t], (half, where))

    def line(t, way):
        step = 2 * way - 1
        return remote(
            block(t, spot, 1, 0, width),
            zin.at[way, t],
            zs.at[way, t],
            zr.at[way, t],
            (half, place + step * PLANE),
        )

    def add_rows(t, start, n, lo, hi, piece):
        def one(i, carry):
            r = pl.multiple_of(i * 16, 16)
            at = (t, pl.ds(pl.multiple_of(start + r, 16), 16), pl.ds(lo, hi - lo))
            new = piece(pl.ds(r, 16)).astype(jnp.float32)
            acc[at] = (acc[at].astype(jnp.float32) + new).astype(acc.dtype)
            return carry

        lax.fori_loop(0, n // 16, one, 0)

    def stage_a(t):
        for k in range(count):
            kept(k, t).wait()
            given(k, t).wait_recv()
        add_rows(t, 0, group, 0, width, lambda r: inc[t, r, :])
        for turn in range(3):
            first(t, turn).start()

    def stage_b(t):
        first(t, 0).wait_recv()
        add_rows(t, pair * rows, 2 * rows, 0, cut, lambda r: one_a[t, r, :])
        second(t, 0).start()
        for turn in range(2):
            first(t, 1 + turn).wait_recv()
            add_rows(
                t,
                (spot % 2 + 2 * turn) * rows,
                rows,
                cut,
                width,
                lambda r: one_b[t, turn, r, :],
            )
        second(t, 1).start()

    def stage_c(t):
        second(t, 0).wait_recv()
        add_rows(t, spot * rows, rows, 0, cut, lambda r: two_a[t, r, :])
        second(t, 1).wait_recv()
        add_rows(t, spot * rows, rows, cut, width, lambda r: two_b[t, r, :])

        def take(way):
            line(t, way).wait_recv()
            add_rows(t, spot * rows, rows, 0, width, lambda r: zin[way, t, r, :])

        @pl.when((t >= level) & (level > 0))
        def _():
            take(1)

        @pl.when((t <= level) & (level < depth - 1))
        def _():
            take(0)

        @pl.when(t > level)
        def _():
            line(t, 1).start()

        @pl.when(t < level)
        def _():
            line(t, 0).start()

    def visit(index, act):
        if index >= depth or index < 0:
            return
        step = depth - 1 - index
        if step == 0:
            act(level)
            return

        @pl.when(level + step < depth)
        def _():
            act(level + step)

        @pl.when(level - step >= 0)
        def _():
            act(level - step)

    def begin(t):
        for k in range(count):
            given(k, t).start()
            kept(k, t).start()

    for index in range(depth):
        visit(index, begin)
    move_start, move_finish = exchange_along(
        depth,
        half,
        place,
        move_in,
        lambda source: move_out.at[source],
        move_sem.at[0],
        ms,
        mr,
    )
    move_start()
    for index in range(depth + 2):
        visit(index, stage_a)
        visit(index - 1, stage_b)
        visit(index - 2, stage_c)

    def emit(i, carry):
        r = pl.multiple_of(i * 16, 16)
        at = pl.ds(pl.multiple_of(spot * rows + r, 16), 16)
        out_ref[pl.ds(r, 16), :] = acc[level, at, :].astype(out_ref.dtype)
        return carry
    lax.fori_loop(0, rows // 16, emit, 0)
    move_finish()

    def finish(t, carry):
        for k in range(count):
            given(k, t).wait_send()
        for turn in range(3):
            first(t, turn).wait_send()
        for turn in range(2):
            second(t, turn).wait_send()

        @pl.when(t > level)
        def _():
            line(t, 1).wait_send()

        @pl.when(t < level)
        def _():
            line(t, 0).wait_send()
        return carry

    lax.fori_loop(0, depth, finish, 0)


def reduce_rows(parts, moved, cut):
    total = lax.axis_size("expert")
    depth = total // PLANE
    rows = parts[0].shape[0] // (2 * total)
    width = sum(part.shape[1] for part in parts)
    group = PLANE * rows
    n = len(parts)
    semaphores = pltpu.SemaphoreType.DMA
    low = parts[0].dtype
    return pl.pallas_call(
        functools.partial(reduce_kernel, depth, n, cut),
        out_shape=[
            jax.ShapeDtypeStruct((rows, width), jnp.float32),
            jax.ShapeDtypeStruct(moved.shape, moved.dtype),
        ],
        in_specs=[pl.BlockSpec(memory_space=pl.ANY)] * (n + 1),
        out_specs=[
            pl.BlockSpec(memory_space=pltpu.VMEM),
            pl.BlockSpec(memory_space=pl.ANY),
        ],
        scratch_shapes=[
            pltpu.VMEM((depth, group, width), low),
            pltpu.VMEM((depth, group, width), low),
            pltpu.VMEM((depth, 2 * rows, cut), low),
            pltpu.VMEM((depth, 2, rows, width - cut), low),
            pltpu.VMEM((depth, rows, cut), low),
            pltpu.VMEM((depth, rows, width - cut), low),
            pltpu.VMEM((2, depth, rows, width), low),
            semaphores((n, depth)),
            semaphores((n, depth)),
            semaphores((n, depth)),
            semaphores((3, depth)),
            semaphores((3, depth)),
            semaphores((2, depth)),
            semaphores((2, depth)),
            semaphores((2, depth)),
            semaphores((2, depth)),
            semaphores((1,)),
            semaphores((depth,)),
            semaphores((depth,)),
        ],
        cost_estimate=LONG,
        compiler_params=pltpu.CompilerParams(
            collective_id=2, has_side_effects=True, vmem_limit_bytes=60 * MEBIBYTE
        ),
    )(*parts, moved)


def body(
    tokens,
    segments,
    routes,
    slot_index,
    cotangent,
    attention_norm,
    query_weight,
    latent_down,
    latent_norm,
    latent_up,
    output_weight,
    feed_norm,
    router_weight,
    shared_gate,
    shared_up,
    shared_down,
    expert_gate,
    expert_up,
    expert_down,
):
    row_count = tokens.shape[1]
    expert_total = lax.axis_size("expert")
    depth = expert_total // PLANE
    plane, line = groups(expert_total)
    place = lax.axis_index("expert")
    level = place // PLANE
    device_half = lax.axis_index("fsdp")
    capacity = row_count * TOPK // expert_total
    line_rows = depth * row_count
    inputs = tokens[0].astype(jnp.float32)

    part_rows = query_weight.shape[0]
    gain_width = attention_norm.shape[0]
    latent_width = latent_norm.shape[0]
    small = jnp.concatenate([attention_norm, latent_norm, feed_norm, router_weight.reshape(-1)])
    cuts = [
        0,
        gain_width,
        gain_width + latent_width,
        2 * gain_width + latent_width,
        small.shape[0],
    ]
    small = jnp.pad(small, (0, 128 * part_rows - small.shape[0])).reshape(part_rows, 128)
    query_width = query_weight.shape[1]
    down_width = latent_down.shape[1]
    entry_width = query_width + down_width + (-down_width) % 128
    up_width = HEADS * (NOPE + VALUE)
    quarters = part_rows // latent_up.shape[0]
    packed = jnp.concatenate(
        [
            query_weight,
            jnp.pad(latent_down, ((0, 0), (0, (-down_width) % 128))),
            latent_up.reshape(latent_up.shape[0], quarters, -1)
            .transpose(1, 0, 2)
            .reshape(part_rows, -1),
            small,
        ],
        axis=1,
    )
    cut = packed.shape[1] // 256 * 128
    route_rows = routes[0]
    slot_rows = slot_index[0]
    target = jnp.where(
        slot_rows >= 0, route_rows * capacity + slot_rows, expert_total * capacity
    )
    target = jnp.pad(target, ((0, 0), (0, 8 - TOPK)), constant_values=expert_total * capacity).T
    shared_width = shared_gate.shape[1] // (2 * depth)
    shared_both = jnp.stack([shared_gate, shared_up]).reshape(
        2, part_rows, 2, depth, shared_width
    )
    shared_both = shared_both.transpose(3, 1, 0, 2, 4)
    shared_both = shared_both.reshape(depth, part_rows, 2, 2 * shared_width)
    shared_padded = 2 * shared_width + (-2 * shared_width) % 128
    shared_both = jnp.pad(
        shared_both, ((0, 0), (0, 0), (0, 0), (0, shared_padded - 2 * shared_width))
    ).reshape(depth, part_rows, 2 * shared_padded)
    packed_full, grad_line, target_line, shared_full, sdown_full = gather_rows(
        packed, cotangent[0], target, shared_both, shared_down, cut
    )
    shared_full = shared_full.reshape(D, 2 * shared_padded)
    sdown_full = sdown_full.reshape(2 * shared_width, D)
    expert_gate_full = lax.all_gather(expert_gate[0], "fsdp", axis=0, tiled=True)
    expert_up_full = lax.all_gather(expert_up[0], "fsdp", axis=0, tiled=True)
    expert_down_full = lax.all_gather(expert_down[0], "fsdp", axis=1, tiled=True)
    packed_full, grad_line, target_line, expert_gate_full, expert_up_full, expert_down_full = (
        lax.optimization_barrier(
            (
                packed_full,
                grad_line,
                target_line,
                expert_gate_full,
                expert_up_full,
                expert_down_full,
            )
        )
    )
    output_rows, packed_full = lax.optimization_barrier((output_weight, packed_full))
    output_full = lax.all_gather(output_rows, ("fsdp", "expert"), axis=0, tiled=True)
    grad_line = grad_line.reshape(line_rows, D)
    entry_full = packed_full[:, :entry_width]
    up_parts = packed_full.reshape(2 * expert_total, quarters, latent_up.shape[0], -1)
    up_full = jnp.concatenate(
        [up_parts[:, k, :, entry_width:-128].reshape(LATENT, -1) for k in range(quarters)],
        axis=1,
    )
    small_full = packed_full[:, -128:].reshape(2 * expert_total, -1)
    gain_one, gain_latent, gain_feed, router_full = (
        small_full[:, cuts[0] : cuts[1]].reshape(-1),
        small_full[:, cuts[1] : cuts[2]].reshape(-1),
        small_full[:, cuts[2] : cuts[3]].reshape(-1),
        small_full[:, cuts[3] : cuts[4]].reshape(-1, expert_total),
    )

    slot_names = level * PLANE * capacity + jnp.arange(PLANE * capacity)
    hits = target_line[:, :TOPK, None, :] == slot_names[None, None, :, None]
    choose_rows = jnp.any(hits, axis=1).astype(jnp.bfloat16)

    def to_experts(rows_line):
        placed = jnp.einsum(
            "zst,ztd->zsd",
            choose_rows,
            rows_line.reshape(depth, row_count, D),
            preferred_element_type=jnp.float32,
        ).astype(jnp.bfloat16)
        placed = placed.reshape(depth, PLANE, capacity, D).transpose(1, 0, 2, 3)
        return lax.all_to_all(
            placed, "expert", split_axis=0, concat_axis=0, axis_index_groups=plane, tiled=True
        ).reshape(expert_total * capacity, D)

    def from_experts(rows):
        return lax.all_to_all(
            rows.reshape(PLANE, depth, capacity, -1),
            "expert",
            split_axis=0,
            concat_axis=0,
            axis_index_groups=plane,
            tiled=True,
        )

    cosine, sine_table = rotary_table(row_count, device_half * row_count, ROPE)
    score_scale = (NOPE + ROPE) ** (-0.5)
    gain_first = gain_one.astype(jnp.float32)
    normed_low = norm_rows(inputs, gain_first).astype(jnp.bfloat16)
    entry = matmul(normed_low, entry_full)
    query_raw = entry[:, :query_width].reshape(row_count, HEADS, NOPE + ROPE)
    queries = jnp.concatenate(
        [
            query_raw[..., :NOPE],
            rotate_forward(query_raw[..., NOPE:], cosine[:, None, :], sine_table[:, None, :]),
        ],
        axis=-1,
    ).astype(jnp.bfloat16)
    compressed = entry[:, query_width : query_width + down_width]
    latent_gain = gain_latent.astype(jnp.float32)
    latent = norm_rows(compressed[:, :LATENT], latent_gain).astype(jnp.bfloat16)
    key_rope = rotate_forward(compressed[:, LATENT:], cosine, sine_table).astype(jnp.bfloat16)
    prior_latent, prior_rope = passed_along((latent, key_rope), "fsdp", 1)
    key_latent = jnp.concatenate([prior_latent, latent], axis=0)
    keys_rope = jnp.concatenate([prior_rope, key_rope], axis=0)
    expanded = (
        matmul(key_latent, up_full).astype(jnp.bfloat16).reshape(2 * row_count, HEADS, NOPE + VALUE)
    )
    query_place = device_half * row_count + jnp.arange(row_count)
    key_place = (device_half - 1) * row_count + jnp.arange(2 * row_count)
    padded_segments = jnp.concatenate([jnp.full((row_count,), -1, jnp.int32), segments[0]])
    key_segment = lax.dynamic_slice_in_dim(padded_segments, device_half * row_count, 2 * row_count)
    query_segment = lax.dynamic_slice_in_dim(segments[0], device_half * row_count, row_count)
    visible = (key_place[None, :] <= query_place[:, None]) & (
        key_segment[None, :] == query_segment[:, None]
    )
    scores = attention_scores(queries, expanded, keys_rope, visible, score_scale)
    top_score = jnp.max(scores, axis=-1, keepdims=True)
    log_total = top_score + jnp.log(jnp.sum(jnp.exp(scores - top_score), axis=-1, keepdims=True))
    weight_low = jnp.exp(scores - log_total).astype(jnp.bfloat16)
    mixed_heads = (
        jnp.einsum(
            "hqk,khd->qhd", weight_low, expanded[..., NOPE:], preferred_element_type=jnp.float32
        )
        .reshape(row_count, HEADS * VALUE)
        .astype(jnp.bfloat16)
    )
    residual = inputs + matmul(mixed_heads, output_full)
    feed_gain = gain_feed.astype(jnp.float32)
    mixed_low = norm_rows(residual, feed_gain).astype(jnp.bfloat16)
    grad_rows = to_experts(grad_line)
    choose_slots = choose_rows.reshape(depth, PLANE, capacity, row_count)
    mixed_low, grad_rows = lax.optimization_barrier((mixed_low, grad_rows))
    mixed_rows, shared_out, shared_back, shared_grad, sdown_grad = dispatch(
        mixed_low, choose_slots, grad_line.reshape(depth, row_count, D), shared_full, sdown_full
    )
    mixed_rows = mixed_rows.reshape(expert_total * capacity, D)
    shared_out = shared_out.reshape(line_rows, D)
    hidden_grad_raw = right_matmul(grad_rows, expert_down_full)
    slot_probs = jax.nn.softmax(matmul(mixed_rows, router_full), axis=-1)
    gate_column = lax.dynamic_slice_in_dim(slot_probs, place, 1, axis=1)

    gate_part = matmul(mixed_rows, expert_gate_full)
    up_portion = matmul(mixed_rows, expert_up_full)
    hidden_wide = jax.nn.silu(gate_part) * up_portion
    hidden = hidden_wide.astype(jnp.bfloat16)
    slot_grad = jnp.sum(hidden.astype(jnp.float32) * hidden_grad_raw, axis=-1)
    hidden_grad = hidden_grad_raw * gate_column
    gate_part_grad, up_part_grad = swiglu_back(gate_part, up_portion, hidden_grad)
    gate_low = gate_part_grad.astype(jnp.bfloat16)
    up_low = up_part_grad.astype(jnp.bfloat16)
    input_grad = (
        right_matmul(gate_low, expert_gate_full) + right_matmul(up_low, expert_up_full)
    ).astype(jnp.bfloat16)
    hidden_scaled = (hidden.astype(jnp.float32) * gate_column).astype(jnp.bfloat16)
    slot_grad = jnp.pad(
        slot_grad.reshape(PLANE, depth, 1, capacity), ((0, 0), (0, 0), (0, 0), (0, 128 - capacity))
    )
    back_and_shared, prob_parts, expert_gate_piece, expert_up_piece, expert_down_piece = give_back(
        input_grad.reshape(PLANE, depth, capacity, D),
        jnp.broadcast_to(slot_grad, (PLANE, depth, 8, 128)),
        choose_slots,
        shared_back,
        [mixed_rows, gate_low, up_low, hidden_scaled, grad_rows],
    )
    back_and_shared, hidden = lax.optimization_barrier((back_and_shared, hidden))
    expert_out = (matmul(hidden, expert_down_full) * gate_column).astype(jnp.bfloat16)
    returned = from_experts(expert_out)

    sdown_grad = sdown_grad[: 2 * shared_width]

    def scatter_plane(value):
        part = lax.psum_scatter(value, "fsdp", scatter_dimension=0, tiled=True)
        return lax.psum_scatter(
            part, "expert", scatter_dimension=0, axis_index_groups=plane, tiled=True
        )

    shared_grad = shared_grad.reshape(2, depth, PLANE, part_rows, -1).transpose(0, 2, 1, 3, 4)
    shared_summed = scatter_plane(shared_grad.reshape(2 * PLANE, depth, part_rows, -1))[0]
    sdown_piece = scatter_plane(sdown_grad).astype(jnp.float32)

    out_grad = cotangent[0].astype(jnp.float32)
    probabilities = jax.nn.softmax(matmul(mixed_low, router_full), axis=-1)
    prob_grad = prob_parts[:, :PLANE].reshape(expert_total, row_count).T
    logit_low = (
        probabilities * (prob_grad - jnp.sum(probabilities * prob_grad, axis=-1, keepdims=True))
    ).astype(jnp.bfloat16)
    router_grad = left_matmul(mixed_low, logit_low)
    mixed_grad = right_matmul(logit_low, router_full) + back_and_shared
    residual_add, feed_gain_grad = norm_back(residual, feed_gain, mixed_grad)
    residual_grad = out_grad + residual_add
    attended_low = residual_grad.astype(jnp.bfloat16)
    output_grad = left_matmul(mixed_heads, attended_low)
    heads_low = (
        right_matmul(attended_low, output_full)
        .astype(jnp.bfloat16)
        .reshape(row_count, HEADS, VALUE)
    )
    scores_again = attention_scores(queries, expanded, keys_rope, visible, score_scale)
    probs_again = jnp.exp(scores_again - log_total)
    weights_again = probs_again.astype(jnp.bfloat16)
    weight_grad = jnp.einsum(
        "qhd,khd->hqk", heads_low, expanded[..., NOPE:], preferred_element_type=jnp.float32
    )
    value_grad = jnp.einsum(
        "hqk,qhd->khd", weights_again, heads_low, preferred_element_type=jnp.float32
    )
    delta_rows = jnp.sum(probs_again * weight_grad, axis=-1, keepdims=True)
    score_low = (probs_again * (weight_grad - delta_rows)).astype(jnp.bfloat16)
    query_nope_grad = (
        jnp.einsum(
            "hqk,khd->qhd", score_low, expanded[..., :NOPE], preferred_element_type=jnp.float32
        )
        * score_scale
    )
    query_rope_grad = (
        jnp.einsum("hqk,kd->qhd", score_low, keys_rope, preferred_element_type=jnp.float32)
        * score_scale
    )
    key_nope_grad = (
        jnp.einsum(
            "hqk,qhd->khd", score_low, queries[..., :NOPE], preferred_element_type=jnp.float32
        )
        * score_scale
    )
    key_rope_grad = (
        jnp.einsum(
            "hqk,qhd->kd", score_low, queries[..., NOPE:], preferred_element_type=jnp.float32
        )
        * score_scale
    )
    expanded_grad = jnp.concatenate([key_nope_grad, value_grad], axis=-1).reshape(
        2 * row_count, HEADS * (NOPE + VALUE)
    )
    returned_expanded, returned_rope = (
        passed_along(expanded_grad[:row_count].astype(jnp.bfloat16), "fsdp", -1).astype(
            jnp.float32
        ),
        passed_along(key_rope_grad[:row_count].astype(jnp.bfloat16), "fsdp", -1).astype(
            jnp.float32
        ),
    )
    expanded_low = (expanded_grad[row_count:] + returned_expanded).astype(jnp.bfloat16)
    own_rope = key_rope_grad[row_count:] + returned_rope
    latent_grad = right_matmul(expanded_low, up_full)
    quarter = up_width // quarters
    up_weight_grad = jnp.stack(
        [
            left_matmul(latent, expanded_low[:, k * quarter : (k + 1) * quarter])
            .astype(jnp.bfloat16)
            .reshape(2 * expert_total, latent_up.shape[0], quarter)
            for k in range(quarters)
        ],
        axis=1,
    ).reshape(2 * expert_total * part_rows, quarter)
    compressed_latent_grad, latent_gain_grad = norm_back(
        compressed[:, :LATENT], latent_gain, latent_grad
    )
    compressed_low = jnp.concatenate(
        [compressed_latent_grad, rotate_backward(own_rope, cosine, sine_table)], axis=-1
    ).astype(jnp.bfloat16)
    query_low = (
        jnp.concatenate(
            [
                query_nope_grad,
                rotate_backward(query_rope_grad, cosine[:, None, :], sine_table[:, None, :]),
            ],
            axis=-1,
        )
        .reshape(row_count, HEADS * (NOPE + ROPE))
        .astype(jnp.bfloat16)
    )
    entry_low = jnp.concatenate(
        [query_low, jnp.pad(compressed_low, ((0, 0), (0, (-down_width) % 128)))], axis=1
    )
    normed_grad = right_matmul(entry_low, entry_full)
    entry_grad = left_matmul(normed_low, entry_low).astype(jnp.bfloat16)
    input_add, first_gain_grad = norm_back(inputs, gain_first, normed_grad)
    token_grad = residual_grad + input_add
    late = entry_low[0, 0].astype(jnp.float32) * 0.0
    routed = jnp.einsum(
        "zst,zsd->ztd",
        choose_rows,
        returned.transpose(1, 0, 2, 3).reshape(depth, PLANE * capacity, D),
        preferred_element_type=jnp.float32,
    )
    routed_and_shared = lax.psum_scatter(
        (routed.reshape(line_rows, D) + shared_out + late).astype(jnp.bfloat16),
        "expert",
        scatter_dimension=0,
        axis_index_groups=line,
        tiled=True,
    ).astype(jnp.float32)
    output = (residual + routed_and_shared).astype(jnp.bfloat16)

    small_grad = jnp.concatenate(
        [
            first_gain_grad.reshape(-1, gain_width),
            latent_gain_grad.reshape(-1, latent_width),
            feed_gain_grad.reshape(-1, gain_width),
            router_grad.reshape(2 * expert_total, -1),
        ],
        axis=1,
    )
    small_grad = jnp.pad(small_grad, ((0, 0), (0, 128 * part_rows - small_grad.shape[1])))
    packed_piece, shared_back_moved = reduce_rows(
        [
            entry_grad,
            up_weight_grad,
            output_grad.astype(jnp.bfloat16),
            small_grad.astype(jnp.bfloat16).reshape(-1, 128),
        ],
        shared_summed,
        (packed.shape[1] + D) // 256 * 128,
    )
    small_piece = packed_piece[:, -128:].reshape(-1)
    shared_pieces = (
        shared_back_moved.reshape(depth, part_rows, 2, shared_padded)[..., : 2 * shared_width]
        .reshape(depth, part_rows, 2, 2, shared_width)
        .transpose(2, 1, 3, 0, 4)
        .reshape((2,) + shared_gate.shape)
        .astype(jnp.float32)
    )
    output_piece = packed_piece[:, -128 - D : -128]

    return (
        output[None],
        token_grad[None],
        small_piece[cuts[0] : cuts[1]],
        packed_piece[:, :query_width],
        packed_piece[:, query_width : query_width + down_width],
        small_piece[cuts[1] : cuts[2]],
        packed_piece[:, entry_width : -128 - D]
        .reshape(quarters, latent_up.shape[0], -1)
        .transpose(1, 0, 2)
        .reshape(latent_up.shape),
        output_piece,
        small_piece[cuts[2] : cuts[3]],
        small_piece[cuts[3] : cuts[4]].reshape(gain_width, expert_total),
        shared_pieces[0],
        shared_pieces[1],
        sdown_piece,
        expert_gate_piece.astype(jnp.float32)[None],
        expert_up_piece.astype(jnp.float32)[None],
        expert_down_piece.astype(jnp.float32)[None],
    )


def solution(mesh):
    return jax.shard_map(
        body,
        mesh=mesh,
        in_specs=(
            P("expert", "fsdp", None),
            P("expert", None),
            P("expert", "fsdp", None),
            P("expert", "fsdp", None),
            P("expert", "fsdp", None),
            P(("fsdp", "expert")),
            P(("fsdp", "expert"), None),
            P(("fsdp", "expert"), None),
            P(("fsdp", "expert")),
            P(("fsdp", "expert"), None),
            P(("fsdp", "expert"), None),
            P(("fsdp", "expert")),
            P(("fsdp", "expert"), None),
            P(("fsdp", "expert"), None),
            P(("fsdp", "expert"), None),
            P(("fsdp", "expert"), None),
            P("expert", "fsdp", None),
            P("expert", "fsdp", None),
            P("expert", None, "fsdp"),
        ),
        out_specs=(
            P("expert", "fsdp", None),
            P("expert", "fsdp", None),
            P(("fsdp", "expert")),
            P(("fsdp", "expert"), None),
            P(("fsdp", "expert"), None),
            P(("fsdp", "expert")),
            P(("fsdp", "expert"), None),
            P(("fsdp", "expert"), None),
            P(("fsdp", "expert")),
            P(("fsdp", "expert"), None),
            P(("fsdp", "expert"), None),
            P(("fsdp", "expert"), None),
            P(("fsdp", "expert"), None),
            P("expert", "fsdp", None),
            P("expert", "fsdp", None),
            P("expert", None, "fsdp"),
        ),
        check_vma=False,
    )
```

```python
import functools
import math

import jax
import jax.numpy as jnp
from jax import lax
from jax.experimental import pallas as pl
from jax.experimental.pallas import tpu as pltpu
from jax.sharding import PartitionSpec as P

D = 2048
HEADS = 16
NOPE = 128
ROPE = 64
VALUE = 128
LATENT = 512
TOPK = 6


EPSILON = 1e-06
FLOOR_SCORE = -1e30


def norm_rows(values, gain):
    return values * lax.rsqrt(jnp.mean(values * values, axis=-1, keepdims=True) + EPSILON) * gain


def norm_back(values, gain, incoming):
    primal_out, pullback = jax.vjp(norm_rows, values, gain)
    return pullback(incoming)


def swiglu_back(gate_part, up_portion, incoming):
    primal_out, pullback = jax.vjp(
        lambda former, latter: jax.nn.silu(former) * latter, gate_part, up_portion
    )
    return pullback(incoming)


def rotary_table(row_total, offset, rope_width):
    frequency_steps = jnp.arange(rope_width // 2, dtype=jnp.float32)
    inverse = jnp.exp(frequency_steps * (-2.0 * math.log(10000.0) / rope_width))
    places = (offset + jnp.arange(row_total)).astype(jnp.float32)
    angles = places[:, None] * inverse[None, :]
    return (jnp.cos(angles), jnp.sin(angles))


def matmul(former, latter):
    return jnp.dot(former, latter, preferred_element_type=jnp.float32)


def left_matmul(former, latter):
    return lax.dot_general(
        former, latter, (((0,), (0,)), ((), ())), preferred_element_type=jnp.float32
    )


def right_matmul(former, latter):
    return lax.dot_general(
        former, latter, (((1,), (1,)), ((), ())), preferred_element_type=jnp.float32
    )


PLANE = 4
MESH = pl.DeviceIdType.MESH
MEBIBYTE = 1024 * 1024
LONG = pl.CostEstimate(flops=100 * 10**9, bytes_accessed=0, transcendentals=0)
MIDDLE = pl.CostEstimate(flops=40 * 10**9, bytes_accessed=0, transcendentals=0)


def groups(count):
    lines = count // PLANE
    plane = [[row * PLANE + spot for spot in range(PLANE)] for row in range(lines)]
    line = [[row * PLANE + spot for row in range(lines)] for spot in range(PLANE)]
    return plane, line


def remote(source, target, send, receive, where):
    return pltpu.make_async_remote_copy(
        src_ref=source,
        dst_ref=target,
        send_sem=send,
        recv_sem=receive,
        device_id=where,
        device_id_type=MESH,
    )


def plane_mates(place):
    spot = place % PLANE
    return (place + 1 - 2 * (spot % 2), place + 2 - 4 * (spot // 2))


def greet(partners):
    barrier = pltpu.get_barrier_semaphore()
    for where in partners:
        pl.semaphore_signal(barrier, inc=1, device_id=where, device_id_type=MESH)
    pl.semaphore_wait(barrier, len(partners))


def line_others(half, place, depth):
    total = depth * PLANE
    return [(half, (place + offset * PLANE) % total) for offset in range(1, depth)]


def plane_others(half, place):
    spot = place % PLANE
    return [(half, place - spot + (spot + offset) % PLANE) for offset in range(1, PLANE)]


def greet_neighbours(half, place, depth):
    mates = [(half, mate) for mate in plane_mates(place)]
    greet(line_others(half, place, depth) + mates + [(1 - half, place)])


def exchange_along(depth, half, place, in_ref, land, own_sem, send, receive):
    level = place // PLANE
    total = depth * PLANE

    def own():
        return pltpu.make_async_copy(in_ref.at[level], land(level), own_sem)

    def to(offset):
        where = (place + offset * PLANE) % total
        return remote(
            in_ref.at[where // PLANE],
            land(level),
            send.at[offset],
            receive.at[offset],
            (half, where),
        )

    def start():
        own().start()
        for offset in range(1, depth):
            to(offset).start()

    def finish():
        own().wait()
        for offset in range(1, depth):
            to(offset).wait()

    return start, finish


def exchange_plane(half, place, source_of, target_of, own_sem, send, receive):
    spot = place % PLANE

    def to(offset, level):
        mate = (spot + offset) % PLANE
        return remote(
            source_of(mate, level),
            target_of(spot, level),
            send.at[offset, level],
            receive.at[offset, level],
            (half, place - spot + mate),
        )

    def came(offset, level):
        mate = (spot + PLANE - offset) % PLANE
        block = target_of(mate, level)
        return remote(
            block,
            block,
            send.at[offset, level],
            receive.at[offset, level],
            (half, place - spot + mate),
        )

    def own(level):
        return pltpu.make_async_copy(
            source_of(spot, level), target_of(spot, level), own_sem.at[level]
        )

    def start(level):
        for offset in range(1, PLANE):
            to(offset, level).start()
        own(level).start()

    def finish(level):
        own(level).wait()
        for offset in range(1, PLANE):
            came(offset, level).wait_recv()
            to(offset, level).wait_send()

    return start, finish


def place_rows(choose_ref, source, block, placed):
    def columns(n, carry):
        at = lanes_at(n * 512, 512)
        for mate in range(PLANE):
            placed[mate, :, at] = jnp.dot(
                choose_ref[source, mate], block[:, at], preferred_element_type=jnp.float32
            ).astype(placed.dtype)
        return carry

    lax.fori_loop(0, block.shape[1] // 512, columns, 0)


def gather_kernel(depth, cut, *refs):
    in_ref, *line_ins, move_in, down_in = refs[:5]
    out_ref, *line_outs, shared_out, down_out = refs[5:10]
    own_sem, zs, zr, ps, pr, qs, qr, cs, cr, ls, lr, ms, mr, *shared_sems = refs[10:]
    os, ore, ts, tr, us, ur = shared_sems
    half = lax.axis_index("fsdp")
    place = lax.axis_index("expert")
    level = place // PLANE
    spot = place % PLANE
    total = depth * PLANE
    mates = plane_mates(place)
    rows, width = in_ref.shape
    columns = (pl.ds(0, cut), pl.ds(cut, width - cut))
    greet_neighbours(half, place, depth)

    def at(which, block, count=1):
        start = pl.multiple_of((half * total + block) * rows, rows)
        return out_ref.at[pl.ds(start, count * rows), columns[which]]

    def along(which, way, source, own=False):
        target = at(which, source * PLANE + spot)
        start = in_ref.at[:, columns[which]] if own else target
        return remote(
            start,
            target,
            zs.at[which, way, source],
            zr.at[which, source],
            (half, place + (2 * way - 1) * PLANE),
        )

    def plane_one(which, source, own=False):
        target = at(which, source * PLANE + spot)
        start = in_ref.at[:, columns[which]] if own else target
        return remote(
            start, target, ps.at[which, source], pr.at[which, source], (half, mates[which])
        )

    def plane_two(which, source, turn):
        base = source * PLANE
        if which == 0:
            block = at(0, base + spot - spot % 2, 2)
        else:
            block = at(1, base + (spot + 2 * turn) % PLANE)
        slot = which + turn
        return remote(
            block, block, qs.at[slot, source], qr.at[slot, source], (half, mates[1 - which])
        )

    def core(which, source):
        block = at(which, source * PLANE, PLANE)
        return remote(
            block, block, cs.at[which, source], cr.at[which, source], (1 - half, place)
        )

    def trail(which, way, source, own=False):
        target = line_outs[which].at[source]
        return remote(
            line_ins[which] if own else target,
            target,
            ls.at[which, way, source],
            lr.at[which, source],
            (half, place + (2 * way - 1) * PLANE),
        )

    def trail_own(which):
        return pltpu.make_async_copy(
            line_ins[which], line_outs[which].at[level], own_sem.at[2 + which]
        )

    move_start, move_finish = exchange_along(
        depth,
        half,
        place,
        move_in,
        lambda source: shared_out.at[half, source, spot],
        own_sem.at[4],
        ms,
        mr,
    )
    items = range(depth + 2)
    down_own = pltpu.make_async_copy(down_in, down_out.at[half, spot], own_sem.at[5])

    def shared_at(item, first, count):
        if item < depth:
            return shared_out.at[half, item, pl.ds(first, count)]
        span = down_in.shape[1] // 2
        return down_out.at[
            half, pl.ds(first, count), :, pl.ds((item - depth) * span, span)
        ]

    def shared_route(item):
        return (0 if item < depth // 2 else 1) if item < depth else item - depth

    def shared_one(item):
        block = shared_at(item, spot, 1)
        mate = mates[shared_route(item)]
        return remote(block, block, os.at[item], ore.at[item], (half, mate))

    def shared_two(item):
        if shared_route(item) == 0:
            blocks = [shared_at(item, spot - spot % 2, 2)]
        else:
            blocks = [shared_at(item, (spot + 2 * turn) % PLANE, 1) for turn in range(2)]
        mate = mates[1 - shared_route(item)]
        return [
            remote(block, block, ts.at[turn, item], tr.at[turn, item], (half, mate))
            for turn, block in enumerate(blocks)
        ]

    def shared_core(item):
        block = shared_at(item, 0, PLANE)
        return remote(block, block, us.at[item], ur.at[item], (1 - half, place))

    seconds = ((0, 0), (1, 0), (1, 1))

    def own_copy(which):
        return pltpu.make_async_copy(
            in_ref.at[:, columns[which]], at(which, place), own_sem.at[which]
        )

    for which in range(2):

        @pl.when(level > 0)
        def _():
            along(which, 0, level, True).start()

        @pl.when(level < depth - 1)
        def _():
            along(which, 1, level, True).start()

        plane_one(which, level, True).start()
        own_copy(which).start()
    move_start()
    down_own.start()
    for which in range(2):
        trail_own(which).start()
    for which in range(2):
        own_copy(which).wait()

    def trail_first():
        for which in range(2):

            @pl.when(level > 0)
            def _():
                trail(which, 0, level, True).start()

            @pl.when(level < depth - 1)
            def _():
                trail(which, 1, level, True).start()

    def trail_on(source, way):
        for which in range(2):
            trail(which, way, source).wait_recv()

            @pl.when((level < depth - 1) if way == 1 else (level > 0))
            def _():
                trail(which, way, source).start()

    def visit(step, act):
        if step == 0:
            act(level, None)
            return

        @pl.when(level - step >= 0)
        def _():
            act(level - step, 1)

        @pl.when(level + step < depth)
        def _():
            act(level + step, 0)

    def arrive(source, way):
        for which in range(2):
            along(which, way, source).wait_recv()

            @pl.when((level < depth - 1) if way == 1 else (level > 0))
            def _():
                along(which, way, source).start()

            plane_one(which, source).start()

    def spread(source, way):
        for which in range(2):
            plane_one(which, source).wait_recv()
            for kind, turn in seconds:
                if kind == which:
                    plane_two(kind, source, turn).start()

    def share(source, way):
        for which in range(2):
            for kind, turn in seconds:
                if kind == which:
                    plane_two(kind, source, turn).wait_recv()
            core(which, source).start()

    visit(0, spread)
    for step in range(1, depth):
        visit(step, arrive)
        if step == 1:
            move_finish()
            down_own.wait()
            for item in items:
                shared_one(item).start()
        if step == 2:
            trail_first()
        if step >= 3:
            visit(step - 2, trail_on)
        if step >= 2:
            visit(step - 1, spread)
        if step == 2:
            for item in items:
                shared_one(item).wait_recv()
                for copy in shared_two(item):
                    copy.start()
        if step >= 3:
            visit(step - 3, share)
    visit(depth - 1, spread)
    visit(depth - 2, trail_on)
    visit(depth - 3, share)
    for item in items:
        for copy in shared_two(item):
            copy.wait_recv()
        shared_core(item).start()
    visit(depth - 2, share)
    visit(depth - 1, trail_on)
    visit(depth - 1, share)
    for item in items:
        shared_one(item).wait_send()
        for copy in shared_two(item):
            copy.wait_send()
        shared_core(item).wait()
    for which in range(2):
        trail_own(which).wait()

    def finish(source, carry):
        for which in range(2):

            @pl.when((source <= level) & (level < depth - 1))
            def _():
                trail(which, 1, source).wait_send()

            @pl.when((source >= level) & (level > 0))
            def _():
                trail(which, 0, source).wait_send()

            core(which, source).wait_recv()
            core(which, source).wait_send()
            plane_one(which, source).wait_send()

            @pl.when((source <= level) & (level < depth - 1))
            def _():
                along(which, 1, source).wait_send()

            @pl.when((source >= level) & (level > 0))
            def _():
                along(which, 0, source).wait_send()

        for kind, turn in seconds:
            plane_two(kind, source, turn).wait_send()
        return carry

    lax.fori_loop(0, depth, finish, 0)


def gather_rows(value, first, second, moved, down, cut):
    rows, width = value.shape
    total = lax.axis_size("expert")
    depth = total // PLANE
    semaphores = pltpu.SemaphoreType.DMA
    return pl.pallas_call(
        functools.partial(gather_kernel, depth, cut),
        out_shape=[
            jax.ShapeDtypeStruct((2 * total * rows, width), value.dtype),
            jax.ShapeDtypeStruct((depth,) + first.shape, first.dtype),
            jax.ShapeDtypeStruct((depth,) + second.shape, second.dtype),
            jax.ShapeDtypeStruct((2, depth, PLANE) + moved.shape[1:], moved.dtype),
            jax.ShapeDtypeStruct((2, PLANE) + down.shape, down.dtype),
        ],
        in_specs=[pl.BlockSpec(memory_space=pl.ANY)] * 5,
        out_specs=[pl.BlockSpec(memory_space=pl.ANY)] * 5,
        scratch_shapes=[
            semaphores((6,)),
            semaphores((2, 2, depth)),
            semaphores((2, depth)),
            semaphores((2, depth)),
            semaphores((2, depth)),
            semaphores((3, depth)),
            semaphores((3, depth)),
            semaphores((2, depth)),
            semaphores((2, depth)),
            semaphores((2, 2, depth)),
            semaphores((2, depth)),
            semaphores((depth,)),
            semaphores((depth,)),
            semaphores((depth + 2,)),
            semaphores((depth + 2,)),
            semaphores((2, depth + 2)),
            semaphores((2, depth + 2)),
            semaphores((depth + 2,)),
            semaphores((depth + 2,)),
        ],
        compiler_params=pltpu.CompilerParams(collective_id=1, has_side_effects=True),
        cost_estimate=LONG,
    )(value, first, second, moved, down)


def dot_nt(former, latter):
    return lax.dot_general(
        former, latter, (((1,), (1,)), ((), ())), preferred_element_type=jnp.float32
    )


def dot_tn(former, latter):
    return lax.dot_general(
        former, latter, (((0,), (0,)), ((), ())), preferred_element_type=jnp.float32
    )


def dispatch_kernel(depth, *refs):
    x_ref, choose_ref, grad_in, shared_in, down_in = refs[:5]
    rows_out, forth_out, back_out, wide_out, tall_out, grad_out = refs[6:12]
    lines, placed, grads, weights, downs, low_ref, hidden_ref, forth_ref, back_ref = refs[12:21]
    wide_ref, tall_ref, grad_placed, load_sem, out_sem, zs, zr, es, er, own_sem = refs[21:31]
    done_sem, gs, gr, grad_sem = refs[31:]
    half = lax.axis_index("fsdp")
    place = lax.axis_index("expert")
    level = place // PLANE
    spot = place % PLANE
    padded, width = downs.shape
    true = down_in.shape[0]
    chunk = 256 if padded % 256 == 0 else 128
    greet(line_others(half, place, depth) + plane_others(half, place))

    def along(way, source):
        block = lines.at[source]
        where = (half, place + (2 * way - 1) * PLANE)
        return remote(block, block, zs.at[way, source], zr.at[source], where)

    loads = [
        pltpu.make_async_copy(shared_in, weights, load_sem.at[0]),
        pltpu.make_async_copy(down_in, downs.at[pl.ds(0, true), :], load_sem.at[1]),
        pltpu.make_async_copy(grad_in, grads, load_sem.at[2]),
    ]
    lines[level] = x_ref[...]

    def pass_on(way, source):
        @pl.when((level < depth - 1) if way == 1 else (level > 0))
        def _():
            along(way, source).start()

    for way in range(2):
        pass_on(way, level)
    for load in loads:
        load.start()
    if padded > true:
        downs[pl.ds(true, padded - true), :] = jnp.zeros((padded - true, width), downs.dtype)

    rows_start, rows_finish = exchange_plane(
        half,
        place,
        lambda mate, source: placed.at[source, mate],
        lambda mate, source: rows_out.at[mate, source],
        own_sem,
        es,
        er,
    )
    grad_start, grad_finish = exchange_plane(
        half,
        place,
        lambda mate, source: grad_placed.at[source // 2, mate],
        lambda mate, source: grad_out.at[mate, source],
        grad_sem,
        gs,
        gr,
    )

    def give(source):
        place_rows(choose_ref, source, lines.at[source], placed.at[source])
        rows_start(source)

    def give_grad(n, carry):
        source = 2 * n + 1
        place_rows(choose_ref, source, grads.at[source], grad_placed.at[n])
        grad_start(source)
        return carry

    def shared(source):
        def inner(n, carry):
            at = pl.ds(pl.multiple_of(n * chunk, chunk), chunk)
            after = pl.ds(pl.multiple_of(padded + n * chunk, 128), chunk)
            x = lines[source]
            gate = jnp.dot(x, weights[:, at], preferred_element_type=jnp.float32)
            up = jnp.dot(x, weights[:, after], preferred_element_type=jnp.float32)
            dh = dot_nt(grads[source], downs[at, :])
            sig = 1.0 / (1.0 + jnp.exp(-gate))
            act = gate * sig
            hidden_ref[source, :, at] = (act * up).astype(hidden_ref.dtype)
            low_ref[source, :, at] = (dh * up * (sig + act * (1.0 - sig))).astype(low_ref.dtype)
            low_ref[source, :, after] = (dh * act).astype(low_ref.dtype)
            return carry

        lax.fori_loop(0, padded // chunk, inner, 0)

        def outer(n, carry):
            at = pl.ds(pl.multiple_of(n * 512, 512), 512)
            forth_ref[:, at] = jnp.dot(
                hidden_ref[source], downs[:, at], preferred_element_type=jnp.float32
            ).astype(forth_ref.dtype)
            back_ref[:, at] = dot_nt(low_ref[source], weights[at, :]).astype(back_ref.dtype)
            return carry

        lax.fori_loop(0, width // 512, outer, 0)
        outs = [
            pltpu.make_async_copy(forth_ref, forth_out.at[source], out_sem.at[0]),
            pltpu.make_async_copy(back_ref, back_out.at[source], out_sem.at[1]),
        ]
        for out in outs:
            out.start()
        for out in outs:
            out.wait()

    give(level)
    for load in loads:
        load.wait()
    lax.fori_loop(0, depth // 2, give_grad, 0)
    shared(level)

    def step(s, carry):
        @pl.when(level - s >= 0)
        def _():
            along(1, level - s).wait_recv()
            pass_on(1, level - s)

        @pl.when(level + s < depth)
        def _():
            along(0, level + s).wait_recv()
            pass_on(0, level + s)

        def one(way, act):
            source = level + (1 - 2 * way) * s

            @pl.when((source >= 0) & (source < depth))
            def _():
                act(source)

        def both(way, carry):
            one(way, give)
            return carry

        def both_shared(way, carry):
            one(way, shared)
            return carry

        lax.fori_loop(0, 2, both, 0)
        lax.fori_loop(0, 2, both_shared, 0)
        return carry

    lax.fori_loop(1, depth, step, 0)

    tokens = x_ref.shape[0]

    def all_lines(ref, at):
        return ref[:, :, at].reshape(depth * tokens, -1)

    part = wide_ref.shape[2]
    chunk_rows = max(PLANE * part, 128)
    per_chunk = chunk_rows // (PLANE * part)

    def write_wide(k):
        return pltpu.make_async_copy(
            wide_ref.at[k % 2], wide_out.at[k // depth, :, k % depth], done_sem.at[0, k % 2]
        )

    def wide_tile(n, carry):
        at = pl.ds(pl.multiple_of(n * chunk_rows, chunk_rows), chunk_rows)
        value = dot_tn(
            all_lines(lines, at), low_ref[...].reshape(depth * tokens, -1)
        ).astype(wide_ref.dtype)
        for j in range(per_chunk):
            k = n * per_chunk + j

            @pl.when(k >= 2)
            def _():
                write_wide(k - 2).wait()

            for spot_at in range(PLANE):
                first = (j * PLANE + spot_at) * part
                wide_ref[k % 2, spot_at] = value[first : first + part]
            write_wide(k).start()
        return carry

    lax.fori_loop(0, width // chunk_rows, wide_tile, 0)
    for k in (2 * depth - 2, 2 * depth - 1):
        write_wide(k).wait()
    tall_rows = tall_ref.shape[1]
    tall_count = -(-true // tall_rows)

    def write_tall(k, size):
        return pltpu.make_async_copy(
            tall_ref.at[k % 2, pl.ds(0, size), :],
            tall_out.at[pl.ds(k * tall_rows, size), :],
            done_sem.at[1, k % 2],
        )

    writes = []
    for k in range(tall_count):
        if k >= 2:
            writes[k - 2].wait()
        tall_ref[k % 2] = dot_tn(
            all_lines(hidden_ref, pl.ds(k * tall_rows, tall_rows)),
            grads[...].reshape(depth * tokens, -1),
        ).astype(tall_ref.dtype)
        writes.append(write_tall(k, min(tall_rows, true - k * tall_rows)))
        writes[k].start()
    for write in writes[-2:]:
        write.wait()

    def finish_grad(n, carry):
        grad_finish(2 * n + 1)
        return carry

    lax.fori_loop(0, depth // 2, finish_grad, 0)

    def finish(source, carry):
        rows_finish(source)

        @pl.when((source <= level) & (level < depth - 1))
        def _():
            along(1, source).wait_send()

        @pl.when((source >= level) & (level > 0))
        def _():
            along(0, source).wait_send()

        return carry

    lax.fori_loop(0, depth, finish, 0)


def dispatch(x, choose, grad_line, shared_full, down_full, grad_rows):
    depth = choose.shape[0]
    tokens, width = x.shape
    capacity = choose.shape[2]
    padded = shared_full.shape[1] // 2
    part = width // (2 * PLANE * depth)
    semaphores = pltpu.SemaphoreType.DMA
    low = x.dtype
    anywhere = pl.BlockSpec(memory_space=pl.ANY)
    local = pl.BlockSpec(memory_space=pltpu.VMEM)
    return pl.pallas_call(
        functools.partial(dispatch_kernel, depth),
        out_shape=[
            jax.ShapeDtypeStruct((PLANE, depth, capacity, width), low),
            jax.ShapeDtypeStruct((depth, tokens, width), low),
            jax.ShapeDtypeStruct((depth, tokens, width), low),
            jax.ShapeDtypeStruct((2, PLANE, depth, part, 2 * padded), low),
            jax.ShapeDtypeStruct(down_full.shape, low),
            jax.ShapeDtypeStruct(grad_rows.shape, low),
        ],
        in_specs=[local, local] + [anywhere] * 4,
        out_specs=[anywhere] * 6,
        input_output_aliases={5: 5},
        scratch_shapes=[
            pltpu.VMEM((depth, tokens, width), low),
            pltpu.VMEM((depth, PLANE, capacity, width), low),
            pltpu.VMEM((depth, tokens, width), low),
            pltpu.VMEM((width, 2 * padded), low),
            pltpu.VMEM((padded, width), low),
            pltpu.VMEM((depth, tokens, 2 * padded), low),
            pltpu.VMEM((depth, tokens, padded), low),
            pltpu.VMEM((tokens, width), low),
            pltpu.VMEM((tokens, width), low),
            pltpu.VMEM((2, PLANE, part, 2 * padded), low),
            pltpu.VMEM((2, 128, width), low),
            pltpu.VMEM((depth // 2, PLANE, capacity, width), low),
            semaphores((3,)),
            semaphores((2,)),
            semaphores((2, depth)),
            semaphores((depth,)),
            semaphores((PLANE, depth)),
            semaphores((PLANE, depth)),
            semaphores((depth,)),
            semaphores((2, 2)),
            semaphores((PLANE, depth)),
            semaphores((PLANE, depth)),
            semaphores((depth,)),
        ],
        compiler_params=pltpu.CompilerParams(
            collective_id=3, has_side_effects=True, vmem_limit_bytes=56 * MEBIBYTE
        ),
        cost_estimate=LONG,
    )(x, choose, grad_line, shared_full, down_full, grad_rows)


def return_kernel(depth, *refs):
    rows_in, scalars_in, choose_ref, shared_in = refs[:4]
    operands_in = refs[4:9]
    back_ref, prob_ref, gate_out, up_out, down_out = refs[9:14]
    came, scalars, shared, onward, incoming, prob_send, prob_land = refs[14:21]
    held = refs[21:26]
    give_wide, give_tall, take_wide, take_tall, done_wide, done_tall = refs[26:32]
    own_sem, es, er, ss, sr, load_sem, shared_sem, cs, cr, ps, pr = refs[32:43]
    ws, wr, ts, tr, wide_sem, tall_sem = refs[43:]
    x_held, gate_held, up_held, hidden_held, grad_held = held
    half = lax.axis_index("fsdp")
    place = lax.axis_index("expert")
    level = place // PLANE
    spot = place % PLANE
    other = (1 - half, place)
    tokens, width = back_ref.shape
    capacity = choose_ref.shape[2]
    wide_count, wide_rows = take_wide.shape[1:3]
    tall_count, tall_rows, tall_width = take_tall.shape
    greet(line_others(half, place, depth) + plane_others(half, place) + [other])

    def rows_to(offset, source):
        mate = (spot + offset) % PLANE
        where = (half, place - spot + mate)
        return (
            remote(
                rows_in.at[mate, source],
                came.at[spot, source],
                es.at[offset, source],
                er.at[offset, source],
                where,
            ),
            remote(
                scalars_in.at[mate, source],
                scalars.at[spot, source],
                ss.at[offset, source],
                sr.at[offset, source],
                where,
            ),
        )

    def rows_from(offset, source):
        mate = (spot + PLANE - offset) % PLANE
        where = (half, place - spot + mate)
        block, small = came.at[mate, source], scalars.at[mate, source]
        return (
            remote(block, block, es.at[offset, source], er.at[offset, source], where),
            remote(small, small, ss.at[offset, source], sr.at[offset, source], where),
        )

    def own_rows(source):
        return (
            pltpu.make_async_copy(
                rows_in.at[spot, source], came.at[spot, source], own_sem.at[0, source]
            ),
            pltpu.make_async_copy(
                scalars_in.at[spot, source], scalars.at[spot, source], own_sem.at[1, source]
            ),
        )

    def shared_load(slot, source):
        return pltpu.make_async_copy(shared_in.at[source], shared.at[slot], shared_sem.at[slot])

    def each_way(s, act):
        def one(way, carry):
            source = level + (2 * way - 1) * s

            @pl.when((source >= 0) & (source < depth) & ((s > 0) | (way == 0)))
            def _():
                act(way, source)

            return carry

        lax.fori_loop(0, 2, one, 0)

    def begin(way, source):
        for offset in range(1, PLANE):
            for copy in rows_to(offset, source):
                copy.start()
        for copy in own_rows(source):
            copy.start()

    def begin_step(i, carry):
        each_way(depth - 1 - i, begin)
        return carry

    lax.fori_loop(0, depth, begin_step, 0)
    loads = [
        pltpu.make_async_copy(source, target, load_sem.at[k])
        for k, (source, target) in enumerate(zip(operands_in, held))
    ]
    for load in loads:
        load.start()
    for load in loads:
        load.wait()

    def wide_tiles(owner, k):
        at = pl.ds(pl.multiple_of((owner * wide_count + k) * wide_rows, wide_rows), wide_rows)
        x = x_held[:, at]
        return dot_tn(x, gate_held[...]), dot_tn(x, up_held[...])

    def tall_tile(owner, k):
        at = pl.ds(pl.multiple_of(k * tall_rows, tall_rows), tall_rows)
        over = pl.ds(pl.multiple_of(owner * tall_width, tall_width), tall_width)
        return dot_tn(hidden_held[:, at], grad_held[:, over])

    def wide_send(which, k):
        slot = k % 2
        return remote(
            give_wide.at[slot, which],
            take_wide.at[which, k],
            ws.at[slot, which],
            wr.at[which, k],
            other,
        )

    def tall_send(k):
        slot = k % 2
        return remote(give_tall.at[slot], take_tall.at[k], ts.at[slot], tr.at[k], other)

    def wide_write(which, k):
        target = (gate_out, up_out)[which]
        at = pl.ds(pl.multiple_of(k * wide_rows, wide_rows), wide_rows)
        return pltpu.make_async_copy(done_wide.at[which], target.at[at, :], wide_sem.at[which])

    def tall_write(k):
        slot = k % 2
        at = pl.ds(pl.multiple_of(k * tall_rows, tall_rows), tall_rows)
        return pltpu.make_async_copy(done_tall.at[slot], down_out.at[at, :], tall_sem.at[slot])

    def give_wide_tile(k):
        @pl.when(k >= 2)
        def _():
            for which in range(2):
                wide_send(which, k - 2).wait_send()

        for which, tile in enumerate(wide_tiles(1 - half, k)):
            give_wide[k % 2, which] = tile.astype(give_wide.dtype)
            wide_send(which, k).start()

    def give_tall_tile(k):
        @pl.when(k >= 2)
        def _():
            tall_send(k - 2).wait_send()

        give_tall[k % 2] = tall_tile(1 - half, k).astype(give_tall.dtype)
        tall_send(k).start()

    def keep_wide_tile(k):
        @pl.when(k >= 1)
        def _():
            for which in range(2):
                wide_write(which, k - 1).wait()

        for which, tile in enumerate(wide_tiles(half, k)):
            wide_send(which, k).wait_recv()
            tile = tile + take_wide[which, k].astype(jnp.float32)
            done_wide[which] = tile.astype(done_wide.dtype)
            wide_write(which, k).start()

    def keep_tall_tile(k):
        @pl.when(k >= 2)
        def _():
            tall_write(k - 2).wait()

        tile = tall_tile(half, k)
        tall_send(k).wait_recv()
        tile = tile + take_tall[k].astype(jnp.float32)
        done_tall[k % 2] = tile.astype(done_tall.dtype)
        tall_write(k).start()

    units = 2 * (wide_count + tall_count)
    each = -(-units // depth)
    bounds = (0, wide_count, wide_count + tall_count, units - tall_count, units)
    acts = (give_wide_tile, give_tall_tile, keep_wide_tile, keep_tall_tile)

    def fill(unit, carry):
        for act, low, high in zip(acts, bounds[:-1], bounds[1:]):

            @pl.when((unit >= low) & (unit < high))
            def _():
                act(unit - low)

        return carry

    def chain_out(source):
        up = jnp.where(source > level, 1, 0)
        step = 2 * up - 1
        slot = jnp.where(source == level - 1, depth, source)
        return remote(
            onward.at[up],
            incoming.at[slot],
            cs.at[source],
            cr.at[slot],
            (half, place + step * PLANE),
        )

    def chain_in(slot):
        block = incoming.at[slot]
        return remote(block, block, cs.at[0], cr.at[slot], (half, place))

    def prob_to(source):
        return remote(
            prob_send.at[source],
            prob_land.at[level],
            ps.at[source],
            pr.at[level],
            (half, source * PLANE + spot),
        )

    def prob_from(source):
        block = prob_land.at[source]
        return remote(block, block, ps.at[source], pr.at[source], (half, source * PLANE + spot))

    def add_incoming(slot):
        chain_in(slot).wait_recv()
        back_ref[...] += incoming[slot].astype(jnp.float32)

    def settle(way, source):
        for copy in own_rows(source):
            copy.wait()
        for offset in range(1, PLANE):
            for copy in rows_from(offset, source):
                copy.wait_recv()
        shared_load(way, source).wait()

        def columns(n, carry):
            at = pl.ds(pl.multiple_of(n * 512, 512), 512)
            total = shared[way, :, at].astype(jnp.float32)
            for mate in range(PLANE):
                total = total + dot_tn(choose_ref[source, mate], came[mate, source, :, at])
            back_ref[:, at] = total
            return carry

        lax.fori_loop(0, width // 512, columns, 0)
        lines = lax.broadcasted_iota(jnp.int32, (8, tokens), 0)
        probs = jnp.zeros((8, tokens), jnp.float32)
        for mate in range(PLANE):
            part = jnp.dot(
                scalars[mate, source, :, :capacity],
                choose_ref[source, mate].astype(jnp.float32),
                preferred_element_type=jnp.float32,
                precision=lax.Precision.HIGHEST,
            )
            probs = jnp.where(lines == mate, part, probs)

        @pl.when((source >= level) & (level > 0))
        def _():
            add_incoming(source)

        @pl.when((source < level) & (level < depth - 1))
        def _():
            add_incoming(source)

        @pl.when((source == level) & (level < depth - 1))
        def _():
            add_incoming(depth)

        @pl.when(source == level)
        def _():
            prob_land[level] = probs

        @pl.when(source != level)
        def _():
            prob_send[source] = probs
            prob_to(source).start()
            former = source + 2 * way - 1

            @pl.when((former >= 0) & (former < depth))
            def _():
                chain_out(former).wait_send()

            onward[way] = back_ref[...].astype(onward.dtype)
            chain_out(source).start()

    def step(i, carry):
        s = depth - 1 - i
        each_way(s, lambda way, source: shared_load(way, source).start())
        lax.fori_loop(i * each, jnp.minimum((i + 1) * each, units), fill, 0)
        each_way(s, settle)
        return carry

    lax.fori_loop(0, depth, step, 0)
    for which in range(2):
        wide_write(which, wide_count - 1).wait()
        for k in (wide_count - 2, wide_count - 1):
            wide_send(which, k).wait_send()
    for k in (tall_count - 2, tall_count - 1):
        tall_write(k).wait()
        tall_send(k).wait_send()

    def finish(source, carry):
        for offset in range(1, PLANE):
            for copy in rows_to(offset, source):
                copy.wait_send()

        @pl.when((source == level - 1) | (source == level + 1))
        def _():
            chain_out(source).wait_send()

        @pl.when(source != level)
        def _():
            prob_to(source).wait_send()
            prob_from(source).wait_recv()

        prob_ref[source] = prob_land[source]
        return carry

    lax.fori_loop(0, depth, finish, 0)


def give_back(rows, scalars, choose, shared_back, operands):
    depth, _, capacity, tokens = choose.shape
    width = rows.shape[-1]
    slots, inner = operands[1].shape
    wide_rows, tall_rows = 256 if depth <= PLANE else 128, 128
    wide_count = width // 2 // wide_rows
    tall_count = inner // tall_rows
    semaphores = pltpu.SemaphoreType.DMA
    low = rows.dtype
    wide = jnp.float32
    anywhere = pl.BlockSpec(memory_space=pl.ANY)
    local = pl.BlockSpec(memory_space=pltpu.VMEM)
    return pl.pallas_call(
        functools.partial(return_kernel, depth),
        out_shape=[
            jax.ShapeDtypeStruct((tokens, width), wide),
            jax.ShapeDtypeStruct((depth, 8, tokens), wide),
            jax.ShapeDtypeStruct((width // 2, inner), low),
            jax.ShapeDtypeStruct((width // 2, inner), low),
            jax.ShapeDtypeStruct((inner, width // 2), low),
        ],
        in_specs=[anywhere, anywhere, local, anywhere] + [anywhere] * 5,
        out_specs=[local, local, anywhere, anywhere, anywhere],
        scratch_shapes=[
            pltpu.VMEM((PLANE, depth, capacity, width), low),
            pltpu.VMEM((PLANE, depth, 8, 128), wide),
            pltpu.VMEM((2, tokens, width), low),
            pltpu.VMEM((2, tokens, width), low),
            pltpu.VMEM((depth + 1, tokens, width), low),
            pltpu.VMEM((depth, 8, tokens), wide),
            pltpu.VMEM((depth, 8, tokens), wide),
        ]
        + [pltpu.VMEM(operand.shape, low) for operand in operands]
        + [
            pltpu.VMEM((2, 2, wide_rows, inner), low),
            pltpu.VMEM((2, tall_rows, width // 2), low),
            pltpu.VMEM((2, wide_count, wide_rows, inner), low),
            pltpu.VMEM((tall_count, tall_rows, width // 2), low),
            pltpu.VMEM((2, wide_rows, inner), low),
            pltpu.VMEM((2, tall_rows, width // 2), low),
            semaphores((2, depth)),
            semaphores((PLANE, depth)),
            semaphores((PLANE, depth)),
            semaphores((PLANE, depth)),
            semaphores((PLANE, depth)),
            semaphores((5,)),
            semaphores((2,)),
            semaphores((depth,)),
            semaphores((depth + 1,)),
            semaphores((depth,)),
            semaphores((depth,)),
            semaphores((2, 2)),
            semaphores((2, wide_count)),
            semaphores((2,)),
            semaphores((tall_count,)),
            semaphores((2,)),
            semaphores((2,)),
        ],
        compiler_params=pltpu.CompilerParams(
            collective_id=4, has_side_effects=True, vmem_limit_bytes=62 * MEBIBYTE
        ),
        cost_estimate=LONG,
    )(rows, scalars, choose, shared_back, *operands)


def reduce_kernel(depth, count, cut, *refs):
    parts = refs[:count]
    move_in, out_ref, move_out = refs[count : count + 3]
    acc, inc, one_a, one_b, two_a, two_b, zin = refs[count + 3 : count + 10]
    own_sem, cs, cr, ps, pr, qs, qr, zs, zr, move_sem, ms, mr = refs[count + 10 :]
    half = lax.axis_index("fsdp")
    place = lax.axis_index("expert")
    level = place // PLANE
    spot = place % PLANE
    total = depth * PLANE
    mates = plane_mates(place)
    rows = out_ref.shape[0]
    group = PLANE * rows
    width = out_ref.shape[1]
    greet_neighbours(half, place, depth)

    starts = [sum(part.shape[1] for part in parts[:k]) for k in range(count)]

    def rows_of(k, owner, t):
        start = pl.multiple_of((owner * total + t * PLANE) * rows, group)
        return parts[k].at[pl.ds(start, group), :]

    def kept(k, t):
        return pltpu.make_async_copy(
            rows_of(k, half, t),
            acc.at[t, :, pl.ds(starts[k], parts[k].shape[1])],
            own_sem.at[k, t],
        )

    def given(k, t):
        return remote(
            rows_of(k, 1 - half, t),
            inc.at[t, :, pl.ds(starts[k], parts[k].shape[1])],
            cs.at[k, t],
            cr.at[k, t],
            (1 - half, place),
        )

    def block(t, q, n, lo, hi):
        return acc.at[t, pl.ds(pl.multiple_of(q * rows, rows), n * rows), pl.ds(lo, hi - lo)]

    pair = spot - spot % 2

    def first(t, turn):
        low = spot % 2
        if turn == 0:
            source = block(t, 2 - pair, 2, 0, cut)
            target, where = one_a.at[t], mates[1]
        else:
            source = block(t, 2 * turn - 1 - low, 1, cut, width)
            target, where = one_b.at[t, turn - 1], mates[0]
        return remote(source, target, ps.at[turn, t], pr.at[turn, t], (half, where))

    def second(t, turn):
        if turn == 0:
            source = block(t, pair + 1 - spot % 2, 1, 0, cut)
            target, where = two_a.at[t], mates[0]
        else:
            source = block(t, (spot + 2) % PLANE, 1, cut, width)
            target, where = two_b.at[t], mates[1]
        return remote(source, target, qs.at[turn, t], qr.at[turn, t], (half, where))

    def line(t, way):
        step = 2 * way - 1
        return remote(
            block(t, spot, 1, 0, width),
            zin.at[way, t],
            zs.at[way, t],
            zr.at[way, t],
            (half, place + step * PLANE),
        )

    def add_rows(t, start, n, lo, hi, piece):
        def one(i, carry):
            r = pl.multiple_of(i * 16, 16)
            at = (t, pl.ds(pl.multiple_of(start + r, 16), 16), pl.ds(lo, hi - lo))
            new = piece(pl.ds(r, 16)).astype(jnp.float32)
            acc[at] = (acc[at].astype(jnp.float32) + new).astype(acc.dtype)
            return carry

        lax.fori_loop(0, n // 16, one, 0)

    def stage_a(t):
        for k in range(count):
            kept(k, t).wait()
            given(k, t).wait_recv()
        add_rows(t, 0, group, 0, width, lambda r: inc[t, r, :])
        for turn in range(3):
            first(t, turn).start()

    def stage_b(t):
        first(t, 0).wait_recv()
        add_rows(t, pair * rows, 2 * rows, 0, cut, lambda r: one_a[t, r, :])
        second(t, 0).start()
        for turn in range(2):
            first(t, 1 + turn).wait_recv()
            add_rows(
                t,
                (spot % 2 + 2 * turn) * rows,
                rows,
                cut,
                width,
                lambda r: one_b[t, turn, r, :],
            )
        second(t, 1).start()

    def stage_c(t):
        second(t, 0).wait_recv()
        add_rows(t, spot * rows, rows, 0, cut, lambda r: two_a[t, r, :])
        second(t, 1).wait_recv()
        add_rows(t, spot * rows, rows, cut, width, lambda r: two_b[t, r, :])

        def take(way):
            line(t, way).wait_recv()
            add_rows(t, spot * rows, rows, 0, width, lambda r: zin[way, t, r, :])

        @pl.when((t >= level) & (level > 0))
        def _():
            take(1)

        @pl.when((t <= level) & (level < depth - 1))
        def _():
            take(0)

        @pl.when(t > level)
        def _():
            line(t, 1).start()

        @pl.when(t < level)
        def _():
            line(t, 0).start()

    def visit(index, act):
        if index >= depth or index < 0:
            return
        step = depth - 1 - index
        if step == 0:
            act(level)
            return

        @pl.when(level + step < depth)
        def _():
            act(level + step)

        @pl.when(level - step >= 0)
        def _():
            act(level - step)

    def begin(t):
        for k in range(count):
            given(k, t).start()
            kept(k, t).start()

    for index in range(depth):
        visit(index, begin)
    move_start, move_finish = exchange_along(
        depth,
        half,
        place,
        move_in,
        lambda source: move_out.at[source],
        move_sem.at[0],
        ms,
        mr,
    )
    move_start()
    for index in range(depth + 2):
        visit(index, stage_a)
        visit(index - 1, stage_b)
        visit(index - 2, stage_c)

    def emit(i, carry):
        r = pl.multiple_of(i * 16, 16)
        at = pl.ds(pl.multiple_of(spot * rows + r, 16), 16)
        out_ref[pl.ds(r, 16), :] = acc[level, at, :].astype(out_ref.dtype)
        return carry
    lax.fori_loop(0, rows // 16, emit, 0)
    move_finish()

    def finish(t, carry):
        for k in range(count):
            given(k, t).wait_send()
        for turn in range(3):
            first(t, turn).wait_send()
        for turn in range(2):
            second(t, turn).wait_send()

        @pl.when(t > level)
        def _():
            line(t, 1).wait_send()

        @pl.when(t < level)
        def _():
            line(t, 0).wait_send()
        return carry

    lax.fori_loop(0, depth, finish, 0)


def reduce_rows(parts, moved, cut):
    total = lax.axis_size("expert")
    depth = total // PLANE
    rows = parts[0].shape[0] // (2 * total)
    width = sum(part.shape[1] for part in parts)
    group = PLANE * rows
    n = len(parts)
    semaphores = pltpu.SemaphoreType.DMA
    low = parts[0].dtype
    return pl.pallas_call(
        functools.partial(reduce_kernel, depth, n, cut),
        out_shape=[
            jax.ShapeDtypeStruct((rows, width), jnp.float32),
            jax.ShapeDtypeStruct(moved.shape, moved.dtype),
        ],
        in_specs=[pl.BlockSpec(memory_space=pl.ANY)] * (n + 1),
        out_specs=[
            pl.BlockSpec(memory_space=pltpu.VMEM),
            pl.BlockSpec(memory_space=pl.ANY),
        ],
        scratch_shapes=[
            pltpu.VMEM((depth, group, width), low),
            pltpu.VMEM((depth, group, width), low),
            pltpu.VMEM((depth, 2 * rows, cut), low),
            pltpu.VMEM((depth, 2, rows, width - cut), low),
            pltpu.VMEM((depth, rows, cut), low),
            pltpu.VMEM((depth, rows, width - cut), low),
            pltpu.VMEM((2, depth, rows, width), low),
            semaphores((n, depth)),
            semaphores((n, depth)),
            semaphores((n, depth)),
            semaphores((3, depth)),
            semaphores((3, depth)),
            semaphores((2, depth)),
            semaphores((2, depth)),
            semaphores((2, depth)),
            semaphores((2, depth)),
            semaphores((1,)),
            semaphores((depth,)),
            semaphores((depth,)),
        ],
        cost_estimate=LONG,
        compiler_params=pltpu.CompilerParams(
            collective_id=2, has_side_effects=True, vmem_limit_bytes=60 * MEBIBYTE
        ),
    )(*parts, moved)


def turned(values):
    width = values.shape[1]
    lanes = lax.broadcasted_iota(jnp.int32, values.shape, 1)
    return jnp.where(
        lanes % ROPE < ROPE // 2,
        pltpu.roll(values, width - ROPE // 2, 1),
        pltpu.roll(values, ROPE // 2, 1),
    )


def row_scale(values):
    return lax.rsqrt(jnp.mean(values * values, axis=-1, keepdims=True) + EPSILON)


def head_lanes(values, head):
    lanes = lax.broadcasted_iota(jnp.int32, values.shape, 1)
    return jnp.where(lanes // ROPE == head % 2, values, jnp.zeros_like(values))


def lanes_at(start, size):
    return pl.ds(pl.multiple_of(start, 128), size)


def attend_kernel(layout, *refs):
    x_ref, packed, up_in, first_gain, latent_gain, feed_gain, cosine, sine, mask = refs[:9]
    choose_ref, grad_in = refs[9:11]
    normed, residual, mixed, queries, latent, compressed = refs[11:17]
    expanded, keys_rope, log_total, heads, grad_out = refs[17:22]
    entry, ups, outs, prior_latent, prior_rope, grads, grad_placed = refs[22:29]
    load_sem, up_sem, send_sem, receive_sem, gl, gs, gr, grad_sem = refs[29:]
    entry_width, out_start = layout
    half = lax.axis_index("fsdp")
    place = lax.axis_index("expert")
    other = (1 - half, place)
    rows, width = x_ref.shape
    low = x_ref.dtype
    scale = (NOPE + ROPE) ** (-0.5)
    loads = [
        pltpu.make_async_copy(packed.at[:, pl.ds(0, entry_width)], entry, load_sem.at[0]),
        pltpu.make_async_copy(packed.at[:, pl.ds(out_start, width)], outs, load_sem.at[1]),
    ]
    up_loads = load_ups(up_in, ups, up_sem, layout)
    depth = grad_in.shape[0]

    def grad_load(n):
        return pltpu.make_async_copy(grad_in.at[2 * n], grads.at[n], gl.at[n])

    grad_start, grad_finish = exchange_plane(
        half,
        place,
        lambda mate, source: grad_placed.at[source // 2, mate],
        lambda mate, source: grad_out.at[mate, source],
        grad_sem,
        gs,
        gr,
    )

    def each_grad(act):
        def one(n, carry):
            act(n)
            return carry

        lax.fori_loop(0, depth // 2, one, 0)

    def give_grad(n):
        grad_load(n).wait()
        place_rows(choose_ref, 2 * n, grads.at[n], grad_placed.at[n])
        grad_start(2 * n)

    each_grad(lambda n: grad_load(n).start())
    for load in loads[:1] + up_loads + loads[1:]:
        load.start()
    greet([other] + plane_others(half, place))
    each_grad(give_grad)
    x = x_ref[...].astype(jnp.float32)
    normed[...] = (x * row_scale(x) * first_gain[...]).astype(low)
    loads[0].wait()
    nope_width = HEADS * NOPE
    query_width = HEADS * (NOPE + ROPE)

    def through(start, size):
        return jnp.dot(
            normed[...], entry[:, lanes_at(start, size)], preferred_element_type=jnp.float32
        )

    def rotary(values):
        return values * cosine[...] + turned(values) * sine[...]

    squeezed = through(query_width, LATENT)
    compressed[...] = squeezed
    latent[...] = (squeezed * row_scale(squeezed) * latent_gain[...]).astype(low)
    key = rotary(through(query_width + LATENT, 128))
    keys_rope[pl.ds(rows, rows), :] = (key + pltpu.roll(key, ROPE, 1)).astype(low)
    sends = [
        remote(latent, prior_latent, send_sem.at[0], receive_sem.at[0], other),
        remote(
            keys_rope.at[pl.ds(rows, rows), :],
            prior_rope,
            send_sem.at[1],
            receive_sem.at[1],
            other,
        ),
    ]

    @pl.when(half == 0)
    def _():
        for send in sends:
            send.start()

    def nope_part(n, carry):
        queries[:, lanes_at(n * 512, 512)] = through(n * 512, 512).astype(low)
        return carry

    lax.fori_loop(0, nope_width // 512, nope_part, 0)

    def rope_part(n, carry):
        values = through(nope_width + n * 512, 512)
        for k in range(4):
            tile = rotary(values[:, k * 128 : (k + 1) * 128])
            queries[:, lanes_at(nope_width + n * 512 + k * 128, 128)] = tile.astype(low)
        return carry

    lax.fori_loop(0, HEADS * ROPE // 512, rope_part, 0)
    for load in up_loads:
        load.wait()
    quarters, span = ups.shape[0], ups.shape[-1]

    def expand(source, first):
        def one(n, carry):
            expanded[pl.ds(first, rows), lanes_at(n * span, span)] = jnp.dot(
                source[...], whole(ups[n]), preferred_element_type=jnp.float32
            ).astype(low)
            return carry

        lax.fori_loop(0, quarters, one, 0)

    expand(latent, rows)

    @pl.when(half == 0)
    def _():
        expanded[pl.ds(0, rows), :] = jnp.zeros((rows, quarters * span), low)
        keys_rope[pl.ds(0, rows), :] = jnp.zeros((rows, 128), low)
        for send in sends:
            send.wait_send()

    @pl.when(half == 1)
    def _():
        for send in sends:
            send.wait_recv()
        keys_rope[pl.ds(0, rows), :] = prior_rope[...]
        expand(prior_latent, 0)

    def head(h, totals):
        pair = queries[:, lanes_at(nope_width + (h // 2) * 128, 128)]
        scores = dot_nt(
            queries[:, lanes_at(h * NOPE, NOPE)], expanded[:, lanes_at(h * 256, NOPE)]
        )
        scores = scores + dot_nt(head_lanes(pair, h), keys_rope[...])
        scores = jnp.where(mask[...] > 0, scores * scale, FLOOR_SCORE)
        top = jnp.max(scores, axis=-1, keepdims=True)
        weights = jnp.exp(scores - top)
        total = jnp.sum(weights, axis=-1, keepdims=True)
        heads[:, lanes_at(h * VALUE, VALUE)] = jnp.dot(
            (weights / total).astype(low),
            expanded[:, lanes_at(h * 256 + NOPE, VALUE)],
            preferred_element_type=jnp.float32,
        ).astype(low)
        lanes = lax.broadcasted_iota(jnp.int32, totals.shape, 1)
        return jnp.where(lanes == h, top + jnp.log(total), totals)

    log_total[...] = lax.fori_loop(0, HEADS, head, jnp.zeros((rows, 128), jnp.float32))
    loads[1].wait()

    def project(n, carry):
        at = lanes_at(n * 512, 512)
        residual[:, at] = x_ref[:, at].astype(jnp.float32) + jnp.dot(
            heads[...], outs[:, at], preferred_element_type=jnp.float32
        )
        return carry

    lax.fori_loop(0, width // 512, project, 0)
    total = residual[...]
    mixed[...] = (total * row_scale(total) * feed_gain[...]).astype(low)
    each_grad(lambda n: grad_finish(2 * n))


def attend(x, packed, ups, ups_shape, gains, tables, mask, choose, grad_line, layout):
    rows, width = x.shape
    low, wide = x.dtype, jnp.float32
    semaphores = pltpu.SemaphoreType.DMA
    anywhere = pl.BlockSpec(memory_space=pl.ANY)
    local = pl.BlockSpec(memory_space=pltpu.VMEM)
    expanded_width = HEADS * (NOPE + VALUE)
    depth, _, capacity, _ = choose.shape
    shapes = [
        ((rows, width), low),
        ((rows, width), wide),
        ((rows, width), low),
        ((rows, HEADS * (NOPE + ROPE)), low),
        ((rows, LATENT), low),
        ((rows, LATENT), wide),
        ((2 * rows, expanded_width), low),
        ((2 * rows, 128), low),
        ((rows, 128), wide),
        ((rows, HEADS * VALUE), low),
        ((PLANE, depth, capacity, width), low),
    ]
    return pl.pallas_call(
        functools.partial(attend_kernel, layout),
        out_shape=[jax.ShapeDtypeStruct(shape, dtype) for shape, dtype in shapes],
        in_specs=[local, anywhere, anywhere] + [local] * 7 + [anywhere],
        out_specs=[local] * (len(shapes) - 1) + [anywhere],
        scratch_shapes=[
            pltpu.VMEM((packed.shape[0], layout[0]), low),
            pltpu.VMEM(ups_shape, low),
            pltpu.VMEM((packed.shape[0], width), low),
            pltpu.VMEM((rows, LATENT), low),
            pltpu.VMEM((rows, 128), low),
            pltpu.VMEM((depth // 2, rows, width), low),
            pltpu.VMEM((depth // 2, PLANE, capacity, width), low),
            semaphores((2,)),
            semaphores((ups_shape[0],)),
            semaphores((2,)),
            semaphores((2,)),
            semaphores((depth // 2,)),
            semaphores((PLANE, depth)),
            semaphores((PLANE, depth)),
            semaphores((depth,)),
        ],
        compiler_params=pltpu.CompilerParams(
            collective_id=5, has_side_effects=True, vmem_limit_bytes=56 * MEBIBYTE
        ),
        cost_estimate=MIDDLE,
    )(x, packed, ups, *gains, *tables, mask, choose, grad_line)


def load_ups(up_in, ups, sem, layout):
    if up_in.shape == ups.shape:
        return [pltpu.make_async_copy(up_in, ups, sem.at[0])]
    span = ups.shape[-1]
    return [
        pltpu.make_async_copy(
            up_in.at[:, k, :, pl.ds(layout[0], span)], ups.at[k], sem.at[k]
        )
        for k in range(ups.shape[0])
    ]


def whole(block):
    return block.reshape(-1, block.shape[-1])


def attend_back_kernel(layout, count, *refs):
    d_ref, packed, up_in, queries, expanded, keys_rope, log_total = refs[:7]
    latent, compressed, normed, heads, x_ref, above = refs[7:13]
    latent_gain, first_gain, cosine, sine, mask, rows_in = refs[13:19]
    refs = refs[19 + count :]
    token_grad, up_grad, gain_grad, first_grad, entry_grad, out_grad, rows_out = refs[:7]
    outs, ups, d_heads, own, prior, came, prior_rope, came_rope, total_low = refs[7:16]
    entry, entry_low, up_tile, entry_tile, out_tile = refs[16:21]
    load_sem, up_sem, send_sem, receive_sem, write_sem, es, er, own_sem = refs[21:]
    entry_width, out_start = layout
    half = lax.axis_index("fsdp")
    place = lax.axis_index("expert")
    other = (1 - half, place)
    rows, width = d_ref.shape
    low = d_ref.dtype
    wide = jnp.float32
    scale = (NOPE + ROPE) ** (-0.5)
    nope_width = HEADS * NOPE
    query_width = HEADS * (NOPE + ROPE)
    loads = [
        pltpu.make_async_copy(packed.at[:, pl.ds(out_start, width)], outs, load_sem.at[0]),
        pltpu.make_async_copy(packed.at[:, pl.ds(0, entry_width)], entry, load_sem.at[1]),
    ]
    up_loads = load_ups(up_in, ups, up_sem, layout)
    for load in loads + up_loads:
        load.start()
    greet([other] + plane_others(half, place))
    rows_start, rows_finish = exchange_plane(
        half,
        place,
        lambda mate, level: rows_in.at[mate, level],
        lambda mate, level: rows_out.at[mate, level],
        own_sem,
        es,
        er,
    )

    def each_level(act):
        def one(level, carry):
            act(level)
            return carry

        lax.fori_loop(0, rows_in.shape[1], one, 0)

    each_level(rows_start)

    def write(kind, k):
        staged, target = ((out_tile, out_grad), (entry_tile, entry_grad), (up_tile, up_grad))[kind]
        size = staged.shape[1]
        if kind == 2:
            place_at = up_grad.at[k] if up_grad.shape[0] == ups.shape[0] else up_grad.at[:, k]
        else:
            place_at = target.at[pl.ds(pl.multiple_of(k * size, size), size), :]
        return pltpu.make_async_copy(
            staged.at[k % 2], place_at, write_sem.at[kind, k % 2]
        )

    def put(kind, k, value):
        staged = (out_tile, entry_tile, up_tile)[kind]

        @pl.when(k >= 2)
        def _():
            write(kind, k - 2).wait()

        staged[k % 2] = value.astype(low).reshape(staged.shape[1:])
        write(kind, k).start()

    def settle(kind, total):
        for k in range(max(0, total - 2), total):
            write(kind, k).wait()

    def out_part(k, carry):
        size = out_tile.shape[1]
        put(0, k, dot_tn(heads[:, lanes_at(k * size, size)], d_ref[...]))
        return carry

    out_count = heads.shape[1] // out_tile.shape[1]
    lax.fori_loop(0, out_count, out_part, 0)
    loads[0].wait()

    def head_part(n, carry):
        at = lanes_at(n * 512, 512)
        d_heads[:, at] = dot_nt(d_ref[...], outs[at, :]).astype(low)
        return carry

    lax.fori_loop(0, width // 512, head_part, 0)

    def turn_back(values):
        return values * cosine[...] - turned(values) * sine[...]

    def pair_of_heads(n, rope_sum):
        pair = queries[:, lanes_at(nope_width + n * 128, 128)]
        query_rope = jnp.zeros((rows, 128), wide)
        for k in range(2):
            h = 2 * n + k
            query = queries[:, lanes_at(h * NOPE, NOPE)]
            key = expanded[:, lanes_at(h * 256, NOPE)]
            value = expanded[:, lanes_at(h * 256 + NOPE, VALUE)]
            d_head = d_heads[:, lanes_at(h * VALUE, VALUE)]
            own_pair = head_lanes(pair, k)
            scores = dot_nt(query, key) + dot_nt(own_pair, keys_rope[...])
            scores = jnp.where(mask[...] > 0, scores * scale, FLOOR_SCORE)
            lanes = lax.broadcasted_iota(jnp.int32, log_total.shape, 1)
            log_sum = jnp.sum(
                jnp.where(lanes == h, log_total[...], 0.0), axis=-1, keepdims=True
            )
            probs = jnp.exp(scores - log_sum)
            d_probs = dot_nt(d_head, value)
            delta = jnp.sum(probs * d_probs, axis=-1, keepdims=True)
            d_scores = (probs * (d_probs - delta)).astype(low)
            entry_low[:, lanes_at(h * NOPE, NOPE)] = (
                jnp.dot(d_scores, key, preferred_element_type=wide) * scale
            ).astype(low)
            query_rope = query_rope + head_lanes(
                jnp.dot(d_scores, keys_rope[...], preferred_element_type=wide), k
            )
            d_key = dot_tn(d_scores, query) * scale
            d_value = dot_tn(probs.astype(low), d_head)
            own[:, lanes_at(h * 256, NOPE)] = d_key[rows:]
            own[:, lanes_at(h * 256 + NOPE, VALUE)] = d_value[rows:]
            prior[:, lanes_at(h * 256, NOPE)] = d_key[:rows].astype(low)
            prior[:, lanes_at(h * 256 + NOPE, VALUE)] = d_value[:rows].astype(low)
            rope_sum = rope_sum + dot_tn(d_scores, own_pair)
        entry_low[:, lanes_at(nope_width + n * 128, 128)] = (
            turn_back(query_rope) * scale
        ).astype(low)
        return rope_sum

    rope_sum = lax.fori_loop(
        0, HEADS // 2, pair_of_heads, jnp.zeros((2 * rows, 128), wide)
    )
    rope_sum = (rope_sum + pltpu.roll(rope_sum, ROPE, 1)) * scale
    prior_rope[...] = rope_sum[:rows].astype(low)
    sends = [
        remote(prior, came, send_sem.at[0], receive_sem.at[0], other),
        remote(prior_rope, came_rope, send_sem.at[1], receive_sem.at[1], other),
    ]

    @pl.when(half == 1)
    def _():
        for send in sends:
            send.start()
        came_rope[...] = jnp.zeros((rows, 128), low)
        total_low[...] = own[...].astype(low)
        for send in sends:
            send.wait_send()

    @pl.when(half == 0)
    def _():
        for send in sends:
            send.wait_recv()
        total_low[...] = (own[...] + came[...].astype(wide)).astype(low)

    for load in up_loads:
        load.wait()
    quarters, span = ups.shape[0], ups.shape[-1]

    def spread(n, d_latent):
        part = total_low[:, lanes_at(n * span, span)]
        put(2, n, dot_tn(latent[...], part))
        return d_latent + dot_nt(part, whole(ups[n]))

    d_latent = lax.fori_loop(0, quarters, spread, jnp.zeros((rows, LATENT), wide))
    values = compressed[...]
    root = row_scale(values)
    gain_grad[...] = jnp.broadcast_to(
        jnp.sum(d_latent * values * root, axis=0, keepdims=True), gain_grad.shape
    )
    scaled = latent_gain[...] * d_latent
    inner = jnp.mean(values * scaled, axis=-1, keepdims=True)
    entry_low[:, lanes_at(query_width, LATENT)] = (
        root * scaled - values * (root * root * root) * inner
    ).astype(low)
    key = rope_sum[rows:] + came_rope[...].astype(wide)
    entry_low[:, lanes_at(query_width + LATENT, 128)] = turn_back(head_lanes(key, 0)).astype(low)

    def entry_part(k, carry):
        size = entry_tile.shape[1]
        put(1, k, dot_tn(normed[:, lanes_at(k * size, size)], entry_low[...]))
        return carry

    entry_count = width // entry_tile.shape[1]
    lax.fori_loop(0, entry_count, entry_part, 0)
    loads[1].wait()

    def normed_part(n, carry):
        at = lanes_at(n * 512, 512)
        token_grad[:, at] = dot_nt(entry_low[...], entry[at, :])
        return carry

    lax.fori_loop(0, width // 512, normed_part, 0)
    x = x_ref[...].astype(wide)
    root = row_scale(x)
    scaled = first_gain[...] * token_grad[...]
    first_grad[...] = jnp.broadcast_to(
        jnp.sum(token_grad[...] * x * root, axis=0, keepdims=True), first_grad.shape
    )
    inner = jnp.mean(x * scaled, axis=-1, keepdims=True)
    token_grad[...] = above[...] + root * scaled - x * (root * root * root) * inner
    settle(0, out_count)
    settle(1, entry_count)
    settle(2, quarters)
    each_level(rows_finish)


def attend_back(
    d, packed, ups, ups_shape, kept, gains, tables, mask, returning, before, layout
):
    rows, width = d.shape
    low, wide = d.dtype, jnp.float32
    semaphores = pltpu.SemaphoreType.DMA
    anywhere = pl.BlockSpec(memory_space=pl.ANY)
    local = pl.BlockSpec(memory_space=pltpu.VMEM)
    expanded_width = HEADS * (NOPE + VALUE)
    quarters, blocks, part, span = ups_shape
    up_grad = (blocks, quarters, part, span) if blocks > 1 else ups_shape
    return pl.pallas_call(
        functools.partial(attend_back_kernel, layout, len(before)),
        out_shape=[
            jax.ShapeDtypeStruct((rows, width), wide),
            jax.ShapeDtypeStruct(up_grad, low),
            jax.ShapeDtypeStruct((8, LATENT), wide),
            jax.ShapeDtypeStruct((8, width), wide),
            jax.ShapeDtypeStruct((width, layout[0]), low),
            jax.ShapeDtypeStruct((HEADS * VALUE, width), low),
            jax.ShapeDtypeStruct(returning.shape, low),
        ],
        in_specs=[local, anywhere, anywhere] + [local] * 15 + [anywhere] * (1 + len(before)),
        out_specs=[local, anywhere, local, local] + [anywhere] * 3,
        scratch_shapes=[
            pltpu.VMEM((packed.shape[0], width), low),
            pltpu.VMEM(ups_shape, low),
            pltpu.VMEM((rows, HEADS * VALUE), low),
            pltpu.VMEM((rows, expanded_width), wide),
            pltpu.VMEM((rows, expanded_width), low),
            pltpu.VMEM((rows, expanded_width), low),
            pltpu.VMEM((rows, 128), low),
            pltpu.VMEM((rows, 128), low),
            pltpu.VMEM((rows, expanded_width), low),
            pltpu.VMEM((packed.shape[0], layout[0]), low),
            pltpu.VMEM((rows, layout[0]), low),
            pltpu.VMEM((2,) + ups_shape[1:], low),
            pltpu.VMEM((2, 128, layout[0]), low),
            pltpu.VMEM((2, 256, width), low),
            semaphores((2,)),
            semaphores((quarters,)),
            semaphores((2,)),
            semaphores((2,)),
            semaphores((3, 2)),
            semaphores((PLANE, returning.shape[1])),
            semaphores((PLANE, returning.shape[1])),
            semaphores((returning.shape[1],)),
        ],
        compiler_params=pltpu.CompilerParams(
            collective_id=6, has_side_effects=True, vmem_limit_bytes=62 * MEBIBYTE
        ),
        cost_estimate=LONG,
    )(d, packed, ups, *kept, *gains, *tables, mask, returning, *before)


def body(
    tokens,
    segments,
    routes,
    slot_index,
    cotangent,
    attention_norm,
    query_weight,
    latent_down,
    latent_norm,
    latent_up,
    output_weight,
    feed_norm,
    router_weight,
    shared_gate,
    shared_up,
    shared_down,
    expert_gate,
    expert_up,
    expert_down,
):
    row_count = tokens.shape[1]
    expert_total = lax.axis_size("expert")
    depth = expert_total // PLANE
    plane, line = groups(expert_total)
    place = lax.axis_index("expert")
    level = place // PLANE
    device_half = lax.axis_index("fsdp")
    capacity = row_count * TOPK // expert_total
    line_rows = depth * row_count
    inputs = tokens[0].astype(jnp.float32)

    part_rows = query_weight.shape[0]
    gain_width = attention_norm.shape[0]
    latent_width = latent_norm.shape[0]
    small = jnp.concatenate([attention_norm, latent_norm, feed_norm, router_weight.reshape(-1)])
    cuts = [
        0,
        gain_width,
        gain_width + latent_width,
        2 * gain_width + latent_width,
        small.shape[0],
    ]
    small = jnp.pad(small, (0, 128 * part_rows - small.shape[0])).reshape(part_rows, 128)
    query_width = query_weight.shape[1]
    down_width = latent_down.shape[1]
    entry_width = query_width + down_width + (-down_width) % 128
    up_width = HEADS * (NOPE + VALUE)
    quarters = part_rows // latent_up.shape[0]
    by_head = query_weight.reshape(part_rows, HEADS, NOPE + ROPE)
    packed = jnp.concatenate(
        [
            by_head[..., :NOPE].reshape(part_rows, -1),
            by_head[..., NOPE:].reshape(part_rows, -1),
            jnp.pad(latent_down, ((0, 0), (0, (-down_width) % 128))),
            latent_up.reshape(latent_up.shape[0], quarters, -1)
            .transpose(1, 0, 2)
            .reshape(part_rows, -1),
            output_weight,
            small,
        ],
        axis=1,
    )
    cut = packed.shape[1] // 256 * 128
    route_rows = routes[0]
    slot_rows = slot_index[0]
    target = jnp.where(
        slot_rows >= 0, route_rows * capacity + slot_rows, expert_total * capacity
    )
    target = jnp.pad(target, ((0, 0), (0, 8 - TOPK)), constant_values=expert_total * capacity).T
    shared_width = shared_gate.shape[1] // (2 * depth)
    shared_both = jnp.stack([shared_gate, shared_up]).reshape(
        2, part_rows, 2, depth, shared_width
    )
    shared_both = shared_both.transpose(3, 1, 0, 2, 4)
    shared_both = shared_both.reshape(depth, part_rows, 2, 2 * shared_width)
    shared_padded = 2 * shared_width + (-2 * shared_width) % 128
    shared_both = jnp.pad(
        shared_both, ((0, 0), (0, 0), (0, 0), (0, shared_padded - 2 * shared_width))
    ).reshape(depth, part_rows, 2 * shared_padded)
    packed_full, grad_line, target_line, shared_full, sdown_full = gather_rows(
        packed, cotangent[0], target, shared_both, shared_down, cut
    )
    shared_full = shared_full.reshape(D, 2 * shared_padded)
    sdown_full = sdown_full.reshape(2 * shared_width, D)
    expert_gate_full = lax.all_gather(expert_gate[0], "fsdp", axis=0, tiled=True)
    expert_up_full = lax.all_gather(expert_up[0], "fsdp", axis=0, tiled=True)
    expert_down_full = lax.all_gather(expert_down[0], "fsdp", axis=1, tiled=True)
    packed_full, grad_line, target_line, expert_gate_full, expert_up_full, expert_down_full = (
        lax.optimization_barrier(
            (
                packed_full,
                grad_line,
                target_line,
                expert_gate_full,
                expert_up_full,
                expert_down_full,
            )
        )
    )
    up_rows = latent_up.shape[0]
    up_parts = packed_full.reshape(2 * expert_total, quarters, up_rows, -1)
    if up_rows % 16 == 0:
        up_full = up_parts
        ups_shape = (quarters, 2 * expert_total, up_rows, up_width // quarters)
    else:
        up_full = up_parts[..., entry_width : -128 - D].transpose(1, 0, 2, 3)
        up_full = up_full.reshape(quarters, 1, LATENT, -1)
        ups_shape = up_full.shape
    small_full = packed_full[:, -128:].reshape(2 * expert_total, -1)
    gain_one, gain_latent, gain_feed, router_full = (
        small_full[:, cuts[0] : cuts[1]].reshape(-1),
        small_full[:, cuts[1] : cuts[2]].reshape(-1),
        small_full[:, cuts[2] : cuts[3]].reshape(-1),
        small_full[:, cuts[3] : cuts[4]].reshape(-1, expert_total),
    )

    slot_names = level * PLANE * capacity + jnp.arange(PLANE * capacity)
    hits = target_line[:, :TOPK, None, :] == slot_names[None, None, :, None]
    choose_rows = jnp.any(hits, axis=1).astype(jnp.bfloat16)

    choose_slots = choose_rows.reshape(depth, PLANE, capacity, row_count)
    grad_line = grad_line.reshape(depth, row_count, D)

    cosine, sine_table = rotary_table(row_count, device_half * row_count, ROPE)
    tables = (
        jnp.concatenate([cosine] * 4, axis=1),
        jnp.concatenate([-sine_table, sine_table] * 2, axis=1),
    )
    gain_first = gain_one.astype(jnp.float32)
    latent_gain = gain_latent.astype(jnp.float32)
    feed_gain = gain_feed.astype(jnp.float32)
    query_place = device_half * row_count + jnp.arange(row_count)
    key_place = (device_half - 1) * row_count + jnp.arange(2 * row_count)
    padded_segments = jnp.concatenate([jnp.full((row_count,), -1, jnp.int32), segments[0]])
    key_segment = lax.dynamic_slice_in_dim(padded_segments, device_half * row_count, 2 * row_count)
    query_segment = lax.dynamic_slice_in_dim(segments[0], device_half * row_count, row_count)
    visible = (key_place[None, :] <= query_place[:, None]) & (
        key_segment[None, :] == query_segment[:, None]
    )
    mask = visible.astype(jnp.float32)
    layout = (entry_width, packed.shape[1] - 128 - D)
    (
        normed_low,
        residual,
        mixed_low,
        queries,
        latent,
        compressed,
        expanded,
        keys_rope,
        log_total,
        mixed_heads,
        grad_rows,
    ) = attend(
        tokens[0],
        packed_full,
        up_full,
        ups_shape,
        (gain_first[None], latent_gain[None], feed_gain[None]),
        tables,
        mask,
        choose_slots,
        grad_line,
        layout,
    )
    mixed_rows, shared_out, shared_back, shared_grad, sdown_grad, grad_rows = dispatch(
        mixed_low, choose_slots, grad_line, shared_full, sdown_full, grad_rows
    )
    grad_rows = grad_rows.reshape(expert_total * capacity, D)
    mixed_rows = mixed_rows.reshape(expert_total * capacity, D)
    shared_out = shared_out.reshape(line_rows, D)
    hidden_grad_raw = right_matmul(grad_rows, expert_down_full)
    slot_probs = jax.nn.softmax(matmul(mixed_rows, router_full), axis=-1)
    gate_column = lax.dynamic_slice_in_dim(slot_probs, place, 1, axis=1)

    gate_part = matmul(mixed_rows, expert_gate_full)
    up_portion = matmul(mixed_rows, expert_up_full)
    hidden_wide = jax.nn.silu(gate_part) * up_portion
    hidden = hidden_wide.astype(jnp.bfloat16)
    slot_grad = jnp.sum(hidden.astype(jnp.float32) * hidden_grad_raw, axis=-1)
    hidden_grad = hidden_grad_raw * gate_column
    gate_part_grad, up_part_grad = swiglu_back(gate_part, up_portion, hidden_grad)
    gate_low = gate_part_grad.astype(jnp.bfloat16)
    up_low = up_part_grad.astype(jnp.bfloat16)
    input_grad = (
        right_matmul(gate_low, expert_gate_full) + right_matmul(up_low, expert_up_full)
    ).astype(jnp.bfloat16)
    hidden_scaled = (hidden.astype(jnp.float32) * gate_column).astype(jnp.bfloat16)
    slot_grad = jnp.pad(
        slot_grad.reshape(PLANE, depth, 1, capacity), ((0, 0), (0, 0), (0, 0), (0, 128 - capacity))
    )
    back_and_shared, prob_parts, expert_gate_piece, expert_up_piece, expert_down_piece = give_back(
        input_grad.reshape(PLANE, depth, capacity, D),
        jnp.broadcast_to(slot_grad, (PLANE, depth, 8, 128)),
        choose_slots,
        shared_back,
        [mixed_rows, gate_low, up_low, hidden_scaled, grad_rows],
    )
    back_and_shared, hidden = lax.optimization_barrier((back_and_shared, hidden))
    expert_out = (matmul(hidden, expert_down_full) * gate_column).astype(jnp.bfloat16)
    def scatter_plane(value):
        part = lax.psum_scatter(value, "fsdp", scatter_dimension=0, tiled=True)
        return lax.psum_scatter(
            part, "expert", scatter_dimension=0, axis_index_groups=plane, tiled=True
        )

    shared_summed = scatter_plane(shared_grad.reshape(2 * PLANE, depth, part_rows, -1))[0]
    sdown_summed = scatter_plane(sdown_grad)

    out_grad = cotangent[0].astype(jnp.float32)
    probabilities = jax.nn.softmax(matmul(mixed_low, router_full), axis=-1)
    prob_grad = prob_parts[:, :PLANE].reshape(expert_total, row_count).T
    logit_low = (
        probabilities * (prob_grad - jnp.sum(probabilities * prob_grad, axis=-1, keepdims=True))
    ).astype(jnp.bfloat16)
    router_grad = left_matmul(mixed_low, logit_low)
    mixed_grad = right_matmul(logit_low, router_full) + back_and_shared
    residual_add, feed_gain_grad = norm_back(residual, feed_gain, mixed_grad)
    residual_grad = out_grad + residual_add
    attended_low = residual_grad.astype(jnp.bfloat16)
    (
        token_grad,
        up_weight_grad,
        latent_gain_grad,
        first_gain_grad,
        entry_grad,
        output_grad,
        returned,
    ) = attend_back(
        attended_low,
        packed_full,
        up_full,
        ups_shape,
        (
            queries,
            expanded,
            keys_rope,
            log_total,
            latent,
            compressed,
            normed_low,
            mixed_heads,
            tokens[0],
            residual_grad,
        ),
        (latent_gain[None], gain_first[None]),
        tables,
        mask,
        expert_out.reshape(PLANE, depth, capacity, D),
        (shared_summed, sdown_summed),
        layout,
    )
    if up_rows % 16 != 0:
        up_weight_grad = up_weight_grad.reshape(quarters, 2 * expert_total, up_rows, -1)
        up_weight_grad = up_weight_grad.transpose(1, 0, 2, 3)
    latent_gain_grad = latent_gain_grad[0]
    first_gain_grad = first_gain_grad[0]
    routed = jnp.einsum(
        "zst,zsd->ztd",
        choose_rows,
        returned.transpose(1, 0, 2, 3).reshape(depth, PLANE * capacity, D),
        preferred_element_type=jnp.float32,
    )
    routed_and_shared = lax.psum_scatter(
        (routed.reshape(line_rows, D) + shared_out).astype(jnp.bfloat16),
        "expert",
        scatter_dimension=0,
        axis_index_groups=line,
        tiled=True,
    ).astype(jnp.float32)
    output = (residual + routed_and_shared).astype(jnp.bfloat16)

    small_grad = jnp.concatenate(
        [
            first_gain_grad.reshape(-1, gain_width),
            latent_gain_grad.reshape(-1, latent_width),
            feed_gain_grad.reshape(-1, gain_width),
            router_grad.reshape(2 * expert_total, -1),
        ],
        axis=1,
    )
    small_grad = jnp.pad(small_grad, ((0, 0), (0, 128 * part_rows - small_grad.shape[1])))
    packed_piece, shared_back_moved = reduce_rows(
        [
            entry_grad,
            up_weight_grad.reshape(2 * expert_total * part_rows, -1),
            output_grad,
            small_grad.astype(jnp.bfloat16).reshape(-1, 128),
        ],
        shared_summed,
        cut,
    )
    small_piece = packed_piece[:, -128:].reshape(-1)
    shared_pieces = (
        shared_back_moved.reshape(depth, part_rows, 2, shared_padded)[..., : 2 * shared_width]
        .reshape(depth, part_rows, 2, 2, shared_width)
        .transpose(2, 1, 3, 0, 4)
        .reshape((2,) + shared_gate.shape)
        .astype(jnp.float32)
    )
    output_piece = packed_piece[:, -128 - D : -128]
    nope_width = HEADS * NOPE
    query_piece = jnp.concatenate(
        [
            packed_piece[:, :nope_width].reshape(part_rows, HEADS, NOPE),
            packed_piece[:, nope_width:query_width].reshape(part_rows, HEADS, ROPE),
        ],
        axis=2,
    ).reshape(part_rows, query_width)

    return (
        output[None],
        token_grad[None],
        small_piece[cuts[0] : cuts[1]],
        query_piece,
        packed_piece[:, query_width : query_width + down_width],
        small_piece[cuts[1] : cuts[2]],
        packed_piece[:, entry_width : -128 - D]
        .reshape(quarters, latent_up.shape[0], -1)
        .transpose(1, 0, 2)
        .reshape(latent_up.shape),
        output_piece,
        small_piece[cuts[2] : cuts[3]],
        small_piece[cuts[3] : cuts[4]].reshape(gain_width, expert_total),
        shared_pieces[0],
        shared_pieces[1],
        sdown_summed.astype(jnp.float32),
        expert_gate_piece.astype(jnp.float32)[None],
        expert_up_piece.astype(jnp.float32)[None],
        expert_down_piece.astype(jnp.float32)[None],
    )


def solution(mesh):
    return jax.shard_map(
        body,
        mesh=mesh,
        in_specs=(
            P("expert", "fsdp", None),
            P("expert", None),
            P("expert", "fsdp", None),
            P("expert", "fsdp", None),
            P("expert", "fsdp", None),
            P(("fsdp", "expert")),
            P(("fsdp", "expert"), None),
            P(("fsdp", "expert"), None),
            P(("fsdp", "expert")),
            P(("fsdp", "expert"), None),
            P(("fsdp", "expert"), None),
            P(("fsdp", "expert")),
            P(("fsdp", "expert"), None),
            P(("fsdp", "expert"), None),
            P(("fsdp", "expert"), None),
            P(("fsdp", "expert"), None),
            P("expert", "fsdp", None),
            P("expert", "fsdp", None),
            P("expert", None, "fsdp"),
        ),
        out_specs=(
            P("expert", "fsdp", None),
            P("expert", "fsdp", None),
            P(("fsdp", "expert")),
            P(("fsdp", "expert"), None),
            P(("fsdp", "expert"), None),
            P(("fsdp", "expert")),
            P(("fsdp", "expert"), None),
            P(("fsdp", "expert"), None),
            P(("fsdp", "expert")),
            P(("fsdp", "expert"), None),
            P(("fsdp", "expert"), None),
            P(("fsdp", "expert"), None),
            P(("fsdp", "expert"), None),
            P("expert", "fsdp", None),
            P("expert", "fsdp", None),
            P("expert", None, "fsdp"),
        ),
        check_vma=False,
    )
```

```python
import functools
import math

import jax
import jax.numpy as jnp
from jax import lax
from jax.experimental import pallas as pl
from jax.experimental.pallas import tpu as pltpu
from jax.sharding import PartitionSpec as P

D = 2048
HEADS = 16
NOPE = 128
ROPE = 64
VALUE = 128
LATENT = 512
TOPK = 6


EPSILON = 1e-06
FLOOR_SCORE = -1e30


def norm_rows(values, gain):
    return values * lax.rsqrt(jnp.mean(values * values, axis=-1, keepdims=True) + EPSILON) * gain


def norm_back(values, gain, incoming):
    primal_out, pullback = jax.vjp(norm_rows, values, gain)
    return pullback(incoming)


def swiglu_back(gate_part, up_portion, incoming):
    primal_out, pullback = jax.vjp(
        lambda former, latter: jax.nn.silu(former) * latter, gate_part, up_portion
    )
    return pullback(incoming)


def rotary_table(row_total, offset, rope_width):
    frequency_steps = jnp.arange(rope_width // 2, dtype=jnp.float32)
    inverse = jnp.exp(frequency_steps * (-2.0 * math.log(10000.0) / rope_width))
    places = (offset + jnp.arange(row_total)).astype(jnp.float32)
    angles = places[:, None] * inverse[None, :]
    return (jnp.cos(angles), jnp.sin(angles))


def matmul(former, latter):
    return jnp.dot(former, latter, preferred_element_type=jnp.float32)


def left_matmul(former, latter):
    return lax.dot_general(
        former, latter, (((0,), (0,)), ((), ())), preferred_element_type=jnp.float32
    )


def right_matmul(former, latter):
    return lax.dot_general(
        former, latter, (((1,), (1,)), ((), ())), preferred_element_type=jnp.float32
    )


PLANE = 4
MESH = pl.DeviceIdType.MESH
MEBIBYTE = 1024 * 1024
GROUPS = 4
LONG = pl.CostEstimate(flops=100 * 10**9, bytes_accessed=0, transcendentals=0)
MIDDLE = pl.CostEstimate(flops=40 * 10**9, bytes_accessed=0, transcendentals=0)


def groups(count):
    lines = count // PLANE
    plane = [[row * PLANE + spot for spot in range(PLANE)] for row in range(lines)]
    line = [[row * PLANE + spot for row in range(lines)] for spot in range(PLANE)]
    return plane, line


def remote(source, target, send, receive, where):
    return pltpu.make_async_remote_copy(
        src_ref=source,
        dst_ref=target,
        send_sem=send,
        recv_sem=receive,
        device_id=where,
        device_id_type=MESH,
    )


def plane_mates(place):
    spot = place % PLANE
    return (place + 1 - 2 * (spot % 2), place + 2 - 4 * (spot // 2))


def greet(partners):
    barrier = pltpu.get_barrier_semaphore()
    for where in partners:
        pl.semaphore_signal(barrier, inc=1, device_id=where, device_id_type=MESH)
    pl.semaphore_wait(barrier, len(partners))


def line_others(half, place, depth):
    total = depth * PLANE
    return [(half, (place + offset * PLANE) % total) for offset in range(1, depth)]


def plane_others(half, place):
    spot = place % PLANE
    return [(half, place - spot + (spot + offset) % PLANE) for offset in range(1, PLANE)]


def greet_neighbours(half, place, depth):
    mates = [(half, mate) for mate in plane_mates(place)]
    greet(line_others(half, place, depth) + mates + [(1 - half, place)])


def exchange_along(depth, half, place, in_ref, land, own_sem, send, receive):
    level = place // PLANE
    total = depth * PLANE

    def own():
        return pltpu.make_async_copy(in_ref.at[level], land(level), own_sem)

    def to(offset):
        where = (place + offset * PLANE) % total
        return remote(
            in_ref.at[where // PLANE],
            land(level),
            send.at[offset],
            receive.at[offset],
            (half, where),
        )

    def start():
        own().start()
        for offset in range(1, depth):
            to(offset).start()

    def finish():
        own().wait()
        for offset in range(1, depth):
            to(offset).wait()

    return start, finish


def exchange_plane(half, place, source_of, target_of, own_sem, send, receive, own_there=False):
    spot = place % PLANE

    def to(offset, level):
        mate = (spot + offset) % PLANE
        return remote(
            source_of(mate, level),
            target_of(spot, level),
            send.at[offset, level],
            receive.at[offset, level],
            (half, place - spot + mate),
        )

    def came(offset, level):
        mate = (spot + PLANE - offset) % PLANE
        block = target_of(mate, level)
        return remote(
            block,
            block,
            send.at[offset, level],
            receive.at[offset, level],
            (half, place - spot + mate),
        )

    def own(level):
        return pltpu.make_async_copy(
            source_of(spot, level), target_of(spot, level), own_sem.at[level]
        )

    def start(level):
        for offset in range(1, PLANE):
            to(offset, level).start()
        if not own_there:
            own(level).start()

    def finish(level):
        if not own_there:
            own(level).wait()
        for offset in range(1, PLANE):
            came(offset, level).wait_recv()
            to(offset, level).wait_send()

    return start, finish


def place_rows(choose_ref, source, block, placed):
    def columns(n, carry):
        at = lanes_at(n * 512, 512)
        for mate in range(PLANE):
            placed[mate, :, at] = jnp.dot(
                choose_ref[source, mate], block[:, at], preferred_element_type=jnp.float32
            ).astype(placed.dtype)
        return carry

    lax.fori_loop(0, block.shape[1] // 512, columns, 0)


def cuts_of(width, count):
    return [width * k // count // 128 * 128 for k in range(count)] + [width]


def gather_kernel(depth, cuts, *refs):
    in_ref, *line_ins, move_in, down_in = refs[:5]
    out_ref, *line_outs, shared_out, down_out = refs[5:10]
    own_sem, zs, zr, ps, pr, qs, qr, cs, cr, ls, lr, ms, mr, *shared_sems = refs[10:]
    os, ore, ts, tr, us, ur = shared_sems
    half = lax.axis_index("fsdp")
    place = lax.axis_index("expert")
    level = place // PLANE
    spot = place % PLANE
    total = depth * PLANE
    mates = plane_mates(place)
    rows, width = in_ref.shape
    columns = [pl.ds(low, high - low) for low, high in zip(cuts[:-1], cuts[1:])]
    count = len(columns)
    greet_neighbours(half, place, depth)

    def at(which, block, count=1):
        start = pl.multiple_of((half * total + block) * rows, rows)
        return out_ref.at[pl.ds(start, count * rows), columns[which]]

    def along(which, way, source, own=False):
        target = at(which, source * PLANE + spot)
        start = in_ref.at[:, columns[which]] if own else target
        return remote(
            start,
            target,
            zs.at[which, way, source],
            zr.at[which, source],
            (half, place + (2 * way - 1) * PLANE),
        )

    def plane_one(which, source, own=False):
        target = at(which, source * PLANE + spot)
        start = in_ref.at[:, columns[which]] if own else target
        return remote(
            start,
            target,
            ps.at[which, source],
            pr.at[which, source],
            (half, mates[which % 2]),
        )

    def plane_two(which, source, turn):
        base = source * PLANE
        if which % 2 == 0:
            block = at(which, base + spot - spot % 2, 2)
        else:
            block = at(which, base + (spot + 2 * turn) % PLANE)
        return remote(
            block,
            block,
            qs.at[which, turn, source],
            qr.at[which, turn, source],
            (half, mates[1 - which % 2]),
        )

    def core(which, source):
        block = at(which, source * PLANE, PLANE)
        return remote(
            block, block, cs.at[which, source], cr.at[which, source], (1 - half, place)
        )

    def trail(which, way, source, own=False):
        target = line_outs[which].at[source]
        return remote(
            line_ins[which] if own else target,
            target,
            ls.at[which, way, source],
            lr.at[which, source],
            (half, place + (2 * way - 1) * PLANE),
        )

    def trail_own(which):
        return pltpu.make_async_copy(
            line_ins[which], line_outs[which].at[level], own_sem.at[count + which]
        )

    move_start, move_finish = exchange_along(
        depth,
        half,
        place,
        move_in,
        lambda source: shared_out.at[half, source, spot],
        own_sem.at[count + 2],
        ms,
        mr,
    )
    items = range(depth + 2)
    down_own = pltpu.make_async_copy(down_in, down_out.at[half, spot], own_sem.at[count + 3])

    def shared_at(item, first, count):
        if item < depth:
            return shared_out.at[half, item, pl.ds(first, count)]
        span = down_in.shape[1] // 2
        return down_out.at[
            half, pl.ds(first, count), :, pl.ds((item - depth) * span, span)
        ]

    def shared_route(item):
        return (0 if item < depth // 2 else 1) if item < depth else item - depth

    def shared_one(item):
        block = shared_at(item, spot, 1)
        mate = mates[shared_route(item)]
        return remote(block, block, os.at[item], ore.at[item], (half, mate))

    def shared_two(item):
        if shared_route(item) == 0:
            blocks = [shared_at(item, spot - spot % 2, 2)]
        else:
            blocks = [shared_at(item, (spot + 2 * turn) % PLANE, 1) for turn in range(2)]
        mate = mates[1 - shared_route(item)]
        return [
            remote(block, block, ts.at[turn, item], tr.at[turn, item], (half, mate))
            for turn, block in enumerate(blocks)
        ]

    def shared_core(item):
        block = shared_at(item, 0, PLANE)
        return remote(block, block, us.at[item], ur.at[item], (1 - half, place))

    seconds = [(which, turn) for which in range(count) for turn in range(1 + which % 2)]

    def own_copy(which):
        return pltpu.make_async_copy(
            in_ref.at[:, columns[which]], at(which, place), own_sem.at[which]
        )

    for which in range(count):

        @pl.when(level > 0)
        def _():
            along(which, 0, level, True).start()

        @pl.when(level < depth - 1)
        def _():
            along(which, 1, level, True).start()

        plane_one(which, level, True).start()
        own_copy(which).start()
    move_start()
    down_own.start()
    for which in range(2):
        trail_own(which).start()

    def trail_first():
        for which in range(2):

            @pl.when(level > 0)
            def _():
                trail(which, 0, level, True).start()

            @pl.when(level < depth - 1)
            def _():
                trail(which, 1, level, True).start()

    def trail_on(source, way):
        for which in range(2):
            trail(which, way, source).wait_recv()

            @pl.when((level < depth - 1) if way == 1 else (level > 0))
            def _():
                trail(which, way, source).start()

    def visit(step, act):
        if step == 0:
            act(level, None)
            return

        @pl.when(level - step >= 0)
        def _():
            act(level - step, 1)

        @pl.when(level + step < depth)
        def _():
            act(level + step, 0)

    def arrive(source, way):
        for which in range(count):
            along(which, way, source).wait_recv()

            @pl.when((level < depth - 1) if way == 1 else (level > 0))
            def _():
                along(which, way, source).start()

            plane_one(which, source).start()

    def spread(source, way):
        for which in range(count):
            plane_one(which, source).wait_recv()
            for kind, turn in seconds:
                if kind == which:
                    plane_two(kind, source, turn).start()

    def share(source, way):
        for which in range(count):
            for kind, turn in seconds:
                if kind == which:
                    plane_two(kind, source, turn).wait_recv()
            core(which, source).start()

    for which in range(count):
        own_copy(which).wait()
    visit(0, spread)
    for step in range(1, depth):
        visit(step, arrive)
        if step == 1:
            move_finish()
            down_own.wait()
            for item in items:
                shared_one(item).start()
        if step == 2:
            trail_first()
        if step >= 3:
            visit(step - 2, trail_on)
        if step >= 2:
            visit(step - 1, spread)
        if step == 2:
            for item in items:
                shared_one(item).wait_recv()
                for copy in shared_two(item):
                    copy.start()
        if step >= 3:
            visit(step - 3, share)
    visit(depth - 1, spread)
    visit(depth - 2, trail_on)
    visit(depth - 3, share)
    for item in items:
        for copy in shared_two(item):
            copy.wait_recv()
        shared_core(item).start()
    visit(depth - 2, share)
    visit(depth - 1, trail_on)
    visit(depth - 1, share)
    for item in items:
        shared_one(item).wait_send()
        for copy in shared_two(item):
            copy.wait_send()
        shared_core(item).wait()
    for which in range(2):
        trail_own(which).wait()

    def finish(source, carry):
        for which in range(2):

            @pl.when((source <= level) & (level < depth - 1))
            def _():
                trail(which, 1, source).wait_send()

            @pl.when((source >= level) & (level > 0))
            def _():
                trail(which, 0, source).wait_send()

        for which in range(count):
            core(which, source).wait_recv()
            core(which, source).wait_send()
            plane_one(which, source).wait_send()

            @pl.when((source <= level) & (level < depth - 1))
            def _():
                along(which, 1, source).wait_send()

            @pl.when((source >= level) & (level > 0))
            def _():
                along(which, 0, source).wait_send()

        for kind, turn in seconds:
            plane_two(kind, source, turn).wait_send()
        return carry

    lax.fori_loop(0, depth, finish, 0)


def gather_rows(value, first, second, moved, down, cuts):
    rows, width = value.shape
    total = lax.axis_size("expert")
    depth = total // PLANE
    count = len(cuts) - 1
    semaphores = pltpu.SemaphoreType.DMA
    return pl.pallas_call(
        functools.partial(gather_kernel, depth, cuts),
        out_shape=[
            jax.ShapeDtypeStruct((2 * total * rows, width), value.dtype),
            jax.ShapeDtypeStruct((depth,) + first.shape, first.dtype),
            jax.ShapeDtypeStruct((depth,) + second.shape, second.dtype),
            jax.ShapeDtypeStruct((2, depth, PLANE) + moved.shape[1:], moved.dtype),
            jax.ShapeDtypeStruct((2, PLANE) + down.shape, down.dtype),
        ],
        in_specs=[pl.BlockSpec(memory_space=pltpu.VMEM)] * 5,
        out_specs=[pl.BlockSpec(memory_space=pl.ANY)] * 5,
        scratch_shapes=[
            semaphores((count + 4,)),
            semaphores((count, 2, depth)),
            semaphores((count, depth)),
            semaphores((count, depth)),
            semaphores((count, depth)),
            semaphores((count, 2, depth)),
            semaphores((count, 2, depth)),
            semaphores((count, depth)),
            semaphores((count, depth)),
            semaphores((2, 2, depth)),
            semaphores((2, depth)),
            semaphores((depth,)),
            semaphores((depth,)),
            semaphores((depth + 2,)),
            semaphores((depth + 2,)),
            semaphores((2, depth + 2)),
            semaphores((2, depth + 2)),
            semaphores((depth + 2,)),
            semaphores((depth + 2,)),
        ],
        compiler_params=pltpu.CompilerParams(collective_id=1, has_side_effects=True),
        cost_estimate=LONG,
    )(value, first, second, moved, down)


def dot_nt(former, latter):
    return lax.dot_general(
        former, latter, (((1,), (1,)), ((), ())), preferred_element_type=jnp.float32
    )


def dot_tn(former, latter):
    return lax.dot_general(
        former, latter, (((0,), (0,)), ((), ())), preferred_element_type=jnp.float32
    )


def dispatch_kernel(depth, *refs):
    x_ref, choose_ref, grad_in, shared_in, down_in = refs[:5]
    rows_out, forth_out, back_out, wide_out, tall_out, grad_out = refs[6:12]
    lines, placed, grads, weights, downs, low_ref, hidden_ref, forth_ref, back_ref = refs[12:21]
    wide_ref, tall_ref, grad_placed, wide_give, wide_take, tall_give, tall_take = refs[21:28]
    load_sem, out_sem, zs, zr, es, er, own_sem, done_sem, gs, gr, grad_sem = refs[28:39]
    ws, wr, ts, tr = refs[39:]
    half = lax.axis_index("fsdp")
    place = lax.axis_index("expert")
    other = (1 - half, place)
    level = place // PLANE
    spot = place % PLANE
    padded, width = downs.shape
    share = padded // 2
    true = down_in.shape[1]
    chunk = padded
    greet(line_others(half, place, depth) + plane_others(half, place) + [other])

    def along(way, source):
        block = lines.at[source]
        where = (half, place + (2 * way - 1) * PLANE)
        return remote(block, block, zs.at[way, source], zr.at[source], where)

    loads = [
        pltpu.make_async_copy(shared_in, weights, load_sem.at[0]),
        pltpu.make_async_copy(grad_in, grads, load_sem.at[1]),
    ] + [
        pltpu.make_async_copy(
            down_in.at[k], downs.at[pl.ds(k * share, true), :], load_sem.at[2 + k]
        )
        for k in range(2)
    ]
    lines[level] = x_ref[...]

    def pass_on(way, source):
        @pl.when((level < depth - 1) if way == 1 else (level > 0))
        def _():
            along(way, source).start()

    for way in range(2):
        pass_on(way, level)
    for load in loads:
        load.start()
    if share > true:
        for k in range(2):
            downs[pl.ds(k * share + true, share - true), :] = jnp.zeros(
                (share - true, width), downs.dtype
            )

    rows_start, rows_finish = exchange_plane(
        half,
        place,
        lambda mate, source: placed.at[source, mate],
        lambda mate, source: rows_out.at[source, mate],
        own_sem,
        es,
        er,
    )
    grad_start, grad_finish = exchange_plane(
        half,
        place,
        lambda mate, source: grad_placed.at[source // 2, mate],
        lambda mate, source: grad_out.at[source, mate],
        grad_sem,
        gs,
        gr,
    )

    def give(source):
        place_rows(choose_ref, source, lines.at[source], placed.at[source])
        rows_start(source)

    def give_grad(n, carry):
        source = 2 * n + 1
        place_rows(choose_ref, source, grads.at[source], grad_placed.at[n])
        grad_start(source)
        return carry

    def shared(source):
        def inner(n, carry):
            at = pl.ds(pl.multiple_of(n * chunk, chunk), chunk)
            after = pl.ds(pl.multiple_of(padded + n * chunk, 128), chunk)
            x = lines[source]
            gate = jnp.dot(x, weights[:, at], preferred_element_type=jnp.float32)
            up = jnp.dot(x, weights[:, after], preferred_element_type=jnp.float32)
            dh = dot_nt(grads[source], downs[at, :])
            sig = 1.0 / (1.0 + jnp.exp(-gate))
            act = gate * sig
            hidden_ref[source, :, at] = (act * up).astype(hidden_ref.dtype)
            low_ref[source, :, at] = (dh * up * (sig + act * (1.0 - sig))).astype(low_ref.dtype)
            low_ref[source, :, after] = (dh * act).astype(low_ref.dtype)
            return carry

        lax.fori_loop(0, padded // chunk, inner, 0)

        def outer(n, carry):
            at = pl.ds(pl.multiple_of(n * 1024, 1024), 1024)
            forth_ref[:, at] = jnp.dot(
                hidden_ref[source], downs[:, at], preferred_element_type=jnp.float32
            ).astype(forth_ref.dtype)
            back_ref[:, at] = dot_nt(low_ref[source], weights[at, :]).astype(back_ref.dtype)
            return carry

        lax.fori_loop(0, width // 1024, outer, 0)
        outs = [
            pltpu.make_async_copy(forth_ref, forth_out.at[source], out_sem.at[0]),
            pltpu.make_async_copy(back_ref, back_out.at[source], out_sem.at[1]),
        ]
        for out in outs:
            out.start()
        for out in outs:
            out.wait()

    give(level)
    for load in loads:
        load.wait()
    lax.fori_loop(0, depth // 2, give_grad, 0)
    shared(level)

    def step(s, carry):
        @pl.when(level - s >= 0)
        def _():
            along(1, level - s).wait_recv()
            pass_on(1, level - s)

        @pl.when(level + s < depth)
        def _():
            along(0, level + s).wait_recv()
            pass_on(0, level + s)

        def one(way, act):
            source = level + (1 - 2 * way) * s

            @pl.when((source >= 0) & (source < depth))
            def _():
                act(source)

        def both(way, carry):
            one(way, give)
            return carry

        def both_shared(way, carry):
            one(way, shared)
            return carry

        lax.fori_loop(0, 2, both, 0)
        lax.fori_loop(0, 2, both_shared, 0)
        return carry

    lax.fori_loop(1, depth, step, 0)

    tokens = x_ref.shape[0]

    def all_lines(ref, at):
        return ref[:, :, at].reshape(depth * tokens, -1)

    part = wide_ref.shape[2]
    chunk_rows = max(PLANE * part, 128)
    per_chunk = chunk_rows // (PLANE * part)
    core_rows = width // 2
    tall_rows = tall_ref.shape[1]
    tall_count = share // tall_rows

    def wide_value(owner, n):
        at = pl.ds(pl.multiple_of(owner * core_rows + n * chunk_rows, chunk_rows), chunk_rows)
        return dot_tn(all_lines(lines, at), low_ref[...].reshape(depth * tokens, -1))

    def tall_value(owner, k):
        at = pl.ds(pl.multiple_of(owner * share + k * tall_rows, tall_rows), tall_rows)
        return dot_tn(all_lines(hidden_ref, at), grads[...].reshape(depth * tokens, -1))

    def wide_send(k):
        return remote(wide_give.at[k], wide_take.at[k], ws.at[k], wr.at[k], other)

    def tall_send(k):
        return remote(tall_give.at[k], tall_take.at[k], ts.at[k], tr.at[k], other)

    def split(value, j):
        first = j * PLANE * part
        return [value[first + k * part : first + (k + 1) * part] for k in range(PLANE)]

    def give_wide(n, carry):
        value = wide_value(1 - half, n)
        for j in range(per_chunk):
            for k, block in enumerate(split(value, j)):
                wide_give[n * per_chunk + j, k] = block.astype(wide_give.dtype)
            wide_send(n * per_chunk + j).start()
        return carry

    def give_tall(k, carry):
        tall_give[k] = tall_value(1 - half, k).astype(tall_give.dtype)
        tall_send(k).start()
        return carry

    def write_wide(k):
        return pltpu.make_async_copy(
            wide_ref.at[k % 2], wide_out.at[:, k], done_sem.at[0, k % 2]
        )

    def keep_wide(n, carry):
        value = wide_value(half, n)
        for j in range(per_chunk):
            at = n * per_chunk + j

            @pl.when(at >= 2)
            def _():
                write_wide(at - 2).wait()

            wide_send(at).wait_recv()
            for k, block in enumerate(split(value, j)):
                total = block + wide_take[at, k].astype(jnp.float32)
                wide_ref[at % 2, k] = total.astype(wide_ref.dtype)
            write_wide(at).start()
        return carry

    lax.fori_loop(0, core_rows // chunk_rows, give_wide, 0)
    lax.fori_loop(0, tall_count, give_tall, 0)
    lax.fori_loop(0, core_rows // chunk_rows, keep_wide, 0)
    for k in range(max(0, depth - 2), depth):
        write_wide(k).wait()
    writes = []
    for k in range(tall_count):
        if k >= 2:
            writes[k - 2].wait()
        value = tall_value(half, k)
        tall_send(k).wait_recv()
        total = value + tall_take[k].astype(jnp.float32)
        tall_ref[k % 2] = total.astype(tall_ref.dtype)
        size = min(tall_rows, true - k * tall_rows)
        writes.append(
            pltpu.make_async_copy(
                tall_ref.at[k % 2, pl.ds(0, size), :],
                tall_out.at[pl.ds(k * tall_rows, size), :],
                done_sem.at[1, k % 2],
            )
        )
        writes[k].start()
    for write in writes[-2:]:
        write.wait()

    def given(k, carry):
        wide_send(k).wait_send()
        return carry

    lax.fori_loop(0, depth, given, 0)
    for k in range(tall_count):
        tall_send(k).wait_send()

    def finish_grad(n, carry):
        grad_finish(2 * n + 1)
        return carry

    lax.fori_loop(0, depth // 2, finish_grad, 0)

    def finish(source, carry):
        rows_finish(source)

        @pl.when((source <= level) & (level < depth - 1))
        def _():
            along(1, source).wait_send()

        @pl.when((source >= level) & (level > 0))
        def _():
            along(0, source).wait_send()

        return carry

    lax.fori_loop(0, depth, finish, 0)


def dispatch(x, choose, grad_line, shared_full, down_full, grad_rows):
    depth = choose.shape[0]
    tokens, width = x.shape
    capacity = choose.shape[2]
    padded = shared_full.shape[1] // 2
    part = width // (2 * PLANE * depth)
    semaphores = pltpu.SemaphoreType.DMA
    low = x.dtype
    anywhere = pl.BlockSpec(memory_space=pl.ANY)
    local = pl.BlockSpec(memory_space=pltpu.VMEM)
    return pl.pallas_call(
        functools.partial(dispatch_kernel, depth),
        out_shape=[
            jax.ShapeDtypeStruct((depth, PLANE, capacity, width), low),
            jax.ShapeDtypeStruct((depth, tokens, width), low),
            jax.ShapeDtypeStruct((depth, tokens, width), low),
            jax.ShapeDtypeStruct((PLANE, depth, part, 2 * padded), low),
            jax.ShapeDtypeStruct(down_full.shape[1:], low),
            jax.ShapeDtypeStruct(grad_rows.shape, low),
        ],
        in_specs=[local, local] + [anywhere] * 4,
        out_specs=[anywhere] * 6,
        input_output_aliases={5: 5},
        scratch_shapes=[
            pltpu.VMEM((depth, tokens, width), low),
            pltpu.VMEM((depth, PLANE, capacity, width), low),
            pltpu.VMEM((depth, tokens, width), low),
            pltpu.VMEM((width, 2 * padded), low),
            pltpu.VMEM((padded, width), low),
            pltpu.VMEM((depth, tokens, 2 * padded), low),
            pltpu.VMEM((depth, tokens, padded), low),
            pltpu.VMEM((tokens, width), low),
            pltpu.VMEM((tokens, width), low),
            pltpu.VMEM((2, PLANE, part, 2 * padded), low),
            pltpu.VMEM((2, 128, width), low),
            pltpu.VMEM((depth // 2, PLANE, capacity, width), low),
            pltpu.VMEM((depth, PLANE, part, 2 * padded), low),
            pltpu.VMEM((depth, PLANE, part, 2 * padded), low),
            pltpu.VMEM((padded // 256, 128, width), low),
            pltpu.VMEM((padded // 256, 128, width), low),
            semaphores((4,)),
            semaphores((2,)),
            semaphores((2, depth)),
            semaphores((depth,)),
            semaphores((PLANE, depth)),
            semaphores((PLANE, depth)),
            semaphores((depth,)),
            semaphores((2, 2)),
            semaphores((PLANE, depth)),
            semaphores((PLANE, depth)),
            semaphores((depth,)),
            semaphores((depth,)),
            semaphores((depth,)),
            semaphores((padded // 256,)),
            semaphores((padded // 256,)),
        ],
        compiler_params=pltpu.CompilerParams(
            collective_id=3, has_side_effects=True, vmem_limit_bytes=62 * MEBIBYTE
        ),
        cost_estimate=LONG,
    )(x, choose, grad_line, shared_full, down_full, grad_rows)


def expert_kernel(total, *refs):
    x_ref, grad_ref, gate_in, up_in, down_in, router_ref = refs[:6]
    scaled_ref, d_gate_ref, d_up_ref, back_ref, out_ref, slot_ref = refs[6:12]
    gates, ups, downs, hidden, sem = refs[12:]
    rows = x_ref.shape[0]
    width, inner = gates.shape
    wide = jnp.float32
    loads = [
        pltpu.make_async_copy(source, target, sem.at[k])
        for k, (source, target) in enumerate(zip((gate_in, up_in, down_in), (gates, ups, downs)))
    ]
    first = pl.program_id(0) == 0

    @pl.when(first)
    def _():
        for load in loads:
            load.start()

    logits = jnp.dot(x_ref[...], router_ref[...], preferred_element_type=wide)
    lanes = lax.broadcasted_iota(jnp.int32, logits.shape, 1)
    logits = jnp.where(lanes < total, logits, FLOOR_SCORE)
    powers = jnp.exp(logits - jnp.max(logits, axis=-1, keepdims=True))
    probs = powers / jnp.sum(powers, axis=-1, keepdims=True)
    mine = jnp.where(lanes == lax.axis_index("expert"), probs, 0.0)
    gate = jnp.sum(mine, axis=-1, keepdims=True)

    @pl.when(first)
    def _():
        for load in loads:
            load.wait()

    def columns(start, size, slots):
        at = lanes_at(start, size)
        former = jnp.dot(x_ref[...], gates[:, at], preferred_element_type=wide)
        latter = jnp.dot(x_ref[...], ups[:, at], preferred_element_type=wide)
        raw = dot_nt(grad_ref[...], downs[at, :])
        sig = 1.0 / (1.0 + jnp.exp(-former))
        act = former * sig
        low = (act * latter).astype(hidden.dtype)
        hidden[:, at] = low
        low = low.astype(wide)
        scaled_ref[:, at] = (low * gate).astype(hidden.dtype)
        grad = raw * gate
        d_gate_ref[:, at] = (grad * latter * (sig + act * (1.0 - sig))).astype(hidden.dtype)
        d_up_ref[:, at] = (grad * act).astype(hidden.dtype)
        return slots + jnp.sum(low * raw, axis=-1, keepdims=True)

    full = inner // 256
    slots = lax.fori_loop(
        0, full, lambda n, slots: columns(n * 256, 256, slots), jnp.zeros((rows, 1), wide)
    )
    if inner % 256:
        slots = columns(full * 256, inner % 256, slots)
    slot_ref[...] = jnp.broadcast_to(slots, slot_ref.shape)

    def outward(n, carry):
        at = lanes_at(n * 256, 256)
        back = dot_nt(d_gate_ref[...], gates[at, :]) + dot_nt(d_up_ref[...], ups[at, :])
        back_ref[:, at] = back.astype(back_ref.dtype)
        out = jnp.dot(hidden[...], downs[:, at], preferred_element_type=wide)
        out_ref[:, at] = (out * gate).astype(out_ref.dtype)
        return carry

    lax.fori_loop(0, width // 256, outward, 0)


def run_expert(rows, grads, gate_full, up_full, down_full, router, total):
    count, width = rows.shape
    inner = gate_full.shape[1]
    low, wide = rows.dtype, jnp.float32
    tile = count // 2
    anywhere = pl.BlockSpec(memory_space=pl.ANY)

    def tiles(span):
        return pl.BlockSpec((tile, span), lambda i: (i, 0))

    spans = (inner, inner, inner, width, width)
    return pl.pallas_call(
        functools.partial(expert_kernel, total),
        grid=(2,),
        out_shape=[jax.ShapeDtypeStruct((count, span), low) for span in spans]
        + [jax.ShapeDtypeStruct((count, 128), wide)],
        in_specs=[tiles(width), tiles(width)]
        + [anywhere] * 3
        + [pl.BlockSpec(router.shape, lambda i: (0, 0))],
        out_specs=[tiles(span) for span in spans] + [tiles(128)],
        scratch_shapes=[
            pltpu.VMEM(gate_full.shape, low),
            pltpu.VMEM(up_full.shape, low),
            pltpu.VMEM(down_full.shape, low),
            pltpu.VMEM((tile, inner), low),
            pltpu.SemaphoreType.DMA((3,)),
        ],
        compiler_params=pltpu.CompilerParams(vmem_limit_bytes=62 * MEBIBYTE),
        cost_estimate=MIDDLE,
    )(rows, grads, gate_full, up_full, down_full, router)


def return_kernel(depth, *refs):
    rows_in, scalars_in, choose_ref, shared_in = refs[:4]
    operands_in = refs[4:9]
    back_ref, prob_ref, gate_out, up_out, down_out = refs[9:14]
    came, scalars, shared, onward, incoming, prob_send, prob_land = refs[14:21]
    held = refs[21:26]
    give_wide, give_tall, take_wide, take_tall, done_wide, done_tall = refs[26:32]
    own_sem, es, er, ss, sr, load_sem, shared_sem, cs, cr, ps, pr = refs[32:43]
    ws, wr, ts, tr, wide_sem, tall_sem = refs[43:]
    x_held, gate_held, up_held, hidden_held, grad_held = held
    half = lax.axis_index("fsdp")
    place = lax.axis_index("expert")
    level = place // PLANE
    spot = place % PLANE
    other = (1 - half, place)
    tokens, width = back_ref.shape
    capacity = choose_ref.shape[2]
    wide_count, wide_rows = take_wide.shape[1:3]
    tall_count, tall_rows, tall_width = take_tall.shape
    greet(line_others(half, place, depth) + plane_others(half, place) + [other])

    def rows_to(offset, source):
        mate = (spot + offset) % PLANE
        where = (half, place - spot + mate)
        return (
            remote(
                rows_in.at[source, mate],
                came.at[spot, source],
                es.at[offset, source],
                er.at[offset, source],
                where,
            ),
            remote(
                scalars_in.at[source, mate],
                scalars.at[spot, source],
                ss.at[offset, source],
                sr.at[offset, source],
                where,
            ),
        )

    def rows_from(offset, source):
        mate = (spot + PLANE - offset) % PLANE
        where = (half, place - spot + mate)
        block, small = came.at[mate, source], scalars.at[mate, source]
        return (
            remote(block, block, es.at[offset, source], er.at[offset, source], where),
            remote(small, small, ss.at[offset, source], sr.at[offset, source], where),
        )

    def own_rows(source):
        return (
            pltpu.make_async_copy(
                rows_in.at[source, spot], came.at[spot, source], own_sem.at[0, source]
            ),
            pltpu.make_async_copy(
                scalars_in.at[source, spot], scalars.at[spot, source], own_sem.at[1, source]
            ),
        )

    def shared_load(slot, source):
        return pltpu.make_async_copy(shared_in.at[source], shared.at[slot], shared_sem.at[slot])

    def each_way(s, act):
        def one(way, carry):
            source = level + (2 * way - 1) * s

            @pl.when((source >= 0) & (source < depth) & ((s > 0) | (way == 0)))
            def _():
                act(way, source)

            return carry

        lax.fori_loop(0, 2, one, 0)

    def begin(way, source):
        for offset in range(1, PLANE):
            for copy in rows_to(offset, source):
                copy.start()
        for copy in own_rows(source):
            copy.start()

    def begin_step(i, carry):
        each_way(depth - 1 - i, begin)
        return carry

    lax.fori_loop(0, depth, begin_step, 0)
    loads = [
        pltpu.make_async_copy(source, target, load_sem.at[k])
        for k, (source, target) in enumerate(zip(operands_in, held))
    ]
    for load in loads:
        load.start()
    for load in loads:
        load.wait()

    def wide_tiles(owner, k):
        at = pl.ds(pl.multiple_of((owner * wide_count + k) * wide_rows, wide_rows), wide_rows)
        x = x_held[:, at]
        return dot_tn(x, gate_held[...]), dot_tn(x, up_held[...])

    def tall_tile(owner, k):
        at = pl.ds(pl.multiple_of(k * tall_rows, tall_rows), tall_rows)
        over = pl.ds(pl.multiple_of(owner * tall_width, tall_width), tall_width)
        return dot_tn(hidden_held[:, at], grad_held[:, over])

    def wide_send(which, k):
        slot = k % 2
        return remote(
            give_wide.at[slot, which],
            take_wide.at[which, k],
            ws.at[slot, which],
            wr.at[which, k],
            other,
        )

    def tall_send(k):
        slot = k % 2
        return remote(give_tall.at[slot], take_tall.at[k], ts.at[slot], tr.at[k], other)

    def wide_write(which, k):
        target = (gate_out, up_out)[which]
        at = pl.ds(pl.multiple_of(k * wide_rows, wide_rows), wide_rows)
        return pltpu.make_async_copy(done_wide.at[which], target.at[at, :], wide_sem.at[which])

    def tall_write(k):
        slot = k % 2
        at = pl.ds(pl.multiple_of(k * tall_rows, tall_rows), tall_rows)
        return pltpu.make_async_copy(done_tall.at[slot], down_out.at[at, :], tall_sem.at[slot])

    def give_wide_tile(k):
        @pl.when(k >= 2)
        def _():
            for which in range(2):
                wide_send(which, k - 2).wait_send()

        for which, tile in enumerate(wide_tiles(1 - half, k)):
            give_wide[k % 2, which] = tile.astype(give_wide.dtype)
            wide_send(which, k).start()

    def give_tall_tile(k):
        @pl.when(k >= 2)
        def _():
            tall_send(k - 2).wait_send()

        give_tall[k % 2] = tall_tile(1 - half, k).astype(give_tall.dtype)
        tall_send(k).start()

    def keep_wide_tile(k):
        @pl.when(k >= 1)
        def _():
            for which in range(2):
                wide_write(which, k - 1).wait()

        for which, tile in enumerate(wide_tiles(half, k)):
            wide_send(which, k).wait_recv()
            tile = tile + take_wide[which, k].astype(jnp.float32)
            done_wide[which] = tile.astype(done_wide.dtype)
            wide_write(which, k).start()

    def keep_tall_tile(k):
        @pl.when(k >= 2)
        def _():
            tall_write(k - 2).wait()

        tile = tall_tile(half, k)
        tall_send(k).wait_recv()
        tile = tile + take_tall[k].astype(jnp.float32)
        done_tall[k % 2] = tile.astype(done_tall.dtype)
        tall_write(k).start()

    units = 2 * (wide_count + tall_count)
    each = -(-units // depth)
    bounds = (0, wide_count, wide_count + tall_count, units - tall_count, units)
    acts = (give_wide_tile, give_tall_tile, keep_wide_tile, keep_tall_tile)

    def fill(unit, carry):
        for act, low, high in zip(acts, bounds[:-1], bounds[1:]):

            @pl.when((unit >= low) & (unit < high))
            def _():
                act(unit - low)

        return carry

    def chain_out(source):
        up = jnp.where(source > level, 1, 0)
        step = 2 * up - 1
        slot = jnp.where(source == level - 1, depth, source)
        return remote(
            onward.at[up],
            incoming.at[slot],
            cs.at[source],
            cr.at[slot],
            (half, place + step * PLANE),
        )

    def chain_in(slot):
        block = incoming.at[slot]
        return remote(block, block, cs.at[0], cr.at[slot], (half, place))

    def prob_to(source):
        return remote(
            prob_send.at[source],
            prob_land.at[level],
            ps.at[source],
            pr.at[level],
            (half, source * PLANE + spot),
        )

    def prob_from(source):
        block = prob_land.at[source]
        return remote(block, block, ps.at[source], pr.at[source], (half, source * PLANE + spot))

    def add_incoming(slot):
        chain_in(slot).wait_recv()
        back_ref[...] += incoming[slot].astype(jnp.float32)

    def settle(way, source):
        for copy in own_rows(source):
            copy.wait()
        for offset in range(1, PLANE):
            for copy in rows_from(offset, source):
                copy.wait_recv()
        shared_load(way, source).wait()

        def columns(n, carry):
            at = pl.ds(pl.multiple_of(n * 512, 512), 512)
            total = shared[way, :, at].astype(jnp.float32)
            for mate in range(PLANE):
                total = total + dot_tn(choose_ref[source, mate], came[mate, source, :, at])
            back_ref[:, at] = total
            return carry

        lax.fori_loop(0, width // 512, columns, 0)
        lines = lax.broadcasted_iota(jnp.int32, (8, tokens), 0)
        probs = jnp.zeros((8, tokens), jnp.float32)
        for mate in range(PLANE):
            part = lax.dot_general(
                scalars[mate, source],
                choose_ref[source, mate].astype(jnp.float32),
                (((0,), (0,)), ((), ())),
                preferred_element_type=jnp.float32,
                precision=lax.Precision.HIGHEST,
            )
            probs = jnp.where(lines == mate, part[:8], probs)

        @pl.when((source >= level) & (level > 0))
        def _():
            add_incoming(source)

        @pl.when((source < level) & (level < depth - 1))
        def _():
            add_incoming(source)

        @pl.when((source == level) & (level < depth - 1))
        def _():
            add_incoming(depth)

        @pl.when(source == level)
        def _():
            prob_land[level] = probs

        @pl.when(source != level)
        def _():
            prob_send[source] = probs
            prob_to(source).start()
            former = source + 2 * way - 1

            @pl.when((former >= 0) & (former < depth))
            def _():
                chain_out(former).wait_send()

            onward[way] = back_ref[...].astype(onward.dtype)
            chain_out(source).start()

    def step(i, carry):
        s = depth - 1 - i
        each_way(s, lambda way, source: shared_load(way, source).start())
        lax.fori_loop(i * each, jnp.minimum((i + 1) * each, units), fill, 0)
        each_way(s, settle)
        return carry

    lax.fori_loop(0, depth, step, 0)
    for which in range(2):
        wide_write(which, wide_count - 1).wait()
        for k in (wide_count - 2, wide_count - 1):
            wide_send(which, k).wait_send()
    for k in (tall_count - 2, tall_count - 1):
        tall_write(k).wait()
        tall_send(k).wait_send()

    def finish(source, carry):
        for offset in range(1, PLANE):
            for copy in rows_to(offset, source):
                copy.wait_send()

        @pl.when((source == level - 1) | (source == level + 1))
        def _():
            chain_out(source).wait_send()

        @pl.when(source != level)
        def _():
            prob_to(source).wait_send()
            prob_from(source).wait_recv()

        prob_ref[source] = prob_land[source]
        return carry

    lax.fori_loop(0, depth, finish, 0)


def give_back(rows, scalars, choose, shared_back, operands):
    depth, _, capacity, tokens = choose.shape
    width = rows.shape[-1]
    slots, inner = operands[1].shape
    wide_rows, tall_rows = 256 if depth <= PLANE else 128, 128
    wide_count = width // 2 // wide_rows
    tall_count = inner // tall_rows
    semaphores = pltpu.SemaphoreType.DMA
    low = rows.dtype
    wide = jnp.float32
    anywhere = pl.BlockSpec(memory_space=pl.ANY)
    local = pl.BlockSpec(memory_space=pltpu.VMEM)
    return pl.pallas_call(
        functools.partial(return_kernel, depth),
        out_shape=[
            jax.ShapeDtypeStruct((tokens, width), wide),
            jax.ShapeDtypeStruct((depth, 8, tokens), wide),
            jax.ShapeDtypeStruct((width // 2, inner), low),
            jax.ShapeDtypeStruct((width // 2, inner), low),
            jax.ShapeDtypeStruct((inner, width // 2), low),
        ],
        in_specs=[anywhere, anywhere, local, anywhere] + [anywhere] * 5,
        out_specs=[local, local, anywhere, anywhere, anywhere],
        scratch_shapes=[
            pltpu.VMEM((PLANE, depth, capacity, width), low),
            pltpu.VMEM((PLANE, depth, capacity, 128), wide),
            pltpu.VMEM((2, tokens, width), low),
            pltpu.VMEM((2, tokens, width), low),
            pltpu.VMEM((depth + 1, tokens, width), low),
            pltpu.VMEM((depth, 8, tokens), wide),
            pltpu.VMEM((depth, 8, tokens), wide),
        ]
        + [pltpu.VMEM(operand.shape, low) for operand in operands]
        + [
            pltpu.VMEM((2, 2, wide_rows, inner), low),
            pltpu.VMEM((2, tall_rows, width // 2), low),
            pltpu.VMEM((2, wide_count, wide_rows, inner), low),
            pltpu.VMEM((tall_count, tall_rows, width // 2), low),
            pltpu.VMEM((2, wide_rows, inner), low),
            pltpu.VMEM((2, tall_rows, width // 2), low),
            semaphores((2, depth)),
            semaphores((PLANE, depth)),
            semaphores((PLANE, depth)),
            semaphores((PLANE, depth)),
            semaphores((PLANE, depth)),
            semaphores((5,)),
            semaphores((2,)),
            semaphores((depth,)),
            semaphores((depth + 1,)),
            semaphores((depth,)),
            semaphores((depth,)),
            semaphores((2, 2)),
            semaphores((2, wide_count)),
            semaphores((2,)),
            semaphores((tall_count,)),
            semaphores((2,)),
            semaphores((2,)),
        ],
        compiler_params=pltpu.CompilerParams(
            collective_id=4, has_side_effects=True, vmem_limit_bytes=62 * MEBIBYTE
        ),
        cost_estimate=LONG,
    )(rows, scalars, choose, shared_back, *operands)


def reduce_kernel(depth, count, cut, *refs):
    parts = refs[:count]
    move_in, out_ref, move_out = refs[count : count + 3]
    acc, inc, one_a, one_b, two_a, two_b, zin = refs[count + 3 : count + 10]
    own_sem, cs, cr, ps, pr, qs, qr, zs, zr, move_sem, ms, mr = refs[count + 10 :]
    half = lax.axis_index("fsdp")
    place = lax.axis_index("expert")
    level = place // PLANE
    spot = place % PLANE
    total = depth * PLANE
    mates = plane_mates(place)
    rows = out_ref.shape[0]
    group = PLANE * rows
    width = out_ref.shape[1]
    greet_neighbours(half, place, depth)

    starts = [sum(part.shape[1] for part in parts[:k]) for k in range(count)]

    def rows_of(k, owner, t):
        start = pl.multiple_of((owner * total + t * PLANE) * rows, group)
        return parts[k].at[pl.ds(start, group), :]

    def kept(k, t):
        return pltpu.make_async_copy(
            rows_of(k, half, t),
            acc.at[t, :, pl.ds(starts[k], parts[k].shape[1])],
            own_sem.at[k, t],
        )

    def given(k, t):
        return remote(
            rows_of(k, 1 - half, t),
            inc.at[t, :, pl.ds(starts[k], parts[k].shape[1])],
            cs.at[k, t],
            cr.at[k, t],
            (1 - half, place),
        )

    def block(t, q, n, lo, hi):
        return acc.at[t, pl.ds(pl.multiple_of(q * rows, rows), n * rows), pl.ds(lo, hi - lo)]

    pair = spot - spot % 2

    def first(t, turn):
        low = spot % 2
        if turn == 0:
            source = block(t, 2 - pair, 2, 0, cut)
            target, where = one_a.at[t], mates[1]
        else:
            source = block(t, 2 * turn - 1 - low, 1, cut, width)
            target, where = one_b.at[t, turn - 1], mates[0]
        return remote(source, target, ps.at[turn, t], pr.at[turn, t], (half, where))

    def second(t, turn):
        if turn == 0:
            source = block(t, pair + 1 - spot % 2, 1, 0, cut)
            target, where = two_a.at[t], mates[0]
        else:
            source = block(t, (spot + 2) % PLANE, 1, cut, width)
            target, where = two_b.at[t], mates[1]
        return remote(source, target, qs.at[turn, t], qr.at[turn, t], (half, where))

    def line(t, way):
        step = 2 * way - 1
        return remote(
            block(t, spot, 1, 0, width),
            zin.at[way, t],
            zs.at[way, t],
            zr.at[way, t],
            (half, place + step * PLANE),
        )

    def add_rows(t, start, n, lo, hi, piece):
        def one(i, carry):
            r = pl.multiple_of(i * 16, 16)
            at = (t, pl.ds(pl.multiple_of(start + r, 16), 16), pl.ds(lo, hi - lo))
            new = piece(pl.ds(r, 16)).astype(jnp.float32)
            acc[at] = (acc[at].astype(jnp.float32) + new).astype(acc.dtype)
            return carry

        lax.fori_loop(0, n // 16, one, 0)

    def stage_a(t):
        for k in range(count):
            kept(k, t).wait()
            given(k, t).wait_recv()
        add_rows(t, 0, group, 0, width, lambda r: inc[t, r, :])
        for turn in range(3):
            first(t, turn).start()

    def stage_b(t):
        first(t, 0).wait_recv()
        add_rows(t, pair * rows, 2 * rows, 0, cut, lambda r: one_a[t, r, :])
        second(t, 0).start()
        for turn in range(2):
            first(t, 1 + turn).wait_recv()
            add_rows(
                t,
                (spot % 2 + 2 * turn) * rows,
                rows,
                cut,
                width,
                lambda r: one_b[t, turn, r, :],
            )
        second(t, 1).start()

    def stage_c(t):
        second(t, 0).wait_recv()
        add_rows(t, spot * rows, rows, 0, cut, lambda r: two_a[t, r, :])
        second(t, 1).wait_recv()
        add_rows(t, spot * rows, rows, cut, width, lambda r: two_b[t, r, :])

        def take(way):
            line(t, way).wait_recv()
            add_rows(t, spot * rows, rows, 0, width, lambda r: zin[way, t, r, :])

        @pl.when((t >= level) & (level > 0))
        def _():
            take(1)

        @pl.when((t <= level) & (level < depth - 1))
        def _():
            take(0)

        @pl.when(t > level)
        def _():
            line(t, 1).start()

        @pl.when(t < level)
        def _():
            line(t, 0).start()

    def visit(index, act):
        if index >= depth or index < 0:
            return
        step = depth - 1 - index
        if step == 0:
            act(level)
            return

        @pl.when(level + step < depth)
        def _():
            act(level + step)

        @pl.when(level - step >= 0)
        def _():
            act(level - step)

    def begin(t):
        for k in range(count):
            given(k, t).start()
            kept(k, t).start()

    for index in range(depth):
        visit(index, begin)
    move_start, move_finish = exchange_along(
        depth,
        half,
        place,
        move_in,
        lambda source: move_out.at[source],
        move_sem.at[0],
        ms,
        mr,
    )
    move_start()
    for index in range(depth + 2):
        visit(index, stage_a)
        visit(index - 1, stage_b)
        visit(index - 2, stage_c)

    def emit(i, carry):
        r = pl.multiple_of(i * 16, 16)
        at = pl.ds(pl.multiple_of(spot * rows + r, 16), 16)
        out_ref[pl.ds(r, 16), :] = acc[level, at, :].astype(out_ref.dtype)
        return carry
    lax.fori_loop(0, rows // 16, emit, 0)
    move_finish()

    def finish(t, carry):
        for k in range(count):
            given(k, t).wait_send()
        for turn in range(3):
            first(t, turn).wait_send()
        for turn in range(2):
            second(t, turn).wait_send()

        @pl.when(t > level)
        def _():
            line(t, 1).wait_send()

        @pl.when(t < level)
        def _():
            line(t, 0).wait_send()
        return carry

    lax.fori_loop(0, depth, finish, 0)


def reduce_rows(parts, moved, cut):
    total = lax.axis_size("expert")
    depth = total // PLANE
    rows = parts[0].shape[0] // (2 * total)
    width = sum(part.shape[1] for part in parts)
    group = PLANE * rows
    n = len(parts)
    semaphores = pltpu.SemaphoreType.DMA
    low = parts[0].dtype
    return pl.pallas_call(
        functools.partial(reduce_kernel, depth, n, cut),
        out_shape=[
            jax.ShapeDtypeStruct((rows, width), jnp.float32),
            jax.ShapeDtypeStruct(moved.shape, moved.dtype),
        ],
        in_specs=[pl.BlockSpec(memory_space=pl.ANY)] * (n + 1),
        out_specs=[
            pl.BlockSpec(memory_space=pltpu.VMEM),
            pl.BlockSpec(memory_space=pl.ANY),
        ],
        scratch_shapes=[
            pltpu.VMEM((depth, group, width), low),
            pltpu.VMEM((depth, group, width), low),
            pltpu.VMEM((depth, 2 * rows, cut), low),
            pltpu.VMEM((depth, 2, rows, width - cut), low),
            pltpu.VMEM((depth, rows, cut), low),
            pltpu.VMEM((depth, rows, width - cut), low),
            pltpu.VMEM((2, depth, rows, width), low),
            semaphores((n, depth)),
            semaphores((n, depth)),
            semaphores((n, depth)),
            semaphores((3, depth)),
            semaphores((3, depth)),
            semaphores((2, depth)),
            semaphores((2, depth)),
            semaphores((2, depth)),
            semaphores((2, depth)),
            semaphores((1,)),
            semaphores((depth,)),
            semaphores((depth,)),
        ],
        cost_estimate=LONG,
        compiler_params=pltpu.CompilerParams(
            collective_id=2, has_side_effects=True, vmem_limit_bytes=60 * MEBIBYTE
        ),
    )(*parts, moved)


def turned(values):
    width = values.shape[1]
    lanes = lax.broadcasted_iota(jnp.int32, values.shape, 1)
    return jnp.where(
        lanes % ROPE < ROPE // 2,
        pltpu.roll(values, width - ROPE // 2, 1),
        pltpu.roll(values, ROPE // 2, 1),
    )


def row_scale(values):
    return lax.rsqrt(jnp.mean(values * values, axis=-1, keepdims=True) + EPSILON)


def head_lanes(values, head):
    lanes = lax.broadcasted_iota(jnp.int32, values.shape, 1)
    return jnp.where(lanes // ROPE == head % 2, values, jnp.zeros_like(values))


def lanes_at(start, size):
    return pl.ds(pl.multiple_of(start, 128), size)


def attend_kernel(layout, *refs):
    x_ref, packed, up_in, first_gain, latent_gain, feed_gain, cosine, sine, mask = refs[:9]
    choose_ref, grad_in = refs[9:11]
    normed, residual, mixed, queries, latent, compressed = refs[11:17]
    expanded, keys_rope, log_total, heads, grad_out = refs[17:22]
    entry, ups, outs, prior_latent, prior_rope, grads, grad_placed = refs[22:29]
    load_sem, up_sem, send_sem, receive_sem, gl, gs, gr, grad_sem = refs[29:]
    entry_width, out_start = layout
    half = lax.axis_index("fsdp")
    place = lax.axis_index("expert")
    other = (1 - half, place)
    rows, width = x_ref.shape
    low = x_ref.dtype
    scale = (NOPE + ROPE) ** (-0.5)
    loads = [
        pltpu.make_async_copy(packed.at[:, pl.ds(0, entry_width)], entry, load_sem.at[0]),
        pltpu.make_async_copy(packed.at[:, pl.ds(out_start, width)], outs, load_sem.at[1]),
    ]
    up_loads = load_ups(up_in, ups, up_sem, layout)
    depth = grad_in.shape[0]

    def grad_load(n):
        return pltpu.make_async_copy(grad_in.at[2 * n], grads.at[n], gl.at[n])

    grad_start, grad_finish = exchange_plane(
        half,
        place,
        lambda mate, source: grad_placed.at[source // 2, mate],
        lambda mate, source: grad_out.at[source, mate],
        grad_sem,
        gs,
        gr,
    )

    def each_grad(act):
        def one(n, carry):
            act(n)
            return carry

        lax.fori_loop(0, depth // 2, one, 0)

    def give_grad(n):
        grad_load(n).wait()
        place_rows(choose_ref, 2 * n, grads.at[n], grad_placed.at[n])
        grad_start(2 * n)

    each_grad(lambda n: grad_load(n).start())
    for load in loads[:1] + up_loads + loads[1:]:
        load.start()
    greet([other] + plane_others(half, place))
    each_grad(give_grad)
    x = x_ref[...].astype(jnp.float32)
    normed[...] = (x * row_scale(x) * first_gain[...]).astype(low)
    loads[0].wait()
    nope_width = HEADS * NOPE
    query_width = HEADS * (NOPE + ROPE)

    def through(start, size):
        return jnp.dot(
            normed[...], entry[:, lanes_at(start, size)], preferred_element_type=jnp.float32
        )

    def rotary(values):
        return values * cosine[...] + turned(values) * sine[...]

    squeezed = through(query_width, LATENT)
    compressed[...] = squeezed
    latent[...] = (squeezed * row_scale(squeezed) * latent_gain[...]).astype(low)
    key = rotary(through(query_width + LATENT, 128))
    keys_rope[pl.ds(rows, rows), :] = (key + pltpu.roll(key, ROPE, 1)).astype(low)
    sends = [
        remote(latent, prior_latent, send_sem.at[0], receive_sem.at[0], other),
        remote(
            keys_rope.at[pl.ds(rows, rows), :],
            prior_rope,
            send_sem.at[1],
            receive_sem.at[1],
            other,
        ),
    ]

    @pl.when(half == 0)
    def _():
        for send in sends:
            send.start()

    def nope_part(n, carry):
        queries[:, lanes_at(n * 1024, 1024)] = through(n * 1024, 1024).astype(low)
        return carry

    lax.fori_loop(0, nope_width // 1024, nope_part, 0)

    def rope_part(n, carry):
        values = through(nope_width + n * 512, 512)
        for k in range(4):
            tile = rotary(values[:, k * 128 : (k + 1) * 128])
            queries[:, lanes_at(nope_width + n * 512 + k * 128, 128)] = tile.astype(low)
        return carry

    lax.fori_loop(0, HEADS * ROPE // 512, rope_part, 0)
    for load in up_loads:
        load.wait()
    quarters, span = ups.shape[0], ups.shape[-1]

    def expand(source, first):
        def one(n, carry):
            expanded[pl.ds(first, rows), lanes_at(n * span, span)] = jnp.dot(
                source[...], whole(ups[n]), preferred_element_type=jnp.float32
            ).astype(low)
            return carry

        lax.fori_loop(0, quarters, one, 0)

    expand(latent, rows)

    @pl.when(half == 0)
    def _():
        expanded[pl.ds(0, rows), :] = jnp.zeros((rows, quarters * span), low)
        keys_rope[pl.ds(0, rows), :] = jnp.zeros((rows, 128), low)
        for send in sends:
            send.wait_send()

    @pl.when(half == 1)
    def _():
        for send in sends:
            send.wait_recv()
        keys_rope[pl.ds(0, rows), :] = prior_rope[...]
        expand(prior_latent, 0)

    def head(h, totals):
        pair = queries[:, lanes_at(nope_width + (h // 2) * 128, 128)]
        scores = dot_nt(
            queries[:, lanes_at(h * NOPE, NOPE)], expanded[:, lanes_at(h * 256, NOPE)]
        )
        scores = scores + dot_nt(head_lanes(pair, h), keys_rope[...])
        scores = jnp.where(mask[...] > 0, scores * scale, FLOOR_SCORE)
        top = jnp.max(scores, axis=-1, keepdims=True)
        weights = jnp.exp(scores - top)
        total = jnp.sum(weights, axis=-1, keepdims=True)
        heads[:, lanes_at(h * VALUE, VALUE)] = jnp.dot(
            (weights / total).astype(low),
            expanded[:, lanes_at(h * 256 + NOPE, VALUE)],
            preferred_element_type=jnp.float32,
        ).astype(low)
        lanes = lax.broadcasted_iota(jnp.int32, totals.shape, 1)
        return jnp.where(lanes == h, top + jnp.log(total), totals)

    log_total[...] = lax.fori_loop(0, HEADS, head, jnp.zeros((rows, 128), jnp.float32))
    loads[1].wait()

    def project(n, carry):
        at = lanes_at(n * 1024, 1024)
        residual[:, at] = x_ref[:, at].astype(jnp.float32) + jnp.dot(
            heads[...], outs[:, at], preferred_element_type=jnp.float32
        )
        return carry

    lax.fori_loop(0, width // 1024, project, 0)
    total = residual[...]
    mixed[...] = (total * row_scale(total) * feed_gain[...]).astype(low)
    each_grad(lambda n: grad_finish(2 * n))


def attend(x, packed, ups, ups_shape, gains, tables, mask, choose, grad_line, layout):
    rows, width = x.shape
    low, wide = x.dtype, jnp.float32
    semaphores = pltpu.SemaphoreType.DMA
    anywhere = pl.BlockSpec(memory_space=pl.ANY)
    local = pl.BlockSpec(memory_space=pltpu.VMEM)
    expanded_width = HEADS * (NOPE + VALUE)
    depth, _, capacity, _ = choose.shape
    shapes = [
        ((rows, width), low),
        ((rows, width), wide),
        ((rows, width), low),
        ((rows, HEADS * (NOPE + ROPE)), low),
        ((rows, LATENT), low),
        ((rows, LATENT), wide),
        ((2 * rows, expanded_width), low),
        ((2 * rows, 128), low),
        ((rows, 128), wide),
        ((rows, HEADS * VALUE), low),
        ((depth, PLANE, capacity, width), low),
    ]
    return pl.pallas_call(
        functools.partial(attend_kernel, layout),
        out_shape=[jax.ShapeDtypeStruct(shape, dtype) for shape, dtype in shapes],
        in_specs=[local, anywhere, anywhere] + [local] * 7 + [anywhere],
        out_specs=[local] * (len(shapes) - 1) + [anywhere],
        scratch_shapes=[
            pltpu.VMEM((packed.shape[0], layout[0]), low),
            pltpu.VMEM(ups_shape, low),
            pltpu.VMEM((packed.shape[0], width), low),
            pltpu.VMEM((rows, LATENT), low),
            pltpu.VMEM((rows, 128), low),
            pltpu.VMEM((depth // 2, rows, width), low),
            pltpu.VMEM((depth // 2, PLANE, capacity, width), low),
            semaphores((2,)),
            semaphores((ups_shape[0],)),
            semaphores((2,)),
            semaphores((2,)),
            semaphores((depth // 2,)),
            semaphores((PLANE, depth)),
            semaphores((PLANE, depth)),
            semaphores((depth,)),
        ],
        compiler_params=pltpu.CompilerParams(
            collective_id=5, has_side_effects=True, vmem_limit_bytes=56 * MEBIBYTE
        ),
        cost_estimate=MIDDLE,
    )(x, packed, ups, *gains, *tables, mask, choose, grad_line)


def load_ups(up_in, ups, sem, layout):
    if up_in.shape == ups.shape:
        return [pltpu.make_async_copy(up_in, ups, sem.at[0])]
    span = ups.shape[-1]
    return [
        pltpu.make_async_copy(
            up_in.at[:, k, :, pl.ds(layout[0], span)], ups.at[k], sem.at[k]
        )
        for k in range(ups.shape[0])
    ]


def whole(block):
    return block.reshape(-1, block.shape[-1])


def attend_back_kernel(layout, count, *refs):
    back_in, packed, up_in, queries, expanded, keys_rope, log_total = refs[:7]
    latent, compressed, normed, heads, x_ref, residual, cotangent = refs[7:14]
    d_logits, router, latent_gain, first_gain, feed_gain, cosine, sine, mask = refs[14:22]
    rows_in = refs[22]
    refs = refs[24 + count :]
    token_grad, up_grad, gain_grad, first_grad, feed_grad, entry_grad, out_grad = refs[:7]
    rows_out, outs, ups, d_heads, own, prior, came, prior_rope, came_rope = refs[7:16]
    entry, entry_low, up_tile, entry_tile, out_tile, d_ref = refs[16:22]
    load_sem, up_sem, send_sem, receive_sem, write_sem, es, er = refs[22:]
    entry_width, out_start = layout
    half = lax.axis_index("fsdp")
    place = lax.axis_index("expert")
    other = (1 - half, place)
    rows, width = d_ref.shape
    low = d_ref.dtype
    wide = jnp.float32
    scale = (NOPE + ROPE) ** (-0.5)

    def norm_back(values, gain, incoming):
        root = row_scale(values)
        scaled = gain * incoming
        inner = jnp.mean(values * scaled, axis=-1, keepdims=True)
        gain_sum = jnp.sum(incoming * values * root, axis=0, keepdims=True)
        return root * scaled - values * (root * root * root) * inner, gain_sum

    nope_width = HEADS * NOPE
    query_width = HEADS * (NOPE + ROPE)
    loads = [
        pltpu.make_async_copy(packed.at[:, pl.ds(out_start, width)], outs, load_sem.at[0]),
        pltpu.make_async_copy(packed.at[:, pl.ds(0, entry_width)], entry, load_sem.at[1]),
    ]
    up_loads = load_ups(up_in, ups, up_sem, layout)
    for load in loads + up_loads:
        load.start()
    greet([other] + plane_others(half, place))
    rows_start, rows_finish = exchange_plane(
        half,
        place,
        lambda mate, level: rows_in.at[level, mate],
        lambda mate, level: rows_out.at[level, mate],
        None,
        es,
        er,
        own_there=True,
    )

    def each_level(act):
        def one(level, carry):
            act(level)
            return carry

        lax.fori_loop(0, rows_in.shape[0], one, 0)

    each_level(rows_start)
    mixed_grad = back_in[...] + dot_nt(d_logits[...], router[...])
    through_norm, gain_sum = norm_back(residual[...], feed_gain[...], mixed_grad)
    feed_grad[...] = jnp.broadcast_to(gain_sum, feed_grad.shape)
    token_grad[...] = cotangent[...].astype(wide) + through_norm
    d_ref[...] = token_grad[...].astype(low)

    def write(kind, k):
        staged, target = ((out_tile, out_grad), (entry_tile, entry_grad), (up_tile, up_grad))[kind]
        size = staged.shape[1]
        if kind == 2:
            place_at = up_grad.at[k] if up_grad.shape[0] == ups.shape[0] else up_grad.at[:, k]
        else:
            place_at = target.at[pl.ds(pl.multiple_of(k * size, size), size), :]
        return pltpu.make_async_copy(
            staged.at[k % 2], place_at, write_sem.at[kind, k % 2]
        )

    def put(kind, k, value):
        staged = (out_tile, entry_tile, up_tile)[kind]

        @pl.when(k >= 2)
        def _():
            write(kind, k - 2).wait()

        staged[k % 2] = value.astype(low).reshape(staged.shape[1:])
        write(kind, k).start()

    def settle(kind, total):
        for k in range(max(0, total - 2), total):
            write(kind, k).wait()

    def out_part(k, carry):
        size = out_tile.shape[1]
        put(0, k, dot_tn(heads[:, lanes_at(k * size, size)], d_ref[...]))
        return carry

    out_count = heads.shape[1] // out_tile.shape[1]
    lax.fori_loop(0, out_count, out_part, 0)
    loads[0].wait()

    def head_part(n, carry):
        at = lanes_at(n * 1024, 1024)
        d_heads[:, at] = dot_nt(d_ref[...], outs[at, :]).astype(low)
        return carry

    lax.fori_loop(0, width // 1024, head_part, 0)

    def turn_back(values):
        return values * cosine[...] - turned(values) * sine[...]

    def pair_of_heads(n, rope_sum):
        pair = queries[:, lanes_at(nope_width + n * 128, 128)]
        query_rope = jnp.zeros((rows, 128), wide)
        for k in range(2):
            h = 2 * n + k
            query = queries[:, lanes_at(h * NOPE, NOPE)]
            key = expanded[:, lanes_at(h * 256, NOPE)]
            value = expanded[:, lanes_at(h * 256 + NOPE, VALUE)]
            d_head = d_heads[:, lanes_at(h * VALUE, VALUE)]
            own_pair = head_lanes(pair, k)
            scores = dot_nt(query, key) + dot_nt(own_pair, keys_rope[...])
            scores = jnp.where(mask[...] > 0, scores * scale, FLOOR_SCORE)
            lanes = lax.broadcasted_iota(jnp.int32, log_total.shape, 1)
            log_sum = jnp.sum(
                jnp.where(lanes == h, log_total[...], 0.0), axis=-1, keepdims=True
            )
            probs = jnp.exp(scores - log_sum)
            d_probs = dot_nt(d_head, value)
            delta = jnp.sum(probs * d_probs, axis=-1, keepdims=True)
            d_scores = (probs * (d_probs - delta)).astype(low)
            entry_low[:, lanes_at(h * NOPE, NOPE)] = (
                jnp.dot(d_scores, key, preferred_element_type=wide) * scale
            ).astype(low)
            query_rope = query_rope + head_lanes(
                jnp.dot(d_scores, keys_rope[...], preferred_element_type=wide), k
            )
            d_key = dot_tn(d_scores, query) * scale
            d_value = dot_tn(probs.astype(low), d_head)
            own[:, lanes_at(h * 256, NOPE)] = d_key[rows:]
            own[:, lanes_at(h * 256 + NOPE, VALUE)] = d_value[rows:]
            prior[:, lanes_at(h * 256, NOPE)] = d_key[:rows].astype(low)
            prior[:, lanes_at(h * 256 + NOPE, VALUE)] = d_value[:rows].astype(low)
            rope_sum = rope_sum + dot_tn(d_scores, own_pair)
        entry_low[:, lanes_at(nope_width + n * 128, 128)] = (
            turn_back(query_rope) * scale
        ).astype(low)
        return rope_sum

    rope_sum = lax.fori_loop(
        0, HEADS // 2, pair_of_heads, jnp.zeros((2 * rows, 128), wide)
    )
    rope_sum = (rope_sum + pltpu.roll(rope_sum, ROPE, 1)) * scale
    prior_rope[...] = rope_sum[:rows].astype(low)
    sends = [
        remote(prior, came, send_sem.at[0], receive_sem.at[0], other),
        remote(prior_rope, came_rope, send_sem.at[1], receive_sem.at[1], other),
    ]

    @pl.when(half == 1)
    def _():
        for send in sends:
            send.start()
        came_rope[...] = jnp.zeros((rows, 128), low)
        for send in sends:
            send.wait_send()
        prior[...] = own[...].astype(low)

    @pl.when(half == 0)
    def _():
        for send in sends:
            send.wait_recv()
        prior[...] = (own[...] + came[...].astype(wide)).astype(low)

    for load in up_loads:
        load.wait()
    quarters, span = ups.shape[0], ups.shape[-1]

    def spread(n, d_latent):
        part = prior[:, lanes_at(n * span, span)]
        put(2, n, dot_tn(latent[...], part))
        return d_latent + dot_nt(part, whole(ups[n]))

    d_latent = lax.fori_loop(0, quarters, spread, jnp.zeros((rows, LATENT), wide))
    d_squeezed, gain_sum = norm_back(compressed[...], latent_gain[...], d_latent)
    gain_grad[...] = jnp.broadcast_to(gain_sum, gain_grad.shape)
    entry_low[:, lanes_at(query_width, LATENT)] = d_squeezed.astype(low)
    key = rope_sum[rows:] + came_rope[...].astype(wide)
    entry_low[:, lanes_at(query_width + LATENT, 128)] = turn_back(head_lanes(key, 0)).astype(low)

    def entry_part(k, carry):
        size = entry_tile.shape[1]
        put(1, k, dot_tn(normed[:, lanes_at(k * size, size)], entry_low[...]))
        return carry

    entry_count = width // entry_tile.shape[1]
    lax.fori_loop(0, entry_count, entry_part, 0)
    loads[1].wait()

    def normed_part(n, carry):
        at = lanes_at(n * 1024, 1024)
        own[:, at] = dot_nt(entry_low[...], entry[at, :])
        return carry

    lax.fori_loop(0, width // 1024, normed_part, 0)
    through_norm, gain_sum = norm_back(
        x_ref[...].astype(wide), first_gain[...], own[:, pl.ds(0, width)]
    )
    first_grad[...] = jnp.broadcast_to(gain_sum, first_grad.shape)
    token_grad[...] += through_norm
    settle(0, out_count)
    settle(1, entry_count)
    settle(2, quarters)
    each_level(rows_finish)


def attend_back(
    back, packed, ups, ups_shape, kept, gains, tables, mask, returning, before, layout
):
    rows, width = back.shape
    low, wide = packed.dtype, jnp.float32
    semaphores = pltpu.SemaphoreType.DMA
    anywhere = pl.BlockSpec(memory_space=pl.ANY)
    local = pl.BlockSpec(memory_space=pltpu.VMEM)
    expanded_width = HEADS * (NOPE + VALUE)
    quarters, blocks, part, span = ups_shape
    up_grad = (blocks, quarters, part, span) if blocks > 1 else ups_shape
    return pl.pallas_call(
        functools.partial(attend_back_kernel, layout, len(before)),
        out_shape=[
            jax.ShapeDtypeStruct((rows, width), wide),
            jax.ShapeDtypeStruct(up_grad, low),
            jax.ShapeDtypeStruct((8, LATENT), wide),
            jax.ShapeDtypeStruct((8, width), wide),
            jax.ShapeDtypeStruct((8, width), wide),
            jax.ShapeDtypeStruct((width, layout[0]), low),
            jax.ShapeDtypeStruct((HEADS * VALUE, width), low),
            jax.ShapeDtypeStruct(returning[0].shape, low),
        ],
        in_specs=[local, anywhere, anywhere]
        + [local] * (len(kept) + len(gains) + len(tables) + 1)
        + [anywhere] * (2 + len(before)),
        out_specs=[local, anywhere] + [local] * 3 + [anywhere] * 3,
        input_output_aliases={23: 7},
        scratch_shapes=[
            pltpu.VMEM((packed.shape[0], width), low),
            pltpu.VMEM(ups_shape, low),
            pltpu.VMEM((rows, HEADS * VALUE), low),
            pltpu.VMEM((rows, expanded_width), wide),
            pltpu.VMEM((rows, expanded_width), low),
            pltpu.VMEM((rows, expanded_width), low),
            pltpu.VMEM((rows, 128), low),
            pltpu.VMEM((rows, 128), low),
            pltpu.VMEM((packed.shape[0], layout[0]), low),
            pltpu.VMEM((rows, layout[0]), low),
            pltpu.VMEM((2,) + ups_shape[1:], low),
            pltpu.VMEM((2, 128, layout[0]), low),
            pltpu.VMEM((2, 128, width), low),
            pltpu.VMEM((rows, width), low),
            semaphores((2,)),
            semaphores((quarters,)),
            semaphores((2,)),
            semaphores((2,)),
            semaphores((3, 2)),
            semaphores((PLANE, returning[0].shape[0])),
            semaphores((PLANE, returning[0].shape[0])),
        ],
        compiler_params=pltpu.CompilerParams(
            collective_id=6, has_side_effects=True, vmem_limit_bytes=62 * MEBIBYTE
        ),
        cost_estimate=LONG,
    )(back, packed, ups, *kept, *gains, *tables, mask, *returning, *before)


def run_and_return_kernel(depth, total, *refs):
    x_in, grad_in, gate_in, up_in, down_in, router_ref, choose_ref, shared_in = refs[:8]
    back_ref, prob_ref, gate_out, up_out, down_out, y_out, y_own = refs[8:15]
    came, scalars, shared, onward, incoming, prob_send, prob_land = refs[15:22]
    x_held, gate_held, up_held, hidden_held, grad_held, hidden = refs[22:28]
    gates, ups, downs, sent, scalars_sent, y_stage = refs[28:34]
    es, er, ss, sr, load_sem, shared_sem, cs, cr, ps, pr = refs[34:44]
    ws, wr, ts, tr, wide_sem, tall_sem, y_sem, free_sem = refs[44:]
    half = lax.axis_index("fsdp")
    place = lax.axis_index("expert")
    level = place // PLANE
    spot = place % PLANE
    other = (1 - half, place)
    tokens, width = back_ref.shape
    capacity = choose_ref.shape[2]
    inner = gates.shape[1]
    wide_rows, tall_rows, tall_width = 256, 128, width // 2
    wide_count, tall_count = width // 2 // wide_rows, inner // tall_rows
    wide = jnp.float32

    def take_wide(which, k):
        at = pl.multiple_of((which * wide_count + k) * wide_rows, wide_rows)
        return gates.at[pl.ds(at, wide_rows), :]

    def take_tall(k):
        at = pl.multiple_of(k * tall_rows, tall_rows)
        return ups.at[pl.ds(at, tall_rows), pl.ds(0, tall_width)]

    def give_wide(slot, which):
        at = pl.multiple_of((slot * 2 + which) * wide_rows, wide_rows)
        return downs.at[pl.ds(at, wide_rows), pl.ds(0, inner)]

    def give_tall(slot):
        at = pl.multiple_of(4 * wide_rows + slot * tall_rows, tall_rows)
        return downs.at[pl.ds(at, tall_rows), pl.ds(0, tall_width)]

    def done_wide(which):
        return ups.at[pl.ds(tall_count * tall_rows + which * wide_rows, wide_rows), :]

    def done_tall(slot):
        at = pl.multiple_of(slot * tall_width, tall_width)
        return downs.at[pl.ds(4 * wide_rows + 2 * tall_rows, tall_rows), pl.ds(at, tall_width)]

    greet(line_others(half, place, depth) + plane_others(half, place) + [other])

    def rows_to(offset, way, source):
        mate = (spot + offset) % PLANE
        where = (half, place - spot + mate)
        return (
            remote(
                sent.at[way, mate],
                came.at[spot, source],
                es.at[offset, source],
                er.at[offset, source],
                where,
            ),
            remote(
                scalars_sent.at[way, mate],
                scalars.at[spot, source],
                ss.at[offset, source],
                sr.at[offset, source],
                where,
            ),
        )

    def rows_from(offset, source):
        mate = (spot + PLANE - offset) % PLANE
        where = (half, place - spot + mate)
        block, small = came.at[mate, source], scalars.at[mate, source]
        return (
            remote(block, block, es.at[offset, source], er.at[offset, source], where),
            remote(small, small, ss.at[offset, source], sr.at[offset, source], where),
        )

    def shared_load(slot, source):
        return pltpu.make_async_copy(shared_in.at[source], shared.at[slot], shared_sem.at[slot])

    def each_way(s, act):
        def one(way, carry):
            source = level + (2 * way - 1) * s

            @pl.when((source >= 0) & (source < depth) & ((s > 0) | (way == 0)))
            def _():
                act(way, source)

            return carry

        lax.fori_loop(0, 2, one, 0)

    loads = [
        pltpu.make_async_copy(source, target, load_sem.at[k])
        for k, (source, target) in enumerate(
            (
                (x_in, x_held),
                (gate_in, gates),
                (up_in, ups),
                (grad_in, grad_held),
                (down_in, downs),
            )
        )
    ]
    for load in loads:
        load.start()
    earliest = jnp.where(2 * level >= depth - 1, 0, depth - 1)

    def slot_of(way, source):
        return way + 2 * ((source + level) % 2)

    def compute(way, source):
        def need(*which):
            @pl.when(source == earliest)
            def _():
                for k in which:
                    loads[k].wait()

        need(0)
        slot = slot_of(way, source)
        x = x_held.at[source]
        logits = jnp.dot(x[...], router_ref[...], preferred_element_type=wide)
        lanes = lax.broadcasted_iota(jnp.int32, logits.shape, 1)
        logits = jnp.where(lanes < total, logits, FLOOR_SCORE)
        powers = jnp.exp(logits - jnp.max(logits, axis=-1, keepdims=True))
        probs = powers / jnp.sum(powers, axis=-1, keepdims=True)
        gate = jnp.sum(jnp.where(lanes == place, probs, 0.0), axis=-1, keepdims=True)

        def columns(start, size, slots):
            at = lanes_at(start, size)
            if start == 0:
                need(1)
            former_part = jnp.dot(x[...], gates[:, at], preferred_element_type=wide)
            if start == 0:
                need(2)
            latter_part = jnp.dot(x[...], ups[:, at], preferred_element_type=wide)
            if start == 0:
                need(3, 4)
            raw = dot_nt(grad_held[source], downs[at, :])
            sig = 1.0 / (1.0 + jnp.exp(-former_part))
            act = former_part * sig
            low = (act * latter_part).astype(hidden.dtype)
            hidden[:, at] = low
            low = low.astype(wide)
            hidden_held[source, :, at] = (low * gate).astype(hidden.dtype)
            grad = raw * gate
            d_gate = grad * latter_part * (sig + act * (1.0 - sig))
            gate_held[source, :, at] = d_gate.astype(hidden.dtype)
            up_held[source, :, at] = (grad * act).astype(hidden.dtype)
            return slots + jnp.sum(low * raw, axis=-1, keepdims=True)

        slots = jnp.zeros((PLANE * capacity, 1), wide)
        step_size = 640
        for start in range(0, inner, step_size):
            slots = columns(start, min(step_size, inner - start), slots)

        def blocks(value):
            return [value[m * capacity : (m + 1) * capacity] for m in range(PLANE)]

        former = source + 2 * (2 * way - 1)

        @pl.when((former >= 0) & (former < depth))
        def _():
            for offset in range(1, PLANE):
                for copy in rows_to(offset, slot, former):
                    copy.wait_send()

        for m, block in enumerate(blocks(slots)):
            spread = jnp.broadcast_to(block, (capacity, 128))
            scalars_sent[slot, m] = spread

            @pl.when(spot == m)
            def _():
                scalars[m, source] = spread

        def outward(n, carry):
            at = lanes_at(n * 1024, 1024)
            back = dot_nt(gate_held[source], gates[at, :]) + dot_nt(up_held[source], ups[at, :])
            for m, block in enumerate(blocks(back)):
                sent[slot, m, :, at] = block.astype(sent.dtype)

                @pl.when(spot == m)
                def _():
                    came[m, source, :, at] = block.astype(came.dtype)

            return carry

        lax.fori_loop(0, width // 1024, outward, 0)
        for offset in range(1, PLANE):
            for copy in rows_to(offset, slot, source):
                copy.start()

        def finally_out(n, carry):
            at = lanes_at(n * 1024, 1024)
            out = jnp.dot(hidden[...], downs[:, at], preferred_element_type=wide) * gate
            for m, block in enumerate(blocks(out)):
                y_stage[m, :, at] = block.astype(y_stage.dtype)
            return carry

        lax.fori_loop(0, width // 1024, finally_out, 0)
        writes = [
            pltpu.make_async_copy(y_stage, y_out.at[source], y_sem.at[0]),
            pltpu.make_async_copy(y_stage.at[spot], y_own.at[source, spot], y_sem.at[1]),
        ]
        for write in writes:
            write.start()
        for write in writes:
            write.wait()

    def wide_tiles(owner, k):
        at = pl.ds(pl.multiple_of((owner * wide_count + k) * wide_rows, wide_rows), wide_rows)
        x = whole(x_held[:, :, at])
        return dot_tn(x, whole(gate_held[...])), dot_tn(x, whole(up_held[...]))

    def tall_tile(owner, k):
        at = pl.ds(pl.multiple_of(k * tall_rows, tall_rows), tall_rows)
        over = pl.ds(pl.multiple_of(owner * tall_width, tall_width), tall_width)
        return dot_tn(whole(hidden_held[:, :, at]), whole(grad_held[:, :, over]))

    def wide_send(which, k):
        slot = k % 2
        return remote(
            give_wide(slot, which),
            take_wide(which, k),
            ws.at[slot, which],
            wr.at[which, k],
            other,
        )

    def tall_send(k):
        slot = k % 2
        return remote(give_tall(slot), take_tall(k), ts.at[slot], tr.at[k], other)

    def wide_write(which, k):
        target = (gate_out, up_out)[which]
        at = pl.ds(pl.multiple_of(k * wide_rows, wide_rows), wide_rows)
        return pltpu.make_async_copy(done_wide(which), target.at[at, :], wide_sem.at[which])

    def tall_write(k):
        slot = k % 2
        at = pl.ds(pl.multiple_of(k * tall_rows, tall_rows), tall_rows)
        return pltpu.make_async_copy(done_tall(slot), down_out.at[at, :], tall_sem.at[slot])

    def give_wide_tile(k):
        @pl.when(k >= 2)
        def _():
            for which in range(2):
                wide_send(which, k - 2).wait_send()

        for which, tile in enumerate(wide_tiles(1 - half, k)):
            give_wide(k % 2, which)[...] = tile.astype(gates.dtype)
            wide_send(which, k).start()

    def give_tall_tile(k):
        @pl.when(k >= 2)
        def _():
            tall_send(k - 2).wait_send()

        give_tall(k % 2)[...] = tall_tile(1 - half, k).astype(gates.dtype)
        tall_send(k).start()

    def keep_wide_tile(k):
        @pl.when(k >= 1)
        def _():
            for which in range(2):
                wide_write(which, k - 1).wait()

        for which, tile in enumerate(wide_tiles(half, k)):
            wide_send(which, k).wait_recv()
            tile = tile + take_wide(which, k)[...].astype(wide)
            done_wide(which)[...] = tile.astype(gates.dtype)
            wide_write(which, k).start()

    def keep_tall_tile(k):
        @pl.when(k >= 2)
        def _():
            tall_write(k - 2).wait()

        tile = tall_tile(half, k)
        tall_send(k).wait_recv()
        tile = tile + take_tall(k)[...].astype(wide)
        done_tall(k % 2)[...] = tile.astype(gates.dtype)
        tall_write(k).start()

    units = 2 * (wide_count + tall_count)
    bounds = (0, wide_count, wide_count + tall_count, units - tall_count, units)
    acts = (give_wide_tile, give_tall_tile, keep_wide_tile, keep_tall_tile)

    def fill(unit, carry):
        for act, low, high in zip(acts, bounds[:-1], bounds[1:]):

            @pl.when((unit >= low) & (unit < high))
            def _():
                act(unit - low)

        return carry

    def chain_out(source):
        up = jnp.where(source > level, 1, 0)
        step = 2 * up - 1
        slot = jnp.where(source == level - 1, depth, source)
        return remote(
            onward.at[up],
            incoming.at[slot],
            cs.at[source],
            cr.at[slot],
            (half, place + step * PLANE),
        )

    def chain_in(slot):
        block = incoming.at[slot]
        return remote(block, block, cs.at[0], cr.at[slot], (half, place))

    def prob_to(source):
        return remote(
            prob_send.at[source],
            prob_land.at[level],
            ps.at[source],
            pr.at[level],
            (half, source * PLANE + spot),
        )

    def prob_from(source):
        block = prob_land.at[source]
        return remote(block, block, ps.at[source], pr.at[source], (half, source * PLANE + spot))

    def add_incoming(slot):
        chain_in(slot).wait_recv()
        back_ref[...] += incoming[slot].astype(jnp.float32)

    def settle(way, source):
        load = shared_load(0, source)
        load.start()
        for offset in range(1, PLANE):
            for copy in rows_from(offset, source):
                copy.wait_recv()
        load.wait()

        def columns(n, carry):
            at = pl.ds(pl.multiple_of(n * 512, 512), 512)
            total = shared[0, :, at].astype(jnp.float32)
            for mate in range(PLANE):
                total = total + dot_tn(choose_ref[source, mate], came[mate, source, :, at])
            back_ref[:, at] = total
            return carry

        lax.fori_loop(0, width // 512, columns, 0)
        lines = lax.broadcasted_iota(jnp.int32, (8, tokens), 0)
        probs = jnp.zeros((8, tokens), jnp.float32)
        for mate in range(PLANE):
            part = lax.dot_general(
                scalars[mate, source],
                choose_ref[source, mate].astype(jnp.float32),
                (((0,), (0,)), ((), ())),
                preferred_element_type=jnp.float32,
                precision=lax.Precision.HIGHEST,
            )
            probs = jnp.where(lines == mate, part[:8], probs)

        @pl.when((source >= level) & (level > 0))
        def _():
            add_incoming(source)

        @pl.when((source < level) & (level < depth - 1))
        def _():
            add_incoming(source)

        @pl.when((source == level) & (level < depth - 1))
        def _():
            add_incoming(depth)

        @pl.when(source == level)
        def _():
            prob_land[level] = probs

        @pl.when(source != level)
        def _():
            prob_send[source] = probs
            prob_to(source).start()
            former = source + 2 * way - 1

            @pl.when((former >= 0) & (former < depth))
            def _():
                chain_out(former).wait_send()

            onward[way] = back_ref[...].astype(onward.dtype)
            chain_out(source).start()

    def step(i, carry):
        s = depth - 1 - i
        each_way(s, compute)

        @pl.when(i > 0)
        def _():
            each_way(s + 1, settle)

        return carry

    lax.fori_loop(0, depth, step, 0)
    pl.semaphore_signal(free_sem, inc=1, device_id=other, device_id_type=MESH)
    pl.semaphore_wait(free_sem, 1)
    lax.fori_loop(0, units // 2, fill, 0)
    each_way(0, settle)
    lax.fori_loop(units // 2, units, fill, 0)
    for which in range(2):
        wide_write(which, wide_count - 1).wait()
        for k in (wide_count - 2, wide_count - 1):
            wide_send(which, k).wait_send()
    for k in (tall_count - 2, tall_count - 1):
        tall_write(k).wait()
        tall_send(k).wait_send()

    def finish(source, carry):
        ahead = jnp.where(source > level, 1, 0)
        near = (source >= level - 1) & (source <= level + 2)

        @pl.when(near)
        def _():
            for offset in range(1, PLANE):
                for copy in rows_to(offset, slot_of(ahead, source), source):
                    copy.wait_send()

        @pl.when((source == level - 1) | (source == level + 1))
        def _():
            chain_out(source).wait_send()

        @pl.when(source != level)
        def _():
            prob_to(source).wait_send()
            prob_from(source).wait_recv()

        prob_ref[source] = prob_land[source]
        return carry

    lax.fori_loop(0, depth, finish, 0)


def run_and_return(rows, grads, weights, router, choose, shared_back, total):
    depth, _, capacity, width = rows.shape
    tokens = choose.shape[3]
    inner = weights[0].shape[1]
    tile = PLANE * capacity
    wide_count, tall_count = width // 512, inner // 128
    semaphores = pltpu.SemaphoreType.DMA
    low, wide = rows.dtype, jnp.float32
    anywhere = pl.BlockSpec(memory_space=pl.ANY)
    local = pl.BlockSpec(memory_space=pltpu.VMEM)
    return pl.pallas_call(
        functools.partial(run_and_return_kernel, depth, total),
        out_shape=[
            jax.ShapeDtypeStruct((tokens, width), wide),
            jax.ShapeDtypeStruct((depth, 8, tokens), wide),
            jax.ShapeDtypeStruct((width // 2, inner), low),
            jax.ShapeDtypeStruct((width // 2, inner), low),
            jax.ShapeDtypeStruct((inner, width // 2), low),
            jax.ShapeDtypeStruct(rows.shape, low),
            jax.ShapeDtypeStruct(rows.shape, low),
        ],
        in_specs=[anywhere] * 5 + [local, local, anywhere],
        out_specs=[local, local] + [anywhere] * 5,
        scratch_shapes=[
            pltpu.VMEM((PLANE, depth, capacity, width), low),
            pltpu.VMEM((PLANE, depth, capacity, 128), wide),
            pltpu.VMEM((1, tokens, width), low),
            pltpu.VMEM((2, tokens, width), low),
            pltpu.VMEM((depth + 1, tokens, width), low),
            pltpu.VMEM((depth, 8, tokens), wide),
            pltpu.VMEM((depth, 8, tokens), wide),
            pltpu.VMEM((depth, tile, width), low),
            pltpu.VMEM((depth, tile, inner), low),
            pltpu.VMEM((depth, tile, inner), low),
            pltpu.VMEM((depth, tile, inner), low),
            pltpu.VMEM((depth, tile, width), low),
            pltpu.VMEM((tile, inner), low),
            pltpu.VMEM(weights[0].shape, low),
            pltpu.VMEM(weights[1].shape, low),
            pltpu.VMEM(weights[2].shape, low),
            pltpu.VMEM((4, PLANE, capacity, width), low),
            pltpu.VMEM((4, PLANE, capacity, 128), wide),
            pltpu.VMEM((PLANE, capacity, width), low),
            semaphores((PLANE, depth)),
            semaphores((PLANE, depth)),
            semaphores((PLANE, depth)),
            semaphores((PLANE, depth)),
            semaphores((5,)),
            semaphores((2,)),
            semaphores((depth,)),
            semaphores((depth + 1,)),
            semaphores((depth,)),
            semaphores((depth,)),
            semaphores((2, 2)),
            semaphores((2, wide_count)),
            semaphores((2,)),
            semaphores((tall_count,)),
            semaphores((2,)),
            semaphores((2,)),
            semaphores((2,)),
            pltpu.SemaphoreType.REGULAR,
        ],
        compiler_params=pltpu.CompilerParams(
            collective_id=7, has_side_effects=True, vmem_limit_bytes=63 * MEBIBYTE
        ),
        cost_estimate=LONG,
    )(
        rows.reshape(depth, tile, width),
        grads.reshape(depth, tile, width),
        *weights,
        router,
        choose,
        shared_back,
    )


def body(
    tokens,
    segments,
    routes,
    slot_index,
    cotangent,
    attention_norm,
    query_weight,
    latent_down,
    latent_norm,
    latent_up,
    output_weight,
    feed_norm,
    router_weight,
    shared_gate,
    shared_up,
    shared_down,
    expert_gate,
    expert_up,
    expert_down,
):
    row_count = tokens.shape[1]
    expert_total = lax.axis_size("expert")
    depth = expert_total // PLANE
    plane, line = groups(expert_total)
    place = lax.axis_index("expert")
    level = place // PLANE
    device_half = lax.axis_index("fsdp")
    capacity = row_count * TOPK // expert_total
    line_rows = depth * row_count
    inputs = tokens[0].astype(jnp.float32)

    part_rows = query_weight.shape[0]
    gain_width = attention_norm.shape[0]
    latent_width = latent_norm.shape[0]
    small = jnp.concatenate([attention_norm, latent_norm, feed_norm, router_weight.reshape(-1)])
    cuts = [
        0,
        gain_width,
        gain_width + latent_width,
        2 * gain_width + latent_width,
        small.shape[0],
    ]
    small = jnp.pad(small, (0, 128 * part_rows - small.shape[0])).reshape(part_rows, 128)
    query_width = query_weight.shape[1]
    down_width = latent_down.shape[1]
    entry_width = query_width + down_width + (-down_width) % 128
    up_width = HEADS * (NOPE + VALUE)
    quarters = part_rows // latent_up.shape[0]
    by_head = query_weight.reshape(part_rows, HEADS, NOPE + ROPE)
    packed = jnp.concatenate(
        [
            by_head[..., :NOPE].reshape(part_rows, -1),
            by_head[..., NOPE:].reshape(part_rows, -1),
            jnp.pad(latent_down, ((0, 0), (0, (-down_width) % 128))),
            latent_up.reshape(latent_up.shape[0], quarters, -1)
            .transpose(1, 0, 2)
            .reshape(part_rows, -1),
            output_weight,
            small,
        ],
        axis=1,
    )
    cut = packed.shape[1] // 256 * 128
    route_rows = routes[0]
    slot_rows = slot_index[0]
    target = jnp.where(
        slot_rows >= 0, route_rows * capacity + slot_rows, expert_total * capacity
    )
    target = jnp.pad(target, ((0, 0), (0, 8 - TOPK)), constant_values=expert_total * capacity).T
    shared_width = shared_gate.shape[1] // (2 * depth)
    shared_both = jnp.stack([shared_gate, shared_up]).reshape(
        2, part_rows, 2, depth, shared_width
    )
    shared_both = shared_both.transpose(3, 1, 0, 2, 4)
    spare = (-shared_width) % 128
    shared_both = jnp.pad(shared_both, ((0, 0),) * 4 + ((0, spare),))
    shared_both = shared_both.reshape(depth, part_rows, -1)
    packed_full, grad_line, target_line, shared_full, sdown_full = gather_rows(
        packed, cotangent[0], target, shared_both, shared_down, cuts_of(packed.shape[1], GROUPS)
    )
    shared_full = shared_full.reshape(D, -1)
    sdown_full = sdown_full.reshape(2, shared_width, D)
    expert_gate_full = lax.all_gather(expert_gate[0], "fsdp", axis=0, tiled=True)
    expert_up_full = lax.all_gather(expert_up[0], "fsdp", axis=0, tiled=True)
    expert_down_full = lax.all_gather(expert_down[0], "fsdp", axis=1, tiled=True)
    packed_full, grad_line, target_line, expert_gate_full, expert_up_full, expert_down_full = (
        lax.optimization_barrier(
            (
                packed_full,
                grad_line,
                target_line,
                expert_gate_full,
                expert_up_full,
                expert_down_full,
            )
        )
    )
    up_rows = latent_up.shape[0]
    up_parts = packed_full.reshape(2 * expert_total, quarters, up_rows, -1)
    if up_rows % 16 == 0:
        up_full = up_parts
        ups_shape = (quarters, 2 * expert_total, up_rows, up_width // quarters)
    else:
        up_full = up_parts[..., entry_width : -128 - D].transpose(1, 0, 2, 3)
        up_full = up_full.reshape(quarters, 1, LATENT, -1)
        ups_shape = up_full.shape
    small_full = packed_full[:, -128:].reshape(2 * expert_total, -1)
    gain_one, gain_latent, gain_feed, router_full = (
        small_full[:, cuts[0] : cuts[1]].reshape(-1),
        small_full[:, cuts[1] : cuts[2]].reshape(-1),
        small_full[:, cuts[2] : cuts[3]].reshape(-1),
        small_full[:, cuts[3] : cuts[4]].reshape(-1, expert_total),
    )

    slot_names = level * PLANE * capacity + jnp.arange(PLANE * capacity)
    hits = target_line[:, :TOPK, None, :] == slot_names[None, None, :, None]
    choose_rows = jnp.any(hits, axis=1).astype(jnp.bfloat16)

    choose_slots = choose_rows.reshape(depth, PLANE, capacity, row_count)
    grad_line = grad_line.reshape(depth, row_count, D)

    cosine, sine_table = rotary_table(row_count, device_half * row_count, ROPE)
    tables = (
        jnp.concatenate([cosine] * 4, axis=1),
        jnp.concatenate([-sine_table, sine_table] * 2, axis=1),
    )
    gain_first = gain_one.astype(jnp.float32)
    latent_gain = gain_latent.astype(jnp.float32)
    feed_gain = gain_feed.astype(jnp.float32)
    query_place = device_half * row_count + jnp.arange(row_count)
    key_place = (device_half - 1) * row_count + jnp.arange(2 * row_count)
    padded_segments = jnp.concatenate([jnp.full((row_count,), -1, jnp.int32), segments[0]])
    key_segment = lax.dynamic_slice_in_dim(padded_segments, device_half * row_count, 2 * row_count)
    query_segment = lax.dynamic_slice_in_dim(segments[0], device_half * row_count, row_count)
    visible = (key_place[None, :] <= query_place[:, None]) & (
        key_segment[None, :] == query_segment[:, None]
    )
    mask = visible.astype(jnp.float32)
    layout = (entry_width, packed.shape[1] - 128 - D)
    (
        normed_low,
        residual,
        mixed_low,
        queries,
        latent,
        compressed,
        expanded,
        keys_rope,
        log_total,
        mixed_heads,
        grad_rows,
    ) = attend(
        tokens[0],
        packed_full,
        up_full,
        ups_shape,
        (gain_first[None], latent_gain[None], feed_gain[None]),
        tables,
        mask,
        choose_slots,
        grad_line,
        layout,
    )
    mixed_rows, shared_out, shared_back, shared_grad, sdown_grad, grad_rows = dispatch(
        mixed_low, choose_slots, grad_line, shared_full, sdown_full, grad_rows
    )
    shared_out = shared_out.reshape(line_rows, D)
    router_wide = jnp.pad(router_full, ((0, 0), (0, (-expert_total) % 128)))
    shared_summed = lax.psum_scatter(
        shared_grad, "expert", scatter_dimension=0, axis_index_groups=plane, tiled=True
    )[0]
    sdown_summed = lax.psum_scatter(
        sdown_grad, "expert", scatter_dimension=0, axis_index_groups=plane, tiled=True
    )
    weights = (expert_gate_full, expert_up_full, expert_down_full)
    if depth <= PLANE:
        (
            back_and_shared,
            prob_parts,
            expert_gate_piece,
            expert_up_piece,
            expert_down_piece,
            expert_out,
            own_out,
        ) = run_and_return(
            mixed_rows, grad_rows, weights, router_wide, choose_slots, shared_back, expert_total
        )
    else:
        flat_rows = mixed_rows.reshape(expert_total * capacity, D)
        flat_grads = grad_rows.reshape(expert_total * capacity, D)
        hidden_scaled, gate_low, up_low, input_grad, expert_out, slot_grad = run_expert(
            flat_rows, flat_grads, *weights, router_wide, expert_total
        )
        (
            back_and_shared,
            prob_parts,
            expert_gate_piece,
            expert_up_piece,
            expert_down_piece,
        ) = give_back(
            input_grad.reshape(mixed_rows.shape),
            slot_grad.reshape(depth, PLANE, capacity, 128),
            choose_slots,
            shared_back,
            [flat_rows, gate_low, up_low, hidden_scaled, flat_grads],
        )
        own_out = expert_out
    prob_grad = prob_parts[:, :PLANE].reshape(expert_total, row_count).T
    probabilities = jax.nn.softmax(matmul(mixed_low, router_full), axis=-1)
    prob_grad = prob_parts[:, :PLANE].reshape(expert_total, row_count).T
    logit_low = (
        probabilities * (prob_grad - jnp.sum(probabilities * prob_grad, axis=-1, keepdims=True))
    ).astype(jnp.bfloat16)
    router_grad = left_matmul(mixed_low, logit_low)
    (
        token_grad,
        up_weight_grad,
        latent_gain_grad,
        first_gain_grad,
        feed_gain_grad,
        entry_grad,
        output_grad,
        returned,
    ) = attend_back(
        back_and_shared,
        packed_full,
        up_full,
        ups_shape,
        (
            queries,
            expanded,
            keys_rope,
            log_total,
            latent,
            compressed,
            normed_low,
            mixed_heads,
            tokens[0],
            residual,
            cotangent[0],
            jnp.pad(logit_low, ((0, 0), (0, (-expert_total) % 128))),
            router_wide,
        ),
        (latent_gain[None], gain_first[None], feed_gain[None]),
        tables,
        mask,
        (expert_out.reshape(mixed_rows.shape), own_out.reshape(mixed_rows.shape)),
        (shared_summed, sdown_summed),
        layout,
    )
    if up_rows % 16 != 0:
        up_weight_grad = up_weight_grad.reshape(quarters, 2 * expert_total, up_rows, -1)
        up_weight_grad = up_weight_grad.transpose(1, 0, 2, 3)
    latent_gain_grad = latent_gain_grad[0]
    first_gain_grad = first_gain_grad[0]
    feed_gain_grad = feed_gain_grad[0]
    routed = jnp.einsum(
        "zst,zsd->ztd",
        choose_rows,
        returned.reshape(depth, PLANE * capacity, D),
        preferred_element_type=jnp.float32,
    )
    routed_and_shared = lax.psum_scatter(
        (routed.reshape(line_rows, D) + shared_out).astype(jnp.bfloat16),
        "expert",
        scatter_dimension=0,
        axis_index_groups=line,
        tiled=True,
    ).astype(jnp.float32)
    output = (residual + routed_and_shared).astype(jnp.bfloat16)

    small_grad = jnp.concatenate(
        [
            first_gain_grad.reshape(-1, gain_width),
            latent_gain_grad.reshape(-1, latent_width),
            feed_gain_grad.reshape(-1, gain_width),
            router_grad.reshape(2 * expert_total, -1),
        ],
        axis=1,
    )
    small_grad = jnp.pad(small_grad, ((0, 0), (0, 128 * part_rows - small_grad.shape[1])))
    packed_piece, shared_back_moved = reduce_rows(
        [
            entry_grad,
            up_weight_grad.reshape(2 * expert_total * part_rows, -1),
            output_grad,
            small_grad.astype(jnp.bfloat16).reshape(-1, 128),
        ],
        shared_summed,
        cut,
    )
    small_piece = packed_piece[:, -128:].reshape(-1)
    shared_pieces = (
        shared_back_moved.reshape(depth, part_rows, 2, 2, -1)[..., :shared_width]
        .transpose(2, 1, 3, 0, 4)
        .reshape((2,) + shared_gate.shape)
        .astype(jnp.float32)
    )
    output_piece = packed_piece[:, -128 - D : -128]
    nope_width = HEADS * NOPE
    query_piece = jnp.concatenate(
        [
            packed_piece[:, :nope_width].reshape(part_rows, HEADS, NOPE),
            packed_piece[:, nope_width:query_width].reshape(part_rows, HEADS, ROPE),
        ],
        axis=2,
    ).reshape(part_rows, query_width)

    return (
        output[None],
        token_grad[None],
        small_piece[cuts[0] : cuts[1]],
        query_piece,
        packed_piece[:, query_width : query_width + down_width],
        small_piece[cuts[1] : cuts[2]],
        packed_piece[:, entry_width : -128 - D]
        .reshape(quarters, latent_up.shape[0], -1)
        .transpose(1, 0, 2)
        .reshape(latent_up.shape),
        output_piece,
        small_piece[cuts[2] : cuts[3]],
        small_piece[cuts[3] : cuts[4]].reshape(gain_width, expert_total),
        shared_pieces[0],
        shared_pieces[1],
        sdown_summed.astype(jnp.float32),
        expert_gate_piece.astype(jnp.float32)[None],
        expert_up_piece.astype(jnp.float32)[None],
        expert_down_piece.astype(jnp.float32)[None],
    )


def solution(mesh):
    return jax.shard_map(
        body,
        mesh=mesh,
        in_specs=(
            P("expert", "fsdp", None),
            P("expert", None),
            P("expert", "fsdp", None),
            P("expert", "fsdp", None),
            P("expert", "fsdp", None),
            P(("fsdp", "expert")),
            P(("fsdp", "expert"), None),
            P(("fsdp", "expert"), None),
            P(("fsdp", "expert")),
            P(("fsdp", "expert"), None),
            P(("fsdp", "expert"), None),
            P(("fsdp", "expert")),
            P(("fsdp", "expert"), None),
            P(("fsdp", "expert"), None),
            P(("fsdp", "expert"), None),
            P(("fsdp", "expert"), None),
            P("expert", "fsdp", None),
            P("expert", "fsdp", None),
            P("expert", None, "fsdp"),
        ),
        out_specs=(
            P("expert", "fsdp", None),
            P("expert", "fsdp", None),
            P(("fsdp", "expert")),
            P(("fsdp", "expert"), None),
            P(("fsdp", "expert"), None),
            P(("fsdp", "expert")),
            P(("fsdp", "expert"), None),
            P(("fsdp", "expert"), None),
            P(("fsdp", "expert")),
            P(("fsdp", "expert"), None),
            P(("fsdp", "expert"), None),
            P(("fsdp", "expert"), None),
            P(("fsdp", "expert"), None),
            P("expert", "fsdp", None),
            P("expert", "fsdp", None),
            P("expert", None, "fsdp"),
        ),
        check_vma=False,
    )
```

```python
import functools
import math

import jax
import jax.numpy as jnp
from jax import lax
from jax.experimental import pallas as pl
from jax.experimental.pallas import tpu as pltpu
from jax.sharding import PartitionSpec as P

D = 2048
HEADS = 16
NOPE = 128
ROPE = 64
VALUE = 128
LATENT = 512
TOPK = 6


EPSILON = 1e-06
FLOOR_SCORE = -1e30


def norm_rows(values, gain):
    return values * lax.rsqrt(jnp.mean(values * values, axis=-1, keepdims=True) + EPSILON) * gain


def norm_back(values, gain, incoming):
    primal_out, pullback = jax.vjp(norm_rows, values, gain)
    return pullback(incoming)


def swiglu_back(gate_part, up_portion, incoming):
    primal_out, pullback = jax.vjp(
        lambda former, latter: jax.nn.silu(former) * latter, gate_part, up_portion
    )
    return pullback(incoming)


def rotary_table(row_total, offset, rope_width):
    frequency_steps = jnp.arange(rope_width // 2, dtype=jnp.float32)
    inverse = jnp.exp(frequency_steps * (-2.0 * math.log(10000.0) / rope_width))
    places = (offset + jnp.arange(row_total)).astype(jnp.float32)
    angles = places[:, None] * inverse[None, :]
    return (jnp.cos(angles), jnp.sin(angles))


def matmul(former, latter):
    return jnp.dot(former, latter, preferred_element_type=jnp.float32)


def left_matmul(former, latter):
    return lax.dot_general(
        former, latter, (((0,), (0,)), ((), ())), preferred_element_type=jnp.float32
    )


def right_matmul(former, latter):
    return lax.dot_general(
        former, latter, (((1,), (1,)), ((), ())), preferred_element_type=jnp.float32
    )


PLANE = 4
MESH = pl.DeviceIdType.MESH
MEBIBYTE = 1024 * 1024
GROUPS = 4
PARTS = 2
LONG = pl.CostEstimate(flops=100 * 10**9, bytes_accessed=0, transcendentals=0)
MIDDLE = pl.CostEstimate(flops=40 * 10**9, bytes_accessed=0, transcendentals=0)


def groups(count):
    lines = count // PLANE
    plane = [[row * PLANE + spot for spot in range(PLANE)] for row in range(lines)]
    line = [[row * PLANE + spot for row in range(lines)] for spot in range(PLANE)]
    return plane, line


def remote(source, target, send, receive, where):
    return pltpu.make_async_remote_copy(
        src_ref=source,
        dst_ref=target,
        send_sem=send,
        recv_sem=receive,
        device_id=where,
        device_id_type=MESH,
    )


def plane_mates(place):
    spot = place % PLANE
    return (place + 1 - 2 * (spot % 2), place + 2 - 4 * (spot // 2))


def greet(partners):
    barrier = pltpu.get_barrier_semaphore()
    for where in partners:
        pl.semaphore_signal(barrier, inc=1, device_id=where, device_id_type=MESH)
    pl.semaphore_wait(barrier, len(partners))


def line_others(half, place, depth):
    total = depth * PLANE
    return [(half, (place + offset * PLANE) % total) for offset in range(1, depth)]


def plane_others(half, place):
    spot = place % PLANE
    return [(half, place - spot + (spot + offset) % PLANE) for offset in range(1, PLANE)]


def greet_neighbours(half, place, depth):
    mates = [(half, mate) for mate in plane_mates(place)]
    greet(line_others(half, place, depth) + mates + [(1 - half, place)])


def exchange_along(depth, half, place, in_ref, land, own_sem, send, receive):
    level = place // PLANE
    total = depth * PLANE

    def own():
        return pltpu.make_async_copy(in_ref.at[level], land(level), own_sem)

    def to(offset):
        where = (place + offset * PLANE) % total
        return remote(
            in_ref.at[where // PLANE],
            land(level),
            send.at[offset],
            receive.at[offset],
            (half, where),
        )

    def start():
        own().start()
        for offset in range(1, depth):
            to(offset).start()

    def finish():
        own().wait()
        for offset in range(1, depth):
            to(offset).wait()

    return start, finish


def exchange_plane(half, place, source_of, target_of, own_sem, send, receive, own_there=False):
    spot = place % PLANE

    def to(offset, level):
        mate = (spot + offset) % PLANE
        return remote(
            source_of(mate, level),
            target_of(spot, level),
            send.at[offset, level],
            receive.at[offset, level],
            (half, place - spot + mate),
        )

    def came(offset, level):
        mate = (spot + PLANE - offset) % PLANE
        block = target_of(mate, level)
        return remote(
            block,
            block,
            send.at[offset, level],
            receive.at[offset, level],
            (half, place - spot + mate),
        )

    def own(level):
        return pltpu.make_async_copy(
            source_of(spot, level), target_of(spot, level), own_sem.at[level]
        )

    def start(level):
        for offset in range(1, PLANE):
            to(offset, level).start()
        if not own_there:
            own(level).start()

    def finish(level):
        if not own_there:
            own(level).wait()
        for offset in range(1, PLANE):
            came(offset, level).wait_recv()
            to(offset, level).wait_send()

    return start, finish


def place_rows(choose_ref, source, block, placed):
    def columns(n, carry):
        at = lanes_at(n * 512, 512)
        for mate in range(PLANE):
            placed[mate, :, at] = jnp.dot(
                choose_ref[source, mate], block[:, at], preferred_element_type=jnp.float32
            ).astype(placed.dtype)
        return carry

    lax.fori_loop(0, block.shape[1] // 512, columns, 0)


def cuts_of(width, count):
    return [width * k // count // 128 * 128 for k in range(count)] + [width]


def gather_kernel(depth, cuts, *refs):
    in_ref, *line_ins, move_in, down_in = refs[:5]
    out_ref, *line_outs, shared_out, down_out = refs[5:10]
    own_sem, zs, zr, ps, pr, qs, qr, cs, cr, ls, lr, ms, mr, *shared_sems = refs[10:]
    os, ore, ts, tr, us, ur = shared_sems
    half = lax.axis_index("fsdp")
    place = lax.axis_index("expert")
    level = place // PLANE
    spot = place % PLANE
    total = depth * PLANE
    mates = plane_mates(place)
    rows, width = in_ref.shape
    columns = [pl.ds(low, high - low) for low, high in zip(cuts[:-1], cuts[1:])]
    count = len(columns)
    greet_neighbours(half, place, depth)

    def at(which, block, count=1):
        start = pl.multiple_of((half * total + block) * rows, rows)
        return out_ref.at[pl.ds(start, count * rows), columns[which]]

    def along(which, way, source, own=False):
        target = at(which, source * PLANE + spot)
        start = in_ref.at[:, columns[which]] if own else target
        return remote(
            start,
            target,
            zs.at[which, way, source],
            zr.at[which, source],
            (half, place + (2 * way - 1) * PLANE),
        )

    def plane_one(which, source, own=False):
        target = at(which, source * PLANE + spot)
        start = in_ref.at[:, columns[which]] if own else target
        return remote(
            start,
            target,
            ps.at[which, source],
            pr.at[which, source],
            (half, mates[which % 2]),
        )

    def plane_two(which, source, turn):
        base = source * PLANE
        if which % 2 == 0:
            block = at(which, base + spot - spot % 2, 2)
        else:
            block = at(which, base + (spot + 2 * turn) % PLANE)
        return remote(
            block,
            block,
            qs.at[which, turn, source],
            qr.at[which, turn, source],
            (half, mates[1 - which % 2]),
        )

    def core(which, source):
        block = at(which, source * PLANE, PLANE)
        return remote(
            block, block, cs.at[which, source], cr.at[which, source], (1 - half, place)
        )

    def trail(which, way, source, own=False):
        target = line_outs[which].at[source]
        return remote(
            line_ins[which] if own else target,
            target,
            ls.at[which, way, source],
            lr.at[which, source],
            (half, place + (2 * way - 1) * PLANE),
        )

    def trail_own(which):
        return pltpu.make_async_copy(
            line_ins[which], line_outs[which].at[level], own_sem.at[count + which]
        )

    move_start, move_finish = exchange_along(
        depth,
        half,
        place,
        move_in,
        lambda source: shared_out.at[half, source, spot],
        own_sem.at[count + 2],
        ms,
        mr,
    )
    items = range(depth + 2)
    down_own = pltpu.make_async_copy(down_in, down_out.at[half, spot], own_sem.at[count + 3])

    def shared_at(item, first, count):
        if item < depth:
            return shared_out.at[half, item, pl.ds(first, count)]
        span = down_in.shape[1] // 2
        return down_out.at[
            half, pl.ds(first, count), :, pl.ds((item - depth) * span, span)
        ]

    def shared_route(item):
        return (0 if item < depth // 2 else 1) if item < depth else item - depth

    def shared_one(item):
        block = shared_at(item, spot, 1)
        mate = mates[shared_route(item)]
        return remote(block, block, os.at[item], ore.at[item], (half, mate))

    def shared_two(item):
        if shared_route(item) == 0:
            blocks = [shared_at(item, spot - spot % 2, 2)]
        else:
            blocks = [shared_at(item, (spot + 2 * turn) % PLANE, 1) for turn in range(2)]
        mate = mates[1 - shared_route(item)]
        return [
            remote(block, block, ts.at[turn, item], tr.at[turn, item], (half, mate))
            for turn, block in enumerate(blocks)
        ]

    def shared_core(item):
        block = shared_at(item, 0, PLANE)
        return remote(block, block, us.at[item], ur.at[item], (1 - half, place))

    seconds = [(which, turn) for which in range(count) for turn in range(1 + which % 2)]

    def own_copy(which):
        return pltpu.make_async_copy(
            in_ref.at[:, columns[which]], at(which, place), own_sem.at[which]
        )

    for which in range(count):

        @pl.when(level > 0)
        def _():
            along(which, 0, level, True).start()

        @pl.when(level < depth - 1)
        def _():
            along(which, 1, level, True).start()

        plane_one(which, level, True).start()
        own_copy(which).start()
    move_start()
    down_own.start()
    for which in range(2):
        trail_own(which).start()

    def trail_first():
        for which in range(2):

            @pl.when(level > 0)
            def _():
                trail(which, 0, level, True).start()

            @pl.when(level < depth - 1)
            def _():
                trail(which, 1, level, True).start()

    def trail_on(source, way):
        for which in range(2):
            trail(which, way, source).wait_recv()

            @pl.when((level < depth - 1) if way == 1 else (level > 0))
            def _():
                trail(which, way, source).start()

    def visit(step, act):
        if step == 0:
            act(level, None)
            return

        @pl.when(level - step >= 0)
        def _():
            act(level - step, 1)

        @pl.when(level + step < depth)
        def _():
            act(level + step, 0)

    def arrive(source, way):
        for which in range(count):
            along(which, way, source).wait_recv()

            @pl.when((level < depth - 1) if way == 1 else (level > 0))
            def _():
                along(which, way, source).start()

            plane_one(which, source).start()

    def spread(source, way):
        for which in range(count):
            plane_one(which, source).wait_recv()
            for kind, turn in seconds:
                if kind == which:
                    plane_two(kind, source, turn).start()

    def share(source, way):
        for which in range(count):
            for kind, turn in seconds:
                if kind == which:
                    plane_two(kind, source, turn).wait_recv()
            core(which, source).start()

    for which in range(count):
        own_copy(which).wait()
    visit(0, spread)
    for step in range(1, depth):
        visit(step, arrive)
        if step == 1:
            move_finish()
            down_own.wait()
            for item in items:
                shared_one(item).start()
        if step == 2:
            trail_first()
        if step >= 3:
            visit(step - 2, trail_on)
        if step >= 2:
            visit(step - 1, spread)
        if step == 2:
            for item in items:
                shared_one(item).wait_recv()
                for copy in shared_two(item):
                    copy.start()
        if step >= 3:
            visit(step - 3, share)
    visit(depth - 1, spread)
    visit(depth - 2, trail_on)
    visit(depth - 3, share)
    for item in items:
        for copy in shared_two(item):
            copy.wait_recv()
        shared_core(item).start()
    visit(depth - 2, share)
    visit(depth - 1, trail_on)
    visit(depth - 1, share)
    for item in items:
        shared_one(item).wait_send()
        for copy in shared_two(item):
            copy.wait_send()
        shared_core(item).wait()
    for which in range(2):
        trail_own(which).wait()

    def finish(source, carry):
        for which in range(2):

            @pl.when((source <= level) & (level < depth - 1))
            def _():
                trail(which, 1, source).wait_send()

            @pl.when((source >= level) & (level > 0))
            def _():
                trail(which, 0, source).wait_send()

        for which in range(count):
            core(which, source).wait_recv()
            core(which, source).wait_send()
            plane_one(which, source).wait_send()

            @pl.when((source <= level) & (level < depth - 1))
            def _():
                along(which, 1, source).wait_send()

            @pl.when((source >= level) & (level > 0))
            def _():
                along(which, 0, source).wait_send()

        for kind, turn in seconds:
            plane_two(kind, source, turn).wait_send()
        return carry

    lax.fori_loop(0, depth, finish, 0)


def gather_rows(value, first, second, moved, down, cuts):
    rows, width = value.shape
    total = lax.axis_size("expert")
    depth = total // PLANE
    count = len(cuts) - 1
    semaphores = pltpu.SemaphoreType.DMA
    return pl.pallas_call(
        functools.partial(gather_kernel, depth, cuts),
        out_shape=[
            jax.ShapeDtypeStruct((2 * total * rows, width), value.dtype),
            jax.ShapeDtypeStruct((depth,) + first.shape, first.dtype),
            jax.ShapeDtypeStruct((depth,) + second.shape, second.dtype),
            jax.ShapeDtypeStruct((2, depth, PLANE) + moved.shape[1:], moved.dtype),
            jax.ShapeDtypeStruct((2, PLANE) + down.shape, down.dtype),
        ],
        in_specs=[pl.BlockSpec(memory_space=pltpu.VMEM)] * 5,
        out_specs=[pl.BlockSpec(memory_space=pl.ANY)] * 5,
        scratch_shapes=[
            semaphores((count + 4,)),
            semaphores((count, 2, depth)),
            semaphores((count, depth)),
            semaphores((count, depth)),
            semaphores((count, depth)),
            semaphores((count, 2, depth)),
            semaphores((count, 2, depth)),
            semaphores((count, depth)),
            semaphores((count, depth)),
            semaphores((2, 2, depth)),
            semaphores((2, depth)),
            semaphores((depth,)),
            semaphores((depth,)),
            semaphores((depth + 2,)),
            semaphores((depth + 2,)),
            semaphores((2, depth + 2)),
            semaphores((2, depth + 2)),
            semaphores((depth + 2,)),
            semaphores((depth + 2,)),
        ],
        compiler_params=pltpu.CompilerParams(collective_id=1, has_side_effects=True),
        cost_estimate=LONG,
    )(value, first, second, moved, down)


def dot_nt(former, latter):
    return lax.dot_general(
        former, latter, (((1,), (1,)), ((), ())), preferred_element_type=jnp.float32
    )


def dot_tn(former, latter):
    return lax.dot_general(
        former, latter, (((0,), (0,)), ((), ())), preferred_element_type=jnp.float32
    )


def dispatch_kernel(depth, *refs):
    x_ref, choose_ref, grad_in, shared_in, down_in = refs[:5]
    rows_out, forth_out, back_out, wide_out, tall_out, grad_out = refs[6:12]
    lines, placed, grads, weights, downs, low_ref, hidden_ref, forth_ref, back_ref = refs[12:21]
    wide_ref, tall_ref, grad_placed, wide_give, wide_take, tall_give, tall_take = refs[21:28]
    load_sem, out_sem, zs, zr, es, er, own_sem, done_sem, gs, gr, grad_sem = refs[28:39]
    ws, wr, ts, tr = refs[39:]
    half = lax.axis_index("fsdp")
    place = lax.axis_index("expert")
    other = (1 - half, place)
    level = place // PLANE
    spot = place % PLANE
    padded, width = downs.shape
    share = padded // 2
    true = down_in.shape[1]
    chunk = padded
    greet(line_others(half, place, depth) + plane_others(half, place) + [other])

    def along(part, way, source):
        block = lines.at[source, :, pl.ds(part * (width // PARTS), width // PARTS)]
        where = (half, place + (2 * way - 1) * PLANE)
        return remote(block, block, zs.at[part, way, source], zr.at[part, source], where)

    loads = [
        pltpu.make_async_copy(shared_in, weights, load_sem.at[0]),
        pltpu.make_async_copy(grad_in, grads, load_sem.at[1]),
    ] + [
        pltpu.make_async_copy(
            down_in.at[k], downs.at[pl.ds(k * share, true), :], load_sem.at[2 + k]
        )
        for k in range(2)
    ]
    lines[level] = x_ref[...]

    def pass_on(part, way, source):
        @pl.when((level < depth - 1) if way == 1 else (level > 0))
        def _():
            along(part, way, source).start()

    for part in range(PARTS):
        for way in range(2):
            pass_on(part, way, level)
    for load in loads:
        load.start()
    if share > true:
        for k in range(2):
            downs[pl.ds(k * share + true, share - true), :] = jnp.zeros(
                (share - true, width), downs.dtype
            )

    rows_start, rows_finish = exchange_plane(
        half,
        place,
        lambda mate, source: placed.at[source, mate],
        lambda mate, source: rows_out.at[source, mate],
        own_sem,
        es,
        er,
    )
    grad_start, grad_finish = exchange_plane(
        half,
        place,
        lambda mate, source: grad_placed.at[source // 2, mate],
        lambda mate, source: grad_out.at[source, mate],
        grad_sem,
        gs,
        gr,
    )

    def give(source):
        place_rows(choose_ref, source, lines.at[source], placed.at[source])
        rows_start(source)

    def give_grad(n, carry):
        source = 2 * n + 1
        place_rows(choose_ref, source, grads.at[source], grad_placed.at[n])
        grad_start(source)
        return carry

    def shared(source):
        def inner(n, carry):
            at = pl.ds(pl.multiple_of(n * chunk, chunk), chunk)
            after = pl.ds(pl.multiple_of(padded + n * chunk, 128), chunk)
            x = lines[source]
            gate = jnp.dot(x, weights[:, at], preferred_element_type=jnp.float32)
            up = jnp.dot(x, weights[:, after], preferred_element_type=jnp.float32)
            dh = dot_nt(grads[source], downs[at, :])
            sig = 1.0 / (1.0 + jnp.exp(-gate))
            act = gate * sig
            hidden_ref[source, :, at] = (act * up).astype(hidden_ref.dtype)
            low_ref[source, :, at] = (dh * up * (sig + act * (1.0 - sig))).astype(low_ref.dtype)
            low_ref[source, :, after] = (dh * act).astype(low_ref.dtype)
            return carry

        lax.fori_loop(0, padded // chunk, inner, 0)

        def outer(n, carry):
            at = pl.ds(pl.multiple_of(n * 1024, 1024), 1024)
            forth_ref[:, at] = jnp.dot(
                hidden_ref[source], downs[:, at], preferred_element_type=jnp.float32
            ).astype(forth_ref.dtype)
            back_ref[:, at] = dot_nt(low_ref[source], weights[at, :]).astype(back_ref.dtype)
            return carry

        lax.fori_loop(0, width // 1024, outer, 0)
        outs = [
            pltpu.make_async_copy(forth_ref, forth_out.at[source], out_sem.at[0]),
            pltpu.make_async_copy(back_ref, back_out.at[source], out_sem.at[1]),
        ]
        for out in outs:
            out.start()
        for out in outs:
            out.wait()

    give(level)
    for load in loads:
        load.wait()
    lax.fori_loop(0, depth // 2, give_grad, 0)
    shared(level)

    def step(s, carry):
        for part in range(PARTS):

            @pl.when(level - s >= 0)
            def _():
                along(part, 1, level - s).wait_recv()
                pass_on(part, 1, level - s)

            @pl.when(level + s < depth)
            def _():
                along(part, 0, level + s).wait_recv()
                pass_on(part, 0, level + s)

        def one(way, act):
            source = level + (1 - 2 * way) * s

            @pl.when((source >= 0) & (source < depth))
            def _():
                act(source)

        def both(way, carry):
            one(way, give)
            return carry

        def both_shared(way, carry):
            one(way, shared)
            return carry

        lax.fori_loop(0, 2, both, 0)
        lax.fori_loop(0, 2, both_shared, 0)
        return carry

    lax.fori_loop(1, depth, step, 0)

    tokens = x_ref.shape[0]

    def all_lines(ref, at):
        return ref[:, :, at].reshape(depth * tokens, -1)

    part = wide_ref.shape[2]
    chunk_rows = max(PLANE * part, 128)
    per_chunk = chunk_rows // (PLANE * part)
    core_rows = width // 2
    tall_rows = tall_ref.shape[1]
    tall_count = share // tall_rows

    def wide_value(owner, n):
        at = pl.ds(pl.multiple_of(owner * core_rows + n * chunk_rows, chunk_rows), chunk_rows)
        return dot_tn(all_lines(lines, at), low_ref[...].reshape(depth * tokens, -1))

    def tall_value(owner, k):
        at = pl.ds(pl.multiple_of(owner * share + k * tall_rows, tall_rows), tall_rows)
        return dot_tn(all_lines(hidden_ref, at), grads[...].reshape(depth * tokens, -1))

    def wide_send(k):
        return remote(wide_give.at[k], wide_take.at[k], ws.at[k], wr.at[k], other)

    def tall_send(k):
        return remote(tall_give.at[k], tall_take.at[k], ts.at[k], tr.at[k], other)

    def split(value, j):
        first = j * PLANE * part
        return [value[first + k * part : first + (k + 1) * part] for k in range(PLANE)]

    def give_wide(n, carry):
        value = wide_value(1 - half, n)
        for j in range(per_chunk):
            for k, block in enumerate(split(value, j)):
                wide_give[n * per_chunk + j, k] = block.astype(wide_give.dtype)
            wide_send(n * per_chunk + j).start()
        return carry

    def give_tall(k, carry):
        tall_give[k] = tall_value(1 - half, k).astype(tall_give.dtype)
        tall_send(k).start()
        return carry

    def write_wide(k):
        return pltpu.make_async_copy(
            wide_ref.at[k % 2], wide_out.at[:, k], done_sem.at[0, k % 2]
        )

    def keep_wide(n, carry):
        value = wide_value(half, n)
        for j in range(per_chunk):
            at = n * per_chunk + j

            @pl.when(at >= 2)
            def _():
                write_wide(at - 2).wait()

            wide_send(at).wait_recv()
            for k, block in enumerate(split(value, j)):
                total = block + wide_take[at, k].astype(jnp.float32)
                wide_ref[at % 2, k] = total.astype(wide_ref.dtype)
            write_wide(at).start()
        return carry

    lax.fori_loop(0, core_rows // chunk_rows, give_wide, 0)
    lax.fori_loop(0, tall_count, give_tall, 0)
    lax.fori_loop(0, core_rows // chunk_rows, keep_wide, 0)
    for k in range(max(0, depth - 2), depth):
        write_wide(k).wait()
    writes = []
    for k in range(tall_count):
        if k >= 2:
            writes[k - 2].wait()
        value = tall_value(half, k)
        tall_send(k).wait_recv()
        total = value + tall_take[k].astype(jnp.float32)
        tall_ref[k % 2] = total.astype(tall_ref.dtype)
        size = min(tall_rows, true - k * tall_rows)
        writes.append(
            pltpu.make_async_copy(
                tall_ref.at[k % 2, pl.ds(0, size), :],
                tall_out.at[pl.ds(k * tall_rows, size), :],
                done_sem.at[1, k % 2],
            )
        )
        writes[k].start()
    for write in writes[-2:]:
        write.wait()

    def given(k, carry):
        wide_send(k).wait_send()
        return carry

    lax.fori_loop(0, depth, given, 0)
    for k in range(tall_count):
        tall_send(k).wait_send()

    def finish_grad(n, carry):
        grad_finish(2 * n + 1)
        return carry

    lax.fori_loop(0, depth // 2, finish_grad, 0)

    def finish(source, carry):
        rows_finish(source)

        for part in range(PARTS):

            @pl.when((source <= level) & (level < depth - 1))
            def _():
                along(part, 1, source).wait_send()

            @pl.when((source >= level) & (level > 0))
            def _():
                along(part, 0, source).wait_send()

        return carry

    lax.fori_loop(0, depth, finish, 0)


def dispatch(x, choose, grad_line, shared_full, down_full, grad_rows):
    depth = choose.shape[0]
    tokens, width = x.shape
    capacity = choose.shape[2]
    padded = shared_full.shape[1] // 2
    part = width // (2 * PLANE * depth)
    semaphores = pltpu.SemaphoreType.DMA
    low = x.dtype
    anywhere = pl.BlockSpec(memory_space=pl.ANY)
    local = pl.BlockSpec(memory_space=pltpu.VMEM)
    return pl.pallas_call(
        functools.partial(dispatch_kernel, depth),
        out_shape=[
            jax.ShapeDtypeStruct((depth, PLANE, capacity, width), low),
            jax.ShapeDtypeStruct((depth, tokens, width), low),
            jax.ShapeDtypeStruct((depth, tokens, width), low),
            jax.ShapeDtypeStruct((PLANE, depth, part, 2 * padded), low),
            jax.ShapeDtypeStruct(down_full.shape[1:], low),
            jax.ShapeDtypeStruct(grad_rows.shape, low),
        ],
        in_specs=[local, local] + [anywhere] * 4,
        out_specs=[anywhere] * 6,
        input_output_aliases={5: 5},
        scratch_shapes=[
            pltpu.VMEM((depth, tokens, width), low),
            pltpu.VMEM((depth, PLANE, capacity, width), low),
            pltpu.VMEM((depth, tokens, width), low),
            pltpu.VMEM((width, 2 * padded), low),
            pltpu.VMEM((padded, width), low),
            pltpu.VMEM((depth, tokens, 2 * padded), low),
            pltpu.VMEM((depth, tokens, padded), low),
            pltpu.VMEM((tokens, width), low),
            pltpu.VMEM((tokens, width), low),
            pltpu.VMEM((2, PLANE, part, 2 * padded), low),
            pltpu.VMEM((2, 128, width), low),
            pltpu.VMEM((depth // 2, PLANE, capacity, width), low),
            pltpu.VMEM((depth, PLANE, part, 2 * padded), low),
            pltpu.VMEM((depth, PLANE, part, 2 * padded), low),
            pltpu.VMEM((padded // 256, 128, width), low),
            pltpu.VMEM((padded // 256, 128, width), low),
            semaphores((4,)),
            semaphores((2,)),
            semaphores((PARTS, 2, depth)),
            semaphores((PARTS, depth)),
            semaphores((PLANE, depth)),
            semaphores((PLANE, depth)),
            semaphores((depth,)),
            semaphores((2, 2)),
            semaphores((PLANE, depth)),
            semaphores((PLANE, depth)),
            semaphores((depth,)),
            semaphores((depth,)),
            semaphores((depth,)),
            semaphores((padded // 256,)),
            semaphores((padded // 256,)),
        ],
        compiler_params=pltpu.CompilerParams(
            collective_id=3, has_side_effects=True, vmem_limit_bytes=62 * MEBIBYTE
        ),
        cost_estimate=LONG,
    )(x, choose, grad_line, shared_full, down_full, grad_rows)


def expert_kernel(total, *refs):
    x_ref, grad_ref, gate_in, up_in, down_in, router_ref = refs[:6]
    scaled_ref, d_gate_ref, d_up_ref, back_ref, out_ref, slot_ref = refs[6:12]
    gates, ups, downs, hidden, sem = refs[12:]
    rows = x_ref.shape[0]
    width, inner = gates.shape
    wide = jnp.float32
    loads = [
        pltpu.make_async_copy(source, target, sem.at[k])
        for k, (source, target) in enumerate(zip((gate_in, up_in, down_in), (gates, ups, downs)))
    ]
    first = pl.program_id(0) == 0

    @pl.when(first)
    def _():
        for load in loads:
            load.start()

    logits = jnp.dot(x_ref[...], router_ref[...], preferred_element_type=wide)
    lanes = lax.broadcasted_iota(jnp.int32, logits.shape, 1)
    logits = jnp.where(lanes < total, logits, FLOOR_SCORE)
    powers = jnp.exp(logits - jnp.max(logits, axis=-1, keepdims=True))
    probs = powers / jnp.sum(powers, axis=-1, keepdims=True)
    mine = jnp.where(lanes == lax.axis_index("expert"), probs, 0.0)
    gate = jnp.sum(mine, axis=-1, keepdims=True)

    @pl.when(first)
    def _():
        for load in loads:
            load.wait()

    def columns(start, size, slots):
        at = lanes_at(start, size)
        former = jnp.dot(x_ref[...], gates[:, at], preferred_element_type=wide)
        latter = jnp.dot(x_ref[...], ups[:, at], preferred_element_type=wide)
        raw = dot_nt(grad_ref[...], downs[at, :])
        sig = 1.0 / (1.0 + jnp.exp(-former))
        act = former * sig
        low = (act * latter).astype(hidden.dtype)
        hidden[:, at] = low
        low = low.astype(wide)
        scaled_ref[:, at] = (low * gate).astype(hidden.dtype)
        grad = raw * gate
        d_gate_ref[:, at] = (grad * latter * (sig + act * (1.0 - sig))).astype(hidden.dtype)
        d_up_ref[:, at] = (grad * act).astype(hidden.dtype)
        return slots + jnp.sum(low * raw, axis=-1, keepdims=True)

    full = inner // 256
    slots = lax.fori_loop(
        0, full, lambda n, slots: columns(n * 256, 256, slots), jnp.zeros((rows, 1), wide)
    )
    if inner % 256:
        slots = columns(full * 256, inner % 256, slots)
    slot_ref[...] = jnp.broadcast_to(slots, slot_ref.shape)

    def outward(n, carry):
        at = lanes_at(n * 256, 256)
        back = dot_nt(d_gate_ref[...], gates[at, :]) + dot_nt(d_up_ref[...], ups[at, :])
        back_ref[:, at] = back.astype(back_ref.dtype)
        out = jnp.dot(hidden[...], downs[:, at], preferred_element_type=wide)
        out_ref[:, at] = (out * gate).astype(out_ref.dtype)
        return carry

    lax.fori_loop(0, width // 256, outward, 0)


def run_expert(rows, grads, gate_full, up_full, down_full, router, total):
    count, width = rows.shape
    inner = gate_full.shape[1]
    low, wide = rows.dtype, jnp.float32
    tile = count // 2
    anywhere = pl.BlockSpec(memory_space=pl.ANY)

    def tiles(span):
        return pl.BlockSpec((tile, span), lambda i: (i, 0))

    spans = (inner, inner, inner, width, width)
    return pl.pallas_call(
        functools.partial(expert_kernel, total),
        grid=(2,),
        out_shape=[jax.ShapeDtypeStruct((count, span), low) for span in spans]
        + [jax.ShapeDtypeStruct((count, 128), wide)],
        in_specs=[tiles(width), tiles(width)]
        + [anywhere] * 3
        + [pl.BlockSpec(router.shape, lambda i: (0, 0))],
        out_specs=[tiles(span) for span in spans] + [tiles(128)],
        scratch_shapes=[
            pltpu.VMEM(gate_full.shape, low),
            pltpu.VMEM(up_full.shape, low),
            pltpu.VMEM(down_full.shape, low),
            pltpu.VMEM((tile, inner), low),
            pltpu.SemaphoreType.DMA((3,)),
        ],
        compiler_params=pltpu.CompilerParams(vmem_limit_bytes=62 * MEBIBYTE),
        cost_estimate=MIDDLE,
    )(rows, grads, gate_full, up_full, down_full, router)


def return_kernel(depth, *refs):
    rows_in, scalars_in, choose_ref, shared_in = refs[:4]
    operands_in = refs[4:9]
    back_ref, prob_ref, gate_out, up_out, down_out = refs[9:14]
    came, scalars, shared, onward, incoming, prob_send, prob_land = refs[14:21]
    held = refs[21:26]
    give_wide, give_tall, take_wide, take_tall, done_wide, done_tall = refs[26:32]
    own_sem, es, er, ss, sr, load_sem, shared_sem, cs, cr, ps, pr = refs[32:43]
    ws, wr, ts, tr, wide_sem, tall_sem = refs[43:]
    x_held, gate_held, up_held, hidden_held, grad_held = held
    half = lax.axis_index("fsdp")
    place = lax.axis_index("expert")
    level = place // PLANE
    spot = place % PLANE
    other = (1 - half, place)
    tokens, width = back_ref.shape
    capacity = choose_ref.shape[2]
    wide_count, wide_rows = take_wide.shape[1:3]
    tall_count, tall_rows, tall_width = take_tall.shape
    greet(line_others(half, place, depth) + plane_others(half, place) + [other])

    def rows_to(offset, source):
        mate = (spot + offset) % PLANE
        where = (half, place - spot + mate)
        return (
            remote(
                rows_in.at[source, mate],
                came.at[spot, source],
                es.at[offset, source],
                er.at[offset, source],
                where,
            ),
            remote(
                scalars_in.at[source, mate],
                scalars.at[spot, source],
                ss.at[offset, source],
                sr.at[offset, source],
                where,
            ),
        )

    def rows_from(offset, source):
        mate = (spot + PLANE - offset) % PLANE
        where = (half, place - spot + mate)
        block, small = came.at[mate, source], scalars.at[mate, source]
        return (
            remote(block, block, es.at[offset, source], er.at[offset, source], where),
            remote(small, small, ss.at[offset, source], sr.at[offset, source], where),
        )

    def own_rows(source):
        return (
            pltpu.make_async_copy(
                rows_in.at[source, spot], came.at[spot, source], own_sem.at[0, source]
            ),
            pltpu.make_async_copy(
                scalars_in.at[source, spot], scalars.at[spot, source], own_sem.at[1, source]
            ),
        )

    def shared_load(slot, source):
        return pltpu.make_async_copy(shared_in.at[source], shared.at[slot], shared_sem.at[slot])

    def each_way(s, act):
        def one(way, carry):
            source = level + (2 * way - 1) * s

            @pl.when((source >= 0) & (source < depth) & ((s > 0) | (way == 0)))
            def _():
                act(way, source)

            return carry

        lax.fori_loop(0, 2, one, 0)

    def begin(way, source):
        for offset in range(1, PLANE):
            for copy in rows_to(offset, source):
                copy.start()
        for copy in own_rows(source):
            copy.start()

    def begin_step(i, carry):
        each_way(depth - 1 - i, begin)
        return carry

    lax.fori_loop(0, depth, begin_step, 0)
    loads = [
        pltpu.make_async_copy(source, target, load_sem.at[k])
        for k, (source, target) in enumerate(zip(operands_in, held))
    ]
    for load in loads:
        load.start()
    for load in loads:
        load.wait()

    def wide_tiles(owner, k):
        at = pl.ds(pl.multiple_of((owner * wide_count + k) * wide_rows, wide_rows), wide_rows)
        x = x_held[:, at]
        return dot_tn(x, gate_held[...]), dot_tn(x, up_held[...])

    def tall_tile(owner, k):
        at = pl.ds(pl.multiple_of(k * tall_rows, tall_rows), tall_rows)
        over = pl.ds(pl.multiple_of(owner * tall_width, tall_width), tall_width)
        return dot_tn(hidden_held[:, at], grad_held[:, over])

    def wide_send(which, k):
        slot = k % 2
        return remote(
            give_wide.at[slot, which],
            take_wide.at[which, k],
            ws.at[slot, which],
            wr.at[which, k],
            other,
        )

    def tall_send(k):
        slot = k % 2
        return remote(give_tall.at[slot], take_tall.at[k], ts.at[slot], tr.at[k], other)

    def wide_write(which, k):
        target = (gate_out, up_out)[which]
        at = pl.ds(pl.multiple_of(k * wide_rows, wide_rows), wide_rows)
        return pltpu.make_async_copy(done_wide.at[which], target.at[at, :], wide_sem.at[which])

    def tall_write(k):
        slot = k % 2
        at = pl.ds(pl.multiple_of(k * tall_rows, tall_rows), tall_rows)
        return pltpu.make_async_copy(done_tall.at[slot], down_out.at[at, :], tall_sem.at[slot])

    def give_wide_tile(k):
        @pl.when(k >= 2)
        def _():
            for which in range(2):
                wide_send(which, k - 2).wait_send()

        for which, tile in enumerate(wide_tiles(1 - half, k)):
            give_wide[k % 2, which] = tile.astype(give_wide.dtype)
            wide_send(which, k).start()

    def give_tall_tile(k):
        @pl.when(k >= 2)
        def _():
            tall_send(k - 2).wait_send()

        give_tall[k % 2] = tall_tile(1 - half, k).astype(give_tall.dtype)
        tall_send(k).start()

    def keep_wide_tile(k):
        @pl.when(k >= 1)
        def _():
            for which in range(2):
                wide_write(which, k - 1).wait()

        for which, tile in enumerate(wide_tiles(half, k)):
            wide_send(which, k).wait_recv()
            tile = tile + take_wide[which, k].astype(jnp.float32)
            done_wide[which] = tile.astype(done_wide.dtype)
            wide_write(which, k).start()

    def keep_tall_tile(k):
        @pl.when(k >= 2)
        def _():
            tall_write(k - 2).wait()

        tile = tall_tile(half, k)
        tall_send(k).wait_recv()
        tile = tile + take_tall[k].astype(jnp.float32)
        done_tall[k % 2] = tile.astype(done_tall.dtype)
        tall_write(k).start()

    units = 2 * (wide_count + tall_count)
    each = -(-units // depth)
    bounds = (0, wide_count, wide_count + tall_count, units - tall_count, units)
    acts = (give_wide_tile, give_tall_tile, keep_wide_tile, keep_tall_tile)

    def fill(unit, carry):
        for act, low, high in zip(acts, bounds[:-1], bounds[1:]):

            @pl.when((unit >= low) & (unit < high))
            def _():
                act(unit - low)

        return carry

    def chain_out(source):
        up = jnp.where(source > level, 1, 0)
        step = 2 * up - 1
        slot = jnp.where(source == level - 1, depth, source)
        return remote(
            onward.at[up],
            incoming.at[slot],
            cs.at[source],
            cr.at[slot],
            (half, place + step * PLANE),
        )

    def chain_in(slot):
        block = incoming.at[slot]
        return remote(block, block, cs.at[0], cr.at[slot], (half, place))

    def prob_to(source):
        return remote(
            prob_send.at[source],
            prob_land.at[level],
            ps.at[source],
            pr.at[level],
            (half, source * PLANE + spot),
        )

    def prob_from(source):
        block = prob_land.at[source]
        return remote(block, block, ps.at[source], pr.at[source], (half, source * PLANE + spot))

    def add_incoming(slot):
        chain_in(slot).wait_recv()
        back_ref[...] += incoming[slot].astype(jnp.float32)

    def settle(way, source):
        for copy in own_rows(source):
            copy.wait()
        for offset in range(1, PLANE):
            for copy in rows_from(offset, source):
                copy.wait_recv()
        shared_load(way, source).wait()

        def columns(n, carry):
            at = pl.ds(pl.multiple_of(n * 512, 512), 512)
            total = shared[way, :, at].astype(jnp.float32)
            for mate in range(PLANE):
                total = total + dot_tn(choose_ref[source, mate], came[mate, source, :, at])
            back_ref[:, at] = total
            return carry

        lax.fori_loop(0, width // 512, columns, 0)
        lines = lax.broadcasted_iota(jnp.int32, (8, tokens), 0)
        probs = jnp.zeros((8, tokens), jnp.float32)
        for mate in range(PLANE):
            part = lax.dot_general(
                scalars[mate, source],
                choose_ref[source, mate].astype(jnp.float32),
                (((0,), (0,)), ((), ())),
                preferred_element_type=jnp.float32,
                precision=lax.Precision.HIGHEST,
            )
            probs = jnp.where(lines == mate, part[:8], probs)

        @pl.when((source >= level) & (level > 0))
        def _():
            add_incoming(source)

        @pl.when((source < level) & (level < depth - 1))
        def _():
            add_incoming(source)

        @pl.when((source == level) & (level < depth - 1))
        def _():
            add_incoming(depth)

        @pl.when(source == level)
        def _():
            prob_land[level] = probs

        @pl.when(source != level)
        def _():
            prob_send[source] = probs
            prob_to(source).start()
            former = source + 2 * way - 1

            @pl.when((former >= 0) & (former < depth))
            def _():
                chain_out(former).wait_send()

            onward[way] = back_ref[...].astype(onward.dtype)
            chain_out(source).start()

    def step(i, carry):
        s = depth - 1 - i
        each_way(s, lambda way, source: shared_load(way, source).start())
        lax.fori_loop(i * each, jnp.minimum((i + 1) * each, units), fill, 0)
        each_way(s, settle)
        return carry

    lax.fori_loop(0, depth, step, 0)
    for which in range(2):
        wide_write(which, wide_count - 1).wait()
        for k in (wide_count - 2, wide_count - 1):
            wide_send(which, k).wait_send()
    for k in (tall_count - 2, tall_count - 1):
        tall_write(k).wait()
        tall_send(k).wait_send()

    def finish(source, carry):
        for offset in range(1, PLANE):
            for copy in rows_to(offset, source):
                copy.wait_send()

        @pl.when((source == level - 1) | (source == level + 1))
        def _():
            chain_out(source).wait_send()

        @pl.when(source != level)
        def _():
            prob_to(source).wait_send()
            prob_from(source).wait_recv()

        prob_ref[source] = prob_land[source]
        return carry

    lax.fori_loop(0, depth, finish, 0)


def give_back(rows, scalars, choose, shared_back, operands):
    depth, _, capacity, tokens = choose.shape
    width = rows.shape[-1]
    slots, inner = operands[1].shape
    wide_rows, tall_rows = 256 if depth <= PLANE else 128, 128
    wide_count = width // 2 // wide_rows
    tall_count = inner // tall_rows
    semaphores = pltpu.SemaphoreType.DMA
    low = rows.dtype
    wide = jnp.float32
    anywhere = pl.BlockSpec(memory_space=pl.ANY)
    local = pl.BlockSpec(memory_space=pltpu.VMEM)
    return pl.pallas_call(
        functools.partial(return_kernel, depth),
        out_shape=[
            jax.ShapeDtypeStruct((tokens, width), wide),
            jax.ShapeDtypeStruct((depth, 8, tokens), wide),
            jax.ShapeDtypeStruct((width // 2, inner), low),
            jax.ShapeDtypeStruct((width // 2, inner), low),
            jax.ShapeDtypeStruct((inner, width // 2), low),
        ],
        in_specs=[anywhere, anywhere, local, anywhere] + [anywhere] * 5,
        out_specs=[local, local, anywhere, anywhere, anywhere],
        scratch_shapes=[
            pltpu.VMEM((PLANE, depth, capacity, width), low),
            pltpu.VMEM((PLANE, depth, capacity, 128), wide),
            pltpu.VMEM((2, tokens, width), low),
            pltpu.VMEM((2, tokens, width), low),
            pltpu.VMEM((depth + 1, tokens, width), low),
            pltpu.VMEM((depth, 8, tokens), wide),
            pltpu.VMEM((depth, 8, tokens), wide),
        ]
        + [pltpu.VMEM(operand.shape, low) for operand in operands]
        + [
            pltpu.VMEM((2, 2, wide_rows, inner), low),
            pltpu.VMEM((2, tall_rows, width // 2), low),
            pltpu.VMEM((2, wide_count, wide_rows, inner), low),
            pltpu.VMEM((tall_count, tall_rows, width // 2), low),
            pltpu.VMEM((2, wide_rows, inner), low),
            pltpu.VMEM((2, tall_rows, width // 2), low),
            semaphores((2, depth)),
            semaphores((PLANE, depth)),
            semaphores((PLANE, depth)),
            semaphores((PLANE, depth)),
            semaphores((PLANE, depth)),
            semaphores((5,)),
            semaphores((2,)),
            semaphores((depth,)),
            semaphores((depth + 1,)),
            semaphores((depth,)),
            semaphores((depth,)),
            semaphores((2, 2)),
            semaphores((2, wide_count)),
            semaphores((2,)),
            semaphores((tall_count,)),
            semaphores((2,)),
            semaphores((2,)),
        ],
        compiler_params=pltpu.CompilerParams(
            collective_id=4, has_side_effects=True, vmem_limit_bytes=62 * MEBIBYTE
        ),
        cost_estimate=LONG,
    )(rows, scalars, choose, shared_back, *operands)


def reduce_kernel(depth, count, cut, *refs):
    parts = refs[:count]
    move_in, out_ref, move_out = refs[count : count + 3]
    acc, inc, one_a, one_b, two_a, two_b, zin = refs[count + 3 : count + 10]
    own_sem, cs, cr, ps, pr, qs, qr, zs, zr, move_sem, ms, mr = refs[count + 10 :]
    half = lax.axis_index("fsdp")
    place = lax.axis_index("expert")
    level = place // PLANE
    spot = place % PLANE
    total = depth * PLANE
    mates = plane_mates(place)
    rows = out_ref.shape[0]
    group = PLANE * rows
    width = out_ref.shape[1]
    greet_neighbours(half, place, depth)

    starts = [sum(part.shape[1] for part in parts[:k]) for k in range(count)]

    def rows_of(k, owner, t):
        start = pl.multiple_of((owner * total + t * PLANE) * rows, group)
        return parts[k].at[pl.ds(start, group), :]

    def kept(k, t):
        return pltpu.make_async_copy(
            rows_of(k, half, t),
            acc.at[t, :, pl.ds(starts[k], parts[k].shape[1])],
            own_sem.at[k, t],
        )

    def given(k, t):
        return remote(
            rows_of(k, 1 - half, t),
            inc.at[t, :, pl.ds(starts[k], parts[k].shape[1])],
            cs.at[k, t],
            cr.at[k, t],
            (1 - half, place),
        )

    def block(t, q, n, lo, hi):
        return acc.at[t, pl.ds(pl.multiple_of(q * rows, rows), n * rows), pl.ds(lo, hi - lo)]

    pair = spot - spot % 2

    def first(t, turn):
        low = spot % 2
        if turn == 0:
            source = block(t, 2 - pair, 2, 0, cut)
            target, where = one_a.at[t], mates[1]
        else:
            source = block(t, 2 * turn - 1 - low, 1, cut, width)
            target, where = one_b.at[t, turn - 1], mates[0]
        return remote(source, target, ps.at[turn, t], pr.at[turn, t], (half, where))

    def second(t, turn):
        if turn == 0:
            source = block(t, pair + 1 - spot % 2, 1, 0, cut)
            target, where = two_a.at[t], mates[0]
        else:
            source = block(t, (spot + 2) % PLANE, 1, cut, width)
            target, where = two_b.at[t], mates[1]
        return remote(source, target, qs.at[turn, t], qr.at[turn, t], (half, where))

    def line(t, way):
        step = 2 * way - 1
        return remote(
            block(t, spot, 1, 0, width),
            zin.at[way, t],
            zs.at[way, t],
            zr.at[way, t],
            (half, place + step * PLANE),
        )

    def add_rows(t, start, n, lo, hi, piece):
        def one(i, carry):
            r = pl.multiple_of(i * 16, 16)
            at = (t, pl.ds(pl.multiple_of(start + r, 16), 16), pl.ds(lo, hi - lo))
            new = piece(pl.ds(r, 16)).astype(jnp.float32)
            acc[at] = (acc[at].astype(jnp.float32) + new).astype(acc.dtype)
            return carry

        lax.fori_loop(0, n // 16, one, 0)

    def stage_a(t):
        for k in range(count):
            kept(k, t).wait()
            given(k, t).wait_recv()
        add_rows(t, 0, group, 0, width, lambda r: inc[t, r, :])
        for turn in range(3):
            first(t, turn).start()

    def stage_b(t):
        first(t, 0).wait_recv()
        add_rows(t, pair * rows, 2 * rows, 0, cut, lambda r: one_a[t, r, :])
        second(t, 0).start()
        for turn in range(2):
            first(t, 1 + turn).wait_recv()
            add_rows(
                t,
                (spot % 2 + 2 * turn) * rows,
                rows,
                cut,
                width,
                lambda r: one_b[t, turn, r, :],
            )
        second(t, 1).start()

    def stage_c(t):
        second(t, 0).wait_recv()
        add_rows(t, spot * rows, rows, 0, cut, lambda r: two_a[t, r, :])
        second(t, 1).wait_recv()
        add_rows(t, spot * rows, rows, cut, width, lambda r: two_b[t, r, :])

        def take(way):
            line(t, way).wait_recv()
            add_rows(t, spot * rows, rows, 0, width, lambda r: zin[way, t, r, :])

        @pl.when((t >= level) & (level > 0))
        def _():
            take(1)

        @pl.when((t <= level) & (level < depth - 1))
        def _():
            take(0)

        @pl.when(t > level)
        def _():
            line(t, 1).start()

        @pl.when(t < level)
        def _():
            line(t, 0).start()

    def visit(index, act):
        if index >= depth or index < 0:
            return
        step = depth - 1 - index
        if step == 0:
            act(level)
            return

        @pl.when(level + step < depth)
        def _():
            act(level + step)

        @pl.when(level - step >= 0)
        def _():
            act(level - step)

    def begin(t):
        for k in range(count):
            given(k, t).start()
            kept(k, t).start()

    for index in range(depth):
        visit(index, begin)
    move_start, move_finish = exchange_along(
        depth,
        half,
        place,
        move_in,
        lambda source: move_out.at[source],
        move_sem.at[0],
        ms,
        mr,
    )
    move_start()
    for index in range(depth + 2):
        visit(index, stage_a)
        visit(index - 1, stage_b)
        visit(index - 2, stage_c)

    def emit(i, carry):
        r = pl.multiple_of(i * 16, 16)
        at = pl.ds(pl.multiple_of(spot * rows + r, 16), 16)
        out_ref[pl.ds(r, 16), :] = acc[level, at, :].astype(out_ref.dtype)
        return carry
    lax.fori_loop(0, rows // 16, emit, 0)
    move_finish()

    def finish(t, carry):
        for k in range(count):
            given(k, t).wait_send()
        for turn in range(3):
            first(t, turn).wait_send()
        for turn in range(2):
            second(t, turn).wait_send()

        @pl.when(t > level)
        def _():
            line(t, 1).wait_send()

        @pl.when(t < level)
        def _():
            line(t, 0).wait_send()
        return carry

    lax.fori_loop(0, depth, finish, 0)


def reduce_rows(parts, moved, cut):
    total = lax.axis_size("expert")
    depth = total // PLANE
    rows = parts[0].shape[0] // (2 * total)
    width = sum(part.shape[1] for part in parts)
    group = PLANE * rows
    n = len(parts)
    semaphores = pltpu.SemaphoreType.DMA
    low = parts[0].dtype
    return pl.pallas_call(
        functools.partial(reduce_kernel, depth, n, cut),
        out_shape=[
            jax.ShapeDtypeStruct((rows, width), jnp.float32),
            jax.ShapeDtypeStruct(moved.shape, moved.dtype),
        ],
        in_specs=[pl.BlockSpec(memory_space=pl.ANY)] * (n + 1),
        out_specs=[
            pl.BlockSpec(memory_space=pltpu.VMEM),
            pl.BlockSpec(memory_space=pl.ANY),
        ],
        scratch_shapes=[
            pltpu.VMEM((depth, group, width), low),
            pltpu.VMEM((depth, group, width), low),
            pltpu.VMEM((depth, 2 * rows, cut), low),
            pltpu.VMEM((depth, 2, rows, width - cut), low),
            pltpu.VMEM((depth, rows, cut), low),
            pltpu.VMEM((depth, rows, width - cut), low),
            pltpu.VMEM((2, depth, rows, width), low),
            semaphores((n, depth)),
            semaphores((n, depth)),
            semaphores((n, depth)),
            semaphores((3, depth)),
            semaphores((3, depth)),
            semaphores((2, depth)),
            semaphores((2, depth)),
            semaphores((2, depth)),
            semaphores((2, depth)),
            semaphores((1,)),
            semaphores((depth,)),
            semaphores((depth,)),
        ],
        cost_estimate=LONG,
        compiler_params=pltpu.CompilerParams(
            collective_id=2, has_side_effects=True, vmem_limit_bytes=60 * MEBIBYTE
        ),
    )(*parts, moved)


def turned(values):
    width = values.shape[1]
    lanes = lax.broadcasted_iota(jnp.int32, values.shape, 1)
    return jnp.where(
        lanes % ROPE < ROPE // 2,
        pltpu.roll(values, width - ROPE // 2, 1),
        pltpu.roll(values, ROPE // 2, 1),
    )


def row_scale(values):
    return lax.rsqrt(jnp.mean(values * values, axis=-1, keepdims=True) + EPSILON)


def head_lanes(values, head):
    lanes = lax.broadcasted_iota(jnp.int32, values.shape, 1)
    return jnp.where(lanes // ROPE == head % 2, values, jnp.zeros_like(values))


def lanes_at(start, size):
    return pl.ds(pl.multiple_of(start, 128), size)


def attend_kernel(layout, *refs):
    x_ref, packed, up_in, first_gain, latent_gain, feed_gain, cosine, sine, mask = refs[:9]
    choose_ref, grad_in = refs[9:11]
    normed, residual, mixed, queries, latent, compressed = refs[11:17]
    expanded, keys_rope, log_total, heads, grad_out = refs[17:22]
    entry, ups, outs, prior_latent, prior_rope, grads, grad_placed = refs[22:29]
    load_sem, up_sem, send_sem, receive_sem, gl, gs, gr, grad_sem = refs[29:]
    entry_width, out_start = layout
    half = lax.axis_index("fsdp")
    place = lax.axis_index("expert")
    other = (1 - half, place)
    rows, width = x_ref.shape
    low = x_ref.dtype
    scale = (NOPE + ROPE) ** (-0.5)
    loads = [
        pltpu.make_async_copy(packed.at[:, pl.ds(0, entry_width)], entry, load_sem.at[0]),
        pltpu.make_async_copy(packed.at[:, pl.ds(out_start, width)], outs, load_sem.at[1]),
    ]
    up_loads = load_ups(up_in, ups, up_sem, layout)
    depth = grad_in.shape[0]

    def grad_load(n):
        return pltpu.make_async_copy(grad_in.at[2 * n], grads.at[n], gl.at[n])

    grad_start, grad_finish = exchange_plane(
        half,
        place,
        lambda mate, source: grad_placed.at[source // 2, mate],
        lambda mate, source: grad_out.at[source, mate],
        grad_sem,
        gs,
        gr,
    )

    def each_grad(act):
        def one(n, carry):
            act(n)
            return carry

        lax.fori_loop(0, depth // 2, one, 0)

    def give_grad(n):
        grad_load(n).wait()
        place_rows(choose_ref, 2 * n, grads.at[n], grad_placed.at[n])
        grad_start(2 * n)

    each_grad(lambda n: grad_load(n).start())
    for load in loads[:1] + up_loads + loads[1:]:
        load.start()
    greet([other] + plane_others(half, place))
    each_grad(give_grad)
    x = x_ref[...].astype(jnp.float32)
    normed[...] = (x * row_scale(x) * first_gain[...]).astype(low)
    loads[0].wait()
    nope_width = HEADS * NOPE
    query_width = HEADS * (NOPE + ROPE)

    def through(start, size):
        return jnp.dot(
            normed[...], entry[:, lanes_at(start, size)], preferred_element_type=jnp.float32
        )

    def rotary(values):
        return values * cosine[...] + turned(values) * sine[...]

    squeezed = through(query_width, LATENT)
    compressed[...] = squeezed
    latent[...] = (squeezed * row_scale(squeezed) * latent_gain[...]).astype(low)
    key = rotary(through(query_width + LATENT, 128))
    keys_rope[pl.ds(rows, rows), :] = (key + pltpu.roll(key, ROPE, 1)).astype(low)
    sends = [
        remote(latent, prior_latent, send_sem.at[0], receive_sem.at[0], other),
        remote(
            keys_rope.at[pl.ds(rows, rows), :],
            prior_rope,
            send_sem.at[1],
            receive_sem.at[1],
            other,
        ),
    ]

    @pl.when(half == 0)
    def _():
        for send in sends:
            send.start()

    def nope_part(n, carry):
        queries[:, lanes_at(n * 1024, 1024)] = through(n * 1024, 1024).astype(low)
        return carry

    lax.fori_loop(0, nope_width // 1024, nope_part, 0)

    def rope_part(n, carry):
        values = through(nope_width + n * 512, 512)
        for k in range(4):
            tile = rotary(values[:, k * 128 : (k + 1) * 128])
            queries[:, lanes_at(nope_width + n * 512 + k * 128, 128)] = tile.astype(low)
        return carry

    lax.fori_loop(0, HEADS * ROPE // 512, rope_part, 0)
    for load in up_loads:
        load.wait()
    quarters, span = ups.shape[0], ups.shape[-1]

    def expand(source, first):
        def one(n, carry):
            expanded[pl.ds(first, rows), lanes_at(n * span, span)] = jnp.dot(
                source[...], whole(ups[n]), preferred_element_type=jnp.float32
            ).astype(low)
            return carry

        lax.fori_loop(0, quarters, one, 0)

    expand(latent, rows)

    @pl.when(half == 0)
    def _():
        expanded[pl.ds(0, rows), :] = jnp.zeros((rows, quarters * span), low)
        keys_rope[pl.ds(0, rows), :] = jnp.zeros((rows, 128), low)
        for send in sends:
            send.wait_send()

    @pl.when(half == 1)
    def _():
        for send in sends:
            send.wait_recv()
        keys_rope[pl.ds(0, rows), :] = prior_rope[...]
        expand(prior_latent, 0)

    def head(h, totals):
        pair = queries[:, lanes_at(nope_width + (h // 2) * 128, 128)]
        scores = dot_nt(
            queries[:, lanes_at(h * NOPE, NOPE)], expanded[:, lanes_at(h * 256, NOPE)]
        )
        scores = scores + dot_nt(head_lanes(pair, h), keys_rope[...])
        scores = jnp.where(mask[...] > 0, scores * scale, FLOOR_SCORE)
        top = jnp.max(scores, axis=-1, keepdims=True)
        weights = jnp.exp(scores - top)
        total = jnp.sum(weights, axis=-1, keepdims=True)
        heads[:, lanes_at(h * VALUE, VALUE)] = jnp.dot(
            (weights / total).astype(low),
            expanded[:, lanes_at(h * 256 + NOPE, VALUE)],
            preferred_element_type=jnp.float32,
        ).astype(low)
        lanes = lax.broadcasted_iota(jnp.int32, totals.shape, 1)
        return jnp.where(lanes == h, top + jnp.log(total), totals)

    log_total[...] = lax.fori_loop(0, HEADS, head, jnp.zeros((rows, 128), jnp.float32))
    loads[1].wait()

    def project(n, carry):
        at = lanes_at(n * 1024, 1024)
        residual[:, at] = x_ref[:, at].astype(jnp.float32) + jnp.dot(
            heads[...], outs[:, at], preferred_element_type=jnp.float32
        )
        return carry

    lax.fori_loop(0, width // 1024, project, 0)
    total = residual[...]
    mixed[...] = (total * row_scale(total) * feed_gain[...]).astype(low)
    each_grad(lambda n: grad_finish(2 * n))


def attend(x, packed, ups, ups_shape, gains, tables, mask, choose, grad_line, layout):
    rows, width = x.shape
    low, wide = x.dtype, jnp.float32
    semaphores = pltpu.SemaphoreType.DMA
    anywhere = pl.BlockSpec(memory_space=pl.ANY)
    local = pl.BlockSpec(memory_space=pltpu.VMEM)
    expanded_width = HEADS * (NOPE + VALUE)
    depth, _, capacity, _ = choose.shape
    shapes = [
        ((rows, width), low),
        ((rows, width), wide),
        ((rows, width), low),
        ((rows, HEADS * (NOPE + ROPE)), low),
        ((rows, LATENT), low),
        ((rows, LATENT), wide),
        ((2 * rows, expanded_width), low),
        ((2 * rows, 128), low),
        ((rows, 128), wide),
        ((rows, HEADS * VALUE), low),
        ((depth, PLANE, capacity, width), low),
    ]
    return pl.pallas_call(
        functools.partial(attend_kernel, layout),
        out_shape=[jax.ShapeDtypeStruct(shape, dtype) for shape, dtype in shapes],
        in_specs=[local, anywhere, anywhere] + [local] * 7 + [anywhere],
        out_specs=[local] * (len(shapes) - 1) + [anywhere],
        scratch_shapes=[
            pltpu.VMEM((packed.shape[0], layout[0]), low),
            pltpu.VMEM(ups_shape, low),
            pltpu.VMEM((packed.shape[0], width), low),
            pltpu.VMEM((rows, LATENT), low),
            pltpu.VMEM((rows, 128), low),
            pltpu.VMEM((depth // 2, rows, width), low),
            pltpu.VMEM((depth // 2, PLANE, capacity, width), low),
            semaphores((2,)),
            semaphores((ups_shape[0],)),
            semaphores((2,)),
            semaphores((2,)),
            semaphores((depth // 2,)),
            semaphores((PLANE, depth)),
            semaphores((PLANE, depth)),
            semaphores((depth,)),
        ],
        compiler_params=pltpu.CompilerParams(
            collective_id=5, has_side_effects=True, vmem_limit_bytes=56 * MEBIBYTE
        ),
        cost_estimate=MIDDLE,
    )(x, packed, ups, *gains, *tables, mask, choose, grad_line)


def load_ups(up_in, ups, sem, layout):
    if up_in.shape == ups.shape:
        return [pltpu.make_async_copy(up_in, ups, sem.at[0])]
    span = ups.shape[-1]
    return [
        pltpu.make_async_copy(
            up_in.at[:, k, :, pl.ds(layout[0], span)], ups.at[k], sem.at[k]
        )
        for k in range(ups.shape[0])
    ]


def whole(block):
    return block.reshape(-1, block.shape[-1])


def attend_back_kernel(layout, count, *refs):
    back_in, packed, up_in, queries, expanded, keys_rope, log_total = refs[:7]
    latent, compressed, normed, heads, x_ref, residual, cotangent = refs[7:14]
    d_logits, router, latent_gain, first_gain, feed_gain, cosine, sine, mask = refs[14:22]
    rows_in = refs[22]
    refs = refs[24 + count :]
    token_grad, up_grad, gain_grad, first_grad, feed_grad, entry_grad, out_grad = refs[:7]
    rows_out, outs, ups, d_heads, own, prior, came, prior_rope, came_rope = refs[7:16]
    entry, entry_low, up_tile, entry_tile, out_tile, d_ref = refs[16:22]
    load_sem, up_sem, send_sem, receive_sem, write_sem, es, er = refs[22:]
    entry_width, out_start = layout
    half = lax.axis_index("fsdp")
    place = lax.axis_index("expert")
    other = (1 - half, place)
    rows, width = d_ref.shape
    low = d_ref.dtype
    wide = jnp.float32
    scale = (NOPE + ROPE) ** (-0.5)

    def norm_back(values, gain, incoming):
        root = row_scale(values)
        scaled = gain * incoming
        inner = jnp.mean(values * scaled, axis=-1, keepdims=True)
        gain_sum = jnp.sum(incoming * values * root, axis=0, keepdims=True)
        return root * scaled - values * (root * root * root) * inner, gain_sum

    nope_width = HEADS * NOPE
    query_width = HEADS * (NOPE + ROPE)
    loads = [
        pltpu.make_async_copy(packed.at[:, pl.ds(out_start, width)], outs, load_sem.at[0]),
        pltpu.make_async_copy(packed.at[:, pl.ds(0, entry_width)], entry, load_sem.at[1]),
    ]
    up_loads = load_ups(up_in, ups, up_sem, layout)
    for load in loads + up_loads:
        load.start()
    greet([other] + plane_others(half, place))
    rows_start, rows_finish = exchange_plane(
        half,
        place,
        lambda mate, level: rows_in.at[level, mate],
        lambda mate, level: rows_out.at[level, mate],
        None,
        es,
        er,
        own_there=True,
    )

    def each_level(act):
        def one(level, carry):
            act(level)
            return carry

        lax.fori_loop(0, rows_in.shape[0], one, 0)

    each_level(rows_start)
    mixed_grad = back_in[...] + dot_nt(d_logits[...], router[...])
    through_norm, gain_sum = norm_back(residual[...], feed_gain[...], mixed_grad)
    feed_grad[...] = jnp.broadcast_to(gain_sum, feed_grad.shape)
    token_grad[...] = cotangent[...].astype(wide) + through_norm
    d_ref[...] = token_grad[...].astype(low)

    def write(kind, k):
        staged, target = ((out_tile, out_grad), (entry_tile, entry_grad), (up_tile, up_grad))[kind]
        size = staged.shape[1]
        if kind == 2:
            place_at = up_grad.at[k] if up_grad.shape[0] == ups.shape[0] else up_grad.at[:, k]
        else:
            place_at = target.at[pl.ds(pl.multiple_of(k * size, size), size), :]
        return pltpu.make_async_copy(
            staged.at[k % 2], place_at, write_sem.at[kind, k % 2]
        )

    def put(kind, k, value):
        staged = (out_tile, entry_tile, up_tile)[kind]

        @pl.when(k >= 2)
        def _():
            write(kind, k - 2).wait()

        staged[k % 2] = value.astype(low).reshape(staged.shape[1:])
        write(kind, k).start()

    def settle(kind, total):
        for k in range(max(0, total - 2), total):
            write(kind, k).wait()

    def out_part(k, carry):
        size = out_tile.shape[1]
        put(0, k, dot_tn(heads[:, lanes_at(k * size, size)], d_ref[...]))
        return carry

    out_count = heads.shape[1] // out_tile.shape[1]
    lax.fori_loop(0, out_count, out_part, 0)
    loads[0].wait()

    def head_part(n, carry):
        at = lanes_at(n * 1024, 1024)
        d_heads[:, at] = dot_nt(d_ref[...], outs[at, :]).astype(low)
        return carry

    lax.fori_loop(0, width // 1024, head_part, 0)

    def turn_back(values):
        return values * cosine[...] - turned(values) * sine[...]

    def pair_of_heads(n, rope_sum):
        pair = queries[:, lanes_at(nope_width + n * 128, 128)]
        query_rope = jnp.zeros((rows, 128), wide)
        for k in range(2):
            h = 2 * n + k
            query = queries[:, lanes_at(h * NOPE, NOPE)]
            key = expanded[:, lanes_at(h * 256, NOPE)]
            value = expanded[:, lanes_at(h * 256 + NOPE, VALUE)]
            d_head = d_heads[:, lanes_at(h * VALUE, VALUE)]
            own_pair = head_lanes(pair, k)
            scores = dot_nt(query, key) + dot_nt(own_pair, keys_rope[...])
            scores = jnp.where(mask[...] > 0, scores * scale, FLOOR_SCORE)
            lanes = lax.broadcasted_iota(jnp.int32, log_total.shape, 1)
            log_sum = jnp.sum(
                jnp.where(lanes == h, log_total[...], 0.0), axis=-1, keepdims=True
            )
            probs = jnp.exp(scores - log_sum)
            d_probs = dot_nt(d_head, value)
            delta = jnp.sum(probs * d_probs, axis=-1, keepdims=True)
            d_scores = (probs * (d_probs - delta)).astype(low)
            entry_low[:, lanes_at(h * NOPE, NOPE)] = (
                jnp.dot(d_scores, key, preferred_element_type=wide) * scale
            ).astype(low)
            query_rope = query_rope + head_lanes(
                jnp.dot(d_scores, keys_rope[...], preferred_element_type=wide), k
            )
            d_key = dot_tn(d_scores, query) * scale
            d_value = dot_tn(probs.astype(low), d_head)
            own[:, lanes_at(h * 256, NOPE)] = d_key[rows:]
            own[:, lanes_at(h * 256 + NOPE, VALUE)] = d_value[rows:]
            prior[:, lanes_at(h * 256, NOPE)] = d_key[:rows].astype(low)
            prior[:, lanes_at(h * 256 + NOPE, VALUE)] = d_value[:rows].astype(low)
            rope_sum = rope_sum + dot_tn(d_scores, own_pair)
        entry_low[:, lanes_at(nope_width + n * 128, 128)] = (
            turn_back(query_rope) * scale
        ).astype(low)
        return rope_sum

    rope_sum = lax.fori_loop(
        0, HEADS // 2, pair_of_heads, jnp.zeros((2 * rows, 128), wide)
    )
    rope_sum = (rope_sum + pltpu.roll(rope_sum, ROPE, 1)) * scale
    prior_rope[...] = rope_sum[:rows].astype(low)
    sends = [
        remote(prior, came, send_sem.at[0], receive_sem.at[0], other),
        remote(prior_rope, came_rope, send_sem.at[1], receive_sem.at[1], other),
    ]

    @pl.when(half == 1)
    def _():
        for send in sends:
            send.start()
        came_rope[...] = jnp.zeros((rows, 128), low)
        for send in sends:
            send.wait_send()
        prior[...] = own[...].astype(low)

    @pl.when(half == 0)
    def _():
        for send in sends:
            send.wait_recv()
        prior[...] = (own[...] + came[...].astype(wide)).astype(low)

    for load in up_loads:
        load.wait()
    quarters, span = ups.shape[0], ups.shape[-1]

    def spread(n, d_latent):
        part = prior[:, lanes_at(n * span, span)]
        put(2, n, dot_tn(latent[...], part))
        return d_latent + dot_nt(part, whole(ups[n]))

    d_latent = lax.fori_loop(0, quarters, spread, jnp.zeros((rows, LATENT), wide))
    d_squeezed, gain_sum = norm_back(compressed[...], latent_gain[...], d_latent)
    gain_grad[...] = jnp.broadcast_to(gain_sum, gain_grad.shape)
    entry_low[:, lanes_at(query_width, LATENT)] = d_squeezed.astype(low)
    key = rope_sum[rows:] + came_rope[...].astype(wide)
    entry_low[:, lanes_at(query_width + LATENT, 128)] = turn_back(head_lanes(key, 0)).astype(low)

    def entry_part(k, carry):
        size = entry_tile.shape[1]
        put(1, k, dot_tn(normed[:, lanes_at(k * size, size)], entry_low[...]))
        return carry

    entry_count = width // entry_tile.shape[1]
    lax.fori_loop(0, entry_count, entry_part, 0)
    loads[1].wait()

    def normed_part(n, carry):
        at = lanes_at(n * 1024, 1024)
        own[:, at] = dot_nt(entry_low[...], entry[at, :])
        return carry

    lax.fori_loop(0, width // 1024, normed_part, 0)
    through_norm, gain_sum = norm_back(
        x_ref[...].astype(wide), first_gain[...], own[:, pl.ds(0, width)]
    )
    first_grad[...] = jnp.broadcast_to(gain_sum, first_grad.shape)
    token_grad[...] += through_norm
    settle(0, out_count)
    settle(1, entry_count)
    settle(2, quarters)
    each_level(rows_finish)


def attend_back(
    back, packed, ups, ups_shape, kept, gains, tables, mask, returning, before, layout
):
    rows, width = back.shape
    low, wide = packed.dtype, jnp.float32
    semaphores = pltpu.SemaphoreType.DMA
    anywhere = pl.BlockSpec(memory_space=pl.ANY)
    local = pl.BlockSpec(memory_space=pltpu.VMEM)
    expanded_width = HEADS * (NOPE + VALUE)
    quarters, blocks, part, span = ups_shape
    up_grad = (blocks, quarters, part, span) if blocks > 1 else ups_shape
    return pl.pallas_call(
        functools.partial(attend_back_kernel, layout, len(before)),
        out_shape=[
            jax.ShapeDtypeStruct((rows, width), wide),
            jax.ShapeDtypeStruct(up_grad, low),
            jax.ShapeDtypeStruct((8, LATENT), wide),
            jax.ShapeDtypeStruct((8, width), wide),
            jax.ShapeDtypeStruct((8, width), wide),
            jax.ShapeDtypeStruct((width, layout[0]), low),
            jax.ShapeDtypeStruct((HEADS * VALUE, width), low),
            jax.ShapeDtypeStruct(returning[0].shape, low),
        ],
        in_specs=[local, anywhere, anywhere]
        + [local] * (len(kept) + len(gains) + len(tables) + 1)
        + [anywhere] * (2 + len(before)),
        out_specs=[local, anywhere] + [local] * 3 + [anywhere] * 3,
        input_output_aliases={23: 7},
        scratch_shapes=[
            pltpu.VMEM((packed.shape[0], width), low),
            pltpu.VMEM(ups_shape, low),
            pltpu.VMEM((rows, HEADS * VALUE), low),
            pltpu.VMEM((rows, expanded_width), wide),
            pltpu.VMEM((rows, expanded_width), low),
            pltpu.VMEM((rows, expanded_width), low),
            pltpu.VMEM((rows, 128), low),
            pltpu.VMEM((rows, 128), low),
            pltpu.VMEM((packed.shape[0], layout[0]), low),
            pltpu.VMEM((rows, layout[0]), low),
            pltpu.VMEM((2,) + ups_shape[1:], low),
            pltpu.VMEM((2, 128, layout[0]), low),
            pltpu.VMEM((2, 128, width), low),
            pltpu.VMEM((rows, width), low),
            semaphores((2,)),
            semaphores((quarters,)),
            semaphores((2,)),
            semaphores((2,)),
            semaphores((3, 2)),
            semaphores((PLANE, returning[0].shape[0])),
            semaphores((PLANE, returning[0].shape[0])),
        ],
        compiler_params=pltpu.CompilerParams(
            collective_id=6, has_side_effects=True, vmem_limit_bytes=62 * MEBIBYTE
        ),
        cost_estimate=LONG,
    )(back, packed, ups, *kept, *gains, *tables, mask, *returning, *before)


def run_and_return_kernel(depth, total, *refs):
    x_in, grad_in, gate_in, up_in, down_in, router_ref, choose_ref, shared_in = refs[:8]
    back_ref, prob_ref, gate_out, up_out, down_out, y_out, y_own = refs[8:15]
    came, scalars, shared, onward, incoming, prob_send, prob_land = refs[15:22]
    x_held, gate_held, up_held, hidden_held, grad_held, hidden = refs[22:28]
    gates, ups, downs, sent, scalars_sent, y_stage = refs[28:34]
    es, er, ss, sr, load_sem, shared_sem, cs, cr, ps, pr = refs[34:44]
    ws, wr, ts, tr, wide_sem, tall_sem, y_sem, free_sem = refs[44:]
    half = lax.axis_index("fsdp")
    place = lax.axis_index("expert")
    level = place // PLANE
    spot = place % PLANE
    other = (1 - half, place)
    tokens, width = back_ref.shape
    capacity = choose_ref.shape[2]
    inner = gates.shape[1]
    wide_rows, tall_rows, tall_width = 256, 128, width // 2
    wide_count, tall_count = width // 2 // wide_rows, inner // tall_rows
    wide = jnp.float32

    def take_wide(which, k):
        at = pl.multiple_of((which * wide_count + k) * wide_rows, wide_rows)
        return gates.at[pl.ds(at, wide_rows), :]

    def take_tall(k):
        at = pl.multiple_of(k * tall_rows, tall_rows)
        return ups.at[pl.ds(at, tall_rows), pl.ds(0, tall_width)]

    def give_wide(slot, which):
        at = pl.multiple_of((slot * 2 + which) * wide_rows, wide_rows)
        return downs.at[pl.ds(at, wide_rows), pl.ds(0, inner)]

    def give_tall(slot):
        at = pl.multiple_of(4 * wide_rows + slot * tall_rows, tall_rows)
        return downs.at[pl.ds(at, tall_rows), pl.ds(0, tall_width)]

    def done_wide(which):
        return ups.at[pl.ds(tall_count * tall_rows + which * wide_rows, wide_rows), :]

    def done_tall(slot):
        at = pl.multiple_of(slot * tall_width, tall_width)
        return downs.at[pl.ds(4 * wide_rows + 2 * tall_rows, tall_rows), pl.ds(at, tall_width)]

    greet(line_others(half, place, depth) + plane_others(half, place) + [other])

    def rows_to(offset, way, source):
        mate = (spot + offset) % PLANE
        where = (half, place - spot + mate)
        return (
            remote(
                sent.at[way, mate],
                came.at[spot, source],
                es.at[offset, source],
                er.at[offset, source],
                where,
            ),
            remote(
                scalars_sent.at[way, mate],
                scalars.at[spot, source],
                ss.at[offset, source],
                sr.at[offset, source],
                where,
            ),
        )

    def rows_from(offset, source):
        mate = (spot + PLANE - offset) % PLANE
        where = (half, place - spot + mate)
        block, small = came.at[mate, source], scalars.at[mate, source]
        return (
            remote(block, block, es.at[offset, source], er.at[offset, source], where),
            remote(small, small, ss.at[offset, source], sr.at[offset, source], where),
        )

    def shared_load(slot, source):
        return pltpu.make_async_copy(shared_in.at[source], shared.at[slot], shared_sem.at[slot])

    def each_way(s, act):
        def one(way, carry):
            source = level + (2 * way - 1) * s

            @pl.when((source >= 0) & (source < depth) & ((s > 0) | (way == 0)))
            def _():
                act(way, source)

            return carry

        lax.fori_loop(0, 2, one, 0)

    loads = [
        pltpu.make_async_copy(source, target, load_sem.at[k])
        for k, (source, target) in enumerate(
            (
                (x_in, x_held),
                (gate_in, gates),
                (up_in, ups),
                (grad_in, grad_held),
                (down_in, downs),
            )
        )
    ]
    for load in loads:
        load.start()
    earliest = jnp.where(2 * level >= depth - 1, 0, depth - 1)

    def slot_of(way, source):
        return way + 2 * ((source + level) % 2)

    def compute(way, source):
        def need(*which):
            @pl.when(source == earliest)
            def _():
                for k in which:
                    loads[k].wait()

        need(0)
        slot = slot_of(way, source)
        x = x_held.at[source]
        logits = jnp.dot(x[...], router_ref[...], preferred_element_type=wide)
        lanes = lax.broadcasted_iota(jnp.int32, logits.shape, 1)
        logits = jnp.where(lanes < total, logits, FLOOR_SCORE)
        powers = jnp.exp(logits - jnp.max(logits, axis=-1, keepdims=True))
        probs = powers / jnp.sum(powers, axis=-1, keepdims=True)
        gate = jnp.sum(jnp.where(lanes == place, probs, 0.0), axis=-1, keepdims=True)

        def columns(start, size, slots):
            at = lanes_at(start, size)
            if start == 0:
                need(1)
            former_part = jnp.dot(x[...], gates[:, at], preferred_element_type=wide)
            if start == 0:
                need(2)
            latter_part = jnp.dot(x[...], ups[:, at], preferred_element_type=wide)
            if start == 0:
                need(3, 4)
            raw = dot_nt(grad_held[source], downs[at, :])
            sig = 1.0 / (1.0 + jnp.exp(-former_part))
            act = former_part * sig
            low = (act * latter_part).astype(hidden.dtype)
            hidden[:, at] = low
            low = low.astype(wide)
            hidden_held[source, :, at] = (low * gate).astype(hidden.dtype)
            grad = raw * gate
            d_gate = grad * latter_part * (sig + act * (1.0 - sig))
            gate_held[source, :, at] = d_gate.astype(hidden.dtype)
            up_held[source, :, at] = (grad * act).astype(hidden.dtype)
            return slots + jnp.sum(low * raw, axis=-1, keepdims=True)

        slots = jnp.zeros((PLANE * capacity, 1), wide)
        step_size = 640
        for start in range(0, inner, step_size):
            slots = columns(start, min(step_size, inner - start), slots)

        def blocks(value):
            return [value[m * capacity : (m + 1) * capacity] for m in range(PLANE)]

        former = source + 2 * (2 * way - 1)

        @pl.when((former >= 0) & (former < depth))
        def _():
            for offset in range(1, PLANE):
                for copy in rows_to(offset, slot, former):
                    copy.wait_send()

        for m, block in enumerate(blocks(slots)):
            spread = jnp.broadcast_to(block, (capacity, 128))
            scalars_sent[slot, m] = spread

            @pl.when(spot == m)
            def _():
                scalars[m, source] = spread

        def outward(n, carry):
            at = lanes_at(n * 1024, 1024)
            back = dot_nt(gate_held[source], gates[at, :]) + dot_nt(up_held[source], ups[at, :])
            for m, block in enumerate(blocks(back)):
                sent[slot, m, :, at] = block.astype(sent.dtype)

                @pl.when(spot == m)
                def _():
                    came[m, source, :, at] = block.astype(came.dtype)

            return carry

        lax.fori_loop(0, width // 1024, outward, 0)
        for offset in range(1, PLANE):
            for copy in rows_to(offset, slot, source):
                copy.start()

        def finally_out(n, carry):
            at = lanes_at(n * 1024, 1024)
            out = jnp.dot(hidden[...], downs[:, at], preferred_element_type=wide) * gate
            for m, block in enumerate(blocks(out)):
                y_stage[m, :, at] = block.astype(y_stage.dtype)
            return carry

        lax.fori_loop(0, width // 1024, finally_out, 0)
        writes = [
            pltpu.make_async_copy(y_stage, y_out.at[source], y_sem.at[0]),
            pltpu.make_async_copy(y_stage.at[spot], y_own.at[source, spot], y_sem.at[1]),
        ]
        for write in writes:
            write.start()
        for write in writes:
            write.wait()

    def wide_tiles(owner, k):
        at = pl.ds(pl.multiple_of((owner * wide_count + k) * wide_rows, wide_rows), wide_rows)
        x = whole(x_held[:, :, at])
        return dot_tn(x, whole(gate_held[...])), dot_tn(x, whole(up_held[...]))

    def tall_tile(owner, k):
        at = pl.ds(pl.multiple_of(k * tall_rows, tall_rows), tall_rows)
        over = pl.ds(pl.multiple_of(owner * tall_width, tall_width), tall_width)
        return dot_tn(whole(hidden_held[:, :, at]), whole(grad_held[:, :, over]))

    def wide_send(which, k):
        slot = k % 2
        return remote(
            give_wide(slot, which),
            take_wide(which, k),
            ws.at[slot, which],
            wr.at[which, k],
            other,
        )

    def tall_send(k):
        slot = k % 2
        return remote(give_tall(slot), take_tall(k), ts.at[slot], tr.at[k], other)

    def wide_write(which, k):
        target = (gate_out, up_out)[which]
        at = pl.ds(pl.multiple_of(k * wide_rows, wide_rows), wide_rows)
        return pltpu.make_async_copy(done_wide(which), target.at[at, :], wide_sem.at[which])

    def tall_write(k):
        slot = k % 2
        at = pl.ds(pl.multiple_of(k * tall_rows, tall_rows), tall_rows)
        return pltpu.make_async_copy(done_tall(slot), down_out.at[at, :], tall_sem.at[slot])

    def give_wide_tile(k):
        @pl.when(k >= 2)
        def _():
            for which in range(2):
                wide_send(which, k - 2).wait_send()

        for which, tile in enumerate(wide_tiles(1 - half, k)):
            give_wide(k % 2, which)[...] = tile.astype(gates.dtype)
            wide_send(which, k).start()

    def give_tall_tile(k):
        @pl.when(k >= 2)
        def _():
            tall_send(k - 2).wait_send()

        give_tall(k % 2)[...] = tall_tile(1 - half, k).astype(gates.dtype)
        tall_send(k).start()

    def keep_wide_tile(k):
        @pl.when(k >= 1)
        def _():
            for which in range(2):
                wide_write(which, k - 1).wait()

        for which, tile in enumerate(wide_tiles(half, k)):
            wide_send(which, k).wait_recv()
            tile = tile + take_wide(which, k)[...].astype(wide)
            done_wide(which)[...] = tile.astype(gates.dtype)
            wide_write(which, k).start()

    def keep_tall_tile(k):
        @pl.when(k >= 2)
        def _():
            tall_write(k - 2).wait()

        tile = tall_tile(half, k)
        tall_send(k).wait_recv()
        tile = tile + take_tall(k)[...].astype(wide)
        done_tall(k % 2)[...] = tile.astype(gates.dtype)
        tall_write(k).start()

    units = 2 * (wide_count + tall_count)
    bounds = (0, wide_count, wide_count + tall_count, units - tall_count, units)
    acts = (give_wide_tile, give_tall_tile, keep_wide_tile, keep_tall_tile)

    def fill(unit, carry):
        for act, low, high in zip(acts, bounds[:-1], bounds[1:]):

            @pl.when((unit >= low) & (unit < high))
            def _():
                act(unit - low)

        return carry

    def chain_out(source):
        up = jnp.where(source > level, 1, 0)
        step = 2 * up - 1
        slot = jnp.where(source == level - 1, depth, source)
        return remote(
            onward.at[up],
            incoming.at[slot],
            cs.at[source],
            cr.at[slot],
            (half, place + step * PLANE),
        )

    def chain_in(slot):
        block = incoming.at[slot]
        return remote(block, block, cs.at[0], cr.at[slot], (half, place))

    def prob_to(source):
        return remote(
            prob_send.at[source],
            prob_land.at[level],
            ps.at[source],
            pr.at[level],
            (half, source * PLANE + spot),
        )

    def prob_from(source):
        block = prob_land.at[source]
        return remote(block, block, ps.at[source], pr.at[source], (half, source * PLANE + spot))

    def add_incoming(slot):
        chain_in(slot).wait_recv()
        back_ref[...] += incoming[slot].astype(jnp.float32)

    def settle(way, source):
        load = shared_load(0, source)
        load.start()
        for offset in range(1, PLANE):
            for copy in rows_from(offset, source):
                copy.wait_recv()
        load.wait()

        def columns(n, carry):
            at = pl.ds(pl.multiple_of(n * 512, 512), 512)
            total = shared[0, :, at].astype(jnp.float32)
            for mate in range(PLANE):
                total = total + dot_tn(choose_ref[source, mate], came[mate, source, :, at])
            back_ref[:, at] = total
            return carry

        lax.fori_loop(0, width // 512, columns, 0)
        lines = lax.broadcasted_iota(jnp.int32, (8, tokens), 0)
        probs = jnp.zeros((8, tokens), jnp.float32)
        for mate in range(PLANE):
            part = lax.dot_general(
                scalars[mate, source],
                choose_ref[source, mate].astype(jnp.float32),
                (((0,), (0,)), ((), ())),
                preferred_element_type=jnp.float32,
                precision=lax.Precision.HIGHEST,
            )
            probs = jnp.where(lines == mate, part[:8], probs)

        @pl.when((source >= level) & (level > 0))
        def _():
            add_incoming(source)

        @pl.when((source < level) & (level < depth - 1))
        def _():
            add_incoming(source)

        @pl.when((source == level) & (level < depth - 1))
        def _():
            add_incoming(depth)

        @pl.when(source == level)
        def _():
            prob_land[level] = probs

        @pl.when(source != level)
        def _():
            prob_send[source] = probs
            prob_to(source).start()
            former = source + 2 * way - 1

            @pl.when((former >= 0) & (former < depth))
            def _():
                chain_out(former).wait_send()

            onward[way] = back_ref[...].astype(onward.dtype)
            chain_out(source).start()

    def step(i, carry):
        s = depth - 1 - i
        each_way(s, compute)

        @pl.when(i > 0)
        def _():
            each_way(s + 1, settle)

        return carry

    lax.fori_loop(0, depth, step, 0)
    pl.semaphore_signal(free_sem, inc=1, device_id=other, device_id_type=MESH)
    pl.semaphore_wait(free_sem, 1)
    lax.fori_loop(0, units, fill, 0)
    each_way(0, settle)
    for which in range(2):
        wide_write(which, wide_count - 1).wait()
        for k in (wide_count - 2, wide_count - 1):
            wide_send(which, k).wait_send()
    for k in (tall_count - 2, tall_count - 1):
        tall_write(k).wait()
        tall_send(k).wait_send()

    def finish(source, carry):
        ahead = jnp.where(source > level, 1, 0)
        near = (source >= level - 1) & (source <= level + 2)

        @pl.when(near)
        def _():
            for offset in range(1, PLANE):
                for copy in rows_to(offset, slot_of(ahead, source), source):
                    copy.wait_send()

        @pl.when((source == level - 1) | (source == level + 1))
        def _():
            chain_out(source).wait_send()

        @pl.when(source != level)
        def _():
            prob_to(source).wait_send()
            prob_from(source).wait_recv()

        prob_ref[source] = prob_land[source]
        return carry

    lax.fori_loop(0, depth, finish, 0)


def run_and_return(rows, grads, weights, router, choose, shared_back, total):
    depth, _, capacity, width = rows.shape
    tokens = choose.shape[3]
    inner = weights[0].shape[1]
    tile = PLANE * capacity
    wide_count, tall_count = width // 512, inner // 128
    semaphores = pltpu.SemaphoreType.DMA
    low, wide = rows.dtype, jnp.float32
    anywhere = pl.BlockSpec(memory_space=pl.ANY)
    local = pl.BlockSpec(memory_space=pltpu.VMEM)
    return pl.pallas_call(
        functools.partial(run_and_return_kernel, depth, total),
        out_shape=[
            jax.ShapeDtypeStruct((tokens, width), wide),
            jax.ShapeDtypeStruct((depth, 8, tokens), wide),
            jax.ShapeDtypeStruct((width // 2, inner), low),
            jax.ShapeDtypeStruct((width // 2, inner), low),
            jax.ShapeDtypeStruct((inner, width // 2), low),
            jax.ShapeDtypeStruct(rows.shape, low),
            jax.ShapeDtypeStruct(rows.shape, low),
        ],
        in_specs=[anywhere] * 5 + [local, local, anywhere],
        out_specs=[local, local] + [anywhere] * 5,
        scratch_shapes=[
            pltpu.VMEM((PLANE, depth, capacity, width), low),
            pltpu.VMEM((PLANE, depth, capacity, 128), wide),
            pltpu.VMEM((1, tokens, width), low),
            pltpu.VMEM((2, tokens, width), low),
            pltpu.VMEM((depth + 1, tokens, width), low),
            pltpu.VMEM((depth, 8, tokens), wide),
            pltpu.VMEM((depth, 8, tokens), wide),
            pltpu.VMEM((depth, tile, width), low),
            pltpu.VMEM((depth, tile, inner), low),
            pltpu.VMEM((depth, tile, inner), low),
            pltpu.VMEM((depth, tile, inner), low),
            pltpu.VMEM((depth, tile, width), low),
            pltpu.VMEM((tile, inner), low),
            pltpu.VMEM(weights[0].shape, low),
            pltpu.VMEM(weights[1].shape, low),
            pltpu.VMEM(weights[2].shape, low),
            pltpu.VMEM((4, PLANE, capacity, width), low),
            pltpu.VMEM((4, PLANE, capacity, 128), wide),
            pltpu.VMEM((PLANE, capacity, width), low),
            semaphores((PLANE, depth)),
            semaphores((PLANE, depth)),
            semaphores((PLANE, depth)),
            semaphores((PLANE, depth)),
            semaphores((5,)),
            semaphores((2,)),
            semaphores((depth,)),
            semaphores((depth + 1,)),
            semaphores((depth,)),
            semaphores((depth,)),
            semaphores((2, 2)),
            semaphores((2, wide_count)),
            semaphores((2,)),
            semaphores((tall_count,)),
            semaphores((2,)),
            semaphores((2,)),
            semaphores((2,)),
            pltpu.SemaphoreType.REGULAR,
        ],
        compiler_params=pltpu.CompilerParams(
            collective_id=7, has_side_effects=True, vmem_limit_bytes=63 * MEBIBYTE
        ),
        cost_estimate=LONG,
    )(
        rows.reshape(depth, tile, width),
        grads.reshape(depth, tile, width),
        *weights,
        router,
        choose,
        shared_back,
    )


def finish_kernel(layout, *refs):
    piece, moved, residual, added, sdown, token = refs[:6]
    query_ref, down_ref, up_ref, out_ref, gate_ref, shared_up_ref = refs[6:12]
    sdown_ref, output_ref, token_ref = refs[12:]
    entry_width, out_start = layout
    rows = piece.shape[0]
    nope_width = HEADS * NOPE
    query_width = HEADS * (NOPE + ROPE)
    low_half = lax.broadcasted_iota(jnp.int32, (rows, 128), 1) < ROPE
    for pair in range(HEADS // 2):
        start = pair * 2 * NOPE
        rope = piece[:, nope_width + pair * 128 : nope_width + (pair + 1) * 128]
        latter = pltpu.roll(piece[:, start + NOPE : start + 2 * NOPE], NOPE // 2, 1)
        at = pair * 2 * (NOPE + ROPE)
        query_ref[:, at : at + 128] = piece[:, start : start + NOPE]
        query_ref[:, at + 128 : at + 256] = jnp.where(low_half, rope, latter)
        query_ref[:, at + 256 : at + 384] = jnp.where(low_half, latter, rope)
    down_ref[...] = piece[:, query_width : query_width + down_ref.shape[1]]
    up_rows = up_ref.shape[0]
    span = out_start - entry_width
    for k in range(rows // up_rows):
        up_ref[:, k * span : (k + 1) * span] = piece[
            k * up_rows : (k + 1) * up_rows, entry_width:out_start
        ]
    out_ref[...] = piece[:, out_start : out_start + out_ref.shape[1]]
    depth = moved.shape[0]
    share = gate_ref.shape[1] // (2 * depth)
    padded = moved.shape[2] // 4
    for which, target in enumerate((gate_ref, shared_up_ref)):
        target[...] = jnp.concatenate(
            [
                moved[t, :, (2 * which + k) * padded : (2 * which + k + 1) * padded].astype(
                    jnp.float32
                )[:, :share]
                for k in range(2)
                for t in range(depth)
            ],
            axis=1,
        )
    sdown_ref[...] = sdown[...].astype(jnp.float32)
    output_ref[...] = (residual[...] + added[...].astype(jnp.float32)).astype(output_ref.dtype)
    token_ref[...] = token[...]


def finish(piece, moved, residual, added, sdown, token, shapes, layout):
    wide = jnp.float32
    local = pl.BlockSpec(memory_space=pltpu.VMEM)
    spans = list(shapes) + [sdown.shape]
    return pl.pallas_call(
        functools.partial(finish_kernel, layout),
        out_shape=[jax.ShapeDtypeStruct(shape, wide) for shape in spans]
        + [
            jax.ShapeDtypeStruct(residual.shape, added.dtype),
            jax.ShapeDtypeStruct(token.shape, wide),
        ],
        in_specs=[local] * 6,
        out_specs=[local] * 9,
        compiler_params=pltpu.CompilerParams(vmem_limit_bytes=48 * MEBIBYTE),
    )(piece, moved, residual, added, sdown, token)


def body(
    tokens,
    segments,
    routes,
    slot_index,
    cotangent,
    attention_norm,
    query_weight,
    latent_down,
    latent_norm,
    latent_up,
    output_weight,
    feed_norm,
    router_weight,
    shared_gate,
    shared_up,
    shared_down,
    expert_gate,
    expert_up,
    expert_down,
):
    row_count = tokens.shape[1]
    expert_total = lax.axis_size("expert")
    depth = expert_total // PLANE
    plane, line = groups(expert_total)
    place = lax.axis_index("expert")
    level = place // PLANE
    device_half = lax.axis_index("fsdp")
    capacity = row_count * TOPK // expert_total
    line_rows = depth * row_count
    inputs = tokens[0].astype(jnp.float32)

    part_rows = query_weight.shape[0]
    gain_width = attention_norm.shape[0]
    latent_width = latent_norm.shape[0]
    small = jnp.concatenate([attention_norm, latent_norm, feed_norm, router_weight.reshape(-1)])
    cuts = [
        0,
        gain_width,
        gain_width + latent_width,
        2 * gain_width + latent_width,
        small.shape[0],
    ]
    small = jnp.pad(small, (0, 128 * part_rows - small.shape[0])).reshape(part_rows, 128)
    query_width = query_weight.shape[1]
    down_width = latent_down.shape[1]
    entry_width = query_width + down_width + (-down_width) % 128
    up_width = HEADS * (NOPE + VALUE)
    quarters = part_rows // latent_up.shape[0]
    by_head = query_weight.reshape(part_rows, HEADS, NOPE + ROPE)
    packed = jnp.concatenate(
        [
            by_head[..., :NOPE].reshape(part_rows, -1),
            by_head[..., NOPE:].reshape(part_rows, -1),
            jnp.pad(latent_down, ((0, 0), (0, (-down_width) % 128))),
            latent_up.reshape(latent_up.shape[0], quarters, -1)
            .transpose(1, 0, 2)
            .reshape(part_rows, -1),
            output_weight,
            small,
        ],
        axis=1,
    )
    cut = packed.shape[1] // 256 * 128
    route_rows = routes[0]
    slot_rows = slot_index[0]
    target = jnp.where(
        slot_rows >= 0, route_rows * capacity + slot_rows, expert_total * capacity
    )
    target = jnp.pad(target, ((0, 0), (0, 8 - TOPK)), constant_values=expert_total * capacity).T
    shared_width = shared_gate.shape[1] // (2 * depth)
    shared_both = jnp.stack([shared_gate, shared_up]).reshape(
        2, part_rows, 2, depth, shared_width
    )
    shared_both = shared_both.transpose(3, 1, 0, 2, 4)
    spare = (-shared_width) % 128
    shared_both = jnp.pad(shared_both, ((0, 0),) * 4 + ((0, spare),))
    shared_both = shared_both.reshape(depth, part_rows, -1)
    packed_full, grad_line, target_line, shared_full, sdown_full = gather_rows(
        packed, cotangent[0], target, shared_both, shared_down, cuts_of(packed.shape[1], GROUPS)
    )
    shared_full = shared_full.reshape(D, -1)
    sdown_full = sdown_full.reshape(2, shared_width, D)
    expert_gate_full = lax.all_gather(expert_gate[0], "fsdp", axis=0, tiled=True)
    expert_up_full = lax.all_gather(expert_up[0], "fsdp", axis=0, tiled=True)
    expert_down_full = lax.all_gather(expert_down[0], "fsdp", axis=1, tiled=True)
    packed_full, grad_line, target_line, expert_gate_full, expert_up_full, expert_down_full = (
        lax.optimization_barrier(
            (
                packed_full,
                grad_line,
                target_line,
                expert_gate_full,
                expert_up_full,
                expert_down_full,
            )
        )
    )
    up_rows = latent_up.shape[0]
    up_parts = packed_full.reshape(2 * expert_total, quarters, up_rows, -1)
    if up_rows % 16 == 0:
        up_full = up_parts
        ups_shape = (quarters, 2 * expert_total, up_rows, up_width // quarters)
    else:
        up_full = up_parts[..., entry_width : -128 - D].transpose(1, 0, 2, 3)
        up_full = up_full.reshape(quarters, 1, LATENT, -1)
        ups_shape = up_full.shape
    small_full = packed_full[:, -128:].reshape(2 * expert_total, -1)
    gain_one, gain_latent, gain_feed, router_full = (
        small_full[:, cuts[0] : cuts[1]].reshape(-1),
        small_full[:, cuts[1] : cuts[2]].reshape(-1),
        small_full[:, cuts[2] : cuts[3]].reshape(-1),
        small_full[:, cuts[3] : cuts[4]].reshape(-1, expert_total),
    )

    slot_names = level * PLANE * capacity + jnp.arange(PLANE * capacity)
    hits = target_line[:, :TOPK, None, :] == slot_names[None, None, :, None]
    choose_rows = jnp.sum(hits.astype(jnp.float32), axis=1).astype(jnp.bfloat16)

    choose_slots = choose_rows.reshape(depth, PLANE, capacity, row_count)
    grad_line = grad_line.reshape(depth, row_count, D)

    cosine, sine_table = rotary_table(row_count, device_half * row_count, ROPE)
    tables = (
        jnp.concatenate([cosine] * 4, axis=1),
        jnp.concatenate([-sine_table, sine_table] * 2, axis=1),
    )
    gain_first = gain_one.astype(jnp.float32)
    latent_gain = gain_latent.astype(jnp.float32)
    feed_gain = gain_feed.astype(jnp.float32)
    query_place = device_half * row_count + jnp.arange(row_count)
    key_place = (device_half - 1) * row_count + jnp.arange(2 * row_count)
    padded_segments = jnp.concatenate([jnp.full((row_count,), -1, jnp.int32), segments[0]])
    key_segment = lax.dynamic_slice_in_dim(padded_segments, device_half * row_count, 2 * row_count)
    query_segment = lax.dynamic_slice_in_dim(segments[0], device_half * row_count, row_count)
    visible = (key_place[None, :] <= query_place[:, None]) & (
        key_segment[None, :] == query_segment[:, None]
    )
    mask = visible.astype(jnp.float32)
    layout = (entry_width, packed.shape[1] - 128 - D)
    (
        normed_low,
        residual,
        mixed_low,
        queries,
        latent,
        compressed,
        expanded,
        keys_rope,
        log_total,
        mixed_heads,
        grad_rows,
    ) = attend(
        tokens[0],
        packed_full,
        up_full,
        ups_shape,
        (gain_first[None], latent_gain[None], feed_gain[None]),
        tables,
        mask,
        choose_slots,
        grad_line,
        layout,
    )
    mixed_rows, shared_out, shared_back, shared_grad, sdown_grad, grad_rows = dispatch(
        mixed_low, choose_slots, grad_line, shared_full, sdown_full, grad_rows
    )
    shared_out = shared_out.reshape(line_rows, D)
    router_wide = jnp.pad(router_full, ((0, 0), (0, (-expert_total) % 128)))
    shared_summed = lax.psum_scatter(
        shared_grad, "expert", scatter_dimension=0, axis_index_groups=plane, tiled=True
    )[0]
    sdown_summed = lax.psum_scatter(
        sdown_grad, "expert", scatter_dimension=0, axis_index_groups=plane, tiled=True
    )
    weights = (expert_gate_full, expert_up_full, expert_down_full)
    if depth <= PLANE:
        (
            back_and_shared,
            prob_parts,
            expert_gate_piece,
            expert_up_piece,
            expert_down_piece,
            expert_out,
            own_out,
        ) = run_and_return(
            mixed_rows, grad_rows, weights, router_wide, choose_slots, shared_back, expert_total
        )
    else:
        flat_rows = mixed_rows.reshape(expert_total * capacity, D)
        flat_grads = grad_rows.reshape(expert_total * capacity, D)
        hidden_scaled, gate_low, up_low, input_grad, expert_out, slot_grad = run_expert(
            flat_rows, flat_grads, *weights, router_wide, expert_total
        )
        (
            back_and_shared,
            prob_parts,
            expert_gate_piece,
            expert_up_piece,
            expert_down_piece,
        ) = give_back(
            input_grad.reshape(mixed_rows.shape),
            slot_grad.reshape(depth, PLANE, capacity, 128),
            choose_slots,
            shared_back,
            [flat_rows, gate_low, up_low, hidden_scaled, flat_grads],
        )
        own_out = expert_out
    prob_grad = prob_parts[:, :PLANE].reshape(expert_total, row_count).T
    probabilities = jax.nn.softmax(matmul(mixed_low, router_full), axis=-1)
    prob_grad = prob_parts[:, :PLANE].reshape(expert_total, row_count).T
    logit_low = (
        probabilities * (prob_grad - jnp.sum(probabilities * prob_grad, axis=-1, keepdims=True))
    ).astype(jnp.bfloat16)
    router_grad = left_matmul(mixed_low, logit_low)
    (
        token_grad,
        up_weight_grad,
        latent_gain_grad,
        first_gain_grad,
        feed_gain_grad,
        entry_grad,
        output_grad,
        returned,
    ) = attend_back(
        back_and_shared,
        packed_full,
        up_full,
        ups_shape,
        (
            queries,
            expanded,
            keys_rope,
            log_total,
            latent,
            compressed,
            normed_low,
            mixed_heads,
            tokens[0],
            residual,
            cotangent[0],
            jnp.pad(logit_low, ((0, 0), (0, (-expert_total) % 128))),
            router_wide,
        ),
        (latent_gain[None], gain_first[None], feed_gain[None]),
        tables,
        mask,
        (expert_out.reshape(mixed_rows.shape), own_out.reshape(mixed_rows.shape)),
        (shared_summed, sdown_summed),
        layout,
    )
    if up_rows % 16 != 0:
        up_weight_grad = up_weight_grad.reshape(quarters, 2 * expert_total, up_rows, -1)
        up_weight_grad = up_weight_grad.transpose(1, 0, 2, 3)
    latent_gain_grad = latent_gain_grad[0]
    first_gain_grad = first_gain_grad[0]
    feed_gain_grad = feed_gain_grad[0]
    routed = jnp.einsum(
        "zst,zsd->ztd",
        choose_rows,
        returned.reshape(depth, PLANE * capacity, D),
        preferred_element_type=jnp.float32,
    )
    routed_and_shared = lax.psum_scatter(
        (routed.reshape(line_rows, D) + shared_out).astype(jnp.bfloat16),
        "expert",
        scatter_dimension=0,
        axis_index_groups=line,
        tiled=True,
    )

    small_grad = jnp.concatenate(
        [
            first_gain_grad.reshape(-1, gain_width),
            latent_gain_grad.reshape(-1, latent_width),
            feed_gain_grad.reshape(-1, gain_width),
            router_grad.reshape(2 * expert_total, -1),
        ],
        axis=1,
    )
    small_grad = jnp.pad(small_grad, ((0, 0), (0, 128 * part_rows - small_grad.shape[1])))
    packed_piece, shared_back_moved = reduce_rows(
        [
            entry_grad,
            up_weight_grad.reshape(2 * expert_total * part_rows, -1),
            output_grad,
            small_grad.astype(jnp.bfloat16).reshape(-1, 128),
        ],
        shared_summed,
        cut,
    )
    small_piece = packed_piece[:, -128:].reshape(-1)
    (
        query_piece,
        down_piece,
        up_piece,
        output_piece,
        sgate_piece,
        sup_piece,
        sdown_piece,
        output,
        token_grad,
    ) = finish(
        packed_piece,
        shared_back_moved,
        residual,
        routed_and_shared,
        sdown_summed,
        token_grad,
        (
            query_weight.shape,
            latent_down.shape,
            latent_up.shape,
            output_weight.shape,
            shared_gate.shape,
            shared_up.shape,
        ),
        layout,
    )

    return (
        output[None],
        token_grad[None],
        small_piece[cuts[0] : cuts[1]],
        query_piece,
        down_piece,
        small_piece[cuts[1] : cuts[2]],
        up_piece,
        output_piece,
        small_piece[cuts[2] : cuts[3]],
        small_piece[cuts[3] : cuts[4]].reshape(gain_width, expert_total),
        sgate_piece,
        sup_piece,
        sdown_piece,
        expert_gate_piece.astype(jnp.float32)[None],
        expert_up_piece.astype(jnp.float32)[None],
        expert_down_piece.astype(jnp.float32)[None],
    )


def solution(mesh):
    return jax.shard_map(
        body,
        mesh=mesh,
        in_specs=(
            P("expert", "fsdp", None),
            P("expert", None),
            P("expert", "fsdp", None),
            P("expert", "fsdp", None),
            P("expert", "fsdp", None),
            P(("fsdp", "expert")),
            P(("fsdp", "expert"), None),
            P(("fsdp", "expert"), None),
            P(("fsdp", "expert")),
            P(("fsdp", "expert"), None),
            P(("fsdp", "expert"), None),
            P(("fsdp", "expert")),
            P(("fsdp", "expert"), None),
            P(("fsdp", "expert"), None),
            P(("fsdp", "expert"), None),
            P(("fsdp", "expert"), None),
            P("expert", "fsdp", None),
            P("expert", "fsdp", None),
            P("expert", None, "fsdp"),
        ),
        out_specs=(
            P("expert", "fsdp", None),
            P("expert", "fsdp", None),
            P(("fsdp", "expert")),
            P(("fsdp", "expert"), None),
            P(("fsdp", "expert"), None),
            P(("fsdp", "expert")),
            P(("fsdp", "expert"), None),
            P(("fsdp", "expert"), None),
            P(("fsdp", "expert")),
            P(("fsdp", "expert"), None),
            P(("fsdp", "expert"), None),
            P(("fsdp", "expert"), None),
            P(("fsdp", "expert"), None),
            P("expert", "fsdp", None),
            P("expert", "fsdp", None),
            P("expert", None, "fsdp"),
        ),
        check_vma=False,
    )
```

```python
import functools
import math

import jax
import jax.numpy as jnp
from jax import lax
from jax.experimental import pallas as pl
from jax.experimental.pallas import tpu as pltpu
from jax.sharding import PartitionSpec as P

D = 2048
HEADS = 16
NOPE = 128
ROPE = 64
VALUE = 128
LATENT = 512
TOPK = 6


EPSILON = 1e-06
FLOOR_SCORE = -1e30


def norm_rows(values, gain):
    return values * lax.rsqrt(jnp.mean(values * values, axis=-1, keepdims=True) + EPSILON) * gain


def norm_back(values, gain, incoming):
    primal_out, pullback = jax.vjp(norm_rows, values, gain)
    return pullback(incoming)


def swiglu_back(gate_part, up_portion, incoming):
    primal_out, pullback = jax.vjp(
        lambda former, latter: jax.nn.silu(former) * latter, gate_part, up_portion
    )
    return pullback(incoming)


def rotary_table(row_total, offset, rope_width):
    frequency_steps = jnp.arange(rope_width // 2, dtype=jnp.float32)
    inverse = jnp.exp(frequency_steps * (-2.0 * math.log(10000.0) / rope_width))
    places = (offset + jnp.arange(row_total)).astype(jnp.float32)
    angles = places[:, None] * inverse[None, :]
    return (jnp.cos(angles), jnp.sin(angles))


def matmul(former, latter):
    return jnp.dot(former, latter, preferred_element_type=jnp.float32)


def left_matmul(former, latter):
    return lax.dot_general(
        former, latter, (((0,), (0,)), ((), ())), preferred_element_type=jnp.float32
    )


def right_matmul(former, latter):
    return lax.dot_general(
        former, latter, (((1,), (1,)), ((), ())), preferred_element_type=jnp.float32
    )


PLANE = 4
MESH = pl.DeviceIdType.MESH
MEBIBYTE = 1024 * 1024
GROUPS = 4
PARTS = 2
LONG = pl.CostEstimate(flops=100 * 10**9, bytes_accessed=0, transcendentals=0)
MIDDLE = pl.CostEstimate(flops=40 * 10**9, bytes_accessed=0, transcendentals=0)


def groups(count):
    lines = count // PLANE
    plane = [[row * PLANE + spot for spot in range(PLANE)] for row in range(lines)]
    line = [[row * PLANE + spot for row in range(lines)] for spot in range(PLANE)]
    return plane, line


def remote(source, target, send, receive, where):
    return pltpu.make_async_remote_copy(
        src_ref=source,
        dst_ref=target,
        send_sem=send,
        recv_sem=receive,
        device_id=where,
        device_id_type=MESH,
    )


def plane_mates(place):
    spot = place % PLANE
    return (place + 1 - 2 * (spot % 2), place + 2 - 4 * (spot // 2))


def greet(partners):
    barrier = pltpu.get_barrier_semaphore()
    for where in partners:
        pl.semaphore_signal(barrier, inc=1, device_id=where, device_id_type=MESH)
    pl.semaphore_wait(barrier, len(partners))


def line_others(half, place, depth):
    total = depth * PLANE
    return [(half, (place + offset * PLANE) % total) for offset in range(1, depth)]


def plane_others(half, place):
    spot = place % PLANE
    return [(half, place - spot + (spot + offset) % PLANE) for offset in range(1, PLANE)]


def greet_neighbours(half, place, depth):
    mates = [(half, mate) for mate in plane_mates(place)]
    greet(line_others(half, place, depth) + mates + [(1 - half, place)])


def exchange_along(depth, half, place, in_ref, land, own_sem, send, receive):
    level = place // PLANE
    total = depth * PLANE

    def own():
        return pltpu.make_async_copy(in_ref.at[level], land(level), own_sem)

    def to(offset):
        where = (place + offset * PLANE) % total
        return remote(
            in_ref.at[where // PLANE],
            land(level),
            send.at[offset],
            receive.at[offset],
            (half, where),
        )

    def start():
        own().start()
        for offset in range(1, depth):
            to(offset).start()

    def finish():
        own().wait()
        for offset in range(1, depth):
            to(offset).wait()

    return start, finish


def exchange_plane(half, place, source_of, target_of, own_sem, send, receive, own_there=False):
    spot = place % PLANE

    def to(offset, level):
        mate = (spot + offset) % PLANE
        return remote(
            source_of(mate, level),
            target_of(spot, level),
            send.at[offset, level],
            receive.at[offset, level],
            (half, place - spot + mate),
        )

    def came(offset, level):
        mate = (spot + PLANE - offset) % PLANE
        block = target_of(mate, level)
        return remote(
            block,
            block,
            send.at[offset, level],
            receive.at[offset, level],
            (half, place - spot + mate),
        )

    def own(level):
        return pltpu.make_async_copy(
            source_of(spot, level), target_of(spot, level), own_sem.at[level]
        )

    def start(level):
        for offset in range(1, PLANE):
            to(offset, level).start()
        if not own_there:
            own(level).start()

    def finish(level):
        if not own_there:
            own(level).wait()
        for offset in range(1, PLANE):
            came(offset, level).wait_recv()
            to(offset, level).wait_send()

    return start, finish


def place_rows(choose_ref, source, block, placed):
    def columns(n, carry):
        at = lanes_at(n * 512, 512)
        for mate in range(PLANE):
            placed[mate, :, at] = jnp.dot(
                choose_ref[source, mate], block[:, at], preferred_element_type=jnp.float32
            ).astype(placed.dtype)
        return carry

    lax.fori_loop(0, block.shape[1] // 512, columns, 0)


def cuts_of(width, count):
    return [width * k // count // 128 * 128 for k in range(count)] + [width]


def gather_kernel(depth, cuts, *refs):
    in_ref, *line_ins, move_in, down_in = refs[:5]
    out_ref, *line_outs, shared_out, down_out = refs[5:10]
    own_sem, zs, zr, ps, pr, qs, qr, cs, cr, ls, lr, ms, mr, *shared_sems = refs[10:]
    os, ore, ts, tr, us, ur = shared_sems
    half = lax.axis_index("fsdp")
    place = lax.axis_index("expert")
    level = place // PLANE
    spot = place % PLANE
    total = depth * PLANE
    mates = plane_mates(place)
    rows, width = in_ref.shape
    columns = [pl.ds(low, high - low) for low, high in zip(cuts[:-1], cuts[1:])]
    count = len(columns)
    greet_neighbours(half, place, depth)

    def at(which, block, count=1):
        start = pl.multiple_of((half * total + block) * rows, rows)
        return out_ref.at[pl.ds(start, count * rows), columns[which]]

    def along(which, way, source, own=False):
        target = at(which, source * PLANE + spot)
        start = in_ref.at[:, columns[which]] if own else target
        return remote(
            start,
            target,
            zs.at[which, way, source],
            zr.at[which, source],
            (half, place + (2 * way - 1) * PLANE),
        )

    def plane_one(which, source, own=False):
        target = at(which, source * PLANE + spot)
        start = in_ref.at[:, columns[which]] if own else target
        return remote(
            start,
            target,
            ps.at[which, source],
            pr.at[which, source],
            (half, mates[which % 2]),
        )

    def plane_two(which, source, turn):
        base = source * PLANE
        if which % 2 == 0:
            block = at(which, base + spot - spot % 2, 2)
        else:
            block = at(which, base + (spot + 2 * turn) % PLANE)
        return remote(
            block,
            block,
            qs.at[which, turn, source],
            qr.at[which, turn, source],
            (half, mates[1 - which % 2]),
        )

    def core(which, source):
        block = at(which, source * PLANE, PLANE)
        return remote(
            block, block, cs.at[which, source], cr.at[which, source], (1 - half, place)
        )

    def trail(which, way, source, own=False):
        target = line_outs[which].at[source]
        return remote(
            line_ins[which] if own else target,
            target,
            ls.at[which, way, source],
            lr.at[which, source],
            (half, place + (2 * way - 1) * PLANE),
        )

    def trail_own(which):
        return pltpu.make_async_copy(
            line_ins[which], line_outs[which].at[level], own_sem.at[count + which]
        )

    move_start, move_finish = exchange_along(
        depth,
        half,
        place,
        move_in,
        lambda source: shared_out.at[half, source, spot],
        own_sem.at[count + 2],
        ms,
        mr,
    )
    items = range(depth + 2)
    down_own = pltpu.make_async_copy(down_in, down_out.at[half, spot], own_sem.at[count + 3])

    def shared_at(item, first, count):
        if item < depth:
            return shared_out.at[half, item, pl.ds(first, count)]
        span = down_in.shape[1] // 2
        return down_out.at[
            half, pl.ds(first, count), :, pl.ds((item - depth) * span, span)
        ]

    def shared_route(item):
        return (0 if item < depth // 2 else 1) if item < depth else item - depth

    def shared_one(item):
        block = shared_at(item, spot, 1)
        mate = mates[shared_route(item)]
        return remote(block, block, os.at[item], ore.at[item], (half, mate))

    def shared_two(item):
        if shared_route(item) == 0:
            blocks = [shared_at(item, spot - spot % 2, 2)]
        else:
            blocks = [shared_at(item, (spot + 2 * turn) % PLANE, 1) for turn in range(2)]
        mate = mates[1 - shared_route(item)]
        return [
            remote(block, block, ts.at[turn, item], tr.at[turn, item], (half, mate))
            for turn, block in enumerate(blocks)
        ]

    def shared_core(item):
        block = shared_at(item, 0, PLANE)
        return remote(block, block, us.at[item], ur.at[item], (1 - half, place))

    seconds = [(which, turn) for which in range(count) for turn in range(1 + which % 2)]

    def own_copy(which):
        return pltpu.make_async_copy(
            in_ref.at[:, columns[which]], at(which, place), own_sem.at[which]
        )

    for which in range(count):

        @pl.when(level > 0)
        def _():
            along(which, 0, level, True).start()

        @pl.when(level < depth - 1)
        def _():
            along(which, 1, level, True).start()

        plane_one(which, level, True).start()
        own_copy(which).start()
    move_start()
    down_own.start()
    for which in range(2):
        trail_own(which).start()

    def trail_first():
        for which in range(2):

            @pl.when(level > 0)
            def _():
                trail(which, 0, level, True).start()

            @pl.when(level < depth - 1)
            def _():
                trail(which, 1, level, True).start()

    def trail_on(source, way):
        for which in range(2):
            trail(which, way, source).wait_recv()

            @pl.when((level < depth - 1) if way == 1 else (level > 0))
            def _():
                trail(which, way, source).start()

    def visit(step, act):
        if step == 0:
            act(level, None)
            return

        @pl.when(level - step >= 0)
        def _():
            act(level - step, 1)

        @pl.when(level + step < depth)
        def _():
            act(level + step, 0)

    def arrive(source, way):
        for which in range(count):
            along(which, way, source).wait_recv()

            @pl.when((level < depth - 1) if way == 1 else (level > 0))
            def _():
                along(which, way, source).start()

            plane_one(which, source).start()

    def spread(source, way):
        for which in range(count):
            plane_one(which, source).wait_recv()
            for kind, turn in seconds:
                if kind == which:
                    plane_two(kind, source, turn).start()

    def share(source, way):
        for which in range(count):
            for kind, turn in seconds:
                if kind == which:
                    plane_two(kind, source, turn).wait_recv()
            core(which, source).start()

    for which in range(count):
        own_copy(which).wait()
    visit(0, spread)
    for step in range(1, depth):
        visit(step, arrive)
        if step == 1:
            move_finish()
            down_own.wait()
            for item in items:
                shared_one(item).start()
        if step == 2:
            trail_first()
        if step >= 3:
            visit(step - 2, trail_on)
        if step >= 2:
            visit(step - 1, spread)
        if step == 2:
            for item in items:
                shared_one(item).wait_recv()
                for copy in shared_two(item):
                    copy.start()
        if step >= 3:
            visit(step - 3, share)
    visit(depth - 1, spread)
    visit(depth - 2, trail_on)
    visit(depth - 3, share)
    for item in items:
        for copy in shared_two(item):
            copy.wait_recv()
        shared_core(item).start()
    visit(depth - 2, share)
    visit(depth - 1, trail_on)
    visit(depth - 1, share)
    for item in items:
        shared_one(item).wait_send()
        for copy in shared_two(item):
            copy.wait_send()
        shared_core(item).wait()
    for which in range(2):
        trail_own(which).wait()

    def finish(source, carry):
        for which in range(2):

            @pl.when((source <= level) & (level < depth - 1))
            def _():
                trail(which, 1, source).wait_send()

            @pl.when((source >= level) & (level > 0))
            def _():
                trail(which, 0, source).wait_send()

        for which in range(count):
            core(which, source).wait_recv()
            core(which, source).wait_send()
            plane_one(which, source).wait_send()

            @pl.when((source <= level) & (level < depth - 1))
            def _():
                along(which, 1, source).wait_send()

            @pl.when((source >= level) & (level > 0))
            def _():
                along(which, 0, source).wait_send()

        for kind, turn in seconds:
            plane_two(kind, source, turn).wait_send()
        return carry

    lax.fori_loop(0, depth, finish, 0)


def gather_rows(value, first, second, moved, down, cuts):
    rows, width = value.shape
    total = lax.axis_size("expert")
    depth = total // PLANE
    count = len(cuts) - 1
    semaphores = pltpu.SemaphoreType.DMA
    return pl.pallas_call(
        functools.partial(gather_kernel, depth, cuts),
        out_shape=[
            jax.ShapeDtypeStruct((2 * total * rows, width), value.dtype),
            jax.ShapeDtypeStruct((depth,) + first.shape, first.dtype),
            jax.ShapeDtypeStruct((depth,) + second.shape, second.dtype),
            jax.ShapeDtypeStruct((2, depth, PLANE) + moved.shape[1:], moved.dtype),
            jax.ShapeDtypeStruct((2, PLANE) + down.shape, down.dtype),
        ],
        in_specs=[pl.BlockSpec(memory_space=pltpu.VMEM)] * 5,
        out_specs=[pl.BlockSpec(memory_space=pl.ANY)] * 5,
        scratch_shapes=[
            semaphores((count + 4,)),
            semaphores((count, 2, depth)),
            semaphores((count, depth)),
            semaphores((count, depth)),
            semaphores((count, depth)),
            semaphores((count, 2, depth)),
            semaphores((count, 2, depth)),
            semaphores((count, depth)),
            semaphores((count, depth)),
            semaphores((2, 2, depth)),
            semaphores((2, depth)),
            semaphores((depth,)),
            semaphores((depth,)),
            semaphores((depth + 2,)),
            semaphores((depth + 2,)),
            semaphores((2, depth + 2)),
            semaphores((2, depth + 2)),
            semaphores((depth + 2,)),
            semaphores((depth + 2,)),
        ],
        compiler_params=pltpu.CompilerParams(collective_id=1, has_side_effects=True),
        cost_estimate=LONG,
    )(value, first, second, moved, down)


def dot_nt(former, latter):
    return lax.dot_general(
        former, latter, (((1,), (1,)), ((), ())), preferred_element_type=jnp.float32
    )


def dot_tn(former, latter):
    return lax.dot_general(
        former, latter, (((0,), (0,)), ((), ())), preferred_element_type=jnp.float32
    )


def dispatch_kernel(depth, *refs):
    x_ref, choose_ref, grad_in, shared_in, down_in = refs[:5]
    rows_out, forth_out, back_out, wide_out, tall_out, grad_out = refs[6:12]
    lines, placed, grads, weights, downs, low_ref, hidden_ref, forth_ref, back_ref = refs[12:21]
    wide_ref, tall_ref, grad_placed, wide_give, wide_take, tall_give, tall_take = refs[21:28]
    load_sem, out_sem, zs, zr, es, er, own_sem, done_sem, gs, gr, grad_sem = refs[28:39]
    ws, wr, ts, tr = refs[39:]
    half = lax.axis_index("fsdp")
    place = lax.axis_index("expert")
    other = (1 - half, place)
    level = place // PLANE
    spot = place % PLANE
    padded, width = downs.shape
    share = padded // 2
    true = down_in.shape[1]
    chunk = padded
    greet(line_others(half, place, depth) + plane_others(half, place) + [other])

    def along(part, way, source):
        block = lines.at[source, :, pl.ds(part * (width // PARTS), width // PARTS)]
        where = (half, place + (2 * way - 1) * PLANE)
        return remote(block, block, zs.at[part, way, source], zr.at[part, source], where)

    loads = [
        pltpu.make_async_copy(shared_in, weights, load_sem.at[0]),
        pltpu.make_async_copy(grad_in, grads, load_sem.at[1]),
    ] + [
        pltpu.make_async_copy(
            down_in.at[k], downs.at[pl.ds(k * share, true), :], load_sem.at[2 + k]
        )
        for k in range(2)
    ]
    lines[level] = x_ref[...]

    def pass_on(part, way, source):
        @pl.when((level < depth - 1) if way == 1 else (level > 0))
        def _():
            along(part, way, source).start()

    for part in range(PARTS):
        for way in range(2):
            pass_on(part, way, level)
    for load in loads:
        load.start()
    if share > true:
        for k in range(2):
            downs[pl.ds(k * share + true, share - true), :] = jnp.zeros(
                (share - true, width), downs.dtype
            )

    rows_start, rows_finish = exchange_plane(
        half,
        place,
        lambda mate, source: placed.at[source, mate],
        lambda mate, source: rows_out.at[source, mate],
        own_sem,
        es,
        er,
    )
    grad_start, grad_finish = exchange_plane(
        half,
        place,
        lambda mate, source: grad_placed.at[source // 2, mate],
        lambda mate, source: grad_out.at[source, mate],
        grad_sem,
        gs,
        gr,
    )

    def give(source):
        place_rows(choose_ref, source, lines.at[source], placed.at[source])
        rows_start(source)

    def give_grad(n, carry):
        source = 2 * n + 1
        place_rows(choose_ref, source, grads.at[source], grad_placed.at[n])
        grad_start(source)
        return carry

    def shared(source):
        def inner(n, carry):
            at = pl.ds(pl.multiple_of(n * chunk, chunk), chunk)
            after = pl.ds(pl.multiple_of(padded + n * chunk, 128), chunk)
            x = lines[source]
            gate = jnp.dot(x, weights[:, at], preferred_element_type=jnp.float32)
            up = jnp.dot(x, weights[:, after], preferred_element_type=jnp.float32)
            dh = dot_nt(grads[source], downs[at, :])
            sig = 1.0 / (1.0 + jnp.exp(-gate))
            act = gate * sig
            hidden_ref[source, :, at] = (act * up).astype(hidden_ref.dtype)
            low_ref[source, :, at] = (dh * up * (sig + act * (1.0 - sig))).astype(low_ref.dtype)
            low_ref[source, :, after] = (dh * act).astype(low_ref.dtype)
            return carry

        lax.fori_loop(0, padded // chunk, inner, 0)

        def outer(n, carry):
            at = pl.ds(pl.multiple_of(n * 1024, 1024), 1024)
            forth_ref[:, at] = jnp.dot(
                hidden_ref[source], downs[:, at], preferred_element_type=jnp.float32
            ).astype(forth_ref.dtype)
            back_ref[:, at] = dot_nt(low_ref[source], weights[at, :]).astype(back_ref.dtype)
            return carry

        lax.fori_loop(0, width // 1024, outer, 0)
        outs = [
            pltpu.make_async_copy(forth_ref, forth_out.at[source], out_sem.at[0]),
            pltpu.make_async_copy(back_ref, back_out.at[source], out_sem.at[1]),
        ]
        for out in outs:
            out.start()
        for out in outs:
            out.wait()

    give(level)
    for load in loads:
        load.wait()
    lax.fori_loop(0, depth // 2, give_grad, 0)
    shared(level)

    def step(s, carry):
        for part in range(PARTS):

            @pl.when(level - s >= 0)
            def _():
                along(part, 1, level - s).wait_recv()
                pass_on(part, 1, level - s)

            @pl.when(level + s < depth)
            def _():
                along(part, 0, level + s).wait_recv()
                pass_on(part, 0, level + s)

        def one(way, act):
            source = level + (1 - 2 * way) * s

            @pl.when((source >= 0) & (source < depth))
            def _():
                act(source)

        def both(way, carry):
            one(way, give)
            return carry

        def both_shared(way, carry):
            one(way, shared)
            return carry

        lax.fori_loop(0, 2, both, 0)
        lax.fori_loop(0, 2, both_shared, 0)
        return carry

    lax.fori_loop(1, depth, step, 0)

    tokens = x_ref.shape[0]

    def all_lines(ref, at):
        return ref[:, :, at].reshape(depth * tokens, -1)

    part = wide_ref.shape[2]
    chunk_rows = max(PLANE * part, 128)
    per_chunk = chunk_rows // (PLANE * part)
    core_rows = width // 2
    tall_rows = tall_ref.shape[1]
    tall_count = share // tall_rows

    def wide_value(owner, n):
        at = pl.ds(pl.multiple_of(owner * core_rows + n * chunk_rows, chunk_rows), chunk_rows)
        return dot_tn(all_lines(lines, at), low_ref[...].reshape(depth * tokens, -1))

    def tall_value(owner, k):
        at = pl.ds(pl.multiple_of(owner * share + k * tall_rows, tall_rows), tall_rows)
        return dot_tn(all_lines(hidden_ref, at), grads[...].reshape(depth * tokens, -1))

    def wide_send(k):
        return remote(wide_give.at[k], wide_take.at[k], ws.at[k], wr.at[k], other)

    def tall_send(k):
        return remote(tall_give.at[k], tall_take.at[k], ts.at[k], tr.at[k], other)

    def split(value, j):
        first = j * PLANE * part
        return [value[first + k * part : first + (k + 1) * part] for k in range(PLANE)]

    def give_wide(n, carry):
        value = wide_value(1 - half, n)
        for j in range(per_chunk):
            for k, block in enumerate(split(value, j)):
                wide_give[n * per_chunk + j, k] = block.astype(wide_give.dtype)
            wide_send(n * per_chunk + j).start()
        return carry

    def give_tall(k, carry):
        tall_give[k] = tall_value(1 - half, k).astype(tall_give.dtype)
        tall_send(k).start()
        return carry

    def write_wide(k):
        return pltpu.make_async_copy(
            wide_ref.at[k % 2], wide_out.at[:, k], done_sem.at[0, k % 2]
        )

    def keep_wide(n, carry):
        value = wide_value(half, n)
        for j in range(per_chunk):
            at = n * per_chunk + j

            @pl.when(at >= 2)
            def _():
                write_wide(at - 2).wait()

            wide_send(at).wait_recv()
            for k, block in enumerate(split(value, j)):
                total = block + wide_take[at, k].astype(jnp.float32)
                wide_ref[at % 2, k] = total.astype(wide_ref.dtype)
            write_wide(at).start()
        return carry

    lax.fori_loop(0, core_rows // chunk_rows, give_wide, 0)
    lax.fori_loop(0, tall_count, give_tall, 0)
    lax.fori_loop(0, core_rows // chunk_rows, keep_wide, 0)
    for k in range(max(0, depth - 2), depth):
        write_wide(k).wait()
    writes = []
    for k in range(tall_count):
        if k >= 2:
            writes[k - 2].wait()
        value = tall_value(half, k)
        tall_send(k).wait_recv()
        total = value + tall_take[k].astype(jnp.float32)
        tall_ref[k % 2] = total.astype(tall_ref.dtype)
        size = min(tall_rows, true - k * tall_rows)
        writes.append(
            pltpu.make_async_copy(
                tall_ref.at[k % 2, pl.ds(0, size), :],
                tall_out.at[pl.ds(k * tall_rows, size), :],
                done_sem.at[1, k % 2],
            )
        )
        writes[k].start()
    for write in writes[-2:]:
        write.wait()

    def given(k, carry):
        wide_send(k).wait_send()
        return carry

    lax.fori_loop(0, depth, given, 0)
    for k in range(tall_count):
        tall_send(k).wait_send()

    def finish_grad(n, carry):
        grad_finish(2 * n + 1)
        return carry

    lax.fori_loop(0, depth // 2, finish_grad, 0)

    def finish(source, carry):
        rows_finish(source)

        for part in range(PARTS):

            @pl.when((source <= level) & (level < depth - 1))
            def _():
                along(part, 1, source).wait_send()

            @pl.when((source >= level) & (level > 0))
            def _():
                along(part, 0, source).wait_send()

        return carry

    lax.fori_loop(0, depth, finish, 0)


def dispatch(x, choose, grad_line, shared_full, down_full, grad_rows):
    depth = choose.shape[0]
    tokens, width = x.shape
    capacity = choose.shape[2]
    padded = shared_full.shape[1] // 2
    part = width // (2 * PLANE * depth)
    semaphores = pltpu.SemaphoreType.DMA
    low = x.dtype
    anywhere = pl.BlockSpec(memory_space=pl.ANY)
    local = pl.BlockSpec(memory_space=pltpu.VMEM)
    return pl.pallas_call(
        functools.partial(dispatch_kernel, depth),
        out_shape=[
            jax.ShapeDtypeStruct((depth, PLANE, capacity, width), low),
            jax.ShapeDtypeStruct((depth, tokens, width), low),
            jax.ShapeDtypeStruct((depth, tokens, width), low),
            jax.ShapeDtypeStruct((PLANE, depth, part, 2 * padded), low),
            jax.ShapeDtypeStruct(down_full.shape[1:], low),
            jax.ShapeDtypeStruct(grad_rows.shape, low),
        ],
        in_specs=[local, local] + [anywhere] * 4,
        out_specs=[anywhere] * 6,
        input_output_aliases={5: 5},
        scratch_shapes=[
            pltpu.VMEM((depth, tokens, width), low),
            pltpu.VMEM((depth, PLANE, capacity, width), low),
            pltpu.VMEM((depth, tokens, width), low),
            pltpu.VMEM((width, 2 * padded), low),
            pltpu.VMEM((padded, width), low),
            pltpu.VMEM((depth, tokens, 2 * padded), low),
            pltpu.VMEM((depth, tokens, padded), low),
            pltpu.VMEM((tokens, width), low),
            pltpu.VMEM((tokens, width), low),
            pltpu.VMEM((2, PLANE, part, 2 * padded), low),
            pltpu.VMEM((2, 128, width), low),
            pltpu.VMEM((depth // 2, PLANE, capacity, width), low),
            pltpu.VMEM((depth, PLANE, part, 2 * padded), low),
            pltpu.VMEM((depth, PLANE, part, 2 * padded), low),
            pltpu.VMEM((padded // 256, 128, width), low),
            pltpu.VMEM((padded // 256, 128, width), low),
            semaphores((4,)),
            semaphores((2,)),
            semaphores((PARTS, 2, depth)),
            semaphores((PARTS, depth)),
            semaphores((PLANE, depth)),
            semaphores((PLANE, depth)),
            semaphores((depth,)),
            semaphores((2, 2)),
            semaphores((PLANE, depth)),
            semaphores((PLANE, depth)),
            semaphores((depth,)),
            semaphores((depth,)),
            semaphores((depth,)),
            semaphores((padded // 256,)),
            semaphores((padded // 256,)),
        ],
        compiler_params=pltpu.CompilerParams(
            collective_id=3, has_side_effects=True, vmem_limit_bytes=62 * MEBIBYTE
        ),
        cost_estimate=LONG,
    )(x, choose, grad_line, shared_full, down_full, grad_rows)


def expert_kernel(total, *refs):
    x_ref, grad_ref, gate_in, up_in, down_in, router_ref = refs[:6]
    scaled_ref, d_gate_ref, d_up_ref, back_ref, out_ref, slot_ref = refs[6:12]
    gates, ups, downs, hidden, sem = refs[12:]
    rows = x_ref.shape[0]
    width, inner = gates.shape
    wide = jnp.float32
    loads = [
        pltpu.make_async_copy(source, target, sem.at[k])
        for k, (source, target) in enumerate(zip((gate_in, up_in, down_in), (gates, ups, downs)))
    ]
    first = pl.program_id(0) == 0

    @pl.when(first)
    def _():
        for load in loads:
            load.start()

    logits = jnp.dot(x_ref[...], router_ref[...], preferred_element_type=wide)
    lanes = lax.broadcasted_iota(jnp.int32, logits.shape, 1)
    logits = jnp.where(lanes < total, logits, FLOOR_SCORE)
    powers = jnp.exp(logits - jnp.max(logits, axis=-1, keepdims=True))
    probs = powers / jnp.sum(powers, axis=-1, keepdims=True)
    mine = jnp.where(lanes == lax.axis_index("expert"), probs, 0.0)
    gate = jnp.sum(mine, axis=-1, keepdims=True)

    @pl.when(first)
    def _():
        for load in loads:
            load.wait()

    def columns(start, size, slots):
        at = lanes_at(start, size)
        former = jnp.dot(x_ref[...], gates[:, at], preferred_element_type=wide)
        latter = jnp.dot(x_ref[...], ups[:, at], preferred_element_type=wide)
        raw = dot_nt(grad_ref[...], downs[at, :])
        sig = 1.0 / (1.0 + jnp.exp(-former))
        act = former * sig
        low = (act * latter).astype(hidden.dtype)
        hidden[:, at] = low
        low = low.astype(wide)
        scaled_ref[:, at] = (low * gate).astype(hidden.dtype)
        grad = raw * gate
        d_gate_ref[:, at] = (grad * latter * (sig + act * (1.0 - sig))).astype(hidden.dtype)
        d_up_ref[:, at] = (grad * act).astype(hidden.dtype)
        return slots + jnp.sum(low * raw, axis=-1, keepdims=True)

    full = inner // 256
    slots = lax.fori_loop(
        0, full, lambda n, slots: columns(n * 256, 256, slots), jnp.zeros((rows, 1), wide)
    )
    if inner % 256:
        slots = columns(full * 256, inner % 256, slots)
    slot_ref[...] = jnp.broadcast_to(slots, slot_ref.shape)

    def outward(n, carry):
        at = lanes_at(n * 256, 256)
        back = dot_nt(d_gate_ref[...], gates[at, :]) + dot_nt(d_up_ref[...], ups[at, :])
        back_ref[:, at] = back.astype(back_ref.dtype)
        out = jnp.dot(hidden[...], downs[:, at], preferred_element_type=wide)
        out_ref[:, at] = (out * gate).astype(out_ref.dtype)
        return carry

    lax.fori_loop(0, width // 256, outward, 0)


def run_expert(rows, grads, gate_full, up_full, down_full, router, total):
    count, width = rows.shape
    inner = gate_full.shape[1]
    low, wide = rows.dtype, jnp.float32
    tile = count // 2
    anywhere = pl.BlockSpec(memory_space=pl.ANY)

    def tiles(span):
        return pl.BlockSpec((tile, span), lambda i: (i, 0))

    spans = (inner, inner, inner, width, width)
    return pl.pallas_call(
        functools.partial(expert_kernel, total),
        grid=(2,),
        out_shape=[jax.ShapeDtypeStruct((count, span), low) for span in spans]
        + [jax.ShapeDtypeStruct((count, 128), wide)],
        in_specs=[tiles(width), tiles(width)]
        + [anywhere] * 3
        + [pl.BlockSpec(router.shape, lambda i: (0, 0))],
        out_specs=[tiles(span) for span in spans] + [tiles(128)],
        scratch_shapes=[
            pltpu.VMEM(gate_full.shape, low),
            pltpu.VMEM(up_full.shape, low),
            pltpu.VMEM(down_full.shape, low),
            pltpu.VMEM((tile, inner), low),
            pltpu.SemaphoreType.DMA((3,)),
        ],
        compiler_params=pltpu.CompilerParams(vmem_limit_bytes=62 * MEBIBYTE),
        cost_estimate=MIDDLE,
    )(rows, grads, gate_full, up_full, down_full, router)


def return_kernel(depth, *refs):
    rows_in, scalars_in, choose_ref, shared_in = refs[:4]
    operands_in = refs[4:9]
    back_ref, prob_ref, gate_out, up_out, down_out = refs[9:14]
    came, scalars, shared, onward, incoming, prob_send, prob_land = refs[14:21]
    held = refs[21:26]
    give_wide, give_tall, take_wide, take_tall, done_wide, done_tall = refs[26:32]
    own_sem, es, er, ss, sr, load_sem, shared_sem, cs, cr, ps, pr = refs[32:43]
    ws, wr, ts, tr, wide_sem, tall_sem = refs[43:]
    x_held, gate_held, up_held, hidden_held, grad_held = held
    half = lax.axis_index("fsdp")
    place = lax.axis_index("expert")
    level = place // PLANE
    spot = place % PLANE
    other = (1 - half, place)
    tokens, width = back_ref.shape
    capacity = choose_ref.shape[2]
    wide_count, wide_rows = take_wide.shape[1:3]
    tall_count, tall_rows, tall_width = take_tall.shape
    greet(line_others(half, place, depth) + plane_others(half, place) + [other])

    def rows_to(offset, source):
        mate = (spot + offset) % PLANE
        where = (half, place - spot + mate)
        return (
            remote(
                rows_in.at[source, mate],
                came.at[spot, source],
                es.at[offset, source],
                er.at[offset, source],
                where,
            ),
            remote(
                scalars_in.at[source, mate],
                scalars.at[spot, source],
                ss.at[offset, source],
                sr.at[offset, source],
                where,
            ),
        )

    def rows_from(offset, source):
        mate = (spot + PLANE - offset) % PLANE
        where = (half, place - spot + mate)
        block, small = came.at[mate, source], scalars.at[mate, source]
        return (
            remote(block, block, es.at[offset, source], er.at[offset, source], where),
            remote(small, small, ss.at[offset, source], sr.at[offset, source], where),
        )

    def own_rows(source):
        return (
            pltpu.make_async_copy(
                rows_in.at[source, spot], came.at[spot, source], own_sem.at[0, source]
            ),
            pltpu.make_async_copy(
                scalars_in.at[source, spot], scalars.at[spot, source], own_sem.at[1, source]
            ),
        )

    def shared_load(slot, source):
        return pltpu.make_async_copy(shared_in.at[source], shared.at[slot], shared_sem.at[slot])

    def each_way(s, act):
        def one(way, carry):
            source = level + (2 * way - 1) * s

            @pl.when((source >= 0) & (source < depth) & ((s > 0) | (way == 0)))
            def _():
                act(way, source)

            return carry

        lax.fori_loop(0, 2, one, 0)

    def begin(way, source):
        for offset in range(1, PLANE):
            for copy in rows_to(offset, source):
                copy.start()
        for copy in own_rows(source):
            copy.start()

    def begin_step(i, carry):
        each_way(depth - 1 - i, begin)
        return carry

    lax.fori_loop(0, depth, begin_step, 0)
    loads = [
        pltpu.make_async_copy(source, target, load_sem.at[k])
        for k, (source, target) in enumerate(zip(operands_in, held))
    ]
    for load in loads:
        load.start()
    for load in loads:
        load.wait()

    def wide_tiles(owner, k):
        at = pl.ds(pl.multiple_of((owner * wide_count + k) * wide_rows, wide_rows), wide_rows)
        x = x_held[:, at]
        return dot_tn(x, gate_held[...]), dot_tn(x, up_held[...])

    def tall_tile(owner, k):
        at = pl.ds(pl.multiple_of(k * tall_rows, tall_rows), tall_rows)
        over = pl.ds(pl.multiple_of(owner * tall_width, tall_width), tall_width)
        return dot_tn(hidden_held[:, at], grad_held[:, over])

    def wide_send(which, k):
        slot = k % 2
        return remote(
            give_wide.at[slot, which],
            take_wide.at[which, k],
            ws.at[slot, which],
            wr.at[which, k],
            other,
        )

    def tall_send(k):
        slot = k % 2
        return remote(give_tall.at[slot], take_tall.at[k], ts.at[slot], tr.at[k], other)

    def wide_write(which, k):
        target = (gate_out, up_out)[which]
        at = pl.ds(pl.multiple_of(k * wide_rows, wide_rows), wide_rows)
        return pltpu.make_async_copy(done_wide.at[which], target.at[at, :], wide_sem.at[which])

    def tall_write(k):
        slot = k % 2
        at = pl.ds(pl.multiple_of(k * tall_rows, tall_rows), tall_rows)
        return pltpu.make_async_copy(done_tall.at[slot], down_out.at[at, :], tall_sem.at[slot])

    def give_wide_tile(k):
        @pl.when(k >= 2)
        def _():
            for which in range(2):
                wide_send(which, k - 2).wait_send()

        for which, tile in enumerate(wide_tiles(1 - half, k)):
            give_wide[k % 2, which] = tile.astype(give_wide.dtype)
            wide_send(which, k).start()

    def give_tall_tile(k):
        @pl.when(k >= 2)
        def _():
            tall_send(k - 2).wait_send()

        give_tall[k % 2] = tall_tile(1 - half, k).astype(give_tall.dtype)
        tall_send(k).start()

    def keep_wide_tile(k):
        @pl.when(k >= 1)
        def _():
            for which in range(2):
                wide_write(which, k - 1).wait()

        for which, tile in enumerate(wide_tiles(half, k)):
            wide_send(which, k).wait_recv()
            tile = tile + take_wide[which, k].astype(jnp.float32)
            done_wide[which] = tile.astype(done_wide.dtype)
            wide_write(which, k).start()

    def keep_tall_tile(k):
        @pl.when(k >= 2)
        def _():
            tall_write(k - 2).wait()

        tile = tall_tile(half, k)
        tall_send(k).wait_recv()
        tile = tile + take_tall[k].astype(jnp.float32)
        done_tall[k % 2] = tile.astype(done_tall.dtype)
        tall_write(k).start()

    units = 2 * (wide_count + tall_count)
    each = -(-units // depth)
    bounds = (0, wide_count, wide_count + tall_count, units - tall_count, units)
    acts = (give_wide_tile, give_tall_tile, keep_wide_tile, keep_tall_tile)

    def fill(unit, carry):
        for act, low, high in zip(acts, bounds[:-1], bounds[1:]):

            @pl.when((unit >= low) & (unit < high))
            def _():
                act(unit - low)

        return carry

    def chain_out(source):
        up = jnp.where(source > level, 1, 0)
        step = 2 * up - 1
        slot = jnp.where(source == level - 1, depth, source)
        return remote(
            onward.at[up],
            incoming.at[slot],
            cs.at[source],
            cr.at[slot],
            (half, place + step * PLANE),
        )

    def chain_in(slot):
        block = incoming.at[slot]
        return remote(block, block, cs.at[0], cr.at[slot], (half, place))

    def prob_to(source):
        return remote(
            prob_send.at[source],
            prob_land.at[level],
            ps.at[source],
            pr.at[level],
            (half, source * PLANE + spot),
        )

    def prob_from(source):
        block = prob_land.at[source]
        return remote(block, block, ps.at[source], pr.at[source], (half, source * PLANE + spot))

    def add_incoming(slot):
        chain_in(slot).wait_recv()
        back_ref[...] += incoming[slot].astype(jnp.float32)

    def settle(way, source):
        for copy in own_rows(source):
            copy.wait()
        for offset in range(1, PLANE):
            for copy in rows_from(offset, source):
                copy.wait_recv()
        shared_load(way, source).wait()

        def columns(n, carry):
            at = pl.ds(pl.multiple_of(n * 512, 512), 512)
            total = shared[way, :, at].astype(jnp.float32)
            for mate in range(PLANE):
                total = total + dot_tn(choose_ref[source, mate], came[mate, source, :, at])
            back_ref[:, at] = total
            return carry

        lax.fori_loop(0, width // 512, columns, 0)
        lines = lax.broadcasted_iota(jnp.int32, (8, tokens), 0)
        probs = jnp.zeros((8, tokens), jnp.float32)
        for mate in range(PLANE):
            part = lax.dot_general(
                scalars[mate, source],
                choose_ref[source, mate].astype(jnp.float32),
                (((0,), (0,)), ((), ())),
                preferred_element_type=jnp.float32,
                precision=lax.Precision.HIGHEST,
            )
            probs = jnp.where(lines == mate, part[:8], probs)

        @pl.when((source >= level) & (level > 0))
        def _():
            add_incoming(source)

        @pl.when((source < level) & (level < depth - 1))
        def _():
            add_incoming(source)

        @pl.when((source == level) & (level < depth - 1))
        def _():
            add_incoming(depth)

        @pl.when(source == level)
        def _():
            prob_land[level] = probs

        @pl.when(source != level)
        def _():
            prob_send[source] = probs
            prob_to(source).start()
            former = source + 2 * way - 1

            @pl.when((former >= 0) & (former < depth))
            def _():
                chain_out(former).wait_send()

            onward[way] = back_ref[...].astype(onward.dtype)
            chain_out(source).start()

    def step(i, carry):
        s = depth - 1 - i
        each_way(s, lambda way, source: shared_load(way, source).start())
        lax.fori_loop(i * each, jnp.minimum((i + 1) * each, units), fill, 0)
        each_way(s, settle)
        return carry

    lax.fori_loop(0, depth, step, 0)
    for which in range(2):
        wide_write(which, wide_count - 1).wait()
        for k in (wide_count - 2, wide_count - 1):
            wide_send(which, k).wait_send()
    for k in (tall_count - 2, tall_count - 1):
        tall_write(k).wait()
        tall_send(k).wait_send()

    def finish(source, carry):
        for offset in range(1, PLANE):
            for copy in rows_to(offset, source):
                copy.wait_send()

        @pl.when((source == level - 1) | (source == level + 1))
        def _():
            chain_out(source).wait_send()

        @pl.when(source != level)
        def _():
            prob_to(source).wait_send()
            prob_from(source).wait_recv()

        prob_ref[source] = prob_land[source]
        return carry

    lax.fori_loop(0, depth, finish, 0)


def give_back(rows, scalars, choose, shared_back, operands):
    depth, _, capacity, tokens = choose.shape
    width = rows.shape[-1]
    slots, inner = operands[1].shape
    wide_rows, tall_rows = 256 if depth <= PLANE else 128, 128
    wide_count = width // 2 // wide_rows
    tall_count = inner // tall_rows
    semaphores = pltpu.SemaphoreType.DMA
    low = rows.dtype
    wide = jnp.float32
    anywhere = pl.BlockSpec(memory_space=pl.ANY)
    local = pl.BlockSpec(memory_space=pltpu.VMEM)
    return pl.pallas_call(
        functools.partial(return_kernel, depth),
        out_shape=[
            jax.ShapeDtypeStruct((tokens, width), wide),
            jax.ShapeDtypeStruct((depth, 8, tokens), wide),
            jax.ShapeDtypeStruct((width // 2, inner), low),
            jax.ShapeDtypeStruct((width // 2, inner), low),
            jax.ShapeDtypeStruct((inner, width // 2), low),
        ],
        in_specs=[anywhere, anywhere, local, anywhere] + [anywhere] * 5,
        out_specs=[local, local, anywhere, anywhere, anywhere],
        scratch_shapes=[
            pltpu.VMEM((PLANE, depth, capacity, width), low),
            pltpu.VMEM((PLANE, depth, capacity, 128), wide),
            pltpu.VMEM((2, tokens, width), low),
            pltpu.VMEM((2, tokens, width), low),
            pltpu.VMEM((depth + 1, tokens, width), low),
            pltpu.VMEM((depth, 8, tokens), wide),
            pltpu.VMEM((depth, 8, tokens), wide),
        ]
        + [pltpu.VMEM(operand.shape, low) for operand in operands]
        + [
            pltpu.VMEM((2, 2, wide_rows, inner), low),
            pltpu.VMEM((2, tall_rows, width // 2), low),
            pltpu.VMEM((2, wide_count, wide_rows, inner), low),
            pltpu.VMEM((tall_count, tall_rows, width // 2), low),
            pltpu.VMEM((2, wide_rows, inner), low),
            pltpu.VMEM((2, tall_rows, width // 2), low),
            semaphores((2, depth)),
            semaphores((PLANE, depth)),
            semaphores((PLANE, depth)),
            semaphores((PLANE, depth)),
            semaphores((PLANE, depth)),
            semaphores((5,)),
            semaphores((2,)),
            semaphores((depth,)),
            semaphores((depth + 1,)),
            semaphores((depth,)),
            semaphores((depth,)),
            semaphores((2, 2)),
            semaphores((2, wide_count)),
            semaphores((2,)),
            semaphores((tall_count,)),
            semaphores((2,)),
            semaphores((2,)),
        ],
        compiler_params=pltpu.CompilerParams(
            collective_id=4, has_side_effects=True, vmem_limit_bytes=62 * MEBIBYTE
        ),
        cost_estimate=LONG,
    )(rows, scalars, choose, shared_back, *operands)


def reduce_kernel(depth, count, cut, *refs):
    parts = refs[:count]
    move_in, out_ref, move_out = refs[count : count + 3]
    acc, inc, one_a, one_b, two_a, two_b, zin = refs[count + 3 : count + 10]
    own_sem, cs, cr, ps, pr, qs, qr, zs, zr, move_sem, ms, mr = refs[count + 10 :]
    half = lax.axis_index("fsdp")
    place = lax.axis_index("expert")
    level = place // PLANE
    spot = place % PLANE
    total = depth * PLANE
    mates = plane_mates(place)
    rows = out_ref.shape[0]
    group = PLANE * rows
    width = out_ref.shape[1]
    greet_neighbours(half, place, depth)

    starts = [sum(part.shape[1] for part in parts[:k]) for k in range(count)]

    def rows_of(k, owner, t):
        start = pl.multiple_of((owner * total + t * PLANE) * rows, group)
        return parts[k].at[pl.ds(start, group), :]

    def kept(k, t):
        return pltpu.make_async_copy(
            rows_of(k, half, t),
            acc.at[t, :, pl.ds(starts[k], parts[k].shape[1])],
            own_sem.at[k, t],
        )

    def given(k, t):
        return remote(
            rows_of(k, 1 - half, t),
            inc.at[t, :, pl.ds(starts[k], parts[k].shape[1])],
            cs.at[k, t],
            cr.at[k, t],
            (1 - half, place),
        )

    def block(t, q, n, lo, hi):
        return acc.at[t, pl.ds(pl.multiple_of(q * rows, rows), n * rows), pl.ds(lo, hi - lo)]

    pair = spot - spot % 2

    def first(t, turn):
        low = spot % 2
        if turn == 0:
            source = block(t, 2 - pair, 2, 0, cut)
            target, where = one_a.at[t], mates[1]
        else:
            source = block(t, 2 * turn - 1 - low, 1, cut, width)
            target, where = one_b.at[t, turn - 1], mates[0]
        return remote(source, target, ps.at[turn, t], pr.at[turn, t], (half, where))

    def second(t, turn):
        if turn == 0:
            source = block(t, pair + 1 - spot % 2, 1, 0, cut)
            target, where = two_a.at[t], mates[0]
        else:
            source = block(t, (spot + 2) % PLANE, 1, cut, width)
            target, where = two_b.at[t], mates[1]
        return remote(source, target, qs.at[turn, t], qr.at[turn, t], (half, where))

    def line(t, way):
        step = 2 * way - 1
        return remote(
            block(t, spot, 1, 0, width),
            zin.at[way, t],
            zs.at[way, t],
            zr.at[way, t],
            (half, place + step * PLANE),
        )

    def add_rows(t, start, n, lo, hi, piece):
        def one(i, carry):
            r = pl.multiple_of(i * 16, 16)
            at = (t, pl.ds(pl.multiple_of(start + r, 16), 16), pl.ds(lo, hi - lo))
            new = piece(pl.ds(r, 16)).astype(jnp.float32)
            acc[at] = (acc[at].astype(jnp.float32) + new).astype(acc.dtype)
            return carry

        lax.fori_loop(0, n // 16, one, 0)

    def stage_a(t):
        for k in range(count):
            kept(k, t).wait()
            given(k, t).wait_recv()
        add_rows(t, 0, group, 0, width, lambda r: inc[t, r, :])
        for turn in range(3):
            first(t, turn).start()

    def stage_b(t):
        first(t, 0).wait_recv()
        add_rows(t, pair * rows, 2 * rows, 0, cut, lambda r: one_a[t, r, :])
        second(t, 0).start()
        for turn in range(2):
            first(t, 1 + turn).wait_recv()
            add_rows(
                t,
                (spot % 2 + 2 * turn) * rows,
                rows,
                cut,
                width,
                lambda r: one_b[t, turn, r, :],
            )
        second(t, 1).start()

    def stage_c(t):
        second(t, 0).wait_recv()
        add_rows(t, spot * rows, rows, 0, cut, lambda r: two_a[t, r, :])
        second(t, 1).wait_recv()
        add_rows(t, spot * rows, rows, cut, width, lambda r: two_b[t, r, :])

        def take(way):
            line(t, way).wait_recv()
            add_rows(t, spot * rows, rows, 0, width, lambda r: zin[way, t, r, :])

        @pl.when((t >= level) & (level > 0))
        def _():
            take(1)

        @pl.when((t <= level) & (level < depth - 1))
        def _():
            take(0)

        @pl.when(t > level)
        def _():
            line(t, 1).start()

        @pl.when(t < level)
        def _():
            line(t, 0).start()

    def visit(index, act):
        if index >= depth or index < 0:
            return
        step = depth - 1 - index
        if step == 0:
            act(level)
            return

        @pl.when(level + step < depth)
        def _():
            act(level + step)

        @pl.when(level - step >= 0)
        def _():
            act(level - step)

    def begin(t):
        for k in range(count):
            given(k, t).start()
            kept(k, t).start()

    for index in range(depth):
        visit(index, begin)
    move_start, move_finish = exchange_along(
        depth,
        half,
        place,
        move_in,
        lambda source: move_out.at[source],
        move_sem.at[0],
        ms,
        mr,
    )
    move_start()
    for index in range(depth + 2):
        visit(index, stage_a)
        visit(index - 1, stage_b)
        visit(index - 2, stage_c)

    def emit(i, carry):
        r = pl.multiple_of(i * 16, 16)
        at = pl.ds(pl.multiple_of(spot * rows + r, 16), 16)
        out_ref[pl.ds(r, 16), :] = acc[level, at, :].astype(out_ref.dtype)
        return carry
    lax.fori_loop(0, rows // 16, emit, 0)
    move_finish()

    def finish(t, carry):
        for k in range(count):
            given(k, t).wait_send()
        for turn in range(3):
            first(t, turn).wait_send()
        for turn in range(2):
            second(t, turn).wait_send()

        @pl.when(t > level)
        def _():
            line(t, 1).wait_send()

        @pl.when(t < level)
        def _():
            line(t, 0).wait_send()
        return carry

    lax.fori_loop(0, depth, finish, 0)


def reduce_rows(parts, moved, cut):
    total = lax.axis_size("expert")
    depth = total // PLANE
    rows = parts[0].shape[0] // (2 * total)
    width = sum(part.shape[1] for part in parts)
    group = PLANE * rows
    n = len(parts)
    semaphores = pltpu.SemaphoreType.DMA
    low = parts[0].dtype
    return pl.pallas_call(
        functools.partial(reduce_kernel, depth, n, cut),
        out_shape=[
            jax.ShapeDtypeStruct((rows, width), jnp.float32),
            jax.ShapeDtypeStruct(moved.shape, moved.dtype),
        ],
        in_specs=[pl.BlockSpec(memory_space=pl.ANY)] * (n + 1),
        out_specs=[
            pl.BlockSpec(memory_space=pltpu.VMEM),
            pl.BlockSpec(memory_space=pl.ANY),
        ],
        scratch_shapes=[
            pltpu.VMEM((depth, group, width), low),
            pltpu.VMEM((depth, group, width), low),
            pltpu.VMEM((depth, 2 * rows, cut), low),
            pltpu.VMEM((depth, 2, rows, width - cut), low),
            pltpu.VMEM((depth, rows, cut), low),
            pltpu.VMEM((depth, rows, width - cut), low),
            pltpu.VMEM((2, depth, rows, width), low),
            semaphores((n, depth)),
            semaphores((n, depth)),
            semaphores((n, depth)),
            semaphores((3, depth)),
            semaphores((3, depth)),
            semaphores((2, depth)),
            semaphores((2, depth)),
            semaphores((2, depth)),
            semaphores((2, depth)),
            semaphores((1,)),
            semaphores((depth,)),
            semaphores((depth,)),
        ],
        cost_estimate=LONG,
        compiler_params=pltpu.CompilerParams(
            collective_id=2, has_side_effects=True, vmem_limit_bytes=60 * MEBIBYTE
        ),
    )(*parts, moved)


def turned(values):
    width = values.shape[1]
    lanes = lax.broadcasted_iota(jnp.int32, values.shape, 1)
    return jnp.where(
        lanes % ROPE < ROPE // 2,
        pltpu.roll(values, width - ROPE // 2, 1),
        pltpu.roll(values, ROPE // 2, 1),
    )


def row_scale(values):
    return lax.rsqrt(jnp.mean(values * values, axis=-1, keepdims=True) + EPSILON)


def head_lanes(values, head):
    lanes = lax.broadcasted_iota(jnp.int32, values.shape, 1)
    return jnp.where(lanes // ROPE == head % 2, values, jnp.zeros_like(values))


def lanes_at(start, size):
    return pl.ds(pl.multiple_of(start, 128), size)


def attend_kernel(layout, *refs):
    x_ref, packed, up_in, first_gain, latent_gain, feed_gain, cosine, sine, mask = refs[:9]
    choose_ref, grad_in = refs[9:11]
    normed, residual, mixed, queries, latent, compressed = refs[11:17]
    expanded, keys_rope, log_total, heads, grad_out = refs[17:22]
    entry, ups, outs, prior_latent, prior_rope, grads, grad_placed = refs[22:29]
    load_sem, up_sem, send_sem, receive_sem, gl, gs, gr, grad_sem = refs[29:]
    entry_width, out_start = layout
    half = lax.axis_index("fsdp")
    place = lax.axis_index("expert")
    other = (1 - half, place)
    rows, width = x_ref.shape
    low = x_ref.dtype
    scale = (NOPE + ROPE) ** (-0.5)
    loads = [
        pltpu.make_async_copy(packed.at[:, pl.ds(0, entry_width)], entry, load_sem.at[0]),
        pltpu.make_async_copy(packed.at[:, pl.ds(out_start, width)], outs, load_sem.at[1]),
    ]
    up_loads = load_ups(up_in, ups, up_sem, layout)
    depth = grad_in.shape[0]

    def grad_load(n):
        return pltpu.make_async_copy(grad_in.at[2 * n], grads.at[n], gl.at[n])

    grad_start, grad_finish = exchange_plane(
        half,
        place,
        lambda mate, source: grad_placed.at[source // 2, mate],
        lambda mate, source: grad_out.at[source, mate],
        grad_sem,
        gs,
        gr,
    )

    def each_grad(act):
        def one(n, carry):
            act(n)
            return carry

        lax.fori_loop(0, depth // 2, one, 0)

    def give_grad(n):
        grad_load(n).wait()
        place_rows(choose_ref, 2 * n, grads.at[n], grad_placed.at[n])
        grad_start(2 * n)

    each_grad(lambda n: grad_load(n).start())
    for load in loads[:1] + up_loads + loads[1:]:
        load.start()
    greet([other] + plane_others(half, place))
    each_grad(give_grad)
    x = x_ref[...].astype(jnp.float32)
    normed[...] = (x * row_scale(x) * first_gain[...]).astype(low)
    loads[0].wait()
    nope_width = HEADS * NOPE
    query_width = HEADS * (NOPE + ROPE)

    def through(start, size):
        return jnp.dot(
            normed[...], entry[:, lanes_at(start, size)], preferred_element_type=jnp.float32
        )

    def rotary(values):
        return values * cosine[...] + turned(values) * sine[...]

    squeezed = through(query_width, LATENT)
    compressed[...] = squeezed
    latent[...] = (squeezed * row_scale(squeezed) * latent_gain[...]).astype(low)
    key = rotary(through(query_width + LATENT, 128))
    keys_rope[pl.ds(rows, rows), :] = (key + pltpu.roll(key, ROPE, 1)).astype(low)
    sends = [
        remote(latent, prior_latent, send_sem.at[0], receive_sem.at[0], other),
        remote(
            keys_rope.at[pl.ds(rows, rows), :],
            prior_rope,
            send_sem.at[1],
            receive_sem.at[1],
            other,
        ),
    ]

    @pl.when(half == 0)
    def _():
        for send in sends:
            send.start()

    def nope_part(n, carry):
        queries[:, lanes_at(n * 1024, 1024)] = through(n * 1024, 1024).astype(low)
        return carry

    lax.fori_loop(0, nope_width // 1024, nope_part, 0)

    def rope_part(n, carry):
        values = through(nope_width + n * 512, 512)
        for k in range(4):
            tile = rotary(values[:, k * 128 : (k + 1) * 128])
            queries[:, lanes_at(nope_width + n * 512 + k * 128, 128)] = tile.astype(low)
        return carry

    lax.fori_loop(0, HEADS * ROPE // 512, rope_part, 0)
    for load in up_loads:
        load.wait()
    quarters, span = ups.shape[0], ups.shape[-1]

    def expand(source, first):
        def one(n, carry):
            expanded[pl.ds(first, rows), lanes_at(n * span, span)] = jnp.dot(
                source[...], whole(ups[n]), preferred_element_type=jnp.float32
            ).astype(low)
            return carry

        lax.fori_loop(0, quarters, one, 0)

    expand(latent, rows)

    @pl.when(half == 0)
    def _():
        expanded[pl.ds(0, rows), :] = jnp.zeros((rows, quarters * span), low)
        keys_rope[pl.ds(0, rows), :] = jnp.zeros((rows, 128), low)
        for send in sends:
            send.wait_send()

    @pl.when(half == 1)
    def _():
        for send in sends:
            send.wait_recv()
        keys_rope[pl.ds(0, rows), :] = prior_rope[...]
        expand(prior_latent, 0)

    def head(h, totals):
        pair = queries[:, lanes_at(nope_width + (h // 2) * 128, 128)]
        scores = dot_nt(
            queries[:, lanes_at(h * NOPE, NOPE)], expanded[:, lanes_at(h * 256, NOPE)]
        )
        scores = scores + dot_nt(head_lanes(pair, h), keys_rope[...])
        scores = jnp.where(mask[...] > 0, scores * scale, FLOOR_SCORE)
        top = jnp.max(scores, axis=-1, keepdims=True)
        weights = jnp.exp(scores - top)
        total = jnp.sum(weights, axis=-1, keepdims=True)
        heads[:, lanes_at(h * VALUE, VALUE)] = jnp.dot(
            (weights / total).astype(low),
            expanded[:, lanes_at(h * 256 + NOPE, VALUE)],
            preferred_element_type=jnp.float32,
        ).astype(low)
        lanes = lax.broadcasted_iota(jnp.int32, totals.shape, 1)
        return jnp.where(lanes == h, top + jnp.log(total), totals)

    log_total[...] = lax.fori_loop(0, HEADS, head, jnp.zeros((rows, 128), jnp.float32))
    loads[1].wait()

    def project(n, carry):
        at = lanes_at(n * 1024, 1024)
        residual[:, at] = x_ref[:, at].astype(jnp.float32) + jnp.dot(
            heads[...], outs[:, at], preferred_element_type=jnp.float32
        )
        return carry

    lax.fori_loop(0, width // 1024, project, 0)
    total = residual[...]
    mixed[...] = (total * row_scale(total) * feed_gain[...]).astype(low)
    each_grad(lambda n: grad_finish(2 * n))


def attend(x, packed, ups, ups_shape, gains, tables, mask, choose, grad_line, layout):
    rows, width = x.shape
    low, wide = x.dtype, jnp.float32
    semaphores = pltpu.SemaphoreType.DMA
    anywhere = pl.BlockSpec(memory_space=pl.ANY)
    local = pl.BlockSpec(memory_space=pltpu.VMEM)
    expanded_width = HEADS * (NOPE + VALUE)
    depth, _, capacity, _ = choose.shape
    shapes = [
        ((rows, width), low),
        ((rows, width), wide),
        ((rows, width), low),
        ((rows, HEADS * (NOPE + ROPE)), low),
        ((rows, LATENT), low),
        ((rows, LATENT), wide),
        ((2 * rows, expanded_width), low),
        ((2 * rows, 128), low),
        ((rows, 128), wide),
        ((rows, HEADS * VALUE), low),
        ((depth, PLANE, capacity, width), low),
    ]
    return pl.pallas_call(
        functools.partial(attend_kernel, layout),
        out_shape=[jax.ShapeDtypeStruct(shape, dtype) for shape, dtype in shapes],
        in_specs=[local, anywhere, anywhere] + [local] * 7 + [anywhere],
        out_specs=[local] * (len(shapes) - 1) + [anywhere],
        scratch_shapes=[
            pltpu.VMEM((packed.shape[0], layout[0]), low),
            pltpu.VMEM(ups_shape, low),
            pltpu.VMEM((packed.shape[0], width), low),
            pltpu.VMEM((rows, LATENT), low),
            pltpu.VMEM((rows, 128), low),
            pltpu.VMEM((depth // 2, rows, width), low),
            pltpu.VMEM((depth // 2, PLANE, capacity, width), low),
            semaphores((2,)),
            semaphores((ups_shape[0],)),
            semaphores((2,)),
            semaphores((2,)),
            semaphores((depth // 2,)),
            semaphores((PLANE, depth)),
            semaphores((PLANE, depth)),
            semaphores((depth,)),
        ],
        compiler_params=pltpu.CompilerParams(
            collective_id=5, has_side_effects=True, vmem_limit_bytes=56 * MEBIBYTE
        ),
        cost_estimate=MIDDLE,
    )(x, packed, ups, *gains, *tables, mask, choose, grad_line)


def load_ups(up_in, ups, sem, layout):
    if up_in.shape == ups.shape:
        return [pltpu.make_async_copy(up_in, ups, sem.at[0])]
    span = ups.shape[-1]
    return [
        pltpu.make_async_copy(
            up_in.at[:, k, :, pl.ds(layout[0], span)], ups.at[k], sem.at[k]
        )
        for k in range(ups.shape[0])
    ]


def whole(block):
    return block.reshape(-1, block.shape[-1])


def attend_back_kernel(layout, count, *refs):
    back_in, packed, up_in, queries, expanded, keys_rope, log_total = refs[:7]
    latent, compressed, normed, heads, x_ref, residual, cotangent = refs[7:14]
    d_logits, router, latent_gain, first_gain, feed_gain, cosine, sine, mask = refs[14:22]
    rows_in = refs[22]
    refs = refs[24 + count :]
    token_grad, up_grad, gain_grad, first_grad, feed_grad, entry_grad, out_grad = refs[:7]
    rows_out, outs, ups, d_heads, own, prior, came, prior_rope, came_rope = refs[7:16]
    entry, entry_low, up_tile, entry_tile, out_tile, d_ref = refs[16:22]
    load_sem, up_sem, send_sem, receive_sem, write_sem, es, er = refs[22:]
    entry_width, out_start = layout
    half = lax.axis_index("fsdp")
    place = lax.axis_index("expert")
    other = (1 - half, place)
    rows, width = d_ref.shape
    low = d_ref.dtype
    wide = jnp.float32
    scale = (NOPE + ROPE) ** (-0.5)

    def norm_back(values, gain, incoming):
        root = row_scale(values)
        scaled = gain * incoming
        inner = jnp.mean(values * scaled, axis=-1, keepdims=True)
        gain_sum = jnp.sum(incoming * values * root, axis=0, keepdims=True)
        return root * scaled - values * (root * root * root) * inner, gain_sum

    nope_width = HEADS * NOPE
    query_width = HEADS * (NOPE + ROPE)
    loads = [
        pltpu.make_async_copy(packed.at[:, pl.ds(out_start, width)], outs, load_sem.at[0]),
        pltpu.make_async_copy(packed.at[:, pl.ds(0, entry_width)], entry, load_sem.at[1]),
    ]
    up_loads = load_ups(up_in, ups, up_sem, layout)
    for load in loads + up_loads:
        load.start()
    greet([other] + plane_others(half, place))
    rows_start, rows_finish = exchange_plane(
        half,
        place,
        lambda mate, level: rows_in.at[level, mate],
        lambda mate, level: rows_out.at[level, mate],
        None,
        es,
        er,
        own_there=True,
    )

    def each_level(act):
        def one(level, carry):
            act(level)
            return carry

        lax.fori_loop(0, rows_in.shape[0], one, 0)

    each_level(rows_start)
    mixed_grad = back_in[...] + dot_nt(d_logits[...], router[...])
    through_norm, gain_sum = norm_back(residual[...], feed_gain[...], mixed_grad)
    feed_grad[...] = jnp.broadcast_to(gain_sum, feed_grad.shape)
    token_grad[...] = cotangent[...].astype(wide) + through_norm
    d_ref[...] = token_grad[...].astype(low)

    def write(kind, k):
        staged, target = ((out_tile, out_grad), (entry_tile, entry_grad), (up_tile, up_grad))[kind]
        size = staged.shape[1]
        if kind == 2:
            place_at = up_grad.at[k] if up_grad.shape[0] == ups.shape[0] else up_grad.at[:, k]
        else:
            place_at = target.at[pl.ds(pl.multiple_of(k * size, size), size), :]
        return pltpu.make_async_copy(
            staged.at[k % 2], place_at, write_sem.at[kind, k % 2]
        )

    def put(kind, k, value):
        staged = (out_tile, entry_tile, up_tile)[kind]

        @pl.when(k >= 2)
        def _():
            write(kind, k - 2).wait()

        staged[k % 2] = value.astype(low).reshape(staged.shape[1:])
        write(kind, k).start()

    def settle(kind, total):
        for k in range(max(0, total - 2), total):
            write(kind, k).wait()

    def out_part(k, carry):
        size = out_tile.shape[1]
        put(0, k, dot_tn(heads[:, lanes_at(k * size, size)], d_ref[...]))
        return carry

    out_count = heads.shape[1] // out_tile.shape[1]
    lax.fori_loop(0, out_count, out_part, 0)
    loads[0].wait()

    def head_part(n, carry):
        at = lanes_at(n * 1024, 1024)
        d_heads[:, at] = dot_nt(d_ref[...], outs[at, :]).astype(low)
        return carry

    lax.fori_loop(0, width // 1024, head_part, 0)

    def turn_back(values):
        return values * cosine[...] - turned(values) * sine[...]

    def pair_of_heads(n, rope_sum):
        pair = queries[:, lanes_at(nope_width + n * 128, 128)]
        query_rope = jnp.zeros((rows, 128), wide)
        for k in range(2):
            h = 2 * n + k
            query = queries[:, lanes_at(h * NOPE, NOPE)]
            key = expanded[:, lanes_at(h * 256, NOPE)]
            value = expanded[:, lanes_at(h * 256 + NOPE, VALUE)]
            d_head = d_heads[:, lanes_at(h * VALUE, VALUE)]
            own_pair = head_lanes(pair, k)
            scores = dot_nt(query, key) + dot_nt(own_pair, keys_rope[...])
            scores = jnp.where(mask[...] > 0, scores * scale, FLOOR_SCORE)
            lanes = lax.broadcasted_iota(jnp.int32, log_total.shape, 1)
            log_sum = jnp.sum(
                jnp.where(lanes == h, log_total[...], 0.0), axis=-1, keepdims=True
            )
            probs = jnp.exp(scores - log_sum)
            d_probs = dot_nt(d_head, value)
            delta = jnp.sum(probs * d_probs, axis=-1, keepdims=True)
            d_scores = (probs * (d_probs - delta)).astype(low)
            entry_low[:, lanes_at(h * NOPE, NOPE)] = (
                jnp.dot(d_scores, key, preferred_element_type=wide) * scale
            ).astype(low)
            query_rope = query_rope + head_lanes(
                jnp.dot(d_scores, keys_rope[...], preferred_element_type=wide), k
            )
            d_key = dot_tn(d_scores, query) * scale
            d_value = dot_tn(probs.astype(low), d_head)
            own[:, lanes_at(h * 256, NOPE)] = d_key[rows:]
            own[:, lanes_at(h * 256 + NOPE, VALUE)] = d_value[rows:]
            prior[:, lanes_at(h * 256, NOPE)] = d_key[:rows].astype(low)
            prior[:, lanes_at(h * 256 + NOPE, VALUE)] = d_value[:rows].astype(low)
            rope_sum = rope_sum + dot_tn(d_scores, own_pair)
        entry_low[:, lanes_at(nope_width + n * 128, 128)] = (
            turn_back(query_rope) * scale
        ).astype(low)
        return rope_sum

    rope_sum = lax.fori_loop(
        0, HEADS // 2, pair_of_heads, jnp.zeros((2 * rows, 128), wide)
    )
    rope_sum = (rope_sum + pltpu.roll(rope_sum, ROPE, 1)) * scale
    prior_rope[...] = rope_sum[:rows].astype(low)
    sends = [
        remote(prior, came, send_sem.at[0], receive_sem.at[0], other),
        remote(prior_rope, came_rope, send_sem.at[1], receive_sem.at[1], other),
    ]

    @pl.when(half == 1)
    def _():
        for send in sends:
            send.start()
        came_rope[...] = jnp.zeros((rows, 128), low)
        for send in sends:
            send.wait_send()
        prior[...] = own[...].astype(low)

    @pl.when(half == 0)
    def _():
        for send in sends:
            send.wait_recv()
        prior[...] = (own[...] + came[...].astype(wide)).astype(low)

    for load in up_loads:
        load.wait()
    quarters, span = ups.shape[0], ups.shape[-1]

    def spread(n, d_latent):
        part = prior[:, lanes_at(n * span, span)]
        put(2, n, dot_tn(latent[...], part))
        return d_latent + dot_nt(part, whole(ups[n]))

    d_latent = lax.fori_loop(0, quarters, spread, jnp.zeros((rows, LATENT), wide))
    d_squeezed, gain_sum = norm_back(compressed[...], latent_gain[...], d_latent)
    gain_grad[...] = jnp.broadcast_to(gain_sum, gain_grad.shape)
    entry_low[:, lanes_at(query_width, LATENT)] = d_squeezed.astype(low)
    key = rope_sum[rows:] + came_rope[...].astype(wide)
    entry_low[:, lanes_at(query_width + LATENT, 128)] = turn_back(head_lanes(key, 0)).astype(low)

    def entry_part(k, carry):
        size = entry_tile.shape[1]
        put(1, k, dot_tn(normed[:, lanes_at(k * size, size)], entry_low[...]))
        return carry

    entry_count = width // entry_tile.shape[1]
    lax.fori_loop(0, entry_count, entry_part, 0)
    loads[1].wait()

    def normed_part(n, carry):
        at = lanes_at(n * 1024, 1024)
        own[:, at] = dot_nt(entry_low[...], entry[at, :])
        return carry

    lax.fori_loop(0, width // 1024, normed_part, 0)
    through_norm, gain_sum = norm_back(
        x_ref[...].astype(wide), first_gain[...], own[:, pl.ds(0, width)]
    )
    first_grad[...] = jnp.broadcast_to(gain_sum, first_grad.shape)
    token_grad[...] += through_norm
    settle(0, out_count)
    settle(1, entry_count)
    settle(2, quarters)
    each_level(rows_finish)


def attend_back(
    back, packed, ups, ups_shape, kept, gains, tables, mask, returning, before, layout
):
    rows, width = back.shape
    low, wide = packed.dtype, jnp.float32
    semaphores = pltpu.SemaphoreType.DMA
    anywhere = pl.BlockSpec(memory_space=pl.ANY)
    local = pl.BlockSpec(memory_space=pltpu.VMEM)
    expanded_width = HEADS * (NOPE + VALUE)
    quarters, blocks, part, span = ups_shape
    up_grad = (blocks, quarters, part, span) if blocks > 1 else ups_shape
    return pl.pallas_call(
        functools.partial(attend_back_kernel, layout, len(before)),
        out_shape=[
            jax.ShapeDtypeStruct((rows, width), wide),
            jax.ShapeDtypeStruct(up_grad, low),
            jax.ShapeDtypeStruct((8, LATENT), wide),
            jax.ShapeDtypeStruct((8, width), wide),
            jax.ShapeDtypeStruct((8, width), wide),
            jax.ShapeDtypeStruct((width, layout[0]), low),
            jax.ShapeDtypeStruct((HEADS * VALUE, width), low),
            jax.ShapeDtypeStruct(returning[0].shape, low),
        ],
        in_specs=[local, anywhere, anywhere]
        + [local] * (len(kept) + len(gains) + len(tables) + 1)
        + [anywhere] * (2 + len(before)),
        out_specs=[local, anywhere] + [local] * 3 + [anywhere] * 3,
        input_output_aliases={23: 7},
        scratch_shapes=[
            pltpu.VMEM((packed.shape[0], width), low),
            pltpu.VMEM(ups_shape, low),
            pltpu.VMEM((rows, HEADS * VALUE), low),
            pltpu.VMEM((rows, expanded_width), wide),
            pltpu.VMEM((rows, expanded_width), low),
            pltpu.VMEM((rows, expanded_width), low),
            pltpu.VMEM((rows, 128), low),
            pltpu.VMEM((rows, 128), low),
            pltpu.VMEM((packed.shape[0], layout[0]), low),
            pltpu.VMEM((rows, layout[0]), low),
            pltpu.VMEM((2,) + ups_shape[1:], low),
            pltpu.VMEM((2, 128, layout[0]), low),
            pltpu.VMEM((2, 128, width), low),
            pltpu.VMEM((rows, width), low),
            semaphores((2,)),
            semaphores((quarters,)),
            semaphores((2,)),
            semaphores((2,)),
            semaphores((3, 2)),
            semaphores((PLANE, returning[0].shape[0])),
            semaphores((PLANE, returning[0].shape[0])),
        ],
        compiler_params=pltpu.CompilerParams(
            collective_id=6, has_side_effects=True, vmem_limit_bytes=62 * MEBIBYTE
        ),
        cost_estimate=LONG,
    )(back, packed, ups, *kept, *gains, *tables, mask, *returning, *before)


def run_and_return_kernel(depth, total, *refs):
    x_in, grad_in, gate_in, up_in, down_in, router_ref, choose_ref, shared_in = refs[:8]
    back_ref, prob_ref, gate_out, up_out, down_out, y_out, y_own = refs[8:15]
    came, scalars, shared, onward, incoming, prob_send, prob_land = refs[15:22]
    x_held, gate_held, up_held, hidden_held, grad_held, hidden = refs[22:28]
    gates, ups, downs, sent, scalars_sent, y_stage = refs[28:34]
    es, er, ss, sr, load_sem, shared_sem, cs, cr, ps, pr = refs[34:44]
    ws, wr, ts, tr, wide_sem, tall_sem, y_sem, free_sem = refs[44:]
    half = lax.axis_index("fsdp")
    place = lax.axis_index("expert")
    level = place // PLANE
    spot = place % PLANE
    other = (1 - half, place)
    tokens, width = back_ref.shape
    capacity = choose_ref.shape[2]
    inner = gates.shape[1]
    wide_rows, tall_rows, tall_width = 256, 128, width // 2
    wide_count, tall_count = width // 2 // wide_rows, inner // tall_rows
    wide = jnp.float32

    def take_wide(which, k):
        at = pl.multiple_of((which * wide_count + k) * wide_rows, wide_rows)
        return gates.at[pl.ds(at, wide_rows), :]

    def take_tall(k):
        at = pl.multiple_of(k * tall_rows, tall_rows)
        return ups.at[pl.ds(at, tall_rows), pl.ds(0, tall_width)]

    def give_wide(slot, which):
        at = pl.multiple_of((slot * 2 + which) * wide_rows, wide_rows)
        return downs.at[pl.ds(at, wide_rows), pl.ds(0, inner)]

    def give_tall(slot):
        at = pl.multiple_of(4 * wide_rows + slot * tall_rows, tall_rows)
        return downs.at[pl.ds(at, tall_rows), pl.ds(0, tall_width)]

    def done_wide(which):
        return ups.at[pl.ds(tall_count * tall_rows + which * wide_rows, wide_rows), :]

    def done_tall(slot):
        at = pl.multiple_of(slot * tall_width, tall_width)
        return downs.at[pl.ds(4 * wide_rows + 2 * tall_rows, tall_rows), pl.ds(at, tall_width)]

    greet(line_others(half, place, depth) + plane_others(half, place) + [other])

    def rows_to(offset, way, source):
        mate = (spot + offset) % PLANE
        where = (half, place - spot + mate)
        return (
            remote(
                sent.at[way, mate],
                came.at[spot, source],
                es.at[offset, source],
                er.at[offset, source],
                where,
            ),
            remote(
                scalars_sent.at[way, mate],
                scalars.at[spot, source],
                ss.at[offset, source],
                sr.at[offset, source],
                where,
            ),
        )

    def rows_from(offset, source):
        mate = (spot + PLANE - offset) % PLANE
        where = (half, place - spot + mate)
        block, small = came.at[mate, source], scalars.at[mate, source]
        return (
            remote(block, block, es.at[offset, source], er.at[offset, source], where),
            remote(small, small, ss.at[offset, source], sr.at[offset, source], where),
        )

    def shared_load(slot, source):
        return pltpu.make_async_copy(shared_in.at[source], shared.at[slot], shared_sem.at[slot])

    def each_way(s, act):
        def one(way, carry):
            source = level + (2 * way - 1) * s

            @pl.when((source >= 0) & (source < depth) & ((s > 0) | (way == 0)))
            def _():
                act(way, source)

            return carry

        lax.fori_loop(0, 2, one, 0)

    loads = [
        pltpu.make_async_copy(source, target, load_sem.at[k])
        for k, (source, target) in enumerate(
            (
                (x_in, x_held),
                (gate_in, gates),
                (up_in, ups),
                (grad_in, grad_held),
                (down_in, downs),
            )
        )
    ]
    for load in loads:
        load.start()
    earliest = jnp.where(2 * level >= depth - 1, 0, depth - 1)

    def slot_of(way, source):
        return way + 2 * ((source + level) % 2)

    def compute(way, source):
        def need(*which):
            @pl.when(source == earliest)
            def _():
                for k in which:
                    loads[k].wait()

        need(0)
        slot = slot_of(way, source)
        x = x_held.at[source]
        logits = jnp.dot(x[...], router_ref[...], preferred_element_type=wide)
        lanes = lax.broadcasted_iota(jnp.int32, logits.shape, 1)
        logits = jnp.where(lanes < total, logits, FLOOR_SCORE)
        powers = jnp.exp(logits - jnp.max(logits, axis=-1, keepdims=True))
        probs = powers / jnp.sum(powers, axis=-1, keepdims=True)
        gate = jnp.sum(jnp.where(lanes == place, probs, 0.0), axis=-1, keepdims=True)

        def columns(start, size, slots):
            at = lanes_at(start, size)
            if start == 0:
                need(1)
            former_part = jnp.dot(x[...], gates[:, at], preferred_element_type=wide)
            if start == 0:
                need(2)
            latter_part = jnp.dot(x[...], ups[:, at], preferred_element_type=wide)
            if start == 0:
                need(3, 4)
            raw = dot_nt(grad_held[source], downs[at, :])
            sig = 1.0 / (1.0 + jnp.exp(-former_part))
            act = former_part * sig
            low = (act * latter_part).astype(hidden.dtype)
            hidden[:, at] = low
            low = low.astype(wide)
            hidden_held[source, :, at] = (low * gate).astype(hidden.dtype)
            grad = raw * gate
            d_gate = grad * latter_part * (sig + act * (1.0 - sig))
            gate_held[source, :, at] = d_gate.astype(hidden.dtype)
            up_held[source, :, at] = (grad * act).astype(hidden.dtype)
            return slots + jnp.sum(low * raw, axis=-1, keepdims=True)

        slots = jnp.zeros((PLANE * capacity, 1), wide)
        step_size = 640
        for start in range(0, inner, step_size):
            slots = columns(start, min(step_size, inner - start), slots)

        def blocks(value):
            return [value[m * capacity : (m + 1) * capacity] for m in range(PLANE)]

        former = source + 2 * (2 * way - 1)

        @pl.when((former >= 0) & (former < depth))
        def _():
            for offset in range(1, PLANE):
                for copy in rows_to(offset, slot, former):
                    copy.wait_send()

        for m, block in enumerate(blocks(slots)):
            spread = jnp.broadcast_to(block, (capacity, 128))
            scalars_sent[slot, m] = spread

            @pl.when(spot == m)
            def _():
                scalars[m, source] = spread

        def outward(n, carry):
            at = lanes_at(n * 1024, 1024)
            back = dot_nt(gate_held[source], gates[at, :]) + dot_nt(up_held[source], ups[at, :])
            for m, block in enumerate(blocks(back)):
                sent[slot, m, :, at] = block.astype(sent.dtype)

                @pl.when(spot == m)
                def _():
                    came[m, source, :, at] = block.astype(came.dtype)

            return carry

        lax.fori_loop(0, width // 1024, outward, 0)
        for offset in range(1, PLANE):
            for copy in rows_to(offset, slot, source):
                copy.start()

        def finally_out(n, carry):
            at = lanes_at(n * 1024, 1024)
            out = jnp.dot(hidden[...], downs[:, at], preferred_element_type=wide) * gate
            for m, block in enumerate(blocks(out)):
                y_stage[m, :, at] = block.astype(y_stage.dtype)
            return carry

        lax.fori_loop(0, width // 1024, finally_out, 0)
        writes = [
            pltpu.make_async_copy(y_stage, y_out.at[source], y_sem.at[0]),
            pltpu.make_async_copy(y_stage.at[spot], y_own.at[source, spot], y_sem.at[1]),
        ]
        for write in writes:
            write.start()
        for write in writes:
            write.wait()

    def wide_tiles(owner, k):
        at = pl.ds(pl.multiple_of((owner * wide_count + k) * wide_rows, wide_rows), wide_rows)
        x = whole(x_held[:, :, at])
        return dot_tn(x, whole(gate_held[...])), dot_tn(x, whole(up_held[...]))

    def tall_tile(owner, k):
        at = pl.ds(pl.multiple_of(k * tall_rows, tall_rows), tall_rows)
        over = pl.ds(pl.multiple_of(owner * tall_width, tall_width), tall_width)
        return dot_tn(whole(hidden_held[:, :, at]), whole(grad_held[:, :, over]))

    def wide_send(which, k):
        slot = k % 2
        return remote(
            give_wide(slot, which),
            take_wide(which, k),
            ws.at[slot, which],
            wr.at[which, k],
            other,
        )

    def tall_send(k):
        slot = k % 2
        return remote(give_tall(slot), take_tall(k), ts.at[slot], tr.at[k], other)

    def wide_write(which, k):
        target = (gate_out, up_out)[which]
        at = pl.ds(pl.multiple_of(k * wide_rows, wide_rows), wide_rows)
        return pltpu.make_async_copy(done_wide(which), target.at[at, :], wide_sem.at[which])

    def tall_write(k):
        slot = k % 2
        at = pl.ds(pl.multiple_of(k * tall_rows, tall_rows), tall_rows)
        return pltpu.make_async_copy(done_tall(slot), down_out.at[at, :], tall_sem.at[slot])

    def give_wide_tile(k):
        @pl.when(k >= 2)
        def _():
            for which in range(2):
                wide_send(which, k - 2).wait_send()

        for which, tile in enumerate(wide_tiles(1 - half, k)):
            give_wide(k % 2, which)[...] = tile.astype(gates.dtype)
            wide_send(which, k).start()

    def give_tall_tile(k):
        @pl.when(k >= 2)
        def _():
            tall_send(k - 2).wait_send()

        give_tall(k % 2)[...] = tall_tile(1 - half, k).astype(gates.dtype)
        tall_send(k).start()

    def keep_wide_tile(k):
        @pl.when(k >= 1)
        def _():
            for which in range(2):
                wide_write(which, k - 1).wait()

        for which, tile in enumerate(wide_tiles(half, k)):
            wide_send(which, k).wait_recv()
            tile = tile + take_wide(which, k)[...].astype(wide)
            done_wide(which)[...] = tile.astype(gates.dtype)
            wide_write(which, k).start()

    def keep_tall_tile(k):
        @pl.when(k >= 2)
        def _():
            tall_write(k - 2).wait()

        tile = tall_tile(half, k)
        tall_send(k).wait_recv()
        tile = tile + take_tall(k)[...].astype(wide)
        done_tall(k % 2)[...] = tile.astype(gates.dtype)
        tall_write(k).start()

    units = 2 * (wide_count + tall_count)
    bounds = (0, wide_count, wide_count + tall_count, units - tall_count, units)
    acts = (give_wide_tile, give_tall_tile, keep_wide_tile, keep_tall_tile)

    def fill(unit, carry):
        for act, low, high in zip(acts, bounds[:-1], bounds[1:]):

            @pl.when((unit >= low) & (unit < high))
            def _():
                act(unit - low)

        return carry

    def chain_out(source):
        up = jnp.where(source > level, 1, 0)
        step = 2 * up - 1
        slot = jnp.where(source == level - 1, depth, source)
        return remote(
            onward.at[up],
            incoming.at[slot],
            cs.at[source],
            cr.at[slot],
            (half, place + step * PLANE),
        )

    def chain_in(slot):
        block = incoming.at[slot]
        return remote(block, block, cs.at[0], cr.at[slot], (half, place))

    def prob_to(source):
        return remote(
            prob_send.at[source],
            prob_land.at[level],
            ps.at[source],
            pr.at[level],
            (half, source * PLANE + spot),
        )

    def prob_from(source):
        block = prob_land.at[source]
        return remote(block, block, ps.at[source], pr.at[source], (half, source * PLANE + spot))

    def add_incoming(slot):
        chain_in(slot).wait_recv()
        back_ref[...] += incoming[slot].astype(jnp.float32)

    def settle(way, source):
        load = shared_load(0, source)
        load.start()
        for offset in range(1, PLANE):
            for copy in rows_from(offset, source):
                copy.wait_recv()
        load.wait()

        def columns(n, carry):
            at = pl.ds(pl.multiple_of(n * 512, 512), 512)
            total = shared[0, :, at].astype(jnp.float32)
            for mate in range(PLANE):
                total = total + dot_tn(choose_ref[source, mate], came[mate, source, :, at])
            back_ref[:, at] = total
            return carry

        lax.fori_loop(0, width // 512, columns, 0)
        lines = lax.broadcasted_iota(jnp.int32, (8, tokens), 0)
        probs = jnp.zeros((8, tokens), jnp.float32)
        for mate in range(PLANE):
            part = lax.dot_general(
                scalars[mate, source],
                choose_ref[source, mate].astype(jnp.float32),
                (((0,), (0,)), ((), ())),
                preferred_element_type=jnp.float32,
                precision=lax.Precision.HIGHEST,
            )
            probs = jnp.where(lines == mate, part[:8], probs)

        @pl.when((source >= level) & (level > 0))
        def _():
            add_incoming(source)

        @pl.when((source < level) & (level < depth - 1))
        def _():
            add_incoming(source)

        @pl.when((source == level) & (level < depth - 1))
        def _():
            add_incoming(depth)

        @pl.when(source == level)
        def _():
            prob_land[level] = probs

        @pl.when(source != level)
        def _():
            prob_send[source] = probs
            prob_to(source).start()
            former = source + 2 * way - 1

            @pl.when((former >= 0) & (former < depth))
            def _():
                chain_out(former).wait_send()

            onward[way] = back_ref[...].astype(onward.dtype)
            chain_out(source).start()

    def step(i, carry):
        s = depth - 1 - i
        each_way(s, compute)

        @pl.when(i > 0)
        def _():
            each_way(s + 1, settle)

        return carry

    lax.fori_loop(0, depth, step, 0)
    pl.semaphore_signal(free_sem, inc=1, device_id=other, device_id_type=MESH)
    pl.semaphore_wait(free_sem, 1)
    lax.fori_loop(0, units, fill, 0)
    each_way(0, settle)
    for which in range(2):
        wide_write(which, wide_count - 1).wait()
        for k in (wide_count - 2, wide_count - 1):
            wide_send(which, k).wait_send()
    for k in (tall_count - 2, tall_count - 1):
        tall_write(k).wait()
        tall_send(k).wait_send()

    def finish(source, carry):
        ahead = jnp.where(source > level, 1, 0)
        near = (source >= level - 1) & (source <= level + 2)

        @pl.when(near)
        def _():
            for offset in range(1, PLANE):
                for copy in rows_to(offset, slot_of(ahead, source), source):
                    copy.wait_send()

        @pl.when((source == level - 1) | (source == level + 1))
        def _():
            chain_out(source).wait_send()

        @pl.when(source != level)
        def _():
            prob_to(source).wait_send()
            prob_from(source).wait_recv()

        prob_ref[source] = prob_land[source]
        return carry

    lax.fori_loop(0, depth, finish, 0)


def run_and_return(rows, grads, weights, router, choose, shared_back, total):
    depth, _, capacity, width = rows.shape
    tokens = choose.shape[3]
    inner = weights[0].shape[1]
    tile = PLANE * capacity
    wide_count, tall_count = width // 512, inner // 128
    semaphores = pltpu.SemaphoreType.DMA
    low, wide = rows.dtype, jnp.float32
    anywhere = pl.BlockSpec(memory_space=pl.ANY)
    local = pl.BlockSpec(memory_space=pltpu.VMEM)
    return pl.pallas_call(
        functools.partial(run_and_return_kernel, depth, total),
        out_shape=[
            jax.ShapeDtypeStruct((tokens, width), wide),
            jax.ShapeDtypeStruct((depth, 8, tokens), wide),
            jax.ShapeDtypeStruct((width // 2, inner), low),
            jax.ShapeDtypeStruct((width // 2, inner), low),
            jax.ShapeDtypeStruct((inner, width // 2), low),
            jax.ShapeDtypeStruct(rows.shape, low),
            jax.ShapeDtypeStruct(rows.shape, low),
        ],
        in_specs=[anywhere] * 5 + [local, local, anywhere],
        out_specs=[local, local] + [anywhere] * 5,
        scratch_shapes=[
            pltpu.VMEM((PLANE, depth, capacity, width), low),
            pltpu.VMEM((PLANE, depth, capacity, 128), wide),
            pltpu.VMEM((1, tokens, width), low),
            pltpu.VMEM((2, tokens, width), low),
            pltpu.VMEM((depth + 1, tokens, width), low),
            pltpu.VMEM((depth, 8, tokens), wide),
            pltpu.VMEM((depth, 8, tokens), wide),
            pltpu.VMEM((depth, tile, width), low),
            pltpu.VMEM((depth, tile, inner), low),
            pltpu.VMEM((depth, tile, inner), low),
            pltpu.VMEM((depth, tile, inner), low),
            pltpu.VMEM((depth, tile, width), low),
            pltpu.VMEM((tile, inner), low),
            pltpu.VMEM(weights[0].shape, low),
            pltpu.VMEM(weights[1].shape, low),
            pltpu.VMEM(weights[2].shape, low),
            pltpu.VMEM((4, PLANE, capacity, width), low),
            pltpu.VMEM((4, PLANE, capacity, 128), wide),
            pltpu.VMEM((PLANE, capacity, width), low),
            semaphores((PLANE, depth)),
            semaphores((PLANE, depth)),
            semaphores((PLANE, depth)),
            semaphores((PLANE, depth)),
            semaphores((5,)),
            semaphores((2,)),
            semaphores((depth,)),
            semaphores((depth + 1,)),
            semaphores((depth,)),
            semaphores((depth,)),
            semaphores((2, 2)),
            semaphores((2, wide_count)),
            semaphores((2,)),
            semaphores((tall_count,)),
            semaphores((2,)),
            semaphores((2,)),
            semaphores((2,)),
            pltpu.SemaphoreType.REGULAR,
        ],
        compiler_params=pltpu.CompilerParams(
            collective_id=7, has_side_effects=True, vmem_limit_bytes=63 * MEBIBYTE
        ),
        cost_estimate=LONG,
    )(
        rows.reshape(depth, tile, width),
        grads.reshape(depth, tile, width),
        *weights,
        router,
        choose,
        shared_back,
    )


def finish_kernel(layout, *refs):
    piece, moved, residual, added, sdown, token = refs[:6]
    query_ref, down_ref, up_ref, out_ref, gate_ref, shared_up_ref = refs[6:12]
    sdown_ref, output_ref, token_ref = refs[12:]
    entry_width, out_start = layout
    rows = piece.shape[0]
    nope_width = HEADS * NOPE
    query_width = HEADS * (NOPE + ROPE)
    low_half = lax.broadcasted_iota(jnp.int32, (rows, 128), 1) < ROPE
    for pair in range(HEADS // 2):
        start = pair * 2 * NOPE
        rope = piece[:, nope_width + pair * 128 : nope_width + (pair + 1) * 128]
        latter = pltpu.roll(piece[:, start + NOPE : start + 2 * NOPE], NOPE // 2, 1)
        at = pair * 2 * (NOPE + ROPE)
        query_ref[:, at : at + 128] = piece[:, start : start + NOPE]
        query_ref[:, at + 128 : at + 256] = jnp.where(low_half, rope, latter)
        query_ref[:, at + 256 : at + 384] = jnp.where(low_half, latter, rope)
    down_ref[...] = piece[:, query_width : query_width + down_ref.shape[1]]
    up_rows = up_ref.shape[0]
    span = out_start - entry_width
    for k in range(rows // up_rows):
        up_ref[:, k * span : (k + 1) * span] = piece[
            k * up_rows : (k + 1) * up_rows, entry_width:out_start
        ]
    out_ref[...] = piece[:, out_start : out_start + out_ref.shape[1]]
    depth = moved.shape[0]
    share = gate_ref.shape[1] // (2 * depth)
    padded = moved.shape[2] // 4
    for which, target in enumerate((gate_ref, shared_up_ref)):
        target[...] = jnp.concatenate(
            [
                moved[t, :, (2 * which + k) * padded : (2 * which + k + 1) * padded].astype(
                    jnp.float32
                )[:, :share]
                for k in range(2)
                for t in range(depth)
            ],
            axis=1,
        )
    sdown_ref[...] = sdown[...].astype(jnp.float32)
    output_ref[...] = (residual[...] + added[...].astype(jnp.float32)).astype(output_ref.dtype)
    token_ref[...] = token[...]


def finish(piece, moved, residual, added, sdown, token, shapes, layout):
    wide = jnp.float32
    local = pl.BlockSpec(memory_space=pltpu.VMEM)
    spans = list(shapes) + [sdown.shape]
    return pl.pallas_call(
        functools.partial(finish_kernel, layout),
        out_shape=[jax.ShapeDtypeStruct(shape, wide) for shape in spans]
        + [
            jax.ShapeDtypeStruct(residual.shape, added.dtype),
            jax.ShapeDtypeStruct(token.shape, wide),
        ],
        in_specs=[local] * 6,
        out_specs=[local] * 9,
        compiler_params=pltpu.CompilerParams(vmem_limit_bytes=48 * MEBIBYTE),
    )(piece, moved, residual, added, sdown, token)


def body(
    tokens,
    segments,
    routes,
    slot_index,
    cotangent,
    attention_norm,
    query_weight,
    latent_down,
    latent_norm,
    latent_up,
    output_weight,
    feed_norm,
    router_weight,
    shared_gate,
    shared_up,
    shared_down,
    expert_gate,
    expert_up,
    expert_down,
):
    row_count = tokens.shape[1]
    expert_total = lax.axis_size("expert")
    depth = expert_total // PLANE
    plane, line = groups(expert_total)
    place = lax.axis_index("expert")
    level = place // PLANE
    device_half = lax.axis_index("fsdp")
    capacity = row_count * TOPK // expert_total
    line_rows = depth * row_count
    inputs = tokens[0].astype(jnp.float32)

    part_rows = query_weight.shape[0]
    gain_width = attention_norm.shape[0]
    latent_width = latent_norm.shape[0]
    small = jnp.concatenate([attention_norm, latent_norm, feed_norm, router_weight.reshape(-1)])
    cuts = [
        0,
        gain_width,
        gain_width + latent_width,
        2 * gain_width + latent_width,
        small.shape[0],
    ]
    small = jnp.pad(small, (0, 128 * part_rows - small.shape[0])).reshape(part_rows, 128)
    query_width = query_weight.shape[1]
    down_width = latent_down.shape[1]
    entry_width = query_width + down_width + (-down_width) % 128
    up_width = HEADS * (NOPE + VALUE)
    quarters = part_rows // latent_up.shape[0]
    by_head = query_weight.reshape(part_rows, HEADS, NOPE + ROPE)
    packed = jnp.concatenate(
        [
            by_head[..., :NOPE].reshape(part_rows, -1),
            by_head[..., NOPE:].reshape(part_rows, -1),
            jnp.pad(latent_down, ((0, 0), (0, (-down_width) % 128))),
            latent_up.reshape(latent_up.shape[0], quarters, -1)
            .transpose(1, 0, 2)
            .reshape(part_rows, -1),
            output_weight,
            small,
        ],
        axis=1,
    )
    cut = packed.shape[1] // 256 * 128
    route_rows = routes[0]
    slot_rows = slot_index[0]
    target = jnp.where(
        slot_rows >= 0, route_rows * capacity + slot_rows, expert_total * capacity
    )
    target = jnp.pad(target, ((0, 0), (0, 8 - TOPK)), constant_values=expert_total * capacity).T
    shared_width = shared_gate.shape[1] // (2 * depth)
    shared_both = jnp.stack([shared_gate, shared_up]).reshape(
        2, part_rows, 2, depth, shared_width
    )
    shared_both = shared_both.transpose(3, 1, 0, 2, 4)
    spare = (-shared_width) % 128
    shared_both = jnp.pad(shared_both, ((0, 0),) * 4 + ((0, spare),))
    shared_both = shared_both.reshape(depth, part_rows, -1)
    packed_full, grad_line, target_line, shared_full, sdown_full = gather_rows(
        packed, cotangent[0], target, shared_both, shared_down, cuts_of(packed.shape[1], GROUPS)
    )
    shared_full = shared_full.reshape(D, -1)
    sdown_full = sdown_full.reshape(2, shared_width, D)
    expert_gate_full = lax.all_gather(expert_gate[0], "fsdp", axis=0, tiled=True)
    expert_up_full = lax.all_gather(expert_up[0], "fsdp", axis=0, tiled=True)
    expert_down_full = lax.all_gather(expert_down[0], "fsdp", axis=1, tiled=True)
    packed_full, grad_line, target_line, expert_gate_full, expert_up_full, expert_down_full = (
        lax.optimization_barrier(
            (
                packed_full,
                grad_line,
                target_line,
                expert_gate_full,
                expert_up_full,
                expert_down_full,
            )
        )
    )
    up_rows = latent_up.shape[0]
    up_parts = packed_full.reshape(2 * expert_total, quarters, up_rows, -1)
    if up_rows % 16 == 0:
        up_full = up_parts
        ups_shape = (quarters, 2 * expert_total, up_rows, up_width // quarters)
    else:
        up_full = up_parts[..., entry_width : -128 - D].transpose(1, 0, 2, 3)
        up_full = up_full.reshape(quarters, 1, LATENT, -1)
        ups_shape = up_full.shape
    small_full = packed_full[:, -128:].reshape(2 * expert_total, -1)
    gain_one, gain_latent, gain_feed, router_full = (
        small_full[:, cuts[0] : cuts[1]].reshape(-1),
        small_full[:, cuts[1] : cuts[2]].reshape(-1),
        small_full[:, cuts[2] : cuts[3]].reshape(-1),
        small_full[:, cuts[3] : cuts[4]].reshape(-1, expert_total),
    )

    slot_names = level * PLANE * capacity + jnp.arange(PLANE * capacity)
    hits = target_line[:, :TOPK, None, :] == slot_names[None, None, :, None]
    choose_rows = jnp.any(hits, axis=1).astype(jnp.bfloat16)

    choose_slots = choose_rows.reshape(depth, PLANE, capacity, row_count)
    grad_line = grad_line.reshape(depth, row_count, D)

    cosine, sine_table = rotary_table(row_count, device_half * row_count, ROPE)
    tables = (
        jnp.concatenate([cosine] * 4, axis=1),
        jnp.concatenate([-sine_table, sine_table] * 2, axis=1),
    )
    gain_first = gain_one.astype(jnp.float32)
    latent_gain = gain_latent.astype(jnp.float32)
    feed_gain = gain_feed.astype(jnp.float32)
    query_place = device_half * row_count + jnp.arange(row_count)
    key_place = (device_half - 1) * row_count + jnp.arange(2 * row_count)
    padded_segments = jnp.concatenate([jnp.full((row_count,), -1, jnp.int32), segments[0]])
    key_segment = lax.dynamic_slice_in_dim(padded_segments, device_half * row_count, 2 * row_count)
    query_segment = lax.dynamic_slice_in_dim(segments[0], device_half * row_count, row_count)
    visible = (key_place[None, :] <= query_place[:, None]) & (
        key_segment[None, :] == query_segment[:, None]
    )
    mask = visible.astype(jnp.float32)
    layout = (entry_width, packed.shape[1] - 128 - D)
    (
        normed_low,
        residual,
        mixed_low,
        queries,
        latent,
        compressed,
        expanded,
        keys_rope,
        log_total,
        mixed_heads,
        grad_rows,
    ) = attend(
        tokens[0],
        packed_full,
        up_full,
        ups_shape,
        (gain_first[None], latent_gain[None], feed_gain[None]),
        tables,
        mask,
        choose_slots,
        grad_line,
        layout,
    )
    mixed_rows, shared_out, shared_back, shared_grad, sdown_grad, grad_rows = dispatch(
        mixed_low, choose_slots, grad_line, shared_full, sdown_full, grad_rows
    )
    shared_out = shared_out.reshape(line_rows, D)
    router_wide = jnp.pad(router_full, ((0, 0), (0, (-expert_total) % 128)))
    shared_summed = lax.psum_scatter(
        shared_grad, "expert", scatter_dimension=0, axis_index_groups=plane, tiled=True
    )[0]
    sdown_summed = lax.psum_scatter(
        sdown_grad, "expert", scatter_dimension=0, axis_index_groups=plane, tiled=True
    )
    weights = (expert_gate_full, expert_up_full, expert_down_full)
    if depth <= PLANE:
        (
            back_and_shared,
            prob_parts,
            expert_gate_piece,
            expert_up_piece,
            expert_down_piece,
            expert_out,
            own_out,
        ) = run_and_return(
            mixed_rows, grad_rows, weights, router_wide, choose_slots, shared_back, expert_total
        )
    else:
        flat_rows = mixed_rows.reshape(expert_total * capacity, D)
        flat_grads = grad_rows.reshape(expert_total * capacity, D)
        hidden_scaled, gate_low, up_low, input_grad, expert_out, slot_grad = run_expert(
            flat_rows, flat_grads, *weights, router_wide, expert_total
        )
        (
            back_and_shared,
            prob_parts,
            expert_gate_piece,
            expert_up_piece,
            expert_down_piece,
        ) = give_back(
            input_grad.reshape(mixed_rows.shape),
            slot_grad.reshape(depth, PLANE, capacity, 128),
            choose_slots,
            shared_back,
            [flat_rows, gate_low, up_low, hidden_scaled, flat_grads],
        )
        own_out = expert_out
    prob_grad = prob_parts[:, :PLANE].reshape(expert_total, row_count).T
    probabilities = jax.nn.softmax(matmul(mixed_low, router_full), axis=-1)
    prob_grad = prob_parts[:, :PLANE].reshape(expert_total, row_count).T
    logit_low = (
        probabilities * (prob_grad - jnp.sum(probabilities * prob_grad, axis=-1, keepdims=True))
    ).astype(jnp.bfloat16)
    router_grad = left_matmul(mixed_low, logit_low)
    (
        token_grad,
        up_weight_grad,
        latent_gain_grad,
        first_gain_grad,
        feed_gain_grad,
        entry_grad,
        output_grad,
        returned,
    ) = attend_back(
        back_and_shared,
        packed_full,
        up_full,
        ups_shape,
        (
            queries,
            expanded,
            keys_rope,
            log_total,
            latent,
            compressed,
            normed_low,
            mixed_heads,
            tokens[0],
            residual,
            cotangent[0],
            jnp.pad(logit_low, ((0, 0), (0, (-expert_total) % 128))),
            router_wide,
        ),
        (latent_gain[None], gain_first[None], feed_gain[None]),
        tables,
        mask,
        (expert_out.reshape(mixed_rows.shape), own_out.reshape(mixed_rows.shape)),
        (shared_summed, sdown_summed),
        layout,
    )
    if up_rows % 16 != 0:
        up_weight_grad = up_weight_grad.reshape(quarters, 2 * expert_total, up_rows, -1)
        up_weight_grad = up_weight_grad.transpose(1, 0, 2, 3)
    latent_gain_grad = latent_gain_grad[0]
    first_gain_grad = first_gain_grad[0]
    feed_gain_grad = feed_gain_grad[0]
    routed = jnp.einsum(
        "zst,zsd->ztd",
        choose_rows,
        returned.reshape(depth, PLANE * capacity, D),
        preferred_element_type=jnp.float32,
    )
    routed_and_shared = lax.psum_scatter(
        (routed.reshape(line_rows, D) + shared_out).astype(jnp.bfloat16),
        "expert",
        scatter_dimension=0,
        axis_index_groups=line,
        tiled=True,
    )

    small_grad = jnp.concatenate(
        [
            first_gain_grad.reshape(-1, gain_width),
            latent_gain_grad.reshape(-1, latent_width),
            feed_gain_grad.reshape(-1, gain_width),
            router_grad.reshape(2 * expert_total, -1),
        ],
        axis=1,
    )
    small_grad = jnp.pad(small_grad, ((0, 0), (0, 128 * part_rows - small_grad.shape[1])))
    packed_piece, shared_back_moved = reduce_rows(
        [
            entry_grad,
            up_weight_grad.reshape(2 * expert_total * part_rows, -1),
            output_grad,
            small_grad.astype(jnp.bfloat16).reshape(-1, 128),
        ],
        shared_summed,
        cut,
    )
    small_piece = packed_piece[:, -128:].reshape(-1)
    (
        query_piece,
        down_piece,
        up_piece,
        output_piece,
        sgate_piece,
        sup_piece,
        sdown_piece,
        output,
        token_grad,
    ) = finish(
        packed_piece,
        shared_back_moved,
        residual,
        routed_and_shared,
        sdown_summed,
        token_grad,
        (
            query_weight.shape,
            latent_down.shape,
            latent_up.shape,
            output_weight.shape,
            shared_gate.shape,
            shared_up.shape,
        ),
        layout,
    )

    return (
        output[None],
        token_grad[None],
        small_piece[cuts[0] : cuts[1]],
        query_piece,
        down_piece,
        small_piece[cuts[1] : cuts[2]],
        up_piece,
        output_piece,
        small_piece[cuts[2] : cuts[3]],
        small_piece[cuts[3] : cuts[4]].reshape(gain_width, expert_total),
        sgate_piece,
        sup_piece,
        sdown_piece,
        expert_gate_piece.astype(jnp.float32)[None],
        expert_up_piece.astype(jnp.float32)[None],
        expert_down_piece.astype(jnp.float32)[None],
    )


def solution(mesh):
    return jax.shard_map(
        body,
        mesh=mesh,
        in_specs=(
            P("expert", "fsdp", None),
            P("expert", None),
            P("expert", "fsdp", None),
            P("expert", "fsdp", None),
            P("expert", "fsdp", None),
            P(("fsdp", "expert")),
            P(("fsdp", "expert"), None),
            P(("fsdp", "expert"), None),
            P(("fsdp", "expert")),
            P(("fsdp", "expert"), None),
            P(("fsdp", "expert"), None),
            P(("fsdp", "expert")),
            P(("fsdp", "expert"), None),
            P(("fsdp", "expert"), None),
            P(("fsdp", "expert"), None),
            P(("fsdp", "expert"), None),
            P("expert", "fsdp", None),
            P("expert", "fsdp", None),
            P("expert", None, "fsdp"),
        ),
        out_specs=(
            P("expert", "fsdp", None),
            P("expert", "fsdp", None),
            P(("fsdp", "expert")),
            P(("fsdp", "expert"), None),
            P(("fsdp", "expert"), None),
            P(("fsdp", "expert")),
            P(("fsdp", "expert"), None),
            P(("fsdp", "expert"), None),
            P(("fsdp", "expert")),
            P(("fsdp", "expert"), None),
            P(("fsdp", "expert"), None),
            P(("fsdp", "expert"), None),
            P(("fsdp", "expert"), None),
            P("expert", "fsdp", None),
            P("expert", "fsdp", None),
            P("expert", None, "fsdp"),
        ),
        check_vma=False,
    )
```
